32 devices in a mesh: dp: 8 (over z, y), tensor: 4 (over x, core).
Axes of the slice: x: 2, y: 2, z: 4, core: 2. Of those that a mesh axis runs over, the one named last changes fastest.
Arguments:
- tokens: bfloat16 [2, 1536, 2048], P(None, ('dp', 'tensor')), may hold values from -6 to 6
- depth: int32 [2, 1536], P(None, 'dp'), may hold values from 1 to 3, as said below
- lengths: int32 [2, 8, 3], P(None, 'dp'), may hold values from 1 to 128, 192 in all within a row
- cotangent: bfloat16 [2, 1536, 2048], P(None, ('dp', 'tensor')), may hold values from -6 to 6
- w_query: bfloat16 [2048, 2048], P('dp', 'tensor'), may hold values from -0.125 to 0.125
- w_key: bfloat16 [2048, 256], P('dp', 'tensor'), may hold values from -0.125 to 0.125
- w_value: bfloat16 [2048, 256], P('dp', 'tensor'), may hold values from -0.125 to 0.125
- w_out: bfloat16 [2048, 2048], P('tensor', 'dp'), may hold values from -0.75 to 0.75
- w_gate: bfloat16 [2048, 5632], P('dp', 'tensor'), may hold values from -0.125 to 0.125
- w_up: bfloat16 [2048, 5632], P('dp', 'tensor'), may hold values from -0.125 to 0.125
- w_down: bfloat16 [5632, 2048], P('tensor', 'dp'), may hold values from -0.15625 to 0.15625
- attn_gain: float32 [2048], P(('dp', 'tensor')), may hold values from 0.5 to 1.5
- mlp_gain: float32 [2048], P(('dp', 'tensor')), may hold values from 0.5 to 1.5
Outputs:
- activations: bfloat16 [2, 1536, 2048], P(None, ('dp', 'tensor'))
- tokens_grad: float32 [2, 1536, 2048], P(None, ('dp', 'tensor'))
- w_query_grad: float32 [2048, 2048], P('dp', 'tensor')
- w_key_grad: float32 [2048, 256], P('dp', 'tensor')
- w_value_grad: float32 [2048, 256], P('dp', 'tensor')
- w_out_grad: float32 [2048, 2048], P('tensor', 'dp')
- w_gate_grad: float32 [2048, 5632], P('dp', 'tensor')
- w_up_grad: float32 [2048, 5632], P('dp', 'tensor')
- w_down_grad: float32 [5632, 2048], P('tensor', 'dp')
- attn_gain_grad: float32 [2048], P(('dp', 'tensor'))
- mlp_gain_grad: float32 [2048], P(('dp', 'tensor'))
The draws below stay inside these ranges and needn't reach their ends.
Inputs may be any that keep to these rules, and one draw needn't show every extreme that they name: Within each micro-batch and the 192 rows of each dp index, at most 144 rows have depth 2 or more and at most 72 have depth 3; in every micro-batch some dp index has exactly 144 and some exactly 72.
All inputs are finite; a program needn't handle non-finite values.
Results may differ from the reference program's by a relative error of at most 0.035.
Values may be sent and summed in bfloat16 or wider, within the bound.
A program may use at most 256 MiB of HBM per device.

```python
import math
import jax
import jax.numpy as jnp
import numpy as np
from jax import lax

D = 2048
HQ = 32
KVH = 4
HS = 64
FF = 5632
MB = 2
RECUR = 3
NDOC = 3
TOK_DEV = 192
DEPTH_TWO_LIMIT = 144
DEPTH_THREE_LIMIT = 72
DOC_MOST = 128
TOKENS = 1536
N_DP = 8


def draw_depth(key, part):
    key = jax.random.fold_in(key, 11)
    packs = TOKENS // TOK_DEV
    ranks = jnp.arange(TOK_DEV, dtype=jnp.int32)

    def one_batch(batch_key):
        keys = jax.random.split(batch_key, 5)
        deep = jax.random.randint(keys[0], (packs,), DEPTH_TWO_LIMIT // 2, DEPTH_TWO_LIMIT + 1)
        deep = deep.at[jax.random.randint(keys[1], (), 0, packs)].set(DEPTH_TWO_LIMIT)
        deepest = jax.random.randint(keys[2], (packs,), DEPTH_THREE_LIMIT // 2, DEPTH_THREE_LIMIT + 1)
        deepest = deepest.at[jax.random.randint(keys[3], (), 0, packs)].set(DEPTH_THREE_LIMIT)
        pack_keys = jax.random.split(keys[4], packs)

        def one_pack(pack_key, second, third):
            order = jax.random.permutation(pack_key, TOK_DEV)
            levels = 1 + (ranks < second).astype(jnp.int32) + (ranks < third).astype(jnp.int32)
            return jnp.zeros((TOK_DEV,), jnp.int32).at[order].set(levels)
        return jax.vmap(one_pack)(pack_keys, deep, deepest).reshape(TOKENS)
    return jax.vmap(one_batch)(jax.random.split(key, MB)).astype(jnp.int32)


def shard_levels(key, extent, cuts, smallest, top_value):
    level, own = 1.0, jax.random.fold_in(key, 6)
    for position, parts in cuts:
        heights = jnp.exp(jax.random.uniform(jax.random.fold_in(own, position), (parts,), jnp.float32, smallest / len(cuts), top_value / len(cuts)))
        level = level * jnp.repeat(heights, extent[position] // parts).reshape([-1 if axis == position else 1 for axis in range(len(extent))])
    return level


def split_up(number_of, total, limit, lean):
    portions = [(1 << 20) // math.isqrt(grade ** lean) + 1 for grade in range(2, number_of + 1)]
    spare, counts = total - limit - (number_of - 1), [1] * (number_of - 1)
    while spare > 0:
        free = [i for i in range(number_of - 1) if counts[i] < limit]
        pool, remaining = sum([portions[i] for i in free]), spare
        for i in free:
            extra = min(limit - counts[i], max(1, remaining * portions[i] // pool), spare)
            counts[i] = counts[i] + extra
            spare = spare - extra
    return np.array([limit] + counts)


def uneven(own_key, count, total, bound, lean):
    if count == 2:
        one = jax.random.randint(own_key, (), max(1, total - bound), min(bound, total - 1) + 1)
        return jnp.stack([one, total - one])
    tallies = jnp.asarray(split_up(count, total, bound, lean), jnp.int32)
    pairs = (count - 1) // 2
    giver, receiver = tallies[1:1 + 2 * pairs:2], tallies[2:2 + 2 * pairs:2]
    room = jnp.minimum(giver - 1, bound - receiver)
    shifted = jax.random.randint(jax.random.fold_in(own_key, 1), (pairs,), 0, 1 << 20) % (room + 1)
    tallies = tallies.at[1:1 + 2 * pairs:2].set(giver - shifted).at[2:2 + 2 * pairs:2].set(receiver + shifted)
    return tallies[jax.random.permutation(jax.random.fold_in(own_key, 2), count)]


def normal_values(key, shape, deviation, reach, shards=(), held_as=jnp.bfloat16):
    entries = deviation * jax.random.normal(key, shape, jnp.float32)
    if shards:
        entries = entries * shard_levels(key, shape, shards, -0.22, 0.18)
    return jnp.clip(entries, -reach, reach).astype(held_as)


def setup_inputs(seed: int = 0) -> dict:
    splits = jax.random.split(jax.random.key(seed), 14)
    tokens = normal_values(splits[0], (MB, TOKENS, D), 1.0, 6.0, ((1, 32),))
    depth = draw_depth(jax.random.fold_in(splits[13], 71), 0)
    lengths = jax.vmap(lambda own: uneven(own, NDOC, TOK_DEV, DOC_MOST, 2))(jax.random.split(splits[2], MB * N_DP)).reshape((MB, N_DP, NDOC)).astype(jnp.int32)
    cotangent = normal_values(splits[3], (MB, TOKENS, D), 1.0, 6.0, ((1, 32),))
    w_query = normal_values(splits[4], (D, HQ * HS), D ** -0.5, 0.125, ((0, 8), (1, 4)))
    w_key = normal_values(splits[5], (D, KVH * HS), D ** -0.5, 0.125, ((0, 8), (1, 4)))
    w_value = normal_values(splits[6], (D, KVH * HS), D ** -0.5, 0.125, ((0, 8), (1, 4)))
    w_out = normal_values(splits[7], (HQ * HS, D), (HQ * HS // 32) ** -0.5, 0.75, ((0, 4), (1, 8)))
    w_gate = normal_values(splits[8], (D, FF), D ** -0.5, 0.125, ((0, 8), (1, 4)))
    w_up = normal_values(splits[9], (D, FF), D ** -0.5, 0.125, ((0, 8), (1, 4)))
    w_down = normal_values(splits[10], (FF, D), (FF // 4) ** -0.5, 0.15625, ((0, 4), (1, 8)))
    attn_gain = jnp.clip(1.0 + 0.1 * jax.random.normal(splits[11], (D,), jnp.float32), 0.5, 1.5)
    mlp_gain = jnp.clip(1.0 + 0.1 * jax.random.normal(splits[12], (D,), jnp.float32), 0.5, 1.5)
    return dict(tokens=tokens, depth=depth, lengths=lengths, cotangent=cotangent, w_query=w_query, w_key=w_key, w_value=w_value, w_out=w_out, w_gate=w_gate, w_up=w_up, w_down=w_down, attn_gain=attn_gain, mlp_gain=mlp_gain)


HIGHEST = lax.Precision.HIGHEST

@jax.custom_vjp
def low(v):
    return lax.optimization_barrier(v.astype(jnp.bfloat16)).astype(jnp.float32)

@jax.custom_vjp
def low_back(v):
    return v

def low_keep(v):
    return (low(v), None)

def low_pass(kept, grad):
    return (grad,)

def back_keep(v):
    return (v, None)

def back_low(kept, grad):
    return (low(grad),)
low.defvjp(low_keep, low_pass)
low_back.defvjp(back_keep, back_low)

def matmul(left, right):
    return jnp.dot(left, right, precision=HIGHEST, preferred_element_type=jnp.float32)

def normalize(hidden, gain):
    inverse = lax.rsqrt(lax.optimization_barrier(jnp.mean(hidden * hidden, axis=-1, keepdims=True)) + 1e-05)
    return hidden * inverse * gain

def rotate(values, cosine, sine):
    half = values.shape[-1] // 2
    turned = jnp.concatenate([-values[..., half:], values[..., :half]], axis=-1)
    return values * cosine + turned * sine

def layout(lengths_row):
    rows = jnp.arange(TOK_DEV, dtype=jnp.int32)
    ends = jnp.cumsum(lengths_row).astype(jnp.int32)
    starts = (ends - lengths_row).astype(jnp.int32)
    member = ((rows[:, None] >= starts[None, :]) & (rows[:, None] < ends[None, :])).astype(jnp.int32)
    document = lax.optimization_barrier(jnp.sum(member * jnp.arange(NDOC, dtype=jnp.int32)[None, :], axis=1)).astype(jnp.int32)
    offset = (rows - lax.optimization_barrier(jnp.sum(member * starts[None, :], axis=1))).astype(jnp.int32)
    return (document, offset)

def tables(offset):
    freqs = 10000.0 ** (-jnp.arange(0, HS, 2).astype(jnp.float32) / HS)
    angles = offset.astype(jnp.float32)[:, None] * freqs[None, :]
    angles = jnp.concatenate([angles, angles], axis=-1)
    return (jnp.cos(angles), jnp.sin(angles))

def pack_forward(params, inputs):
    w_query, w_key, w_value, w_out, w_gate, w_up, w_down, attn_gain, mlp_gain = params
    hidden, depth_row, lengths_row = inputs
    document, offset = layout(lengths_row)
    cosine, sine = tables(offset)
    cosine = cosine[:, None, :]
    sine = sine[:, None, :]
    rows = jnp.arange(TOK_DEV, dtype=jnp.int32)
    causal = (document[:, None] == document[None, :]) & (rows[None, :] <= rows[:, None])
    diagonal = rows[:, None] == rows[None, :]
    group = HQ // KVH
    scale = HS ** (-0.5)
    for recursion_level in range(1, RECUR + 1):
        active = depth_row >= recursion_level
        gate_row = active.astype(jnp.float32)[:, None]
        allowed = causal & active[None, :] | diagonal
        normed = low(normalize(hidden, attn_gain))
        query = low(rotate(low_back(matmul(normed, w_query)).reshape(TOK_DEV, HQ, HS), cosine, sine))
        key = low(rotate(low_back(matmul(normed, w_key)).reshape(TOK_DEV, KVH, HS), cosine, sine))
        value = low(low_back(matmul(normed, w_value))).reshape(TOK_DEV, KVH, HS)
        query = query.reshape(TOK_DEV, KVH, group, HS)
        attention_scores = low_back(jnp.einsum('ckgd,skd->kgcs', query, key, precision=HIGHEST) * scale)
        attention_scores = jnp.where(allowed[None, None], attention_scores, -1e+30)
        shares = jax.nn.softmax(attention_scores, axis=-1)
        attended = jnp.einsum('kgcs,skd->ckgd', low(shares), value, precision=HIGHEST)
        attended = low(low_back(attended.reshape(TOK_DEV, HQ * HS)))
        hidden = hidden + gate_row * low_back(matmul(attended, w_out))
        mixed = low(normalize(hidden, mlp_gain))
        gate = low_back(matmul(mixed, w_gate))
        upward = low_back(matmul(mixed, w_up))
        product = low(jax.nn.silu(gate) * upward)
        hidden = hidden + gate_row * low_back(matmul(product, w_down))
    return hidden

def reference(tokens, depth, lengths, cotangent, w_query, w_key, w_value, w_out, w_gate, w_up, w_down, attn_gain, mlp_gain):
    packs = TOKENS // TOK_DEV
    flat_tokens = tokens.astype(jnp.float32).reshape(MB * packs, TOK_DEV, D)
    flat_depth = depth.reshape(MB * packs, TOK_DEV)
    flat_lengths = lengths.reshape(MB * packs, NDOC)
    params = (w_query.astype(jnp.float32), w_key.astype(jnp.float32), w_value.astype(jnp.float32), w_out.astype(jnp.float32), w_gate.astype(jnp.float32), w_up.astype(jnp.float32), w_down.astype(jnp.float32), attn_gain.astype(jnp.float32), mlp_gain.astype(jnp.float32))

    def forward(inputs, *weights):
        stepper = jax.checkpoint(lambda item: pack_forward(weights, item))
        return lax.map(stepper, (inputs, flat_depth, flat_lengths))
    output, pullback = jax.vjp(forward, flat_tokens, *params)
    grads = pullback(cotangent.astype(jnp.float32).reshape(MB * packs, TOK_DEV, D))
    return (output.reshape(MB, TOKENS, D).astype(jnp.bfloat16), grads[0].reshape(MB, TOKENS, D), grads[1], grads[2], grads[3], grads[4], grads[5], grads[6], grads[7], grads[8], grads[9])
```

```python
import functools

import jax
import jax.numpy as jnp
import numpy as np
from jax import lax
from jax.experimental import pallas as pl
from jax.experimental.pallas import tpu as pltpu
from jax.sharding import PartitionSpec as P

HQ = 32
KVH = 4
HS = 64
MB = 2
RECUR = 3
SCALE = HS ** (-0.5)
F32 = jnp.float32
BF = jnp.bfloat16
MESH = pl.DeviceIdType.MESH
NN = (((1,), (0,)), ((), ()))
NT = (((1,), (1,)), ((), ()))
TN = (((0,), (0,)), ((), ()))

OWN = (96, 80, 48)
PIECES = ((0, 24, 0), (24, 24, 1), (48, 16, 0), (64, 16, 1), (80, 8, 0), (88, 8, 1))
T = 4
DC = 512
OC = 256
HEADS = 4


def own_table():
    batch, place, seen = [], [], [0, 0]
    for _, rows, b in PIECES:
        for _ in range(rows):
            batch.append(b)
            place.append(seen[b])
            seen[b] += 1
    return np.array(batch), np.array(place)


def split_batches(values, own):
    halves = ([], [])
    for owner in range(T):
        for start, rows, b in PIECES:
            if start < own:
                halves[b].append(values[owner * own + start : owner * own + start + rows])
    return [jnp.concatenate(half, axis=0) for half in halves]


def join_batches(halves, own):
    rows_out, at = [], [0, 0]
    for owner in range(T):
        for start, rows, b in PIECES:
            if start < own:
                rows_out.append(halves[b][at[b] : at[b] + rows])
                at[b] += rows
    return jnp.concatenate(rows_out, axis=0)


def dot(left, right, dims):
    return lax.dot_general(left, right, dims, preferred_element_type=F32)


def swap_halves(tile):
    lane = lax.broadcasted_iota(jnp.int32, tile.shape, 1)
    return jnp.where((lane & 63) < 32, pltpu.roll(tile, 96, 1), pltpu.roll(tile, 32, 1))


def attention_shares(query, key, allowed):
    rows = query.shape[0]
    group = query.shape[1] // HS
    stacked = stack_heads(query)
    scores = dot(stacked, key, NT).reshape(group, rows, rows) * SCALE
    scores = jnp.where(allowed[None] > 0, scores, -1e30)
    raised = jnp.exp(scores - jnp.max(scores, axis=-1, keepdims=True))
    return stacked, raised * (1.0 / jnp.sum(raised, axis=-1, keepdims=True))


def stack_heads(values):
    group = values.shape[1] // HS
    return jnp.concatenate([values[:, h * HS : (h + 1) * HS] for h in range(group)], axis=0)


def unstack_heads(values, rows):
    group = values.shape[0] // rows
    return jnp.concatenate([values[h * rows : (h + 1) * rows] for h in range(group)], axis=1)


def mean_square(values):
    return jnp.mean(values * values, axis=-1, keepdims=True)


class Place:
    def __init__(self, n):
        self.n = n
        self.line = n // 2
        self.dp = lax.axis_index("dp")
        self.t = lax.axis_index("tensor")
        self.a = self.dp // 2
        self.b = lax.rem(self.dp, 2)
        self.hi = self.t // 2
        self.lo = lax.rem(self.t, 2)
        self.has_right = self.a < self.line - 1
        self.has_left = self.a > 0
        self.mate = (self.a * 2 + 1 - self.b, self.t)
        self.right = (jnp.minimum(self.dp + 2, n - 1), self.t)
        self.left = (jnp.maximum(self.dp - 2, 0), self.t)
        self.near = (self.dp, self.hi * 2 + 1 - self.lo)
        self.far = (self.dp, (1 - self.hi) * 2 + self.lo)
        self.diag = (self.dp, (1 - self.hi) * 2 + 1 - self.lo)

    def barrier(self, along):
        sem = pltpu.get_barrier_semaphore()

        def greet(device):
            pl.semaphore_signal(sem, inc=1, device_id=device, device_id_type=MESH)

        for device in (self.near, self.far, self.diag):
            greet(device)
        expected = 3
        if along:
            greet(self.mate)
            pl.when(self.has_right)(lambda: greet(self.right))
            pl.when(self.has_left)(lambda: greet(self.left))
            expected = 4 + self.has_right.astype(jnp.int32) + self.has_left.astype(jnp.int32)
        pl.semaphore_wait(sem, expected)


def remote(src, dst, send, recv, device):
    return pltpu.make_async_remote_copy(
        src_ref=src, dst_ref=dst, send_sem=send, recv_sem=recv, device_id=device, device_id_type=MESH
    )


class LineGather:
    def __init__(self, place, pieces, sems):
        self.p = place
        self.pieces = pieces
        self.local, self.msend, self.mrecv, self.rsend, self.rrecv, self.lsend, self.lrecv = sems

    def toward_left(self, w, k, src, chunk):
        dst = self.pieces[w][1](chunk)
        return remote(src, dst, self.lsend.at[w, k], self.lrecv.at[w, k], self.p.left)

    def toward_right(self, w, k, src, chunk):
        dst = self.pieces[w][1](chunk)
        return remote(src, dst, self.rsend.at[w, k], self.rrecv.at[w, k], self.p.right)

    def toward_mate(self, w, k, src, chunk):
        dst = self.pieces[w][1](chunk)
        return remote(src, dst, self.msend.at[w, k], self.mrecv.at[w, k], self.p.mate)

    def own(self, w):
        p = self.p
        src, dst = self.pieces[w]
        pltpu.make_async_copy(src, dst(p.dp), self.local.at[w]).start()
        pl.when(p.has_left)(lambda: self.toward_left(w, 0, src, p.dp).start())
        pl.when(p.has_right)(lambda: self.toward_right(w, 0, src, p.dp).start())
        self.toward_mate(w, p.a, src, p.dp).start()

    def step(self, w, k):
        p = self.p
        dst = self.pieces[w][1]

        @pl.when(p.a + k < p.line)
        def _():
            chunk = p.dp + 2 * k
            self.toward_left(w, k - 1, dst(chunk), chunk).wait_recv()
            pl.when(p.has_left)(lambda: self.toward_left(w, k, dst(chunk), chunk).start())
            self.toward_mate(w, p.a + k, dst(chunk), chunk).start()

        @pl.when(p.a - k >= 0)
        def _():
            chunk = p.dp - 2 * k
            self.toward_right(w, k - 1, dst(chunk), chunk).wait_recv()
            pl.when(p.has_right)(lambda: self.toward_right(w, k, dst(chunk), chunk).start())
            self.toward_mate(w, p.a - k, dst(chunk), chunk).start()

    def steps(self, w):
        for k in range(1, self.p.line):
            self.step(w, k)

    def arrive(self, w):
        p = self.p
        src, dst = self.pieces[w]
        pltpu.make_async_copy(src, dst(p.dp), self.local.at[w]).wait()
        for i in range(p.line):
            chunk = 2 * i + 1 - p.b
            self.toward_mate(w, i, dst(chunk), chunk).wait_recv()

    def drain(self, w):
        p = self.p
        dst = self.pieces[w][1]
        for i in range(p.line):
            self.toward_mate(w, i, dst(p.dp), p.dp).wait_send()
            pl.when(p.has_left & (p.a + i < p.line))(lambda: self.toward_left(w, i, dst(p.dp), p.dp).wait_send())
            pl.when(p.has_right & (p.a - i >= 0))(lambda: self.toward_right(w, i, dst(p.dp), p.dp).wait_send())


class Rows:
    def __init__(self, place, part, relay, sums, sems):
        self.p = place
        self.part, self.relay, self.sums = part, relay, sums
        self.s1, self.q1, self.s2, self.q2, self.gs, self.gr = sems

    def first_copy(self, i, own, c):
        p = self.p
        cols = pl.ds(pl.multiple_of(c * DC, DC), DC)
        return remote(
            self.part.at[:, 1 - p.lo, pl.ds(0, own), cols],
            self.sums[i][0].at[:, :, cols],
            self.s1.at[i, c],
            self.q1.at[i, c],
            p.near,
        )

    def second_copy(self, i, own, c):
        p = self.p
        cols = pl.ds(pl.multiple_of(c * DC, DC), DC)
        return remote(
            self.relay.at[pl.ds(0, own), cols],
            self.sums[i][1].at[:, cols],
            self.s2.at[i, c],
            self.q2.at[i, c],
            p.far,
        )

    def reduce(self, i, own, tile, finish):
        p = self.p
        part, relay = self.part, self.relay
        r1, r2 = self.sums[i]
        chunks = part.shape[-1] // DC

        @pl.loop(0, chunks)
        def _(c):
            cols = pl.ds(pl.multiple_of(c * DC, DC), DC)
            part[:, :, 0:own, cols] = tile(cols).astype(BF).reshape(2, 2, own, DC)
            self.first_copy(i, own, c).start()

        @pl.loop(0, chunks)
        def _(c):
            cols = pl.ds(pl.multiple_of(c * DC, DC), DC)
            self.first_copy(i, own, c).wait_recv()
            mine = part[1 - p.hi, p.lo, 0:own, cols].astype(F32)
            relay[0:own, cols] = (mine + r1[1 - p.hi, :, cols].astype(F32)).astype(BF)
            self.second_copy(i, own, c).start()

        @pl.loop(0, chunks)
        def _(c):
            cols = pl.ds(pl.multiple_of(c * DC, DC), DC)
            self.second_copy(i, own, c).wait_recv()
            mine = part[p.hi, p.lo, 0:own, cols].astype(F32)
            finish(cols, mine + r1[p.hi, :, cols].astype(F32) + r2[:, cols].astype(F32))

        @pl.loop(0, chunks)
        def _(c):
            self.first_copy(i, own, c).wait_send()
            self.second_copy(i, own, c).wait_send()

    def gather_copy(self, i, buffer, which):
        p = self.p
        here = buffer.at[p.hi, p.lo]
        if which == 0:
            return remote(here, here, self.gs.at[i, 0], self.gr.at[i, 0], p.far)
        if which == 1:
            return remote(here, here, self.gs.at[i, 1], self.gr.at[i, 1], p.near)
        there = buffer.at[1 - p.hi, p.lo]
        return remote(there, there, self.gs.at[i, 2], self.gr.at[i, 2], p.near)

    def gather_start(self, i, buffer):
        self.gather_copy(i, buffer, 0).start()
        self.gather_copy(i, buffer, 1).start()

    def gather_finish(self, i, buffer):
        self.gather_copy(i, buffer, 0).wait_recv()
        self.gather_copy(i, buffer, 2).start()
        self.gather_copy(i, buffer, 1).wait_recv()
        self.gather_copy(i, buffer, 2).wait_recv()
        for which in range(3):
            self.gather_copy(i, buffer, which).wait_send()


def peers_copy(place, src, dst, send, recv, which):
    device = (place.near, place.far, place.diag)[which]
    return remote(src, dst.at[place.t], send.at[which], recv.at[which], device)


def gain_row(gathered, n, row, width):
    each = width // (n * T)
    tiles = []
    for j in range(width // 128):
        total = None
        for i in range(128 // each):
            number = j * (128 // each) + i
            block = gathered[number % T, number // T][row : row + 1]
            total = block if total is None else total + block
        tiles.append(total)
    return jnp.concatenate(tiles, axis=1)


QKV, WO, GU, WD = 0, 640, 1152, 3968
COLS = 5376
RANGES = ((0, 640), (640, 512), (1152, 1536), (2688, 1280), (3968, 768), (4736, 640))


def forward_kernel(n, *refs):
    it = iter(refs)
    (tokens, cotangent, weights, gains, perm, cosine, sine) = [next(it) for _ in range(7)]
    allowed = [next(it) for _ in range(RECUR)]
    act_own = next(it)
    w_out, gain_out, fin_out, cot_own, cot_all = [next(it) for _ in range(5)]
    names = ("normed", "qkv", "att", "mixed", "gu", "prod", "hidden", "first")
    saved_out = [dict((k, next(it)) for k in names) for _ in range(RECUR)]
    w = next(it)
    gbuf, gall = next(it), next(it)
    tok, cot = next(it), next(it)
    saved = [dict((k, next(it)) for k in names) for _ in range(RECUR)]
    after, fin, cown = next(it), next(it), next(it)
    part, relay = next(it), next(it)
    sums = [(next(it), next(it)) for _ in range(2 * RECUR)]
    line_sems = [next(it) for _ in range(7)]
    row_sems = [next(it) for _ in range(6)]
    tsend, trecv, outsem = next(it), next(it), next(it)

    p = Place(n)
    rows_chunk = weights.shape[0]
    width = tokens.shape[-1]

    def piece(start, size):
        return (
            weights.at[:, pl.ds(start, size)],
            lambda chunk: w.at[pl.ds(pl.multiple_of(chunk * rows_chunk, rows_chunk), rows_chunk), pl.ds(start, size)],
        )

    pieces = [(gains, lambda chunk: gbuf.at[chunk])] + [piece(*r) for r in RANGES]
    line = LineGather(p, pieces, line_sems)
    rows = Rows(p, part, relay, sums, row_sems)
    writes = []

    def write(src, dst):
        copy = pltpu.make_async_copy(src, dst, outsem.at[len(writes)])
        copy.start()
        writes.append(copy)

    p.barrier(True)
    line.own(0)
    line.own(1)
    own_copies = []
    for which in range(3):
        peers_copy(p, tokens, tok, tsend.at[0], trecv.at[0], which).start()
    pltpu.make_async_copy(tokens, tok.at[p.t], tsend.at[0, 3]).start()
    line.own(2)
    for which in range(3):
        peers_copy(p, cotangent, cot, tsend.at[1], trecv.at[1], which).start()
    pltpu.make_async_copy(cotangent, cot.at[p.t], tsend.at[1, 3]).start()
    line.own(3)
    line.steps(0)
    line.arrive(0)
    for which in range(3):
        peers_copy(p, gbuf, gall, tsend.at[2], trecv.at[2], which).start()
    pltpu.make_async_copy(gbuf, gall.at[p.t], tsend.at[2, 3]).start()

    def wait_peers(i, src, dst):
        for which in range(3):
            copy = peers_copy(p, src, dst, tsend.at[i], trecv.at[i], which)
            copy.wait_recv()
            copy.wait_send()
        pltpu.make_async_copy(src, dst.at[p.t], tsend.at[i, 3]).wait()

    wait_peers(2, gbuf, gall)
    gain_out[0:1, :] = gain_row(gall, n, 0, width)
    gain_out[1:2, :] = gain_row(gall, n, 1, width)
    gain_out[2:8, :] = jnp.zeros((6, width), F32)

    wait_peers(0, tokens, tok)

    own = OWN[0]
    mine = perm[pl.ds(pl.multiple_of(p.t * own, own), own), :]
    saved[0]["hidden"][...] = dot(mine, tok[...].reshape(T * own, width), NN)

    @pl.loop(0, T)
    def _(owner):
        picked = perm[pl.ds(pl.multiple_of(owner * own, own), own), :]
        hidden = dot(picked, tok[...].reshape(T * own, width), NN)
        inverse = lax.rsqrt(mean_square(hidden) + 1e-05)
        saved[0]["normed"][owner] = (hidden * inverse * gain_out[0:1, :]).astype(BF)

    wait_peers(1, cotangent, cot)
    cown[...] = dot(mine, cot[...].reshape(T * own, width), NN)
    write(cown, cot_own)

    line.steps(1)
    line.own(4)
    line.steps(2)
    line.arrive(1)

    for level in range(RECUR):
        own = OWN[level]
        count = T * own
        half = count // 2
        s = saved[level]
        if level:
            rows.gather_finish(2 * level - 1, s["normed"].reshape(2, 2, own, width))
        x = s["normed"][...].reshape(count, width)
        qkv = dot(x, w[:, QKV : QKV + 640], NN)
        cos = jnp.concatenate([cosine[owner * OWN[0] : owner * OWN[0] + own, :] for owner in range(T)], axis=0)
        sin = jnp.concatenate([sine[owner * OWN[0] : owner * OWN[0] + own, :] for owner in range(T)], axis=0)
        tiles = []
        for j in range(5):
            tile = qkv[:, j * 128 : (j + 1) * 128]
            turned = tile * cos + swap_halves(tile) * sin
            if j == 4:
                lane = lax.broadcasted_iota(jnp.int32, tile.shape, 1)
                turned = jnp.where(lane < HS, turned, tile)
            tiles.append(turned)
        rotated = jnp.concatenate(tiles, axis=1)
        s["qkv"][...] = rotated.astype(BF)
        write(s["qkv"], saved_out[level]["qkv"])
        heads = []
        for b, block in enumerate(split_batches(rotated, own)):
            query, key, value = (
                block[:, 0:512].astype(BF),
                block[:, 512:576].astype(BF),
                block[:, 576:640].astype(BF),
            )
            _, shares = attention_shares(query, key, allowed[level][b])
            out = dot(shares.astype(BF).reshape(8 * half, half), value, NN)
            heads.append(unstack_heads(out, half))
        s["att"][...] = join_batches(heads, own).astype(BF)
        write(s["att"], saved_out[level]["att"])
        if level == 0:
            line.own(5)
            line.steps(3)
            line.arrive(2)
        present = act_own[level, 0:own, :]

        def attention_tile(cols):
            return dot(s["att"][...], w[cols, WO : WO + 512], NT)

        def attention_finish(cols, total):
            s["first"][:, cols] = s["hidden"][:, cols] + present * total

        rows.reduce(2 * level, own, attention_tile, attention_finish)
        first = s["first"][...]
        inverse = lax.rsqrt(mean_square(first) + 1e-05)
        s["mixed"][p.t] = (first * inverse * gain_out[1:2, :]).astype(BF)
        mixed = s["mixed"].reshape(2, 2, own, width)
        rows.gather_start(2 * level, mixed)
        write(s["first"], saved_out[level]["first"])
        if level == 0:
            line.own(6)
            line.steps(4)
            line.arrive(3)
        rows.gather_finish(2 * level, mixed)
        write(s["mixed"], saved_out[level]["mixed"])

        def gate_up(start, stop):
            @pl.loop(start, stop)
            def _(j):
                cols = pl.ds(pl.multiple_of(j * 256, 256), 256)
                wcols = pl.ds(pl.multiple_of(GU + j * 256, 128), 256)
                pair = dot(s["mixed"][...].reshape(count, width), w[:, wcols], NN)
                s["gu"][:, cols] = pair.astype(BF)
                gate = pair[:, 0:128]
                s["prod"][:, pl.ds(pl.multiple_of(j * 128, 128), 128)] = (
                    gate * jax.nn.sigmoid(gate) * pair[:, 128:256]
                ).astype(BF)

        gate_up(0, 6)
        if level == 0:
            line.steps(5)
            line.arrive(4)
        gate_up(6, 11)
        write(s["gu"], saved_out[level]["gu"])
        write(s["prod"], saved_out[level]["prod"])
        if level == 0:
            line.steps(6)
            line.arrive(5)
            line.arrive(6)
            write(w, w_out)

        def mlp_tile(cols):
            return dot(s["prod"][...], w[cols, WD : WD + 1408], NT)

        def mlp_finish(cols, total):
            after[0:own, cols] = s["first"][:, cols] + present * total

        rows.reduce(2 * level + 1, own, mlp_tile, mlp_finish)
        if level < RECUR - 1:
            deeper = OWN[level + 1]
            hidden = after[0:deeper, :]
            saved[level + 1]["hidden"][...] = hidden
            inverse = lax.rsqrt(mean_square(hidden) + 1e-05)
            saved[level + 1]["normed"][p.t] = (hidden * inverse * gain_out[0:1, :]).astype(BF)
            rows.gather_start(2 * level + 1, saved[level + 1]["normed"].reshape(2, 2, deeper, width))
            fin[deeper:own, :] = after[deeper:own, :].astype(BF)
        else:
            fin[0:own, :] = after[0:own, :].astype(BF)
        write(s["hidden"], saved_out[level]["hidden"])
        write(s["normed"], saved_out[level]["normed"])
        if level == 0:
            deepest = OWN[RECUR - 1]

            @pl.loop(0, T)
            def _(owner):
                picked = perm[pl.ds(pl.multiple_of(owner * OWN[0], 32), deepest), :]
                cot_all[owner] = dot(picked, cot[...].reshape(T * OWN[0], width), NN).astype(BF)

    write(fin, fin_out)
    for i in range(len(pieces)):
        line.drain(i)
    for copy in writes:
        copy.wait()


def static_tables():
    batch, place = own_table()
    batch_q = np.tile(batch, T)
    rank_q = np.concatenate([place * T + t for t in range(T)])
    level_ranks = []
    for own in OWN:
        level_ranks.append(np.concatenate([np.arange(own // 2) * T + t for t in range(T)]))
    return batch_q.astype(np.int32), rank_q.astype(np.int32), [r.astype(np.int32) for r in level_ranks]


def prologue(depth, lengths, tensor_index):
    batch_q, rank_q, level_ranks = static_tables()
    rows = depth.shape[1]
    local = rows // T
    index = jnp.arange(rows, dtype=jnp.int32)
    earlier = (depth[:, None, :] > depth[:, :, None]) | (
        (depth[:, None, :] == depth[:, :, None]) & (index[None, None, :] < index[None, :, None])
    )
    rank = jnp.sum(earlier.astype(jnp.int32), axis=2)
    rank_col = rank.reshape(MB, T, local).transpose(1, 0, 2).reshape(-1)
    batch_col = np.tile(np.repeat(np.arange(MB), local), T).astype(np.int32)
    hit = (rank_col[None, :] == rank_q[:, None]) & (batch_col[None, :] == batch_q[:, None])
    perm = hit.astype(BF)
    back = (
        (rank_col[:, None] == rank_q[None, :]) & (batch_col[:, None] == batch_q[None, :])
    ).astype(BF)
    ends = jnp.cumsum(lengths, axis=1)
    starts = ends - lengths

    def documents(position, ends_of, starts_of):
        inside = position[..., None] >= ends_of
        document = jnp.sum(inside.astype(jnp.int32), axis=-1)
        start = jnp.max(jnp.where(position[..., None] >= starts_of, starts_of, 0), axis=-1)
        return document, position - start

    position_col = np.tile(np.arange(rows).reshape(T, 1, local), (1, MB, 1)).reshape(-1).astype(np.int32)
    position = jnp.sum(jnp.where(hit, position_col[None, :], 0), axis=1)
    ends_q = jnp.where(batch_q[:, None] == 0, ends[0][None], ends[1][None])
    starts_q = jnp.where(batch_q[:, None] == 0, starts[0][None], starts[1][None])
    _, offset = documents(position, ends_q, starts_q)
    freqs = 10000.0 ** (-jnp.arange(0, HS, 2).astype(F32) / HS)
    angles = offset.astype(F32)[:, None] * freqs[None, :]
    cos, sin = jnp.cos(angles), jnp.sin(angles)
    cosine = jnp.concatenate([cos] * 4, axis=1)
    sine = jnp.concatenate([-sin, sin, -sin, sin], axis=1)
    counts = [jnp.sum((depth >= level + 1).astype(jnp.int32), axis=1) for level in range(RECUR)]
    masks, act = [], []
    for level in range(RECUR):
        ranks = level_ranks[level]
        at = jnp.sum(jnp.where(rank[:, None, :] == ranks[None, :, None], index[None, None, :], 0), axis=2)
        document, _ = documents(at, ends[:, None, :], starts[:, None, :])
        ok = (document[:, :, None] == document[:, None, :]) & (at[:, None, :] <= at[:, :, None])
        ok = ok & (ranks[None, None, :] < counts[level][:, None, None])
        ok = ok | np.eye(len(ranks), dtype=bool)[None]
        masks.append(ok.astype(F32))
        limit = jnp.where(batch_q == 0, counts[level][0], counts[level][1])
        act.append((rank_q < limit).astype(F32))
    act = jnp.stack(act)
    return perm, back, cosine, sine, masks, act


def forward(n, tokens, cotangent, joined, gains, tables, tensor_index):
    perm, back, cosine, sine, masks, act = tables
    width = tokens.shape[-1]
    act_own = lax.dynamic_slice_in_dim(act, tensor_index * OWN[0], OWN[0], axis=1)[:, :, None]
    hidden_cols = (COLS - GU) // 3
    vmem = pl.BlockSpec(memory_space=pltpu.VMEM)
    hbm = pl.BlockSpec(memory_space=pl.ANY)

    def saved_shapes(own):
        count = T * own
        return {
            "normed": ((T, own, width), BF),
            "qkv": ((count, 640), BF),
            "att": ((count, 512), BF),
            "mixed": ((T, own, width), BF),
            "gu": ((count, 2 * hidden_cols), BF),
            "prod": ((count, hidden_cols), BF),
            "hidden": ((own, width), F32),
            "first": ((own, width), F32),
        }

    shapes = [((width, COLS), BF), ((8, width), F32), ((OWN[0], width), BF), ((OWN[0], width), F32), ((T, OWN[2], width), BF)]
    specs = [hbm, vmem, hbm, hbm, vmem]
    for own in OWN:
        for entry in saved_shapes(own).values():
            shapes.append(entry)
            specs.append(hbm)
    scratch = [pltpu.VMEM((width, COLS), BF), pltpu.VMEM((n, 8, 128), F32), pltpu.VMEM((T, n, 8, 128), F32)]
    scratch += [pltpu.VMEM((T,) + tokens.shape, BF)] * 2
    for own in OWN:
        scratch += [pltpu.VMEM(*entry) for entry in saved_shapes(own).values()]
    scratch += [pltpu.VMEM((OWN[0], width), F32), pltpu.VMEM((OWN[0], width), BF), pltpu.VMEM((OWN[0], width), F32)]
    scratch += [pltpu.VMEM((2, 2, OWN[0], width), BF), pltpu.VMEM((OWN[0], width), BF)]
    for own in OWN:
        for _ in range(2):
            scratch += [pltpu.VMEM((2, own, width), BF), pltpu.VMEM((own, width), BF)]
    dma = pltpu.SemaphoreType.DMA
    count = len(RANGES) + 1
    scratch += [dma((count,))] + [dma((count, n // 2))] * 6
    chunks = width // DC
    scratch += [dma((2 * RECUR, chunks))] * 4 + [dma((2 * RECUR, 3))] * 2
    scratch += [dma((3, 4)), dma((3, 3)), dma((40,))]
    outs = pl.pallas_call(
        functools.partial(forward_kernel, n),
        out_shape=[jax.ShapeDtypeStruct(*entry) for entry in shapes],
        in_specs=[hbm, hbm, hbm, hbm] + [vmem] * 7,
        out_specs=specs,
        scratch_shapes=scratch,
        compiler_params=pltpu.CompilerParams(
            collective_id=1, has_side_effects=True, vmem_limit_bytes=62 << 20
        ),
    )(tokens, cotangent, joined, gains, perm, cosine, sine, *masks, act_own)
    w_all, gain, fin, cot_own, cot_all = outs[:5]
    names = list(saved_shapes(1))
    saved = [dict(zip(names, outs[5 + 8 * level : 13 + 8 * level])) for level in range(RECUR)]
    return w_all, gain, fin, cot_own, cot_all, saved


def join_weights(w_query, w_key, w_value, w_out, w_gate, w_up, w_down):
    rows, hidden = w_gate.shape
    pair = jnp.stack(
        [w_gate.reshape(rows, hidden // 128, 128), w_up.reshape(rows, hidden // 128, 128)], axis=2
    ).reshape(rows, 2 * hidden)
    return jnp.concatenate([w_query, w_key, w_value, w_out.T, pair, w_down.T], axis=1)


def place_gains(n, attn_gain, mlp_gain):
    each = attn_gain.shape[0]
    number = lax.axis_index("dp") * T + lax.axis_index("tensor")
    block = jnp.zeros((8, 128), F32)
    both = jnp.stack([attn_gain, mlp_gain])
    return lax.dynamic_update_slice(block, both, (0, lax.rem(number * each, 128)))


def attention_back(rotated, attended_grad, cos, sin, allowed, own):
    half = T * own // 2
    grads = []
    split = split_batches(rotated, own)
    upstream = split_batches(attended_grad, own)
    for b in range(MB):
        block = split[b]
        query, key, value = block[:, 0:512].astype(BF), block[:, 512:576].astype(BF), block[:, 576:640].astype(BF)
        up_all = upstream[b].astype(BF)
        query_grads, key_grad, value_grad = [], 0.0, 0.0
        for start in range(0, 512, HEADS * HS):
            stacked, shares = attention_shares(query[:, start : start + HEADS * HS], key, allowed[b])
            up = stack_heads(up_all[:, start : start + HEADS * HS])
            low = shares.astype(BF).reshape(HEADS * half, half)
            shares_grad = dot(up, value, NT).reshape(HEADS, half, half)
            value_grad += dot(low, up, TN)
            spread = jnp.sum(shares * shares_grad, axis=-1, keepdims=True)
            score_grad = (shares * (shares_grad - spread)).astype(BF).reshape(HEADS * half, half)
            query_grads.append(unstack_heads(dot(score_grad, key, NN), half) * SCALE)
            key_grad += dot(score_grad, stacked, TN) * SCALE
        query_grad = jnp.concatenate(query_grads, axis=1)
        grads.append(jnp.concatenate([query_grad, key_grad, value_grad], axis=1))
    joined = join_batches(grads, own)
    tiles = []
    for j in range(5):
        tile = joined[:, j * 128 : (j + 1) * 128]
        turned = tile * cos - swap_halves(tile) * sin
        if j == 4:
            lane = lax.broadcasted_iota(jnp.int32, tile.shape, 1)
            turned = jnp.where(lane < HS, turned, tile)
        tiles.append(turned)
    return jnp.concatenate(tiles, axis=1)


def level_rows(table, own):
    return jnp.concatenate([table[owner * OWN[0] : owner * OWN[0] + own, :] for owner in range(T)], axis=0)


def norm_back(source, gain, upstream):
    inverse = lax.rsqrt(mean_square(source) + 1e-05)
    unit = source * inverse
    gain_part = jnp.sum(upstream * unit, axis=0, keepdims=True)
    scaled = upstream * gain
    return inverse * (scaled - unit * jnp.mean(scaled * unit, axis=-1, keepdims=True)), gain_part


def backward_kernel(n, *refs):
    it = iter(refs)
    (w_all, gain, cot_own, cot_all, cosine, sine, act_own, act_last) = [next(it) for _ in range(8)]
    allowed = [None] + [next(it) for _ in range(2)]
    saved_in = []
    for level in range(RECUR):
        names = ("gu", "first") if level == 0 else ("gu", "first", "qkv", "hidden")
        saved_in.append({k: next(it) for k in names})
    dg_out = [next(it) for _ in range(3)]
    gug_out = [next(it) for _ in range(3)]
    og_out = [None] + [next(it) for _ in range(2)]
    qkvg_out = [None] + [next(it) for _ in range(2)]
    grad_out, gain_part = next(it), next(it)
    w = next(it)
    saved = []
    for level in range(RECUR):
        saved.append({k: next(it) for k in saved_in[level]})
    dg = [next(it) for _ in range(3)]
    gug = [next(it) for _ in range(3)]
    og = [None] + [next(it) for _ in range(2)]
    qkvg = [None] + [next(it) for _ in range(2)]
    grad, upstream = next(it), next(it)
    part, relay = next(it), next(it)
    sums = [(next(it), next(it)) for _ in range(5)]
    row_sems = [next(it) for _ in range(6)]
    insem, outsem = next(it), next(it)

    p = Place(n)
    width = w.shape[0]
    rows = Rows(p, part, relay, sums, row_sems)
    hidden_cols = (COLS - GU) // 3
    loads, writes = {}, []

    def load(name, src, dst):
        copy = pltpu.make_async_copy(src, dst, insem.at[len(loads)])
        copy.start()
        loads[name] = copy

    def write(src, dst):
        copy = pltpu.make_async_copy(src, dst, outsem.at[len(writes)])
        copy.start()
        writes.append(copy)

    def columns(start, size):
        load(("w", start), w_all.at[:, pl.ds(start, size)], w.at[:, pl.ds(start, size)])

    columns(WD, hidden_cols)
    load("grad", cot_own, grad)
    last = RECUR - 1
    load(("gu", last), saved_in[last]["gu"], saved[last]["gu"])
    columns(GU, 2 * hidden_cols)
    load(("first", last), saved_in[last]["first"], saved[last]["first"])
    columns(WO, 512)
    for name in ("qkv", "hidden"):
        load((name, last), saved_in[last][name], saved[last][name])
    columns(QKV, 640)
    for level in (1, 0):
        for name in saved_in[level]:
            load((name, level), saved_in[level][name], saved[level][name])
    p.barrier(False)
    gain_part[...] = jnp.zeros_like(gain_part)

    for level in range(last, -1, -1):
        own = OWN[level]
        count = T * own
        s = saved[level]
        base = 2 * (last - level)
        present = act_own[level, 0:own, :]
        if level == last:
            dg[level][...] = (cot_all[...].astype(F32).reshape(count, width) * act_last[...]).astype(BF).reshape(
                T, own, width
            )
            loads["grad"].wait()
        else:
            dg[level][p.t] = (present * grad[0:own, :]).astype(BF)
            view = dg[level].reshape(2, 2, own, width)
            rows.gather_start(base, view)
            rows.gather_finish(base, view)
        write(dg[level], dg_out[level])
        if level == last:
            loads["w", WD].wait()
        loads["gu", level].wait()

        def hidden_block(start, size):
            wcols = pl.ds(pl.multiple_of(WD + start, 128), size)
            product_grad = dot(dg[level][...].reshape(count, width), w[:, wcols], NN)
            for h in range(size // 128):
                at = pl.multiple_of(2 * start + 256 * h, 256)
                gate = s["gu"][:, pl.ds(at, 128)].astype(F32)
                upward = s["gu"][:, pl.ds(at + 128, 128)].astype(F32)
                sigma = jax.nn.sigmoid(gate)
                up = product_grad[:, 128 * h : 128 * h + 128]
                gug[level][:, pl.ds(at, 128)] = (up * upward * sigma * (1.0 + gate * (1.0 - sigma))).astype(BF)
                gug[level][:, pl.ds(at + 128, 128)] = (up * gate * sigma).astype(BF)

        @pl.loop(0, hidden_cols // 256)
        def _(j):
            hidden_block(j * 256, 256)

        if hidden_cols % 256:
            hidden_block(hidden_cols // 256 * 256, 128)
        write(gug[level], gug_out[level])
        if level == last:
            loads["w", GU].wait()

        def mlp_tile(cols):
            return dot(gug[level][...], w[cols, GU : GU + 2 * hidden_cols], NT)

        def take(cols, total):
            upstream[0:own, cols] = total

        rows.reduce(base, own, mlp_tile, take)
        loads["first", level].wait()
        update, add = norm_back(s["first"][...], gain[1:2, :], upstream[0:own, :])
        grad[0:own, :] += update
        gain_part[1:2, :] += add
        if level == 0:
            break
        og[level][p.t] = (present * grad[0:own, :]).astype(BF)
        view = og[level].reshape(2, 2, own, width)
        rows.gather_start(base + 1, view)
        rows.gather_finish(base + 1, view)
        write(og[level], og_out[level])
        if level == last:
            loads["w", WO].wait()
        loads["qkv", level].wait()
        attended_grad = dot(og[level][...].reshape(count, width), w[:, WO : WO + 512], NN)
        cos, sin = level_rows(cosine, own), level_rows(sine, own)
        qkvg[level][...] = attention_back(
            s["qkv"][...].astype(F32), attended_grad, cos, sin, allowed[level], own
        ).astype(BF)
        write(qkvg[level], qkvg_out[level])
        if level == last:
            loads["w", QKV].wait()

        def attention_tile(cols):
            return dot(qkvg[level][...], w[cols, QKV : QKV + 640], NT)

        rows.reduce(base + 1, own, attention_tile, take)
        loads["hidden", level].wait()
        update, add = norm_back(s["hidden"][...], gain[0:1, :], upstream[0:own, :])
        grad[0:own, :] += update
        gain_part[0:1, :] += add

    write(grad, grad_out)
    for copy in writes:
        copy.wait()


def backward(n, w_all, gain, cot_own, cot_all, tables, saved, tensor_index):
    perm, back, cosine, sine, masks, act = tables
    width = w_all.shape[0]
    act_own = lax.dynamic_slice_in_dim(act, tensor_index * OWN[0], OWN[0], axis=1)[:, :, None]
    act_last = act[RECUR - 1].reshape(T, OWN[0])[:, : OWN[2]].reshape(-1)[:, None]
    hidden_cols = (COLS - GU) // 3
    vmem = pl.BlockSpec(memory_space=pltpu.VMEM)
    hbm = pl.BlockSpec(memory_space=pl.ANY)
    operands = [w_all, gain, cot_own, cot_all, cosine, sine, act_own, act_last, masks[1], masks[2]]
    specs = [hbm, vmem, hbm] + [vmem] * 7
    used = []
    for level in range(RECUR):
        for name in ("gu", "first") if level == 0 else ("gu", "first", "qkv", "hidden"):
            operands.append(saved[level][name])
            specs.append(hbm)
            used.append(saved[level][name])
    outs = [((T, own, width), BF) for own in OWN]
    outs += [((T * own, 2 * hidden_cols), BF) for own in OWN]
    outs += [((T, own, width), BF) for own in OWN[1:]]
    outs += [((T * own, 640), BF) for own in OWN[1:]]
    scratch = [pltpu.VMEM(w_all.shape, BF)] + [pltpu.VMEM(u.shape, u.dtype) for u in used]
    scratch += [pltpu.VMEM(*entry) for entry in outs]
    outs += [((OWN[0], width), F32), ((8, width), F32)]
    out_specs = [hbm] * (len(outs) - 1) + [vmem]
    scratch += [pltpu.VMEM((OWN[0], width), F32)] * 2
    scratch += [pltpu.VMEM((2, 2, OWN[0], width), BF), pltpu.VMEM((OWN[0], width), BF)]
    for own in (OWN[2], OWN[2], OWN[1], OWN[1], OWN[0]):
        scratch += [pltpu.VMEM((2, own, width), BF), pltpu.VMEM((own, width), BF)]
    dma = pltpu.SemaphoreType.DMA
    chunks = width // DC
    scratch += [dma((5, chunks))] * 4 + [dma((5, 3))] * 2 + [dma((24,)), dma((16,))]
    res = pl.pallas_call(
        functools.partial(backward_kernel, n),
        out_shape=[jax.ShapeDtypeStruct(*entry) for entry in outs],
        in_specs=specs,
        out_specs=out_specs,
        scratch_shapes=scratch,
        compiler_params=pltpu.CompilerParams(
            collective_id=2, has_side_effects=True, vmem_limit_bytes=62 << 20
        ),
    )(*operands)
    return {
        "dg": res[0:3],
        "gug": res[3:6],
        "og": res[6:8],
        "qkvg": res[8:10],
        "grad": res[10],
        "gain_part": res[11],
    }


GRADS = (
    ("down", 0, 768),
    ("down", 768, 640),
    ("gu", 0, 768),
    ("gu", 768, 768),
    ("gu", 1536, 768),
    ("gu", 2304, 512),
    ("out", 0, 512),
    ("qkv", 0, 384),
    ("qkv", 384, 256),
)
WIDEST = 768
DEPTH = 2


def gradient_kernel(n, *refs):
    it = iter(refs)
    (w_all, gain, cosine, sine, act_own, allowed, back) = [next(it) for _ in range(7)]
    grad_in, gain_in, fin_in, hidden_in, qkv_in = [next(it) for _ in range(5)]
    x_in = {name: [next(it) for _ in range(3)] for name in ("down", "gu", "qkv")}
    x_in["out"] = [None] + [next(it) for _ in range(2)]
    y_in = {name: [next(it) for _ in range(3)] for name in ("down", "gu", "out")}
    y_in["qkv"] = [None] + [next(it) for _ in range(2)]
    (act_out, tok_out, dq, dk, dv, dwo, dgate, dup, dwd, gain_sum) = [next(it) for _ in range(10)]
    og_hbm, fin_all, grad_all = [next(it) for _ in range(3)]
    w = next(it)
    y = {name: next(it) for name in ("down", "gu", "out", "qkv")}
    xm, xl = next(it), next(it)
    og, hidden, qkv, grad, upstream, gains = [next(it) for _ in range(6)]
    gpeers = next(it)
    stage, landed, across, across_own = [next(it) for _ in range(4)]
    window_tmp = next(it)
    gmate_stage, gmate, gline, gline_own = [next(it) for _ in range(4)]
    final = [next(it) for _ in range(2)]
    finalt = next(it)
    chunk_in, chunk_out = next(it), next(it)
    fin_chunk = next(it)
    part, relay = next(it), next(it)
    sums = [(next(it), next(it))]
    row_sems = [next(it) for _ in range(6)]
    msend, mrecv, lsend, lrecv, lrecv2 = [next(it) for _ in range(5)]
    tsend, trecv = next(it), next(it)
    insem, xsem, outsem, finsem, loadsem = [next(it) for _ in range(5)]

    p = Place(n)
    width = w.shape[0]
    line = p.line
    chunk_rows = width // n
    window = max(128, chunk_rows)
    rows = Rows(p, part, relay, sums, row_sems)
    own = OWN[0]
    count = T * own
    starts = [0, T * OWN[0], T * (OWN[0] + OWN[1])]
    total_rows = T * sum(OWN)
    loads, writes = {}, []

    def load(name, src, dst):
        copy = pltpu.make_async_copy(src, dst, insem.at[len(loads)])
        copy.start()
        loads[name] = copy

    def write(src, dst):
        copy = pltpu.make_async_copy(src, dst, outsem.at[len(writes)])
        copy.start()
        writes.append(copy)

    load("grad", grad_in, grad)
    for name in ("down", "gu"):
        for level in range(RECUR):
            load((name, level), y_in[name][level], y[name].at[pl.ds(starts[level], T * OWN[level])])
    load("w", w_all.at[:, pl.ds(0, GU)], w)
    load("qkv", qkv_in, qkv)
    load("hidden", hidden_in, hidden)
    for level in range(RECUR):
        load(("out", level), y_in["out"][level], y["out"].at[pl.ds(starts[level], T * OWN[level])])
    for level in (1, 2):
        load(("qkv", level), y_in["qkv"][level], y["qkv"].at[pl.ds(starts[level], T * OWN[level])])
    p.barrier(True)

    for which in range(3):
        peers_copy(p, fin_in, fin_all, tsend.at[0], trecv.at[0], which).start()
    pltpu.make_async_copy(fin_in, fin_all.at[p.t], tsend.at[0, 3]).start()

    def x_source(which, level):
        return og_hbm if which == "out" and level == 0 else x_in[which][level]

    def level_slice(level):
        return pl.ds(sum(OWN[:level]) * T, OWN[level] * T)

    def x_copy(which, chunk, buffer, slot, level, sem):
        start = pl.multiple_of(chunk * chunk_rows // window * window, window)
        src = x_source(which, level).reshape(T * OWN[level], width)
        return pltpu.make_async_copy(
            src.at[:, pl.ds(start, window)], buffer.at[slot, level_slice(level)], sem.at[slot, level]
        )

    def x_start(which, parity, buffer, sem):
        @pl.loop(0, line)
        def _(i):
            for level in range(RECUR):
                x_copy(which, 2 * i + parity, buffer, i, level, sem).start()

    def tile(k, chunk, buffer, slot, sem):
        which, start, cols = GRADS[k]
        for level in range(RECUR):
            x_copy(which, chunk, buffer, slot, level, sem).wait()
        value = dot(buffer[slot], y[which][:, start : start + cols], TN)
        if window == chunk_rows:
            return value
        window_tmp[:, 0:cols] = value
        shift = pl.multiple_of(lax.rem(chunk, window // chunk_rows) * chunk_rows, chunk_rows)
        return window_tmp[pl.ds(shift, chunk_rows), 0:cols]

    offsets = np.cumsum([0] + [cols for _, _, cols in GRADS])

    def mate_copy(k, i):
        cols = GRADS[k][2]
        return remote(
            stage.at[k % DEPTH, i, :, pl.ds(0, cols)],
            landed.at[i, :, pl.ds(int(offsets[k]), cols)],
            msend.at[k, i],
            mrecv.at[k, i],
            p.mate,
        )

    def mates(k):
        which, start, cols = GRADS[k]
        x_start(which, 1 - p.b, xm, xsem.at[0])
        if k >= DEPTH:

            @pl.loop(0, line)
            def _(i):
                mate_copy(k - DEPTH, i).wait_send()

        @pl.loop(0, line)
        def _(i):
            stage[k % DEPTH, i, :, 0:cols] = tile(k, 2 * i + 1 - p.b, xm, i, xsem.at[0]).astype(BF)
            mate_copy(k, i).start()

    def along(k, i, right):
        cols = GRADS[k][2]
        piece = pl.ds(int(offsets[k]), cols)
        dst = across.at[i, :, piece]
        return remote(
            landed.at[i, :, piece], dst, lsend.at[k, i], lrecv.at[k, i], p.right if right else p.left
        )

    def along_last(k, i):
        cols = GRADS[k][2]
        piece = pl.ds(int(offsets[k]), cols)
        return remote(
            landed.at[i, :, piece], across_own.at[:, piece], lsend.at[k, i], lrecv2.at[k], p.left
        )

    def lines(k, finish):
        which, start, cols = GRADS[k]
        piece = pl.ds(int(offsets[k]), cols)

        @pl.loop(0, line)
        def _(step):
            odd = lax.rem(step, 2)
            i = jnp.where(odd == 1, step // 2, line - 1 - step // 2)

            @pl.when(i != p.a)
            def _():
                value = tile(k, 2 * i + p.b, xl, i, xsem.at[1])
                mate_copy(k, i).wait_recv()
                value = value + landed[i, :, piece].astype(F32)

                def passed(value):
                    landed[i, :, piece] = value.astype(BF)

                inner = ((i > p.a) & p.has_left) | ((i < p.a) & p.has_right)

                @pl.when(inner)
                def _():
                    along(k, i, True).wait_recv()
                    passed(value + across[i, :, piece].astype(F32))

                @pl.when(jnp.logical_not(inner))
                def _():
                    passed(value)

                @pl.when(i > p.a)
                def _():
                    along(k, i, True).start()

                @pl.when((i < p.a) & (i < p.a - 1))
                def _():
                    along(k, i, False).start()

                @pl.when((i < p.a) & (i == p.a - 1))
                def _():
                    along_last(k, i).start()

        value = tile(k, 2 * p.a + p.b, xl, p.a, xsem.at[1])
        mate_copy(k, p.a).wait_recv()
        finish(value + landed[p.a, :, piece].astype(F32))

        @pl.when(p.has_left)
        def _():
            along(k, p.a, True).wait_recv()
            finish(across[p.a, :, piece].astype(F32), True)

        @pl.when(p.has_right)
        def _():
            along_last(k, p.a).wait_recv()
            finish(across_own[:, piece].astype(F32), True)

    def drain(k):
        @pl.loop(0, line)
        def _(i):
            if k >= len(GRADS) - DEPTH:
                mate_copy(k, i).wait_send()

            @pl.when(i != p.a)
            def _():
                along(k, i, True).wait_send()

    staged, turned = {}, []

    def store(k):
        which, start, cols = GRADS[k]
        buffer = final[k % 2]
        for copy in staged.pop(k - 2, ()):
            copy.wait()

        def finish(value, more=False):
            if more:
                buffer[:, 0:cols] += value
            else:
                buffer[:, 0:cols] = value

        lines(k, finish)
        copies = []

        def out(src, dst):
            copy = pltpu.make_async_copy(src, dst, finsem.at[k, len(copies)])
            copy.start()
            copies.append(copy)

        if which in ("down", "out"):
            while turned:
                turned.pop().wait()
            finalt[0:cols, :] = buffer[:, 0:cols].T
            target = dwd if which == "down" else dwo
            out(finalt.at[pl.ds(0, cols)], target.at[pl.ds(start, cols)])
            turned.extend(copies)
            return
        if which == "gu":
            for j in range(cols // 256):
                at = start // 2 + j * 128
                out(buffer.at[:, pl.ds(j * 256, 128)], dgate.at[:, pl.ds(at, 128)])
                out(buffer.at[:, pl.ds(j * 256 + 128, 128)], dup.at[:, pl.ds(at, 128)])
        elif start == 0:
            out(buffer.at[:, pl.ds(0, cols)], dq.at[:, pl.ds(0, cols)])
        else:
            out(buffer.at[:, pl.ds(0, 128)], dq.at[:, pl.ds(start, 128)])
            dk[...] = buffer[:, 128:192]
            dv[...] = buffer[:, 192:256]
        staged[k] = copies

    loads["grad"].wait()
    present = act_own[0, 0:own, :]
    og[p.t] = (present * grad[...]).astype(BF)
    view = og.reshape(2, 2, own, width)
    rows.gather_start(0, view)
    for level in range(RECUR):
        loads["down", level].wait()
    mates(0)
    rows.gather_finish(0, view)
    write(og, og_hbm)
    mates(1)
    loads["w"].wait()
    loads["qkv"].wait()
    attended_grad = dot(og[...].reshape(count, width), w[:, WO : WO + 512], NN)
    y["qkv"][0:count, :] = attention_back(
        qkv[...].astype(F32), attended_grad, cosine[...], sine[...], allowed, own
    ).astype(BF)

    def attention_tile(cols):
        return dot(y["qkv"][0:count, :], w[cols, QKV : QKV + 640], NT)

    def take(cols, total):
        upstream[:, cols] = total

    rows.reduce(0, own, attention_tile, take)
    loads["hidden"].wait()
    update, add = norm_back(hidden[...], gain[0:1, :], upstream[...])
    grad[...] += update
    gains[...] = gain_in[...]
    gains[0:1, :] += add
    for which in range(3):
        peers_copy(p, grad, grad_all, tsend.at[1], trecv.at[1], which).start()
        peers_copy(p, gains, gpeers, tsend.at[2], trecv.at[2], which).start()
    pltpu.make_async_copy(grad, grad_all.at[p.t], tsend.at[1, 3]).start()
    gpeers[p.t] = gains[...]
    for level in range(RECUR):
        loads["gu", level].wait()
        loads["out", level].wait()
    for level in (1, 2):
        loads["qkv", level].wait()
    for copy in writes:
        copy.wait()

    def wait_peers(i, src, dst, local=True):
        for which in range(3):
            copy = peers_copy(p, src, dst, tsend.at[i], trecv.at[i], which)
            copy.wait_recv()
            copy.wait_send()
        if local:
            pltpu.make_async_copy(src, dst.at[p.t], tsend.at[i, 3]).wait()

    def outputs():
        wait_peers(0, fin_in, fin_all)
        wait_peers(1, grad, grad_all)
        mine = back[pl.ds(pl.multiple_of(p.t * own, own), own), :]

        @pl.loop(0, width // OC)
        def _(c):
            cols = pl.ds(pl.multiple_of(c * OC, OC), OC)
            first = pltpu.make_async_copy(fin_all.at[:, :, cols], fin_chunk, loadsem.at[0])
            second = pltpu.make_async_copy(grad_all.at[:, :, cols], chunk_in, loadsem.at[1])
            first.start()
            second.start()
            first.wait()
            second.wait()
            act_out[:, :, cols] = dot(mine, fin_chunk[...].reshape(count, OC), NN).astype(BF).reshape(
                MB, own // MB, OC
            )
            value = chunk_in[...].reshape(count, OC)
            high = value.astype(BF)
            rest = value - high.astype(F32)
            middle = rest.astype(BF)
            low = (rest - middle.astype(F32)).astype(BF)
            total = dot(mine, high, NN) + (dot(mine, middle, NN) + dot(mine, low, NN))
            tok_out[:, :, cols] = total.reshape(MB, own // MB, OC)

    def gain_tile(chunk):
        start = pl.multiple_of(chunk * chunk_rows // window * window, window)
        return (
            gpeers[0, :, pl.ds(start, window)]
            + gpeers[1, :, pl.ds(start, window)]
            + gpeers[2, :, pl.ds(start, window)]
            + gpeers[3, :, pl.ds(start, window)]
        )

    last = len(GRADS)

    def gain_mate(i):
        return remote(gmate_stage.at[i], gmate.at[i], msend.at[last, i], mrecv.at[last, i], p.mate)

    def gain_along(i, right):
        return remote(
            gmate.at[i], gline.at[i], lsend.at[last, i], lrecv.at[last, i], p.right if right else p.left
        )

    def gain_last(i):
        return remote(gmate.at[i], gline_own, lsend.at[last, i], lrecv2.at[last], p.left)

    def gain_mates():
        wait_peers(2, gains, gpeers, False)

        @pl.loop(0, line)
        def _(i):
            gmate_stage[i] = gain_tile(2 * i + 1 - p.b)
            gain_mate(i).start()

    def gain_lines():
        @pl.loop(0, line)
        def _(step):
            odd = lax.rem(step, 2)
            i = jnp.where(odd == 1, step // 2, line - 1 - step // 2)

            @pl.when(i != p.a)
            def _():
                gain_mate(i).wait_recv()
                gmate[i] += gain_tile(2 * i + p.b)

                @pl.when(((i > p.a) & p.has_left) | ((i < p.a) & p.has_right))
                def _():
                    gain_along(i, True).wait_recv()
                    gmate[i] += gline[i]

                pl.when(i > p.a)(lambda: gain_along(i, True).start())
                pl.when(i < p.a - 1)(lambda: gain_along(i, False).start())
                pl.when(i == p.a - 1)(lambda: gain_last(i).start())

        gain_mate(p.a).wait_recv()
        gain_sum[...] = gain_tile(2 * p.a + p.b) + gmate[p.a]

        @pl.when(p.has_left)
        def _():
            gain_along(p.a, True).wait_recv()
            gain_sum[...] += gline[p.a]

        @pl.when(p.has_right)
        def _():
            gain_last(p.a).wait_recv()
            gain_sum[...] += gline_own[...]

        @pl.loop(0, line)
        def _(i):
            gain_mate(i).wait_send()
            pl.when(i != p.a)(lambda: gain_along(i, True).wait_send())

    for k in range(len(GRADS)):
        x_start(GRADS[k][0], p.b, xl, xsem.at[1])
        if k + DEPTH < len(GRADS):
            mates(k + DEPTH)
        if k == 1:
            gain_mates()
        if k == 2:
            gain_lines()
        if k == 3:
            outputs()
        store(k)
    for k in range(len(GRADS)):
        drain(k)
    for copies in list(staged.values()) + [turned]:
        for copy in copies:
            copy.wait()


def gradients(n, w_all, gain, tables, saved, bwd, fin, tensor_index):
    perm, back, cosine, sine, masks, act = tables
    width = w_all.shape[0]
    act_own = lax.dynamic_slice_in_dim(act, tensor_index * OWN[0], OWN[0], axis=1)[:, :, None]
    hidden_cols = (COLS - GU) // 3
    line = n // 2
    chunk_rows = width // n
    window = max(128, chunk_rows)
    vmem = pl.BlockSpec(memory_space=pltpu.VMEM)
    hbm = pl.BlockSpec(memory_space=pl.ANY)
    total_rows = T * sum(OWN)
    own = OWN[0]
    operands = [w_all, gain, cosine, sine, act_own, masks[0], back]
    specs = [hbm] + [vmem] * 6
    operands += [bwd["grad"], bwd["gain_part"], fin, saved[0]["hidden"], saved[0]["qkv"]]
    specs += [hbm, vmem, hbm, hbm, hbm]
    streams = list(bwd["dg"]) + [s["mixed"] for s in saved] + [s["normed"] for s in saved] + list(bwd["og"])
    streams += [s["prod"] for s in saved] + list(bwd["gug"]) + [s["att"] for s in saved] + list(bwd["qkvg"])
    operands += streams
    specs += [hbm] * len(streams)
    outs = [
        ((MB, own // MB, width), BF),
        ((MB, own // MB, width), F32),
        ((chunk_rows, 512), F32),
        ((chunk_rows, HS), F32),
        ((chunk_rows, HS), F32),
        ((512, chunk_rows), F32),
        ((chunk_rows, hidden_cols), F32),
        ((chunk_rows, hidden_cols), F32),
        ((hidden_cols, chunk_rows), F32),
        ((8, window), F32),
        ((T, own, width), BF),
        ((T, own, width), BF),
        ((T, own, width), F32),
    ]
    out_specs = [vmem, vmem, hbm, vmem, vmem, hbm, hbm, hbm, hbm, vmem, hbm, hbm, hbm]
    scratch = [pltpu.VMEM((width, GU), BF)]
    scratch += [pltpu.VMEM((total_rows, c), BF) for c in (hidden_cols, 2 * hidden_cols, 512, 640)]
    scratch += [pltpu.VMEM((line, total_rows, window), BF)] * 2
    scratch += [
        pltpu.VMEM((T, own, width), BF),
        pltpu.VMEM((own, width), F32),
        pltpu.VMEM((T * own, 640), BF),
        pltpu.VMEM((own, width), F32),
        pltpu.VMEM((own, width), F32),
        pltpu.VMEM((8, width), F32),
        pltpu.VMEM((T, 8, width), F32),
    ]
    scratch += [
        pltpu.VMEM((DEPTH, line, chunk_rows, WIDEST), BF),
        pltpu.VMEM((line, chunk_rows, COLS), BF),
        pltpu.VMEM((line, chunk_rows, COLS), BF),
        pltpu.VMEM((chunk_rows, COLS), BF),
        pltpu.VMEM((window, WIDEST) if window > chunk_rows else (8, 128), F32),
    ]
    scratch += [pltpu.VMEM((line, 8, window), F32)] * 3 + [pltpu.VMEM((8, window), F32)]
    scratch += [pltpu.VMEM((chunk_rows, WIDEST), F32)] * 2
    scratch += [pltpu.VMEM((WIDEST, chunk_rows), F32)]
    scratch += [pltpu.VMEM((T, own, OC), F32), pltpu.VMEM((8, 128), F32), pltpu.VMEM((T, own, OC), BF)]
    scratch += [pltpu.VMEM((2, 2, own, width), BF), pltpu.VMEM((own, width), BF)]
    scratch += [pltpu.VMEM((2, own, width), BF), pltpu.VMEM((own, width), BF)]
    dma = pltpu.SemaphoreType.DMA
    chunks = width // DC
    k = len(GRADS) + 1
    scratch += [dma((1, chunks))] * 4 + [dma((1, 3))] * 2
    scratch += [dma((k, line))] * 4 + [dma((k,))]
    scratch += [dma((3, 4)), dma((3, 3))]
    scratch += [dma((24,)), dma((2, line, RECUR)), dma((4,)), dma((k, 8)), dma((2,))]
    res = pl.pallas_call(
        functools.partial(gradient_kernel, n),
        out_shape=[jax.ShapeDtypeStruct(*entry) for entry in outs],
        in_specs=specs,
        out_specs=out_specs,
        scratch_shapes=scratch,
        compiler_params=pltpu.CompilerParams(
            collective_id=3, has_side_effects=True, vmem_limit_bytes=63 << 20
        ),
    )(*operands)
    return res


def shards(n, *args):
    tokens, depth, lengths, cotangent = args[:4]
    attn_gain, mlp_gain = args[11:]
    index = lax.axis_index("tensor")
    tables = prologue(depth, lengths[:, 0], index)
    joined = join_weights(*args[4:11])
    gains = place_gains(n, attn_gain, mlp_gain)
    w_all, gain, fin, cot_own, cot_all, saved = forward(n, tokens, cotangent, joined, gains, tables, index)
    bwd = backward(n, w_all, gain, cot_own, cot_all, tables, saved, index)
    res = gradients(n, w_all, gain, tables, saved, bwd, fin, index)
    activations, tokens_grad, dq, dk, dv, dwo, dgate, dup, dwd, gain_sum = res[:10]
    each = attn_gain.shape[0]
    window = gain_sum.shape[1]
    start = lax.rem((lax.axis_index("dp") * T + index) * each, window)
    both = lax.dynamic_slice_in_dim(gain_sum, start, each, axis=1)
    return (activations, tokens_grad, dq, dk, dv, dwo, dgate, dup, dwd, both[0], both[1])


def solution(mesh):
    rows = P(None, ("dp", "tensor"), None)
    weight_specs = (P("dp", "tensor"),) * 3 + (P("tensor", "dp"),) + (P("dp", "tensor"),) * 2 + (P("tensor", "dp"),)
    gain_specs = (P(("dp", "tensor")),) * 2
    return jax.shard_map(
        functools.partial(shards, mesh.shape["dp"]),
        mesh=mesh,
        in_specs=(rows, P(None, "dp"), P(None, "dp", None), rows) + weight_specs + gain_specs,
        out_specs=(rows, rows) + weight_specs + gain_specs,
        check_vma=False,
    )
```

```python
import functools

import jax
import jax.numpy as jnp
import numpy as np
from jax import lax
from jax.experimental import pallas as pl
from jax.experimental.pallas import tpu as pltpu
from jax.sharding import PartitionSpec as P

HQ = 32
KVH = 4
HS = 64
MB = 2
RECUR = 3
SCALE = HS ** (-0.5)
F32 = jnp.float32
BF = jnp.bfloat16
MESH = pl.DeviceIdType.MESH
NN = (((1,), (0,)), ((), ()))
NT = (((1,), (1,)), ((), ()))
TN = (((0,), (0,)), ((), ()))

OWN = (96, 80, 48)
PIECES = ((0, 24, 0), (24, 24, 1), (48, 16, 0), (64, 16, 1), (80, 8, 0), (88, 8, 1))
T = 4
DC = 512
OC = 256
HEADS = 2


def split_batches(values, own):
    halves = ([], [])
    for owner in range(T):
        for start, rows, b in PIECES:
            if start < own:
                halves[b].append(values[owner * own + start : owner * own + start + rows])
    return [jnp.concatenate(half, axis=0) for half in halves]


def join_batches(halves, own):
    rows_out, at = [], [0, 0]
    for owner in range(T):
        for start, rows, b in PIECES:
            if start < own:
                rows_out.append(halves[b][at[b] : at[b] + rows])
                at[b] += rows
    return jnp.concatenate(rows_out, axis=0)


def dot(left, right, dims):
    return lax.dot_general(left, right, dims, preferred_element_type=F32)


def swap_halves(tile):
    lane = lax.broadcasted_iota(jnp.int32, tile.shape, 1)
    return jnp.where((lane & 63) < 32, pltpu.roll(tile, 96, 1), pltpu.roll(tile, 32, 1))


def attention_shares(query, key, allowed):
    rows = query.shape[0]
    group = query.shape[1] // HS
    stacked = stack_heads(query)
    scores = dot(stacked, key, NT).reshape(group, rows, rows) * SCALE
    scores = jnp.where(allowed.astype(F32)[None] > 0, scores, -1e30)
    raised = jnp.exp(scores - jnp.max(scores, axis=-1, keepdims=True))
    return stacked, raised * (1.0 / jnp.sum(raised, axis=-1, keepdims=True))


def stack_heads(values):
    group = values.shape[1] // HS
    return jnp.concatenate([values[:, h * HS : (h + 1) * HS] for h in range(group)], axis=0)


def unstack_heads(values, rows):
    group = values.shape[0] // rows
    return jnp.concatenate([values[h * rows : (h + 1) * rows] for h in range(group)], axis=1)


def mean_square(values):
    return jnp.mean(values * values, axis=-1, keepdims=True)


class Place:
    def __init__(self, n):
        self.n = n
        self.line = n // 2
        self.dp = lax.axis_index("dp")
        self.t = lax.axis_index("tensor")
        self.a = self.dp // 2
        self.b = lax.rem(self.dp, 2)
        self.hi = self.t // 2
        self.lo = lax.rem(self.t, 2)
        self.has_right = self.a < self.line - 1
        self.has_left = self.a > 0
        self.mate = (self.a * 2 + 1 - self.b, self.t)
        self.right = (jnp.minimum(self.dp + 2, n - 1), self.t)
        self.left = (jnp.maximum(self.dp - 2, 0), self.t)
        self.near = (self.dp, self.hi * 2 + 1 - self.lo)
        self.far = (self.dp, (1 - self.hi) * 2 + self.lo)
        self.diag = (self.dp, (1 - self.hi) * 2 + 1 - self.lo)

    def barrier(self, along):
        sem = pltpu.get_barrier_semaphore()

        def greet(device):
            pl.semaphore_signal(sem, inc=1, device_id=device, device_id_type=MESH)

        for device in (self.near, self.far, self.diag):
            greet(device)
        expected = 3
        if along:
            greet(self.mate)
            pl.when(self.has_right)(lambda: greet(self.right))
            pl.when(self.has_left)(lambda: greet(self.left))
            expected = 4 + self.has_right.astype(jnp.int32) + self.has_left.astype(jnp.int32)
        pl.semaphore_wait(sem, expected)


def remote(src, dst, send, recv, device):
    return pltpu.make_async_remote_copy(
        src_ref=src, dst_ref=dst, send_sem=send, recv_sem=recv, device_id=device, device_id_type=MESH
    )


class LineGather:
    def __init__(self, place, pieces, sems):
        self.p = place
        self.pieces = pieces
        self.msend, self.mrecv, self.rsend, self.rrecv, self.lsend, self.lrecv = sems

    def toward_left(self, w, k, chunk):
        ref = self.pieces[w][1](chunk)
        return remote(ref, ref, self.lsend.at[w, k], self.lrecv.at[w, k], self.p.left)

    def toward_right(self, w, k, chunk):
        ref = self.pieces[w][1](chunk)
        return remote(ref, ref, self.rsend.at[w, k], self.rrecv.at[w, k], self.p.right)

    def toward_mate(self, w, k, chunk):
        ref = self.pieces[w][1](chunk)
        return remote(ref, ref, self.msend.at[w, k], self.mrecv.at[w, k], self.p.mate)

    def first(self, w):
        p = self.p
        return p.a * 2 + 1 - p.b if self.pieces[w][0] == "other" else p.dp

    def own(self, w):
        p = self.p
        kind = self.pieces[w][0]
        chunk = self.first(w)
        if kind == "other":
            self.toward_mate(w - 1, p.a, chunk).wait_recv()
        pl.when(p.has_left)(lambda: self.toward_left(w, 0, chunk).start())
        pl.when(p.has_right)(lambda: self.toward_right(w, 0, chunk).start())
        if kind != "other":
            self.toward_mate(w, p.a, chunk).start()

    def step(self, w, k):
        p = self.p
        normal = self.pieces[w][0] == "normal"

        @pl.when(p.a + k < p.line)
        def _():
            chunk = self.first(w) + 2 * k
            self.toward_left(w, k - 1, chunk).wait_recv()
            pl.when(p.has_left)(lambda: self.toward_left(w, k, chunk).start())
            if normal:
                self.toward_mate(w, p.a + k, chunk).start()

        @pl.when(p.a - k >= 0)
        def _():
            chunk = self.first(w) - 2 * k
            self.toward_right(w, k - 1, chunk).wait_recv()
            pl.when(p.has_right)(lambda: self.toward_right(w, k, chunk).start())
            if normal:
                self.toward_mate(w, p.a - k, chunk).start()

    def steps(self, w):
        for k in range(1, self.p.line):
            self.step(w, k)

    def arrive(self, w):
        p = self.p
        if self.pieces[w][0] == "normal":
            for i in range(p.line):
                self.toward_mate(w, i, 2 * i + 1 - p.b).wait_recv()

    def drain(self, w):
        p = self.p
        kind = self.pieces[w][0]
        if kind == "own":
            self.toward_mate(w, p.a, p.dp).wait_send()
        for i in range(p.line):
            if kind == "normal":
                self.toward_mate(w, i, p.dp).wait_send()
            pl.when(p.has_left & (p.a + i < p.line))(lambda: self.toward_left(w, i, p.dp).wait_send())
            pl.when(p.has_right & (p.a - i >= 0))(lambda: self.toward_right(w, i, p.dp).wait_send())


class Rows:
    def __init__(self, place, part, relay, sums, sems):
        self.p = place
        self.part, self.relay, self.sums = part, relay, sums
        self.s1, self.q1, self.s2, self.q2, self.gs, self.gr = sems

    def first_copy(self, i, own, c):
        p = self.p
        cols = pl.ds(pl.multiple_of(c * DC, DC), DC)
        return remote(
            self.part.at[:, 1 - p.lo, pl.ds(0, own), cols],
            self.sums[i][0].at[:, :, cols],
            self.s1.at[i, c],
            self.q1.at[i, c],
            p.near,
        )

    def second_copy(self, i, own, c):
        p = self.p
        cols = pl.ds(pl.multiple_of(c * DC, DC), DC)
        return remote(
            self.relay.at[pl.ds(0, own), cols],
            self.sums[i][1].at[:, cols],
            self.s2.at[i, c],
            self.q2.at[i, c],
            p.far,
        )

    def reduce(self, i, own, tile, finish):
        p = self.p
        part, relay = self.part, self.relay
        r1, r2 = self.sums[i]
        chunks = part.shape[-1] // DC

        def pass_on(c):
            cols = pl.ds(pl.multiple_of(c * DC, DC), DC)
            self.first_copy(i, own, c).wait_recv()
            mine = part[1 - p.hi, p.lo, 0:own, cols].astype(F32)
            relay[0:own, cols] = (mine + r1[1 - p.hi, :, cols].astype(F32)).astype(BF)
            self.second_copy(i, own, c).start()

        @pl.loop(0, chunks)
        def _(c):
            cols = pl.ds(pl.multiple_of(c * DC, DC), DC)
            part[:, :, 0:own, cols] = tile(cols).astype(BF).reshape(2, 2, own, DC)
            self.first_copy(i, own, c).start()
            pl.when(c > 0)(lambda: pass_on(c - 1))

        pass_on(chunks - 1)

        @pl.loop(0, chunks)
        def _(c):
            cols = pl.ds(pl.multiple_of(c * DC, DC), DC)
            self.second_copy(i, own, c).wait_recv()
            mine = part[p.hi, p.lo, 0:own, cols].astype(F32)
            finish(cols, mine + r1[p.hi, :, cols].astype(F32) + r2[:, cols].astype(F32))

        @pl.loop(0, chunks)
        def _(c):
            self.first_copy(i, own, c).wait_send()
            self.second_copy(i, own, c).wait_send()

    def gather_copy(self, i, buffer, which):
        p = self.p
        here = buffer.at[p.hi, p.lo]
        if which == 0:
            return remote(here, here, self.gs.at[i, 0], self.gr.at[i, 0], p.far)
        if which == 1:
            return remote(here, here, self.gs.at[i, 1], self.gr.at[i, 1], p.near)
        there = buffer.at[1 - p.hi, p.lo]
        return remote(there, there, self.gs.at[i, 2], self.gr.at[i, 2], p.near)

    def gather_start(self, i, buffer):
        self.gather_copy(i, buffer, 0).start()
        self.gather_copy(i, buffer, 1).start()

    def gather_finish(self, i, buffer):
        self.gather_copy(i, buffer, 0).wait_recv()
        self.gather_copy(i, buffer, 2).start()
        self.gather_copy(i, buffer, 1).wait_recv()
        self.gather_copy(i, buffer, 2).wait_recv()
        for which in range(3):
            self.gather_copy(i, buffer, which).wait_send()


def peers_copy(place, src, dst, send, recv, which):
    device = (place.near, place.far, place.diag)[which]
    return remote(src, dst.at[place.t], send.at[which], recv.at[which], device)


def gain_row(gathered, n, row, width):
    each = width // (n * T)
    tiles = []
    for j in range(width // 128):
        total = None
        for i in range(128 // each):
            number = j * (128 // each) + i
            block = gathered[number % T, number // T][row : row + 1]
            total = block if total is None else total + block
        tiles.append(total)
    return jnp.concatenate(tiles, axis=1)


QKV, WO, GU, WD = 0, 640, 1152, 3968
COLS = 5376
RANGES = (
    ("along", 0, 640),
    ("along", 640, 512),
    ("along", 1152, 1408),
    ("along", 2560, 1408),
    ("along", 3968, 512),
    ("across", 4480, 896),
)


def ones(condition):
    return jnp.where(condition, 1.0, 0.0)


def iota(size, axis):
    shape = (size, 1) if axis == 0 else (1, size)
    return lax.broadcasted_iota(jnp.int32, shape, axis).astype(F32)


def quotient(index, step, most):
    total = ones(index >= step)
    for i in range(2, most):
        total = total + ones(index >= step * i)
    return total


def own_places(own_index):
    batch, place, seen = 0.0 * own_index, 0.0 * own_index, [0, 0]
    for start, rows, b in PIECES:
        inside = (own_index >= start) & (own_index < start + rows)
        batch = jnp.where(inside, float(b), batch)
        place = jnp.where(inside, own_index - start + seen[b], place)
        seen[b] += rows
    return batch, place


def fill_tables(p, depth_row, depth_col, lengths, freqs, perm, back, back_own, cosine, sine, allowed, act_own, act_last):
    local = OWN[0] // MB
    total = T * OWN[0]

    def columns(index):
        tensor = quotient(index, OWN[0], T)
        inside = index - tensor * OWN[0]
        batch = ones(inside >= local)
        return batch, tensor * local + inside - batch * local

    batch_row, pos_row = columns(iota(total, 1))
    batch_col, pos_col = columns(iota(total, 0))
    same = batch_row == batch_col
    rank_row = jnp.sum(
        ones(same & ((depth_col > depth_row) | ((depth_col == depth_row) & (pos_col < pos_row)))), axis=0, keepdims=True
    )
    rank_col = jnp.sum(
        ones(same & ((depth_row > depth_col) | ((depth_row == depth_col) & (pos_row < pos_col)))), axis=1, keepdims=True
    )

    def compact(index):
        owner = quotient(index, OWN[0], T)
        batch, place = own_places(index - owner * OWN[0])
        return batch, place * T + owner

    batch_q, rank_q = compact(iota(total, 0))
    hit = (rank_row == rank_q) & (batch_row == batch_q)
    perm[...] = ones(hit).astype(BF)
    batch_p, rank_p = compact(iota(total, 1))
    back[...] = ones((rank_col == rank_p) & (batch_col == batch_p)).astype(BF)
    back_own[...] = back[pl.ds(pl.multiple_of(p.t * OWN[0], OWN[0]), OWN[0]), :]

    ends = []
    for b in range(MB):
        first = lengths[b : b + 1, 0:1].astype(F32)
        ends.append((first, first + lengths[b : b + 1, 1:2].astype(F32)))
    position = jnp.sum(jnp.where(hit, pos_row, 0.0), axis=1, keepdims=True)
    end = [jnp.where(batch_q == 0.0, ends[0][i], ends[1][i]) for i in range(2)]
    start = jnp.where(position >= end[1], end[1], jnp.where(position >= end[0], end[0], 0.0))
    angles = (position - start) * freqs
    cosine[...] = jnp.cos(angles)
    lane = lax.broadcasted_iota(jnp.int32, angles.shape, 1)
    value = jnp.sin(angles)
    sine[...] = jnp.where((lane & 63) < 32, -value, value)

    own_batch, own_place = own_places(iota(OWN[0], 0))
    own_rank = own_place * T + p.t.astype(F32)
    for level in range(RECUR):
        own = OWN[level]
        half = T * own // MB
        counts = [
            jnp.sum(ones((batch_row == float(b)) & (depth_row >= level + 1.0)), axis=1, keepdims=True) for b in range(MB)
        ]
        act_own[level] = ones(own_rank < jnp.where(own_batch == 0.0, counts[0], counts[1]))
        if level == RECUR - 1:
            index = iota(T * own, 0)
            owner = quotient(index, own, T)
            batch, place = own_places(index - owner * own)
            act_last[...] = ones(place * T + owner < jnp.where(batch == 0.0, counts[0], counts[1]))

        def order(index):
            owner = quotient(index, own // MB, T)
            return (index - owner * (own // MB)) * T + owner

        index_col, index_row = iota(half, 0), iota(half, 1)
        order_col, order_row = order(index_col), order(index_row)
        for b in range(MB):
            at_col = jnp.sum(
                jnp.where((rank_row == order_col) & (batch_row == float(b)), pos_row, 0.0), axis=1, keepdims=True
            )
            at_row = jnp.sum(
                jnp.where((rank_col == order_row) & (batch_col == float(b)), pos_col, 0.0), axis=0, keepdims=True
            )
            document_col = ones(at_col >= ends[b][0]) + ones(at_col >= ends[b][1])
            document_row = ones(at_row >= ends[b][0]) + ones(at_row >= ends[b][1])
            ok = (document_col == document_row) & (at_row <= at_col) & (order_row < counts[b])
            allowed[level][b] = ones(ok | (index_col == index_row)).astype(BF)


def forward_kernel(n, *refs):
    it = iter(refs)
    tokens, cotangent, wq, wk, wv, wo, wg, wu, wd = [next(it) for _ in range(9)]
    attn_gain, mlp_gain, depth_row, depth_col, lengths, freqs = [next(it) for _ in range(6)]
    w_out, gain_out, fin_out, cot_own, cot_all = [next(it) for _ in range(5)]
    cosine, sine, back_own, act_own, act_last = [next(it) for _ in range(5)]
    allowed = [next(it) for _ in range(RECUR)]
    names = ("normed", "qkv", "att", "mixed", "gu", "prod", "hidden", "first")
    saved_out = [dict((k, next(it)) for k in names) for _ in range(RECUR)]
    w = next(it)
    perm, back, kv, wo_in, wd_in = [next(it) for _ in range(5)]
    gbuf, gall = next(it), next(it)
    tok, cot = next(it), next(it)
    saved = [dict((k, next(it)) for k in names) for _ in range(RECUR)]
    after, fin, cown = next(it), next(it), next(it)
    part, relay = next(it), next(it)
    sums = [(next(it), next(it)) for _ in range(2 * RECUR)]
    line_sems = [next(it) for _ in range(6)]
    row_sems = [next(it) for _ in range(6)]
    wsem = next(it)
    tsend, trecv, outsem = next(it), next(it), next(it)

    p = Place(n)
    width = tokens.shape[-1]
    rows_chunk = width // n

    def chunk_at(chunk, start, size):
        return w.at[pl.ds(pl.multiple_of(chunk * rows_chunk, rows_chunk), rows_chunk), pl.ds(start, size)]

    pieces = [("normal", lambda chunk: gbuf.at[chunk])]
    number = []
    for kind, start, size in RANGES:
        def at(chunk, start=start, size=size):
            return chunk_at(chunk, start, size)

        number.append(len(pieces))
        pieces += [("own", at), ("other", at)] if kind == "across" else [("normal", at)]
    line = LineGather(p, pieces, line_sems)
    rows = Rows(p, part, relay, sums, row_sems)
    hidden_cols = (COLS - GU) // 3
    writes = []

    def write(src, dst):
        copy = pltpu.make_async_copy(src, dst, outsem.at[len(writes)])
        copy.start()
        writes.append(copy)

    local = [
        pltpu.make_async_copy(wq, chunk_at(p.dp, QKV, 512), wsem.at[0]),
        pltpu.make_async_copy(wk, kv.at[0], wsem.at[1]),
        pltpu.make_async_copy(wv, kv.at[1], wsem.at[2]),
        pltpu.make_async_copy(wo, wo_in, wsem.at[3]),
        pltpu.make_async_copy(wg, chunk_at(p.dp, GU, hidden_cols), wsem.at[4]),
        pltpu.make_async_copy(wu, chunk_at(p.dp, GU + hidden_cols, hidden_cols), wsem.at[5]),
        pltpu.make_async_copy(wd, wd_in, wsem.at[6]),
    ]
    for copy in local:
        copy.start()
    mine_rows = pl.ds(pl.multiple_of(p.dp * rows_chunk, rows_chunk), rows_chunk)
    each = attn_gain.shape[1]
    lane = lax.broadcasted_iota(jnp.int32, (1, 128), 1)
    spot = lax.rem(p.dp * T + p.t, 128 // each)
    inside = (lane >= spot * each) & (lane < (spot + 1) * each)
    for row, gain in enumerate((attn_gain, mlp_gain)):
        value = jnp.concatenate([gain[...]] * (128 // each), axis=1)
        gbuf[p.dp, row : row + 1, :] = jnp.where(inside, value, 0.0)
    gbuf[p.dp, 2:8, :] = jnp.zeros((6, 128), F32)
    p.barrier(True)
    line.own(0)
    for copy in local[0:3]:
        copy.wait()
    w[mine_rows, QKV + 512 : QKV + 640] = jnp.concatenate([kv[0], kv[1]], axis=1)
    heads_piece, out_piece, gate_piece, up_piece, down_piece, down_last = number
    line.own(heads_piece)
    for which in range(3):
        peers_copy(p, tokens, tok, tsend.at[0], trecv.at[0], which).start()
    pltpu.make_async_copy(tokens, tok.at[p.t], tsend.at[0, 3]).start()
    local[3].wait()
    w[mine_rows, WO : WO + 512] = wo_in[...].T
    line.own(out_piece)
    for which in range(3):
        peers_copy(p, cotangent, cot, tsend.at[1], trecv.at[1], which).start()
    pltpu.make_async_copy(cotangent, cot.at[p.t], tsend.at[1, 3]).start()
    for copy in local[4:6]:
        copy.wait()
    line.own(gate_piece)
    line.steps(0)
    line.arrive(0)
    for which in range(3):
        peers_copy(p, gbuf, gall, tsend.at[2], trecv.at[2], which).start()
    pltpu.make_async_copy(gbuf, gall.at[p.t], tsend.at[2, 3]).start()
    fill_tables(
        p, depth_row[...], depth_col[...], lengths, freqs[...], perm, back, back_own, cosine, sine, allowed, act_own, act_last
    )
    line.steps(heads_piece)
    local[6].wait()
    w[mine_rows, WD : WD + hidden_cols] = wd_in[...].T
    line.own(up_piece)
    line.steps(out_piece)

    def wait_peers(i, src, dst):
        for which in range(3):
            copy = peers_copy(p, src, dst, tsend.at[i], trecv.at[i], which)
            copy.wait_recv()
            copy.wait_send()
        pltpu.make_async_copy(src, dst.at[p.t], tsend.at[i, 3]).wait()

    wait_peers(2, gbuf, gall)
    gain_out[0:1, :] = gain_row(gall, n, 0, width)
    gain_out[1:2, :] = gain_row(gall, n, 1, width)
    gain_out[2:8, :] = jnp.zeros((6, width), F32)

    wait_peers(0, tokens, tok)

    own = OWN[0]
    mine = perm[pl.ds(pl.multiple_of(p.t * own, own), own), :]
    saved[0]["hidden"][...] = dot(mine, tok[...].reshape(T * own, width), NN)

    @pl.loop(0, T)
    def _(owner):
        picked = perm[pl.ds(pl.multiple_of(owner * own, own), own), :]
        hidden = dot(picked, tok[...].reshape(T * own, width), NN)
        inverse = lax.rsqrt(mean_square(hidden) + 1e-05)
        saved[0]["normed"][owner] = (hidden * inverse * gain_out[0:1, :]).astype(BF)

    wait_peers(1, cotangent, cot)
    cown[...] = dot(mine, cot[...].reshape(T * own, width), NN)
    write(cown, cot_own)

    line.own(down_piece)
    line.own(down_last)

    @pl.loop(0, T)
    def _(owner):
        picked = perm[pl.ds(pl.multiple_of(owner * OWN[0], 32), OWN[RECUR - 1]), :]
        cot_all[owner] = dot(picked, cot[...].reshape(T * OWN[0], width), NN).astype(BF)

    line.arrive(heads_piece)

    for level in range(RECUR):
        own = OWN[level]
        count = T * own
        half = count // 2
        s = saved[level]
        if level:
            rows.gather_finish(2 * level - 1, s["normed"].reshape(2, 2, own, width))
        x = s["normed"][...].reshape(count, width)
        qkv = dot(x, w[:, QKV : QKV + 640], NN)
        cos = jnp.concatenate([cosine[owner * OWN[0] : owner * OWN[0] + own, :] for owner in range(T)], axis=0)
        sin = jnp.concatenate([sine[owner * OWN[0] : owner * OWN[0] + own, :] for owner in range(T)], axis=0)
        tiles = []
        for j in range(5):
            tile = qkv[:, j * 128 : (j + 1) * 128]
            turned = tile * cos + swap_halves(tile) * sin
            if j == 4:
                lane = lax.broadcasted_iota(jnp.int32, tile.shape, 1)
                turned = jnp.where(lane < HS, turned, tile)
            tiles.append(turned)
        rotated = jnp.concatenate(tiles, axis=1)
        s["qkv"][...] = rotated.astype(BF)
        write(s["qkv"], saved_out[level]["qkv"])
        heads = []
        for b, block in enumerate(split_batches(rotated, own)):
            query, key, value = (
                block[:, 0:512].astype(BF),
                block[:, 512:576].astype(BF),
                block[:, 576:640].astype(BF),
            )
            _, shares = attention_shares(query, key, allowed[level][b])
            out = dot(shares.astype(BF).reshape(8 * half, half), value, NN)
            heads.append(unstack_heads(out, half))
            if level == 0:
                line.step(gate_piece, 1) if b == 0 else [line.step(gate_piece, k) for k in range(2, p.line)]
        s["att"][...] = join_batches(heads, own).astype(BF)
        write(s["att"], saved_out[level]["att"])
        if level == 0:
            line.arrive(out_piece)
        present = act_own[level, 0:own, :]

        def attention_tile(cols):
            return dot(s["att"][...], w[cols, WO : WO + 512], NT)

        def attention_finish(cols, total):
            s["first"][:, cols] = s["hidden"][:, cols] + present * total

        rows.reduce(2 * level, own, attention_tile, attention_finish)
        first = s["first"][...]
        inverse = lax.rsqrt(mean_square(first) + 1e-05)
        s["mixed"][p.t] = (first * inverse * gain_out[1:2, :]).astype(BF)
        mixed = s["mixed"].reshape(2, 2, own, width)
        rows.gather_start(2 * level, mixed)
        write(s["first"], saved_out[level]["first"])
        if level == 0:
            line.steps(up_piece)
            line.own(down_last + 1)
        rows.gather_finish(2 * level, mixed)
        write(s["mixed"], saved_out[level]["mixed"])

        def hidden_block(start, size):
            x = s["mixed"][...].reshape(count, width)
            gate = dot(x, w[:, pl.ds(pl.multiple_of(GU + start, 128), size)], NN)
            upward = dot(x, w[:, pl.ds(pl.multiple_of(GU + hidden_cols + start, 128), size)], NN)
            cols = pl.ds(pl.multiple_of(start, 128), size)
            s["gu"][:, cols] = gate.astype(BF)
            s["gu"][:, pl.ds(pl.multiple_of(hidden_cols + start, 128), size)] = upward.astype(BF)
            s["prod"][:, cols] = (gate * jax.nn.sigmoid(gate) * upward).astype(BF)

        if level == 0:
            line.steps(down_piece)
            line.step(down_last, 1)
            line.step(down_last + 1, 1)
            line.arrive(gate_piece)
            line.arrive(up_piece)

        @pl.loop(0, hidden_cols // 256)
        def _(j):
            hidden_block(j * 256, 256)

        if hidden_cols % 256:
            hidden_block(hidden_cols // 256 * 256, 128)
        write(s["gu"], saved_out[level]["gu"])
        write(s["prod"], saved_out[level]["prod"])
        if level == 0:
            for k in range(2, p.line):
                line.step(down_last, k)
                line.step(down_last + 1, k)
            line.arrive(down_piece)
            write(w, w_out)

        def mlp_tile(cols):
            return dot(s["prod"][...], w[cols, WD : WD + 1408], NT)

        def mlp_finish(cols, total):
            after[0:own, cols] = s["first"][:, cols] + present * total

        rows.reduce(2 * level + 1, own, mlp_tile, mlp_finish)
        if level < RECUR - 1:
            deeper = OWN[level + 1]
            hidden = after[0:deeper, :]
            saved[level + 1]["hidden"][...] = hidden
            inverse = lax.rsqrt(mean_square(hidden) + 1e-05)
            saved[level + 1]["normed"][p.t] = (hidden * inverse * gain_out[0:1, :]).astype(BF)
            rows.gather_start(2 * level + 1, saved[level + 1]["normed"].reshape(2, 2, deeper, width))
            fin[deeper:own, :] = after[deeper:own, :].astype(BF)
        else:
            fin[0:own, :] = after[0:own, :].astype(BF)
        write(s["hidden"], saved_out[level]["hidden"])
        write(s["normed"], saved_out[level]["normed"])
    write(fin, fin_out)
    for i in range(len(pieces)):
        line.drain(i)
    for copy in writes:
        copy.wait()


def forward(n, tokens, depth, lengths, cotangent, weights, attn_gain, mlp_gain):
    width = tokens.shape[-1]
    hidden_cols = weights[4].shape[1]
    local = OWN[0] // MB
    total = T * OWN[0]
    ordered = depth.reshape(MB, T, local).transpose(1, 0, 2).astype(F32)
    freqs = jnp.asarray(np.tile(10000.0 ** (-np.arange(0, HS, 2) / HS), 4)[None].astype(np.float32))
    vmem = pl.BlockSpec(memory_space=pltpu.VMEM)
    hbm = pl.BlockSpec(memory_space=pl.ANY)

    def saved_shapes(own):
        count = T * own
        return {
            "normed": ((T, own, width), BF),
            "qkv": ((count, 640), BF),
            "att": ((count, 512), BF),
            "mixed": ((T, own, width), BF),
            "gu": ((count, 2 * hidden_cols), BF),
            "prod": ((count, hidden_cols), BF),
            "hidden": ((own, width), F32),
            "first": ((own, width), F32),
        }

    shapes = [((width, COLS), BF), ((8, width), F32), ((OWN[0], width), BF), ((OWN[0], width), F32), ((T, OWN[2], width), BF)]
    specs = [hbm, vmem, hbm, hbm, vmem]
    shapes += [((total, 128), F32)] * 2 + [((OWN[0], total), BF), ((RECUR, OWN[0], 1), F32), ((T * OWN[2], 1), F32)]
    shapes += [((MB, T * own // MB, T * own // MB), BF) for own in OWN]
    specs += [vmem] * (5 + RECUR)
    for own in OWN:
        for entry in saved_shapes(own).values():
            shapes.append(entry)
            specs.append(hbm)
    scratch = [pltpu.VMEM((width, COLS), BF)] + [pltpu.VMEM((total, total), BF)] * 2
    scratch += [pltpu.VMEM((2,) + weights[1].shape, BF), pltpu.VMEM(weights[3].shape, BF), pltpu.VMEM(weights[6].shape, BF)]
    scratch += [pltpu.VMEM((n, 8, 128), F32), pltpu.VMEM((T, n, 8, 128), F32)]
    scratch += [pltpu.VMEM((T,) + tokens.shape, BF)] * 2
    for own in OWN:
        scratch += [pltpu.VMEM(*entry) for entry in saved_shapes(own).values()]
    scratch += [pltpu.VMEM((OWN[0], width), F32), pltpu.VMEM((OWN[0], width), BF), pltpu.VMEM((OWN[0], width), F32)]
    scratch += [pltpu.VMEM((2, 2, OWN[0], width), BF), pltpu.VMEM((OWN[0], width), BF)]
    for own in OWN:
        for _ in range(2):
            scratch += [pltpu.VMEM((2, own, width), BF), pltpu.VMEM((own, width), BF)]
    dma = pltpu.SemaphoreType.DMA
    count = 1 + sum(2 if kind == "across" else 1 for kind, _, _ in RANGES)
    scratch += [dma((count, n // 2))] * 6
    chunks = width // DC
    scratch += [dma((2 * RECUR, chunks))] * 4 + [dma((2 * RECUR, 3))] * 2
    scratch += [dma((7,)), dma((3, 4)), dma((3, 3)), dma((40,))]
    outs = pl.pallas_call(
        functools.partial(forward_kernel, n),
        out_shape=[jax.ShapeDtypeStruct(*entry) for entry in shapes],
        in_specs=[hbm] * 9 + [vmem] * 6,
        out_specs=specs,
        scratch_shapes=scratch,
        compiler_params=pltpu.CompilerParams(
            collective_id=1, has_side_effects=True, vmem_limit_bytes=62 << 20
        ),
    )(
        tokens,
        cotangent,
        *weights,
        attn_gain[None],
        mlp_gain[None],
        ordered.reshape(1, total),
        ordered.reshape(total, 1),
        lengths,
        freqs,
    )
    w_all, gain, fin, cot_own, cot_all = outs[:5]
    tables = dict(zip(("cosine", "sine", "back", "act", "act_last"), outs[5:10]))
    tables["masks"] = outs[10:13]
    names = list(saved_shapes(1))
    saved = [dict(zip(names, outs[13 + 8 * level : 21 + 8 * level])) for level in range(RECUR)]
    return w_all, gain, fin, cot_own, cot_all, tables, saved


def attention_back(rotated, attended_grad, cos, sin, allowed, own, between=None):
    half = T * own // 2
    grads = []
    split = split_batches(rotated, own)
    upstream = split_batches(attended_grad, own)
    for b in range(MB):
        block = split[b]
        query, key, value = block[:, 0:512].astype(BF), block[:, 512:576].astype(BF), block[:, 576:640].astype(BF)
        up_all = upstream[b].astype(BF)
        query_grads, key_grad, value_grad = [], 0.0, 0.0
        for start in range(0, 512, HEADS * HS):
            stacked, shares = attention_shares(query[:, start : start + HEADS * HS], key, allowed[b])
            up = stack_heads(up_all[:, start : start + HEADS * HS])
            low = shares.astype(BF).reshape(HEADS * half, half)
            shares_grad = dot(up, value, NT).reshape(HEADS, half, half)
            value_grad += dot(low, up, TN)
            spread = jnp.sum(shares * shares_grad, axis=-1, keepdims=True)
            score_grad = (shares * (shares_grad - spread)).astype(BF).reshape(HEADS * half, half)
            query_grads.append(unstack_heads(dot(score_grad, key, NN), half) * SCALE)
            key_grad += dot(score_grad, stacked, TN) * SCALE
        query_grad = jnp.concatenate(query_grads, axis=1)
        grads.append(jnp.concatenate([query_grad, key_grad, value_grad], axis=1))
        if between is not None:
            between()
    joined = join_batches(grads, own)
    tiles = []
    for j in range(5):
        tile = joined[:, j * 128 : (j + 1) * 128]
        turned = tile * cos - swap_halves(tile) * sin
        if j == 4:
            lane = lax.broadcasted_iota(jnp.int32, tile.shape, 1)
            turned = jnp.where(lane < HS, turned, tile)
        tiles.append(turned)
    return jnp.concatenate(tiles, axis=1)


def level_rows(table, own):
    return jnp.concatenate([table[owner * OWN[0] : owner * OWN[0] + own, :] for owner in range(T)], axis=0)


def norm_back(source, gain, upstream):
    inverse = lax.rsqrt(mean_square(source) + 1e-05)
    unit = source * inverse
    gain_part = jnp.sum(upstream * unit, axis=0, keepdims=True)
    scaled = upstream * gain
    return inverse * (scaled - unit * jnp.mean(scaled * unit, axis=-1, keepdims=True)), gain_part


def backward_kernel(n, *refs):
    it = iter(refs)
    (w_all, gain, cot_own, cot_all, cosine, sine, act_own, act_last) = [next(it) for _ in range(8)]
    allowed = [None] + [next(it) for _ in range(2)]
    saved_in = []
    for level in range(RECUR):
        names = ("gu", "first") if level == 0 else ("gu", "first", "qkv", "hidden")
        saved_in.append({k: next(it) for k in names})
    dg_out = [next(it) for _ in range(3)]
    gug_out = [next(it) for _ in range(3)]
    og_out = [None] + [next(it) for _ in range(2)]
    qkvg_out = [None] + [next(it) for _ in range(2)]
    grad_out, gain_part = next(it), next(it)
    w = next(it)
    saved = []
    for level in range(RECUR):
        saved.append({k: next(it) for k in saved_in[level]})
    dg = [next(it) for _ in range(3)]
    gug = [next(it) for _ in range(3)]
    og = [None] + [next(it) for _ in range(2)]
    qkvg = [None] + [next(it) for _ in range(2)]
    grad, upstream = next(it), next(it)
    part, relay = next(it), next(it)
    sums = [(next(it), next(it)) for _ in range(5)]
    row_sems = [next(it) for _ in range(6)]
    insem, outsem = next(it), next(it)

    p = Place(n)
    width = w.shape[0]
    rows = Rows(p, part, relay, sums, row_sems)
    hidden_cols = (COLS - GU) // 3
    loads, writes = {}, []

    def load(name, src, dst):
        copy = pltpu.make_async_copy(src, dst, insem.at[len(loads)])
        copy.start()
        loads[name] = copy

    def write(src, dst):
        copy = pltpu.make_async_copy(src, dst, outsem.at[len(writes)])
        copy.start()
        writes.append(copy)

    def columns(start, size):
        load(("w", start), w_all.at[:, pl.ds(start, size)], w.at[:, pl.ds(start, size)])

    columns(WD, hidden_cols)
    load("grad", cot_own, grad)
    last = RECUR - 1
    load(("gu", last), saved_in[last]["gu"], saved[last]["gu"])
    columns(GU, 2 * hidden_cols)
    load(("first", last), saved_in[last]["first"], saved[last]["first"])
    columns(WO, 512)
    for name in ("qkv", "hidden"):
        load((name, last), saved_in[last][name], saved[last][name])
    columns(QKV, 640)
    for level in (1, 0):
        for name in saved_in[level]:
            load((name, level), saved_in[level][name], saved[level][name])
    p.barrier(False)
    gain_part[...] = jnp.zeros_like(gain_part)

    for level in range(last, -1, -1):
        own = OWN[level]
        count = T * own
        s = saved[level]
        base = 2 * (last - level)
        present = act_own[level, 0:own, :]
        if level == last:
            dg[level][...] = (cot_all[...].astype(F32).reshape(count, width) * act_last[...]).astype(BF).reshape(
                T, own, width
            )
            loads["grad"].wait()
        else:
            dg[level][p.t] = (present * grad[0:own, :]).astype(BF)
            view = dg[level].reshape(2, 2, own, width)
            rows.gather_start(base, view)
            rows.gather_finish(base, view)
        write(dg[level], dg_out[level])
        if level == last:
            loads["w", WD].wait()
        loads["gu", level].wait()

        def hidden_block(start, size):
            wcols = pl.ds(pl.multiple_of(WD + start, 128), size)
            product_grad = dot(dg[level][...].reshape(count, width), w[:, wcols], NN)
            low = pl.ds(pl.multiple_of(start, 128), size)
            high = pl.ds(pl.multiple_of(hidden_cols + start, 128), size)
            gate = s["gu"][:, low].astype(F32)
            upward = s["gu"][:, high].astype(F32)
            sigma = jax.nn.sigmoid(gate)
            gug[level][:, low] = (product_grad * upward * sigma * (1.0 + gate * (1.0 - sigma))).astype(BF)
            gug[level][:, high] = (product_grad * gate * sigma).astype(BF)

        @pl.loop(0, hidden_cols // 256)
        def _(j):
            hidden_block(j * 256, 256)

        if hidden_cols % 256:
            hidden_block(hidden_cols // 256 * 256, 128)
        write(gug[level], gug_out[level])
        if level == last:
            loads["w", GU].wait()

        def mlp_tile(cols):
            return dot(gug[level][...], w[cols, GU : GU + 2 * hidden_cols], NT)

        def take(cols, total):
            upstream[0:own, cols] = total

        rows.reduce(base, own, mlp_tile, take)
        loads["first", level].wait()
        update, add = norm_back(s["first"][...], gain[1:2, :], upstream[0:own, :])
        grad[0:own, :] += update
        gain_part[1:2, :] += add
        if level == 0:
            break
        og[level][p.t] = (present * grad[0:own, :]).astype(BF)
        view = og[level].reshape(2, 2, own, width)
        rows.gather_start(base + 1, view)
        rows.gather_finish(base + 1, view)
        write(og[level], og_out[level])
        if level == last:
            loads["w", WO].wait()
        loads["qkv", level].wait()
        attended_grad = dot(og[level][...].reshape(count, width), w[:, WO : WO + 512], NN)
        cos, sin = level_rows(cosine, own), level_rows(sine, own)
        qkvg[level][...] = attention_back(
            s["qkv"][...].astype(F32), attended_grad, cos, sin, allowed[level], own
        ).astype(BF)
        write(qkvg[level], qkvg_out[level])
        if level == last:
            loads["w", QKV].wait()

        def attention_tile(cols):
            return dot(qkvg[level][...], w[cols, QKV : QKV + 640], NT)

        rows.reduce(base + 1, own, attention_tile, take)
        loads["hidden", level].wait()
        update, add = norm_back(s["hidden"][...], gain[0:1, :], upstream[0:own, :])
        grad[0:own, :] += update
        gain_part[0:1, :] += add

    write(grad, grad_out)
    for copy in writes:
        copy.wait()


def backward(n, w_all, gain, cot_own, cot_all, tables, saved):
    width = w_all.shape[0]
    hidden_cols = (COLS - GU) // 3
    vmem = pl.BlockSpec(memory_space=pltpu.VMEM)
    hbm = pl.BlockSpec(memory_space=pl.ANY)
    operands = [w_all, gain, cot_own, cot_all, tables["cosine"], tables["sine"], tables["act"], tables["act_last"]]
    operands += list(tables["masks"][1:])
    specs = [hbm, vmem, hbm] + [vmem] * 7
    used = []
    for level in range(RECUR):
        for name in ("gu", "first") if level == 0 else ("gu", "first", "qkv", "hidden"):
            operands.append(saved[level][name])
            specs.append(hbm)
            used.append(saved[level][name])
    outs = [((T, own, width), BF) for own in OWN]
    outs += [((T * own, 2 * hidden_cols), BF) for own in OWN]
    outs += [((T, own, width), BF) for own in OWN[1:]]
    outs += [((T * own, 640), BF) for own in OWN[1:]]
    scratch = [pltpu.VMEM(w_all.shape, BF)] + [pltpu.VMEM(u.shape, u.dtype) for u in used]
    scratch += [pltpu.VMEM(*entry) for entry in outs]
    outs += [((OWN[0], width), F32), ((8, width), F32)]
    out_specs = [hbm] * (len(outs) - 1) + [vmem]
    scratch += [pltpu.VMEM((OWN[0], width), F32)] * 2
    scratch += [pltpu.VMEM((2, 2, OWN[0], width), BF), pltpu.VMEM((OWN[0], width), BF)]
    for own in (OWN[2], OWN[2], OWN[1], OWN[1], OWN[0]):
        scratch += [pltpu.VMEM((2, own, width), BF), pltpu.VMEM((own, width), BF)]
    dma = pltpu.SemaphoreType.DMA
    chunks = width // DC
    scratch += [dma((5, chunks))] * 4 + [dma((5, 3))] * 2 + [dma((24,)), dma((16,))]
    res = pl.pallas_call(
        functools.partial(backward_kernel, n),
        out_shape=[jax.ShapeDtypeStruct(*entry) for entry in outs],
        in_specs=specs,
        out_specs=out_specs,
        scratch_shapes=scratch,
        compiler_params=pltpu.CompilerParams(
            collective_id=2, has_side_effects=True, vmem_limit_bytes=62 << 20
        ),
    )(*operands)
    return {
        "dg": res[0:3],
        "gug": res[3:6],
        "og": res[6:8],
        "qkvg": res[8:10],
        "grad": res[10],
        "gain_part": res[11],
    }


PIECE = 384
SEGMENTS = (("down", 1408), ("gu", 2816), ("out", 512), ("qkv", 640))
DEPTH = 3
FIRST = 2
PLACES = COLS // PIECE + FIRST


def cut_pieces():
    pieces = [[] for _ in range(COLS // PIECE)]
    at = 0
    for which, size in SEGMENTS:
        done = 0
        while done < size:
            k, inside = divmod(at, PIECE)
            cols = min(size - done, PIECE - inside)
            pieces[k].append((which, done, cols, inside))
            done += cols
            at += cols
    return pieces


def gradient_kernel(n, *refs):
    it = iter(refs)
    (w_all, gain, cosine, sine, act_own, allowed, back) = [next(it) for _ in range(7)]
    grad_in, gain_in, fin_in, hidden_in, qkv_in = [next(it) for _ in range(5)]
    x_in = {name: [next(it) for _ in range(3)] for name in ("down", "gu", "qkv")}
    x_in["out"] = [None] + [next(it) for _ in range(2)]
    y_in = {name: [next(it) for _ in range(3)] for name in ("down", "gu", "out")}
    y_in["qkv"] = [None] + [next(it) for _ in range(2)]
    (act_out, tok_out, dq, dk, dv, dwo, dgate, dup, dwd, gain_sum) = [next(it) for _ in range(10)]
    og_hbm, fin_all, grad_all = [next(it) for _ in range(3)]
    w = next(it)
    y = {name: next(it) for name in ("down", "gu", "out", "qkv")}
    xm, xl, xraw = next(it), next(it), next(it)
    og, hidden, qkv, grad, upstream, gains = [next(it) for _ in range(6)]
    gpeers = next(it)
    stage, landed, across, across_own = [next(it) for _ in range(4)]
    window_tmp = next(it)
    gmate_stage, gmate, gline, gline_own = [next(it) for _ in range(4)]
    final, turned, last_stage, last_landed, fsend, frecv = [next(it) for _ in range(6)]
    chunk_in, fin_chunk, act_chunk, tok_chunk = [next(it) for _ in range(4)]
    part, relay = next(it), next(it)
    sums = [(next(it), next(it))]
    row_sems = [next(it) for _ in range(6)]
    msend, mrecv, lsend, lrecv, lrecv2 = [next(it) for _ in range(5)]
    tsend, trecv = next(it), next(it)
    insem, xsem, outsem, finsem, loadsem = [next(it) for _ in range(5)]

    p = Place(n)
    width = w.shape[0]
    line = p.line
    chunk_rows = width // n
    window = max(128, chunk_rows)
    rows = Rows(p, part, relay, sums, row_sems)
    own = OWN[0]
    count = T * own
    starts = [0, T * OWN[0], T * (OWN[0] + OWN[1])]
    total_rows = T * sum(OWN)
    hidden_cols = (COLS - GU) // 3
    loads, writes = {}, []

    def load(name, src, dst):
        copy = pltpu.make_async_copy(src, dst, insem.at[len(loads)])
        copy.start()
        loads[name] = copy

    def write(src, dst):
        copy = pltpu.make_async_copy(src, dst, outsem.at[len(writes)])
        copy.start()
        writes.append(copy)

    load("grad", grad_in, grad)
    for name in ("down", "gu"):
        for level in range(RECUR):
            load((name, level), y_in[name][level], y[name].at[pl.ds(starts[level], T * OWN[level])])
    load("w", w_all.at[:, pl.ds(0, GU)], w)
    load("qkv", qkv_in, qkv)
    load("hidden", hidden_in, hidden)
    for level in range(RECUR):
        load(("out", level), y_in["out"][level], y["out"].at[pl.ds(starts[level], T * OWN[level])])
    for level in (1, 2):
        load(("qkv", level), y_in["qkv"][level], y["qkv"].at[pl.ds(starts[level], T * OWN[level])])
    p.barrier(True)

    for which in range(3):
        peers_copy(p, fin_in, fin_all, tsend.at[0], trecv.at[0], which).start()
    pltpu.make_async_copy(fin_in, fin_all.at[p.t], tsend.at[0, 3]).start()

    def x_source(which, level):
        return og_hbm if which == "out" and level == 0 else x_in[which][level]

    def level_slice(level):
        return pl.ds(sum(OWN[:level]) * T, OWN[level] * T)

    def x_copy(which, chunk, slot, level, sem):
        start = pl.multiple_of(chunk * chunk_rows // window * window, window)
        src = x_source(which, level).reshape(T * OWN[level], width)
        return pltpu.make_async_copy(
            src.at[:, pl.ds(start, window)], xraw.at[slot, level_slice(level)], sem.at[slot, level]
        )

    pieces = cut_pieces()
    count_pieces = len(pieces)
    held = {}

    def x_load(which, parity, buffer, sem):
        if held.get(id(buffer)) == which:
            return
        held[id(buffer)] = which

        @pl.loop(0, line)
        def _(i):
            for level in range(RECUR):
                x_copy(which, 2 * i + parity, 0, level, sem).start()
            for level in range(RECUR):
                x_copy(which, 2 * i + parity, 0, level, sem).wait()
            buffer[i] = xraw[0].T

    def product(which, start, cols, chunk, buffer, slot):
        value = dot(buffer[slot], y[which][:, start : start + cols], NN)
        if window == chunk_rows:
            return value
        window_tmp[:, 0:cols] = value
        shift = pl.multiple_of(lax.rem(chunk, window // chunk_rows) * chunk_rows, chunk_rows)
        return window_tmp[pl.ds(shift, chunk_rows), 0:cols]

    places = []
    for k in range(count_pieces):
        places += [("own", k), ("other", k)] if k < FIRST else [("normal", k)]

    def columns(q):
        return pl.ds(pl.multiple_of(q * PIECE, 128), PIECE)

    def mate_copy(q, i):
        return remote(
            stage.at[lax.rem(q, DEPTH), i], landed.at[i, :, columns(q)], msend.at[q, i], mrecv.at[q, i], p.mate
        )

    def mates(k):
        q = k + FIRST
        if q >= 2 * FIRST + DEPTH:

            @pl.loop(0, line)
            def _(i):
                mate_copy(q - DEPTH, i).wait_send()

        for number, (which, start, cols, inside) in enumerate(pieces[k]):
            x_load(which, 1 - p.b, xm, xsem.at[0])

            @pl.loop(0, line)
            def _(i):
                value = product(which, start, cols, 2 * i + 1 - p.b, xm, i)
                stage[q % DEPTH, i, :, inside : inside + cols] = value.astype(BF)
                if number == len(pieces[k]) - 1:
                    mate_copy(q, i).start()

    def own_terms(q):
        kind, k = places[q]
        for number, (which, start, cols, inside) in enumerate(pieces[k]):
            parity = 1 - p.b if kind == "other" else p.b
            buffer, sem = (xm, xsem.at[0]) if kind == "other" else (xl, xsem.at[1])
            x_load(which, parity, buffer, sem)
            at = pl.ds(q * PIECE + inside, cols)

            @pl.loop(0, line)
            def _(i):
                value = product(which, start, cols, 2 * i + parity, buffer, i)
                if kind == "normal":
                    if number == 0:
                        mate_copy(q, i).wait_recv()
                    value = value + landed[i, :, at].astype(F32)
                landed[i, :, at] = value.astype(BF)

    def along(q, i, right):
        return remote(
            landed.at[i, :, columns(q)],
            across.at[i, :, columns(q)],
            lsend.at[q, i],
            lrecv.at[q, i],
            p.right if right else p.left,
        )

    def along_last(q, i):
        return remote(
            landed.at[i, :, columns(q)], across_own.at[:, columns(q)], lsend.at[q, i], lrecv2.at[q], p.left
        )

    def relay_step(q, i, receives):
        @pl.when(receives)
        def _():
            along(q, i, True).wait_recv()
            landed[i, :, columns(q)] = (
                landed[i, :, columns(q)].astype(F32) + across[i, :, columns(q)].astype(F32)
            ).astype(BF)

    def relay_pieces(slot):
        q_right = slot - p.a
        q_left = slot - (line - 1 - p.a)

        @pl.when((q_right >= 0) & (q_right < PLACES))
        def _():
            @pl.loop(0, line)
            def _(step):
                i = line - 1 - step

                @pl.when(i > p.a)
                def _():
                    relay_step(q_right, i, p.has_left)
                    along(q_right, i, True).start()

        @pl.when((q_left >= 0) & (q_left < PLACES))
        def _():
            @pl.loop(0, line)
            def _(i):
                @pl.when(i < p.a)
                def _():
                    relay_step(q_left, i, p.has_right)
                    pl.when(i < p.a - 1)(lambda: along(q_left, i, False).start())
                    pl.when(i == p.a - 1)(lambda: along_last(q_left, i).start())

    def last_copy(j):
        return remote(last_stage.at[j], last_landed.at[j], fsend.at[j], frecv.at[j], p.mate)

    staged, turning = [], []

    def line_sum(q, buffer):
        here = pl.ds(q * PIECE, PIECE)
        buffer[...] = landed[p.a, :, here].astype(F32)

        @pl.when(p.has_left)
        def _():
            along(q, p.a, True).wait_recv()
            buffer[...] += across[p.a, :, here].astype(F32)

        @pl.when(p.has_right)
        def _():
            along_last(q, p.a).wait_recv()
            buffer[...] += across_own[:, here].astype(F32)

    def finish(q):
        kind, k = places[q]
        if kind == "own":
            return
        if kind == "other":
            if len(staged) >= 2:
                for copy in staged[len(staged) - 2]:
                    copy.wait()
                staged[len(staged) - 2] = []
            buffer = final.at[len(staged) % 2]
            line_sum(q, buffer)
            last_stage[k] = buffer[...].astype(BF)
            last_copy(k).start()
        else:
            results(q)
        if q >= 3 and places[q - 3][0] == "own":
            results(q - 3)

    def results(q):
        kind, k = places[q]
        number = len(staged)
        if number >= 2:
            for copy in staged[number - 2]:
                copy.wait()
        buffer = final.at[number % 2]
        line_sum(q, buffer)
        if kind == "own":
            last_copy(k).wait_recv()
            buffer[...] += last_landed[k].astype(F32)
            last_copy(k).wait_send()
        copies = []

        def out(src, dst):
            copy = pltpu.make_async_copy(src, dst, finsem.at[k, len(copies)])
            copy.start()
            copies.append(copy)

        for which, start, cols, inside in pieces[k]:
            if which in ("down", "out"):
                for copy in turning:
                    copy.wait()
                turning.clear()
                turned[inside : inside + cols, :] = buffer[:, inside : inside + cols].T
                target = dwd if which == "down" else dwo
                copy = pltpu.make_async_copy(
                    turned.at[pl.ds(inside, cols)], target.at[pl.ds(start, cols)], finsem.at[k, 7]
                )
                copy.start()
                turning.append(copy)
            elif which == "gu":
                middle = min(max(hidden_cols - start, 0), cols)
                if middle:
                    out(buffer.at[:, pl.ds(inside, middle)], dgate.at[:, pl.ds(start, middle)])
                if middle < cols:
                    out(
                        buffer.at[:, pl.ds(inside + middle, cols - middle)],
                        dup.at[:, pl.ds(start + middle - hidden_cols, cols - middle)],
                    )
            else:
                queries = min(max(512 - start, 0), cols)
                if queries:
                    out(buffer.at[:, pl.ds(inside, queries)], dq.at[:, pl.ds(start, queries)])
                if queries < cols:
                    dk[...] = buffer[:, inside + queries : inside + queries + HS]
                    dv[...] = buffer[:, inside + queries + HS : inside + queries + 2 * HS]
        staged.append(copies)

    def drain():
        @pl.loop(0, PLACES)
        def _(q):
            @pl.loop(0, line)
            def _(i):
                pl.when(q >= max(PLACES - DEPTH, 2 * FIRST))(lambda: mate_copy(q, i).wait_send())
                pl.when(i != p.a)(lambda: along(q, i, True).wait_send())

    loads["grad"].wait()
    present = act_own[0, 0:own, :]
    og[p.t] = (present * grad[...]).astype(BF)
    view = og.reshape(2, 2, own, width)
    rows.gather_start(0, view)
    for level in range(RECUR):
        loads["down", level].wait()
    sent = [FIRST]

    def mates_upto(k):
        while sent[0] <= min(k, count_pieces - 1):
            mates(sent[0])
            sent[0] += 1

    slots = [0]

    def slot():
        s = slots[0]
        slots[0] += 1
        if s < PLACES:
            own_terms(s)
        relay_pieces(s)
        if 0 <= s - line + 1 < PLACES:
            finish(s - line + 1)
        mates_upto(s - FIRST + DEPTH)

    mates(FIRST)
    sent[0] += 1
    slot()
    rows.gather_finish(0, view)
    write(og, og_hbm)
    for level in range(RECUR):
        loads["gu", level].wait()
    mates_upto(FIRST + 2)
    loads["w"].wait()
    loads["qkv"].wait()
    attended_grad = dot(og[...].reshape(count, width), w[:, WO : WO + 512], NN)
    y["qkv"][0:count, :] = attention_back(
        qkv[...].astype(F32), attended_grad, cosine[...], sine[...], allowed, own, slot
    ).astype(BF)
    slot()

    def attention_tile(cols):
        return dot(y["qkv"][0:count, :], w[cols, QKV : QKV + 640], NT)

    def take(cols, total):
        upstream[:, cols] = total

    rows.reduce(0, own, attention_tile, take)
    loads["hidden"].wait()
    update, add = norm_back(hidden[...], gain[0:1, :], upstream[...])
    grad[...] += update
    gains[...] = gain_in[...]
    gains[0:1, :] += add
    for which in range(3):
        peers_copy(p, grad, grad_all, tsend.at[1], trecv.at[1], which).start()
        peers_copy(p, gains, gpeers, tsend.at[2], trecv.at[2], which).start()
    pltpu.make_async_copy(grad, grad_all.at[p.t], tsend.at[1, 3]).start()
    gpeers[p.t] = gains[...]
    for level in range(RECUR):
        loads["out", level].wait()
    for level in (1, 2):
        loads["qkv", level].wait()
    for copy in writes:
        copy.wait()

    def wait_peers(i, src, dst, local=True):
        for which in range(3):
            copy = peers_copy(p, src, dst, tsend.at[i], trecv.at[i], which)
            copy.wait_recv()
            copy.wait_send()
        if local:
            pltpu.make_async_copy(src, dst.at[p.t], tsend.at[i, 3]).wait()

    def outputs():
        wait_peers(0, fin_in, fin_all)
        wait_peers(1, grad, grad_all)
        mine = back[...]

        @pl.loop(0, width // OC)
        def _(c):
            cols = pl.ds(pl.multiple_of(c * OC, OC), OC)
            first = pltpu.make_async_copy(fin_all.at[:, :, cols], fin_chunk, loadsem.at[0])
            second = pltpu.make_async_copy(grad_all.at[:, :, cols], chunk_in, loadsem.at[1])
            first.start()
            second.start()
            first.wait()
            second.wait()
            act_chunk[...] = dot(mine, fin_chunk[...].reshape(count, OC), NN).astype(BF).reshape(
                MB, own // MB, OC
            )
            value = chunk_in[...].reshape(count, OC)
            high = value.astype(BF)
            rest = value - high.astype(F32)
            middle = rest.astype(BF)
            low = (rest - middle.astype(F32)).astype(BF)
            total = dot(mine, high, NN) + (dot(mine, middle, NN) + dot(mine, low, NN))
            tok_chunk[...] = total.reshape(MB, own // MB, OC)
            third = pltpu.make_async_copy(act_chunk, act_out.at[:, :, cols], loadsem.at[0])
            fourth = pltpu.make_async_copy(tok_chunk, tok_out.at[:, :, cols], loadsem.at[1])
            third.start()
            fourth.start()
            third.wait()
            fourth.wait()

    def gain_tile(chunk):
        start = pl.multiple_of(chunk * chunk_rows // window * window, window)
        return (
            gpeers[0, :, pl.ds(start, window)]
            + gpeers[1, :, pl.ds(start, window)]
            + gpeers[2, :, pl.ds(start, window)]
            + gpeers[3, :, pl.ds(start, window)]
        )

    last = PLACES

    def gain_mate(i):
        return remote(gmate_stage.at[i], gmate.at[i], msend.at[last, i], mrecv.at[last, i], p.mate)

    def gain_along(i, right):
        return remote(
            gmate.at[i], gline.at[i], lsend.at[last, i], lrecv.at[last, i], p.right if right else p.left
        )

    def gain_last(i):
        return remote(gmate.at[i], gline_own, lsend.at[last, i], lrecv2.at[last], p.left)

    def gain_mates():
        wait_peers(2, gains, gpeers, False)

        @pl.loop(0, line)
        def _(i):
            gmate_stage[i] = gain_tile(2 * i + 1 - p.b)
            gain_mate(i).start()

    def gain_lines():
        @pl.loop(0, line)
        def _(step):
            odd = lax.rem(step, 2)
            i = jnp.where(odd == 1, step // 2, line - 1 - step // 2)

            @pl.when(i != p.a)
            def _():
                gain_mate(i).wait_recv()
                gmate[i] += gain_tile(2 * i + p.b)

                @pl.when(((i > p.a) & p.has_left) | ((i < p.a) & p.has_right))
                def _():
                    gain_along(i, True).wait_recv()
                    gmate[i] += gline[i]

                pl.when(i > p.a)(lambda: gain_along(i, True).start())
                pl.when(i < p.a - 1)(lambda: gain_along(i, False).start())
                pl.when(i == p.a - 1)(lambda: gain_last(i).start())

        gain_mate(p.a).wait_recv()
        gain_sum[...] = gain_tile(2 * p.a + p.b) + gmate[p.a]

        @pl.when(p.has_left)
        def _():
            gain_along(p.a, True).wait_recv()
            gain_sum[...] += gline[p.a]

        @pl.when(p.has_right)
        def _():
            gain_last(p.a).wait_recv()
            gain_sum[...] += gline_own[...]

        @pl.loop(0, line)
        def _(i):
            gain_mate(i).wait_send()
            pl.when(i != p.a)(lambda: gain_along(i, True).wait_send())

    for s in range(slots[0], PLACES + line - 1):
        slot()
        if s == 5:
            gain_mates()
        if s == 6:
            gain_lines()
        if s == 8:
            outputs()
    drain()
    for copies in staged[-2:] + [turning]:
        for copy in copies:
            copy.wait()


def gradients(n, w_all, gain, tables, saved, bwd, fin):
    width = w_all.shape[0]
    hidden_cols = (COLS - GU) // 3
    line = n // 2
    chunk_rows = width // n
    window = max(128, chunk_rows)
    vmem = pl.BlockSpec(memory_space=pltpu.VMEM)
    hbm = pl.BlockSpec(memory_space=pl.ANY)
    total_rows = T * sum(OWN)
    own = OWN[0]
    operands = [w_all, gain, tables["cosine"], tables["sine"], tables["act"], tables["masks"][0], tables["back"]]
    specs = [hbm] + [vmem] * 6
    operands += [bwd["grad"], bwd["gain_part"], fin, saved[0]["hidden"], saved[0]["qkv"]]
    specs += [hbm, vmem, hbm, hbm, hbm]
    streams = list(bwd["dg"]) + [s["mixed"] for s in saved] + [s["normed"] for s in saved] + list(bwd["og"])
    streams += [s["prod"] for s in saved] + list(bwd["gug"]) + [s["att"] for s in saved] + list(bwd["qkvg"])
    operands += streams
    specs += [hbm] * len(streams)
    outs = [
        ((MB, own // MB, width), BF),
        ((MB, own // MB, width), F32),
        ((chunk_rows, 512), F32),
        ((chunk_rows, HS), F32),
        ((chunk_rows, HS), F32),
        ((512, chunk_rows), F32),
        ((chunk_rows, hidden_cols), F32),
        ((chunk_rows, hidden_cols), F32),
        ((hidden_cols, chunk_rows), F32),
        ((8, window), F32),
        ((T, own, width), BF),
        ((T, own, width), BF),
        ((T, own, width), F32),
    ]
    out_specs = [hbm, hbm, hbm, vmem, vmem, hbm, hbm, hbm, hbm, vmem, hbm, hbm, hbm]
    scratch = [pltpu.VMEM((width, GU), BF)]
    scratch += [pltpu.VMEM((total_rows, c), BF) for c in (hidden_cols, 2 * hidden_cols, 512, 640)]
    scratch += [pltpu.VMEM((line, window, total_rows), BF)] * 2 + [pltpu.VMEM((1, total_rows, window), BF)]
    scratch += [
        pltpu.VMEM((T, own, width), BF),
        pltpu.VMEM((own, width), F32),
        pltpu.VMEM((T * own, 640), BF),
        pltpu.VMEM((own, width), F32),
        pltpu.VMEM((own, width), F32),
        pltpu.VMEM((8, width), F32),
        pltpu.VMEM((T, 8, width), F32),
    ]
    scratch += [
        pltpu.VMEM((DEPTH, line, chunk_rows, PIECE), BF),
        pltpu.VMEM((line, chunk_rows, PLACES * PIECE), BF),
        pltpu.VMEM((line, chunk_rows, PLACES * PIECE), BF),
        pltpu.VMEM((chunk_rows, PLACES * PIECE), BF),
        pltpu.VMEM((window, PIECE) if window > chunk_rows else (8, 128), F32),
    ]
    scratch += [pltpu.VMEM((line, 8, window), F32)] * 3 + [pltpu.VMEM((8, window), F32)]
    scratch += [pltpu.VMEM((2, chunk_rows, PIECE), F32), pltpu.VMEM((PIECE, chunk_rows), F32)]
    scratch += [pltpu.VMEM((FIRST, chunk_rows, PIECE), BF)] * 2
    scratch += [pltpu.SemaphoreType.DMA((FIRST,))] * 2
    scratch += [pltpu.VMEM((T, own, OC), F32), pltpu.VMEM((T, own, OC), BF)]
    scratch += [pltpu.VMEM((MB, own // MB, OC), BF), pltpu.VMEM((MB, own // MB, OC), F32)]
    scratch += [pltpu.VMEM((2, 2, own, width), BF), pltpu.VMEM((own, width), BF)]
    scratch += [pltpu.VMEM((2, own, width), BF), pltpu.VMEM((own, width), BF)]
    dma = pltpu.SemaphoreType.DMA
    chunks = width // DC
    k = PLACES + 1
    scratch += [dma((1, chunks))] * 4 + [dma((1, 3))] * 2
    scratch += [dma((k, line))] * 4 + [dma((k,))]
    scratch += [dma((3, 4)), dma((3, 3))]
    scratch += [dma((24,)), dma((2, 2, RECUR)), dma((4,)), dma((k, 8)), dma((2,))]
    res = pl.pallas_call(
        functools.partial(gradient_kernel, n),
        out_shape=[jax.ShapeDtypeStruct(*entry) for entry in outs],
        in_specs=specs,
        out_specs=out_specs,
        scratch_shapes=scratch,
        compiler_params=pltpu.CompilerParams(
            collective_id=3, has_side_effects=True, vmem_limit_bytes=63 << 20
        ),
    )(*operands)
    return res


def shards(n, *args):
    tokens, depth, lengths, cotangent = args[:4]
    attn_gain, mlp_gain = args[11:]
    index = lax.axis_index("tensor")
    w_all, gain, fin, cot_own, cot_all, tables, saved = forward(
        n, tokens, depth, lengths[:, 0], cotangent, args[4:11], attn_gain, mlp_gain
    )
    bwd = backward(n, w_all, gain, cot_own, cot_all, tables, saved)
    res = gradients(n, w_all, gain, tables, saved, bwd, fin)
    activations, tokens_grad, dq, dk, dv, dwo, dgate, dup, dwd, gain_sum = res[:10]
    each = attn_gain.shape[0]
    window = gain_sum.shape[1]
    start = lax.rem((lax.axis_index("dp") * T + index) * each, window)
    both = lax.dynamic_slice_in_dim(gain_sum, start, each, axis=1)
    return (activations, tokens_grad, dq, dk, dv, dwo, dgate, dup, dwd, both[0], both[1])


def solution(mesh):
    rows = P(None, ("dp", "tensor"), None)
    weight_specs = (P("dp", "tensor"),) * 3 + (P("tensor", "dp"),) + (P("dp", "tensor"),) * 2 + (P("tensor", "dp"),)
    gain_specs = (P(("dp", "tensor")),) * 2
    return jax.shard_map(
        functools.partial(shards, mesh.shape["dp"]),
        mesh=mesh,
        in_specs=(rows, P(None, "dp"), P(None, "dp", None), rows) + weight_specs + gain_specs,
        out_specs=(rows, rows) + weight_specs + gain_specs,
        check_vma=False,
    )
```

```python
import functools

import jax
import jax.numpy as jnp
import numpy as np
from jax import lax
from jax.experimental import pallas as pl
from jax.experimental.pallas import tpu as pltpu
from jax.sharding import PartitionSpec as P

HQ = 32
KVH = 4
HS = 64
MB = 2
RECUR = 3
SCALE = HS ** (-0.5)
F32 = jnp.float32
BF = jnp.bfloat16
MESH = pl.DeviceIdType.MESH
NN = (((1,), (0,)), ((), ()))
NT = (((1,), (1,)), ((), ()))
TN = (((0,), (0,)), ((), ()))

OWN = (96, 80, 48)
PIECES = ((0, 24, 0), (24, 24, 1), (48, 16, 0), (64, 16, 1), (80, 8, 0), (88, 8, 1))
T = 4
DC = 512
OC = 256
HEADS = 2


def split_batches(values, own):
    halves = ([], [])
    for owner in range(T):
        for start, rows, b in PIECES:
            if start < own:
                halves[b].append(values[owner * own + start : owner * own + start + rows])
    return [jnp.concatenate(half, axis=0) for half in halves]


def join_batches(halves, own):
    rows_out, at = [], [0, 0]
    for owner in range(T):
        for start, rows, b in PIECES:
            if start < own:
                rows_out.append(halves[b][at[b] : at[b] + rows])
                at[b] += rows
    return jnp.concatenate(rows_out, axis=0)


def dot(left, right, dims):
    return lax.dot_general(left, right, dims, preferred_element_type=F32)


def swap_halves(tile):
    lane = lax.broadcasted_iota(jnp.int32, tile.shape, 1)
    return jnp.where((lane & 63) < 32, pltpu.roll(tile, 96, 1), pltpu.roll(tile, 32, 1))


def attention_shares(query, key, allowed):
    rows = query.shape[0]
    group = query.shape[1] // HS
    stacked = stack_heads(query)
    scores = dot(stacked, key, NT).reshape(group, rows, rows) * SCALE
    scores = jnp.where(allowed.astype(F32)[None] > 0, scores, -1e30)
    raised = jnp.exp(scores - jnp.max(scores, axis=-1, keepdims=True))
    return stacked, raised * (1.0 / jnp.sum(raised, axis=-1, keepdims=True))


def stack_heads(values):
    group = values.shape[1] // HS
    return jnp.concatenate([values[:, h * HS : (h + 1) * HS] for h in range(group)], axis=0)


def unstack_heads(values, rows):
    group = values.shape[0] // rows
    return jnp.concatenate([values[h * rows : (h + 1) * rows] for h in range(group)], axis=1)


def mean_square(values):
    return jnp.mean(values * values, axis=-1, keepdims=True)


class Place:
    def __init__(self, n):
        self.n = n
        self.line = n // 2
        self.dp = lax.axis_index("dp")
        self.t = lax.axis_index("tensor")
        self.a = self.dp // 2
        self.b = lax.rem(self.dp, 2)
        self.hi = self.t // 2
        self.lo = lax.rem(self.t, 2)
        self.has_right = self.a < self.line - 1
        self.has_left = self.a > 0
        self.mate = (self.a * 2 + 1 - self.b, self.t)
        self.right = (jnp.minimum(self.dp + 2, n - 1), self.t)
        self.left = (jnp.maximum(self.dp - 2, 0), self.t)
        self.near = (self.dp, self.hi * 2 + 1 - self.lo)
        self.far = (self.dp, (1 - self.hi) * 2 + self.lo)
        self.diag = (self.dp, (1 - self.hi) * 2 + 1 - self.lo)

    def barrier(self, along):
        sem = pltpu.get_barrier_semaphore()

        def greet(device):
            pl.semaphore_signal(sem, inc=1, device_id=device, device_id_type=MESH)

        for device in (self.near, self.far, self.diag):
            greet(device)
        expected = 3
        if along:
            greet(self.mate)
            pl.when(self.has_right)(lambda: greet(self.right))
            pl.when(self.has_left)(lambda: greet(self.left))
            expected = 4 + self.has_right.astype(jnp.int32) + self.has_left.astype(jnp.int32)
        pl.semaphore_wait(sem, expected)


def remote(src, dst, send, recv, device):
    return pltpu.make_async_remote_copy(
        src_ref=src, dst_ref=dst, send_sem=send, recv_sem=recv, device_id=device, device_id_type=MESH
    )


class LineGather:
    def __init__(self, place, pieces, sems):
        self.p = place
        self.pieces = pieces
        self.msend, self.mrecv, self.rsend, self.rrecv, self.lsend, self.lrecv = sems

    def toward_left(self, w, k, chunk):
        ref = self.pieces[w][1](chunk)
        return remote(ref, ref, self.lsend.at[w, k], self.lrecv.at[w, k], self.p.left)

    def toward_right(self, w, k, chunk):
        ref = self.pieces[w][1](chunk)
        return remote(ref, ref, self.rsend.at[w, k], self.rrecv.at[w, k], self.p.right)

    def toward_mate(self, w, k, chunk):
        ref = self.pieces[w][1](chunk)
        return remote(ref, ref, self.msend.at[w, k], self.mrecv.at[w, k], self.p.mate)

    def first(self, w):
        p = self.p
        return p.a * 2 + 1 - p.b if self.pieces[w][0] == "other" else p.dp

    def own(self, w):
        p = self.p
        kind = self.pieces[w][0]
        chunk = self.first(w)
        if kind == "other":
            self.toward_mate(w - 1, p.a, chunk).wait_recv()
        pl.when(p.has_left)(lambda: self.toward_left(w, 0, chunk).start())
        pl.when(p.has_right)(lambda: self.toward_right(w, 0, chunk).start())
        if kind != "other":
            self.toward_mate(w, p.a, chunk).start()

    def step(self, w, k):
        p = self.p
        normal = self.pieces[w][0] == "normal"

        @pl.when(p.a + k < p.line)
        def _():
            chunk = self.first(w) + 2 * k
            self.toward_left(w, k - 1, chunk).wait_recv()
            pl.when(p.has_left)(lambda: self.toward_left(w, k, chunk).start())
            if normal:
                self.toward_mate(w, p.a + k, chunk).start()

        @pl.when(p.a - k >= 0)
        def _():
            chunk = self.first(w) - 2 * k
            self.toward_right(w, k - 1, chunk).wait_recv()
            pl.when(p.has_right)(lambda: self.toward_right(w, k, chunk).start())
            if normal:
                self.toward_mate(w, p.a - k, chunk).start()

    def steps(self, w):
        for k in range(1, self.p.line):
            self.step(w, k)

    def arrive(self, w):
        p = self.p
        if self.pieces[w][0] == "normal":
            for i in range(p.line):
                self.toward_mate(w, i, 2 * i + 1 - p.b).wait_recv()

    def drain(self, w):
        p = self.p
        kind = self.pieces[w][0]
        if kind == "own":
            self.toward_mate(w, p.a, p.dp).wait_send()
        for i in range(p.line):
            if kind == "normal":
                self.toward_mate(w, i, p.dp).wait_send()
            pl.when(p.has_left & (p.a + i < p.line))(lambda: self.toward_left(w, i, p.dp).wait_send())
            pl.when(p.has_right & (p.a - i >= 0))(lambda: self.toward_right(w, i, p.dp).wait_send())


class Rows:
    def __init__(self, place, part, relay, sums, sems):
        self.p = place
        self.part, self.relay, self.sums = part, relay, sums
        self.s1, self.q1, self.s2, self.q2, self.gs, self.gr = sems

    def first_copy(self, i, own, c):
        p = self.p
        cols = pl.ds(pl.multiple_of(c * DC, DC), DC)
        return remote(
            self.part.at[:, 1 - p.lo, pl.ds(0, own), cols],
            self.sums[i][0].at[:, :, cols],
            self.s1.at[i, c],
            self.q1.at[i, c],
            p.near,
        )

    def second_copy(self, i, own, c):
        p = self.p
        cols = pl.ds(pl.multiple_of(c * DC, DC), DC)
        return remote(
            self.relay.at[pl.ds(0, own), cols],
            self.sums[i][1].at[:, cols],
            self.s2.at[i, c],
            self.q2.at[i, c],
            p.far,
        )

    def reduce(self, i, own, tile, finish):
        p = self.p
        part, relay = self.part, self.relay
        r1, r2 = self.sums[i]
        chunks = part.shape[-1] // DC

        def pass_on(c):
            cols = pl.ds(pl.multiple_of(c * DC, DC), DC)
            self.first_copy(i, own, c).wait_recv()
            mine = part[1 - p.hi, p.lo, 0:own, cols].astype(F32)
            relay[0:own, cols] = (mine + r1[1 - p.hi, :, cols].astype(F32)).astype(BF)
            self.second_copy(i, own, c).start()

        @pl.loop(0, chunks)
        def _(c):
            cols = pl.ds(pl.multiple_of(c * DC, DC), DC)
            part[:, :, 0:own, cols] = tile(cols).astype(BF).reshape(2, 2, own, DC)
            self.first_copy(i, own, c).start()
            pl.when(c > 0)(lambda: pass_on(c - 1))

        pass_on(chunks - 1)

        @pl.loop(0, chunks)
        def _(c):
            cols = pl.ds(pl.multiple_of(c * DC, DC), DC)
            self.second_copy(i, own, c).wait_recv()
            mine = part[p.hi, p.lo, 0:own, cols].astype(F32)
            finish(cols, mine + r1[p.hi, :, cols].astype(F32) + r2[:, cols].astype(F32))

        @pl.loop(0, chunks)
        def _(c):
            self.first_copy(i, own, c).wait_send()
            self.second_copy(i, own, c).wait_send()

    def gather_copy(self, i, buffer, which):
        p = self.p
        here = buffer.at[p.hi, p.lo]
        if which == 0:
            return remote(here, here, self.gs.at[i, 0], self.gr.at[i, 0], p.far)
        if which == 1:
            return remote(here, here, self.gs.at[i, 1], self.gr.at[i, 1], p.near)
        there = buffer.at[1 - p.hi, p.lo]
        return remote(there, there, self.gs.at[i, 2], self.gr.at[i, 2], p.near)

    def gather_start(self, i, buffer):
        self.gather_copy(i, buffer, 0).start()
        self.gather_copy(i, buffer, 1).start()

    def gather_finish(self, i, buffer):
        self.gather_copy(i, buffer, 0).wait_recv()
        self.gather_copy(i, buffer, 2).start()
        self.gather_copy(i, buffer, 1).wait_recv()
        self.gather_copy(i, buffer, 2).wait_recv()
        for which in range(3):
            self.gather_copy(i, buffer, which).wait_send()


def peers_copy(place, src, dst, send, recv, which):
    device = (place.near, place.far, place.diag)[which]
    return remote(src, dst.at[place.t], send.at[which], recv.at[which], device)


def gain_row(gathered, n, row, width):
    each = width // (n * T)
    tiles = []
    for j in range(width // 128):
        total = None
        for i in range(128 // each):
            number = j * (128 // each) + i
            block = gathered[number % T, number // T][row : row + 1]
            total = block if total is None else total + block
        tiles.append(total)
    return jnp.concatenate(tiles, axis=1)


QKV, WO, GU, WD = 0, 640, 1152, 3968
COLS = 5376
RANGES = (
    ("along", 0, 640),
    ("along", 640, 512),
    ("along", 1152, 1408),
    ("along", 2560, 1408),
    ("along", 3968, 512),
    ("across", 4480, 896),
)


def ones(condition):
    return jnp.where(condition, 1.0, 0.0)


def iota(size, axis):
    shape = (size, 1) if axis == 0 else (1, size)
    return lax.broadcasted_iota(jnp.int32, shape, axis).astype(F32)


def quotient(index, step, most):
    total = ones(index >= step)
    for i in range(2, most):
        total = total + ones(index >= step * i)
    return total


def own_places(own_index):
    batch, place, seen = 0.0 * own_index, 0.0 * own_index, [0, 0]
    for start, rows, b in PIECES:
        inside = (own_index >= start) & (own_index < start + rows)
        batch = jnp.where(inside, float(b), batch)
        place = jnp.where(inside, own_index - start + seen[b], place)
        seen[b] += rows
    return batch, place


def fill_tables(p, depth_row, depth_col, lengths, freqs, perm, back, back_own, cosine, sine, allowed, act_own, act_last):
    local = OWN[0] // MB
    total = T * OWN[0]

    def columns(index):
        tensor = quotient(index, OWN[0], T)
        inside = index - tensor * OWN[0]
        batch = ones(inside >= local)
        return batch, tensor * local + inside - batch * local

    batch_row, pos_row = columns(iota(total, 1))
    batch_col, pos_col = columns(iota(total, 0))
    same = batch_row == batch_col
    rank_row = jnp.sum(
        ones(same & ((depth_col > depth_row) | ((depth_col == depth_row) & (pos_col < pos_row)))), axis=0, keepdims=True
    )
    rank_col = jnp.sum(
        ones(same & ((depth_row > depth_col) | ((depth_row == depth_col) & (pos_row < pos_col)))), axis=1, keepdims=True
    )

    def compact(index):
        owner = quotient(index, OWN[0], T)
        batch, place = own_places(index - owner * OWN[0])
        return batch, place * T + owner

    batch_q, rank_q = compact(iota(total, 0))
    hit = (rank_row == rank_q) & (batch_row == batch_q)
    perm[...] = ones(hit).astype(BF)
    batch_p, rank_p = compact(iota(total, 1))
    back[...] = ones((rank_col == rank_p) & (batch_col == batch_p)).astype(BF)
    back_own[...] = back[pl.ds(pl.multiple_of(p.t * OWN[0], OWN[0]), OWN[0]), :]

    ends = []
    for b in range(MB):
        first = lengths[b : b + 1, 0:1].astype(F32)
        ends.append((first, first + lengths[b : b + 1, 1:2].astype(F32)))
    position = jnp.sum(jnp.where(hit, pos_row, 0.0), axis=1, keepdims=True)
    end = [jnp.where(batch_q == 0.0, ends[0][i], ends[1][i]) for i in range(2)]
    start = jnp.where(position >= end[1], end[1], jnp.where(position >= end[0], end[0], 0.0))
    angles = (position - start) * freqs
    cosine[...] = jnp.cos(angles)
    lane = lax.broadcasted_iota(jnp.int32, angles.shape, 1)
    value = jnp.sin(angles)
    sine[...] = jnp.where((lane & 63) < 32, -value, value)

    own_batch, own_place = own_places(iota(OWN[0], 0))
    own_rank = own_place * T + p.t.astype(F32)
    for level in range(RECUR):
        own = OWN[level]
        half = T * own // MB
        counts = [
            jnp.sum(ones((batch_row == float(b)) & (depth_row >= level + 1.0)), axis=1, keepdims=True) for b in range(MB)
        ]
        act_own[level] = ones(own_rank < jnp.where(own_batch == 0.0, counts[0], counts[1]))
        if level == RECUR - 1:
            index = iota(T * own, 0)
            owner = quotient(index, own, T)
            batch, place = own_places(index - owner * own)
            act_last[...] = ones(place * T + owner < jnp.where(batch == 0.0, counts[0], counts[1]))

        def order(index):
            owner = quotient(index, own // MB, T)
            return (index - owner * (own // MB)) * T + owner

        index_col, index_row = iota(half, 0), iota(half, 1)
        order_col, order_row = order(index_col), order(index_row)
        for b in range(MB):
            at_col = jnp.sum(
                jnp.where((rank_row == order_col) & (batch_row == float(b)), pos_row, 0.0), axis=1, keepdims=True
            )
            at_row = jnp.sum(
                jnp.where((rank_col == order_row) & (batch_col == float(b)), pos_col, 0.0), axis=0, keepdims=True
            )
            document_col = ones(at_col >= ends[b][0]) + ones(at_col >= ends[b][1])
            document_row = ones(at_row >= ends[b][0]) + ones(at_row >= ends[b][1])
            ok = (document_col == document_row) & (at_row <= at_col) & (order_row < counts[b])
            allowed[level][b] = ones(ok | (index_col == index_row)).astype(BF)


def forward_kernel(n, *refs):
    it = iter(refs)
    tokens, cotangent, wq, wk, wv, wo, wg, wu, wd = [next(it) for _ in range(9)]
    attn_gain, mlp_gain, depth_row, depth_col, lengths, freqs = [next(it) for _ in range(6)]
    w_out, gain_out, fin_out, cot_own, cot_all = [next(it) for _ in range(5)]
    cosine, sine, back_own, act_own, act_last = [next(it) for _ in range(5)]
    allowed = [next(it) for _ in range(RECUR)]
    names = ("normed", "qkv", "att", "mixed", "gu", "prod", "hidden", "first")
    saved_out = [dict((k, next(it)) for k in names) for _ in range(RECUR)]
    w = next(it)
    perm, back, kv, wo_in, wd_in = [next(it) for _ in range(5)]
    gbuf, gall = next(it), next(it)
    tok, cot = next(it), next(it)
    saved = [dict((k, next(it)) for k in names) for _ in range(RECUR)]
    after, fin, cown = next(it), next(it), next(it)
    part, relay = next(it), next(it)
    sums = [(next(it), next(it)) for _ in range(2 * RECUR)]
    line_sems = [next(it) for _ in range(6)]
    row_sems = [next(it) for _ in range(6)]
    wsem = next(it)
    tsend, trecv, outsem = next(it), next(it), next(it)

    p = Place(n)
    width = tokens.shape[-1]
    rows_chunk = width // n

    def chunk_at(chunk, start, size):
        return w.at[pl.ds(pl.multiple_of(chunk * rows_chunk, rows_chunk), rows_chunk), pl.ds(start, size)]

    pieces = [("normal", lambda chunk: gbuf.at[chunk])]
    number = []
    for kind, start, size in RANGES:
        def at(chunk, start=start, size=size):
            return chunk_at(chunk, start, size)

        number.append(len(pieces))
        pieces += [("own", at), ("other", at)] if kind == "across" else [("normal", at)]
    line = LineGather(p, pieces, line_sems)
    rows = Rows(p, part, relay, sums, row_sems)
    hidden_cols = (COLS - GU) // 3
    writes = []

    def write(src, dst):
        copy = pltpu.make_async_copy(src, dst, outsem.at[len(writes)])
        copy.start()
        writes.append(copy)

    local = [
        pltpu.make_async_copy(wq, chunk_at(p.dp, QKV, 512), wsem.at[0]),
        pltpu.make_async_copy(wk, kv.at[0], wsem.at[1]),
        pltpu.make_async_copy(wv, kv.at[1], wsem.at[2]),
        pltpu.make_async_copy(wo, wo_in, wsem.at[3]),
        pltpu.make_async_copy(wg, chunk_at(p.dp, GU, hidden_cols), wsem.at[4]),
        pltpu.make_async_copy(wu, chunk_at(p.dp, GU + hidden_cols, hidden_cols), wsem.at[5]),
        pltpu.make_async_copy(wd, wd_in, wsem.at[6]),
    ]
    for copy in local:
        copy.start()
    mine_rows = pl.ds(pl.multiple_of(p.dp * rows_chunk, rows_chunk), rows_chunk)
    each = attn_gain.shape[1]
    lane = lax.broadcasted_iota(jnp.int32, (1, 128), 1)
    spot = lax.rem(p.dp * T + p.t, 128 // each)
    inside = (lane >= spot * each) & (lane < (spot + 1) * each)
    for row, gain in enumerate((attn_gain, mlp_gain)):
        value = jnp.concatenate([gain[...]] * (128 // each), axis=1)
        gbuf[p.dp, row : row + 1, :] = jnp.where(inside, value, 0.0)
    gbuf[p.dp, 2:8, :] = jnp.zeros((6, 128), F32)
    p.barrier(True)
    line.own(0)
    for copy in local[0:3]:
        copy.wait()
    w[mine_rows, QKV + 512 : QKV + 640] = jnp.concatenate([kv[0], kv[1]], axis=0).T
    heads_piece, out_piece, gate_piece, up_piece, down_piece, down_last = number
    line.own(heads_piece)
    for which in range(3):
        peers_copy(p, tokens, tok, tsend.at[0], trecv.at[0], which).start()
    pltpu.make_async_copy(tokens, tok.at[p.t], tsend.at[0, 3]).start()
    local[3].wait()
    w[mine_rows, WO : WO + 512] = wo_in[...].T
    line.own(out_piece)
    for which in range(3):
        peers_copy(p, cotangent, cot, tsend.at[1], trecv.at[1], which).start()
    pltpu.make_async_copy(cotangent, cot.at[p.t], tsend.at[1, 3]).start()
    for copy in local[4:6]:
        copy.wait()
    line.own(gate_piece)
    line.steps(0)
    line.arrive(0)
    for which in range(3):
        peers_copy(p, gbuf, gall, tsend.at[2], trecv.at[2], which).start()
    pltpu.make_async_copy(gbuf, gall.at[p.t], tsend.at[2, 3]).start()
    fill_tables(
        p, depth_row[...], depth_col[...], lengths, freqs[...], perm, back, back_own, cosine, sine, allowed, act_own, act_last
    )
    line.steps(heads_piece)
    local[6].wait()
    w[mine_rows, WD : WD + hidden_cols] = wd_in[...].T
    line.own(up_piece)
    line.steps(out_piece)

    def wait_peers(i, src, dst):
        for which in range(3):
            copy = peers_copy(p, src, dst, tsend.at[i], trecv.at[i], which)
            copy.wait_recv()
            copy.wait_send()
        pltpu.make_async_copy(src, dst.at[p.t], tsend.at[i, 3]).wait()

    wait_peers(2, gbuf, gall)
    gain_out[0:1, :] = gain_row(gall, n, 0, width)
    gain_out[1:2, :] = gain_row(gall, n, 1, width)
    gain_out[2:8, :] = jnp.zeros((6, width), F32)

    wait_peers(0, tokens, tok)

    own = OWN[0]
    mine = perm[pl.ds(pl.multiple_of(p.t * own, own), own), :]
    saved[0]["hidden"][...] = dot(mine, tok[...].reshape(T * own, width), NN)

    @pl.loop(0, T)
    def _(owner):
        picked = perm[pl.ds(pl.multiple_of(owner * own, own), own), :]
        hidden = dot(picked, tok[...].reshape(T * own, width), NN)
        inverse = lax.rsqrt(mean_square(hidden) + 1e-05)
        saved[0]["normed"][owner] = (hidden * inverse * gain_out[0:1, :]).astype(BF)

    wait_peers(1, cotangent, cot)
    cown[...] = dot(mine, cot[...].reshape(T * own, width), NN)
    write(cown, cot_own)

    line.own(down_piece)
    line.own(down_last)

    @pl.loop(0, T)
    def _(owner):
        picked = perm[pl.ds(pl.multiple_of(owner * OWN[0], 32), OWN[RECUR - 1]), :]
        cot_all[owner] = dot(picked, cot[...].reshape(T * OWN[0], width), NN).astype(BF)

    line.arrive(heads_piece)

    for level in range(RECUR):
        own = OWN[level]
        count = T * own
        half = count // 2
        s = saved[level]
        if level:
            rows.gather_finish(2 * level - 1, s["normed"].reshape(2, 2, own, width))
        x = s["normed"][...].reshape(count, width)
        qkv = dot(x, w[:, QKV : QKV + 640], NN)
        cos = jnp.concatenate([cosine[owner * OWN[0] : owner * OWN[0] + own, :] for owner in range(T)], axis=0)
        sin = jnp.concatenate([sine[owner * OWN[0] : owner * OWN[0] + own, :] for owner in range(T)], axis=0)
        tiles = []
        for j in range(5):
            tile = qkv[:, j * 128 : (j + 1) * 128]
            turned = tile * cos + swap_halves(tile) * sin
            if j == 4:
                lane = lax.broadcasted_iota(jnp.int32, tile.shape, 1)
                turned = jnp.where(lane < HS, turned, tile)
            tiles.append(turned)
        rotated = jnp.concatenate(tiles, axis=1)
        s["qkv"][...] = rotated.astype(BF)
        write(s["qkv"], saved_out[level]["qkv"])
        heads = []
        for b, block in enumerate(split_batches(rotated, own)):
            query, key, value = (
                block[:, 0:512].astype(BF),
                block[:, 512:576].astype(BF),
                block[:, 576:640].astype(BF),
            )
            _, shares = attention_shares(query, key, allowed[level][b])
            out = dot(shares.astype(BF).reshape(8 * half, half), value, NN)
            heads.append(unstack_heads(out, half))
            if level == 0:
                line.step(gate_piece, 1) if b == 0 else [line.step(gate_piece, k) for k in range(2, p.line)]
        s["att"][...] = join_batches(heads, own).astype(BF)
        write(s["att"], saved_out[level]["att"])
        if level == 0:
            line.arrive(out_piece)
        present = act_own[level, 0:own, :]

        def attention_tile(cols):
            return dot(s["att"][...], w[cols, WO : WO + 512], NT)

        def attention_finish(cols, total):
            s["first"][:, cols] = s["hidden"][:, cols] + present * total

        rows.reduce(2 * level, own, attention_tile, attention_finish)
        first = s["first"][...]
        inverse = lax.rsqrt(mean_square(first) + 1e-05)
        s["mixed"][p.t] = (first * inverse * gain_out[1:2, :]).astype(BF)
        mixed = s["mixed"].reshape(2, 2, own, width)
        rows.gather_start(2 * level, mixed)
        write(s["first"], saved_out[level]["first"])
        if level == 0:
            line.steps(up_piece)
            line.own(down_last + 1)
        rows.gather_finish(2 * level, mixed)
        write(s["mixed"], saved_out[level]["mixed"])

        def hidden_block(start, size):
            x = s["mixed"][...].reshape(count, width)
            gate = dot(x, w[:, pl.ds(pl.multiple_of(GU + start, 128), size)], NN)
            upward = dot(x, w[:, pl.ds(pl.multiple_of(GU + hidden_cols + start, 128), size)], NN)
            cols = pl.ds(pl.multiple_of(start, 128), size)
            s["gu"][:, cols] = gate.astype(BF)
            s["gu"][:, pl.ds(pl.multiple_of(hidden_cols + start, 128), size)] = upward.astype(BF)
            s["prod"][:, cols] = (gate * jax.nn.sigmoid(gate) * upward).astype(BF)

        if level == 0:
            line.steps(down_piece)
            line.step(down_last, 1)
            line.step(down_last + 1, 1)
            line.arrive(gate_piece)
            line.arrive(up_piece)

        @pl.loop(0, hidden_cols // 256)
        def _(j):
            hidden_block(j * 256, 256)

        if hidden_cols % 256:
            hidden_block(hidden_cols // 256 * 256, 128)
        write(s["gu"], saved_out[level]["gu"])
        write(s["prod"], saved_out[level]["prod"])
        if level == 0:
            for k in range(2, p.line):
                line.step(down_last, k)
                line.step(down_last + 1, k)
            line.arrive(down_piece)
            write(w, w_out)

        def mlp_tile(cols):
            return dot(s["prod"][...], w[cols, WD : WD + 1408], NT)

        def mlp_finish(cols, total):
            after[0:own, cols] = s["first"][:, cols] + present * total

        rows.reduce(2 * level + 1, own, mlp_tile, mlp_finish)
        if level < RECUR - 1:
            deeper = OWN[level + 1]
            hidden = after[0:deeper, :]
            saved[level + 1]["hidden"][...] = hidden
            inverse = lax.rsqrt(mean_square(hidden) + 1e-05)
            saved[level + 1]["normed"][p.t] = (hidden * inverse * gain_out[0:1, :]).astype(BF)
            rows.gather_start(2 * level + 1, saved[level + 1]["normed"].reshape(2, 2, deeper, width))
            fin[deeper:own, :] = after[deeper:own, :].astype(BF)
        else:
            fin[0:own, :] = after[0:own, :].astype(BF)
        write(s["hidden"], saved_out[level]["hidden"])
        write(s["normed"], saved_out[level]["normed"])
    write(fin, fin_out)
    for i in range(len(pieces)):
        line.drain(i)
    for copy in writes:
        copy.wait()


def forward(n, tokens, depth, lengths, cotangent, weights, attn_gain, mlp_gain):
    width = tokens.shape[-1]
    hidden_cols = weights[4].shape[1]
    local = OWN[0] // MB
    total = T * OWN[0]
    ordered = depth.reshape(MB, T, local).transpose(1, 0, 2).astype(F32)
    freqs = jnp.asarray(np.tile(10000.0 ** (-np.arange(0, HS, 2) / HS), 4)[None].astype(np.float32))
    vmem = pl.BlockSpec(memory_space=pltpu.VMEM)
    hbm = pl.BlockSpec(memory_space=pl.ANY)

    def saved_shapes(own):
        count = T * own
        return {
            "normed": ((T, own, width), BF),
            "qkv": ((count, 640), BF),
            "att": ((count, 512), BF),
            "mixed": ((T, own, width), BF),
            "gu": ((count, 2 * hidden_cols), BF),
            "prod": ((count, hidden_cols), BF),
            "hidden": ((own, width), F32),
            "first": ((own, width), F32),
        }

    shapes = [((width, COLS), BF), ((8, width), F32), ((OWN[0], width), BF), ((OWN[0], width), F32), ((T, OWN[2], width), BF)]
    specs = [hbm, vmem, hbm, hbm, vmem]
    shapes += [((total, 128), F32)] * 2 + [((OWN[0], total), BF), ((RECUR, OWN[0], 1), F32), ((T * OWN[2], 1), F32)]
    shapes += [((MB, T * own // MB, T * own // MB), BF) for own in OWN]
    specs += [vmem] * (5 + RECUR)
    for own in OWN:
        for entry in saved_shapes(own).values():
            shapes.append(entry)
            specs.append(hbm)
    scratch = [pltpu.VMEM((width, COLS), BF)] + [pltpu.VMEM((total, total), BF)] * 2
    scratch += [pltpu.VMEM((2,) + weights[1].shape[::-1], BF), pltpu.VMEM(weights[3].shape, BF), pltpu.VMEM(weights[6].shape, BF)]
    scratch += [pltpu.VMEM((n, 8, 128), F32), pltpu.VMEM((T, n, 8, 128), F32)]
    scratch += [pltpu.VMEM((T,) + tokens.shape, BF)] * 2
    for own in OWN:
        scratch += [pltpu.VMEM(*entry) for entry in saved_shapes(own).values()]
    scratch += [pltpu.VMEM((OWN[0], width), F32), pltpu.VMEM((OWN[0], width), BF), pltpu.VMEM((OWN[0], width), F32)]
    scratch += [pltpu.VMEM((2, 2, OWN[0], width), BF), pltpu.VMEM((OWN[0], width), BF)]
    for own in OWN:
        for _ in range(2):
            scratch += [pltpu.VMEM((2, own, width), BF), pltpu.VMEM((own, width), BF)]
    dma = pltpu.SemaphoreType.DMA
    count = 1 + sum(2 if kind == "across" else 1 for kind, _, _ in RANGES)
    scratch += [dma((count, n // 2))] * 6
    chunks = width // DC
    scratch += [dma((2 * RECUR, chunks))] * 4 + [dma((2 * RECUR, 3))] * 2
    scratch += [dma((7,)), dma((3, 4)), dma((3, 3)), dma((40,))]
    outs = pl.pallas_call(
        functools.partial(forward_kernel, n),
        out_shape=[jax.ShapeDtypeStruct(*entry) for entry in shapes],
        in_specs=[hbm] * 9 + [vmem] * 6,
        out_specs=specs,
        scratch_shapes=scratch,
        compiler_params=pltpu.CompilerParams(
            collective_id=1, has_side_effects=True, vmem_limit_bytes=62 << 20
        ),
    )(
        tokens,
        cotangent,
        weights[0],
        weights[1].T,
        weights[2].T,
        *weights[3:],
        attn_gain[None],
        mlp_gain[None],
        ordered.reshape(1, total),
        ordered.reshape(total, 1),
        lengths,
        freqs,
    )
    w_all, gain, fin, cot_own, cot_all = outs[:5]
    tables = dict(zip(("cosine", "sine", "back", "act", "act_last"), outs[5:10]))
    tables["masks"] = outs[10:13]
    names = list(saved_shapes(1))
    saved = [dict(zip(names, outs[13 + 8 * level : 21 + 8 * level])) for level in range(RECUR)]
    return w_all, gain, fin, cot_own, cot_all, tables, saved


def attention_back(rotated, attended_grad, cos, sin, allowed, own, between=None):
    half = T * own // 2
    grads = []
    split = split_batches(rotated, own)
    upstream = split_batches(attended_grad, own)
    for b in range(MB):
        block = split[b]
        query, key, value = block[:, 0:512].astype(BF), block[:, 512:576].astype(BF), block[:, 576:640].astype(BF)
        up_all = upstream[b].astype(BF)
        query_grads, key_grad, value_grad = [], 0.0, 0.0
        for start in range(0, 512, HEADS * HS):
            stacked, shares = attention_shares(query[:, start : start + HEADS * HS], key, allowed[b])
            up = stack_heads(up_all[:, start : start + HEADS * HS])
            low = shares.astype(BF).reshape(HEADS * half, half)
            shares_grad = dot(up, value, NT).reshape(HEADS, half, half)
            value_grad += dot(low, up, TN)
            spread = jnp.sum(shares * shares_grad, axis=-1, keepdims=True)
            score_grad = (shares * (shares_grad - spread)).astype(BF).reshape(HEADS * half, half)
            query_grads.append(unstack_heads(dot(score_grad, key, NN), half) * SCALE)
            key_grad += dot(score_grad, stacked, TN) * SCALE
        query_grad = jnp.concatenate(query_grads, axis=1)
        grads.append(jnp.concatenate([query_grad, key_grad, value_grad], axis=1))
        if between is not None:
            between()
    joined = join_batches(grads, own)
    tiles = []
    for j in range(5):
        tile = joined[:, j * 128 : (j + 1) * 128]
        turned = tile * cos - swap_halves(tile) * sin
        if j == 4:
            lane = lax.broadcasted_iota(jnp.int32, tile.shape, 1)
            turned = jnp.where(lane < HS, turned, tile)
        tiles.append(turned)
    return jnp.concatenate(tiles, axis=1)


def level_rows(table, own):
    return jnp.concatenate([table[owner * OWN[0] : owner * OWN[0] + own, :] for owner in range(T)], axis=0)


def norm_back(source, gain, upstream):
    inverse = lax.rsqrt(mean_square(source) + 1e-05)
    unit = source * inverse
    gain_part = jnp.sum(upstream * unit, axis=0, keepdims=True)
    scaled = upstream * gain
    return inverse * (scaled - unit * jnp.mean(scaled * unit, axis=-1, keepdims=True)), gain_part


def backward_kernel(n, *refs):
    it = iter(refs)
    (w_all, gain, cot_own, cot_all, cosine, sine, act_own, act_last) = [next(it) for _ in range(8)]
    allowed = [None] + [next(it) for _ in range(2)]
    saved_in = []
    for level in range(RECUR):
        names = ("gu", "first") if level == 0 else ("gu", "first", "qkv", "hidden")
        saved_in.append({k: next(it) for k in names})
    dg_out = [next(it) for _ in range(3)]
    gug_out = [next(it) for _ in range(3)]
    og_out = [None] + [next(it) for _ in range(2)]
    qkvg_out = [None] + [next(it) for _ in range(2)]
    grad_out, gain_part = next(it), next(it)
    w = next(it)
    saved = []
    for level in range(RECUR):
        saved.append({k: next(it) for k in saved_in[level]})
    dg = [next(it) for _ in range(3)]
    gug = [next(it) for _ in range(3)]
    og = [None] + [next(it) for _ in range(2)]
    qkvg = [None] + [next(it) for _ in range(2)]
    grad, upstream = next(it), next(it)
    part, relay = next(it), next(it)
    sums = [(next(it), next(it)) for _ in range(5)]
    row_sems = [next(it) for _ in range(6)]
    insem, outsem = next(it), next(it)

    p = Place(n)
    width = w.shape[0]
    rows = Rows(p, part, relay, sums, row_sems)
    hidden_cols = (COLS - GU) // 3
    loads, writes = {}, []

    def load(name, src, dst):
        copy = pltpu.make_async_copy(src, dst, insem.at[len(loads)])
        copy.start()
        loads[name] = copy

    def write(src, dst):
        copy = pltpu.make_async_copy(src, dst, outsem.at[len(writes)])
        copy.start()
        writes.append(copy)

    def columns(start, size):
        load(("w", start), w_all.at[:, pl.ds(start, size)], w.at[:, pl.ds(start, size)])

    columns(WD, hidden_cols)
    load("grad", cot_own, grad)
    last = RECUR - 1
    load(("gu", last), saved_in[last]["gu"], saved[last]["gu"])
    columns(GU, 2 * hidden_cols)
    load(("first", last), saved_in[last]["first"], saved[last]["first"])
    columns(WO, 512)
    for name in ("qkv", "hidden"):
        load((name, last), saved_in[last][name], saved[last][name])
    columns(QKV, 640)
    for level in (1, 0):
        for name in saved_in[level]:
            load((name, level), saved_in[level][name], saved[level][name])
    p.barrier(False)
    gain_part[...] = jnp.zeros_like(gain_part)

    for level in range(last, -1, -1):
        own = OWN[level]
        count = T * own
        s = saved[level]
        base = 2 * (last - level)
        present = act_own[level, 0:own, :]
        if level == last:
            dg[level][...] = (cot_all[...].astype(F32).reshape(count, width) * act_last[...]).astype(BF).reshape(
                T, own, width
            )
            loads["grad"].wait()
        else:
            dg[level][p.t] = (present * grad[0:own, :]).astype(BF)
            view = dg[level].reshape(2, 2, own, width)
            rows.gather_start(base, view)
            rows.gather_finish(base, view)
        write(dg[level], dg_out[level])
        if level == last:
            loads["w", WD].wait()
        loads["gu", level].wait()

        def hidden_block(start, size):
            wcols = pl.ds(pl.multiple_of(WD + start, 128), size)
            product_grad = dot(dg[level][...].reshape(count, width), w[:, wcols], NN)
            low = pl.ds(pl.multiple_of(start, 128), size)
            high = pl.ds(pl.multiple_of(hidden_cols + start, 128), size)
            gate = s["gu"][:, low].astype(F32)
            upward = s["gu"][:, high].astype(F32)
            sigma = jax.nn.sigmoid(gate)
            gug[level][:, low] = (product_grad * upward * sigma * (1.0 + gate * (1.0 - sigma))).astype(BF)
            gug[level][:, high] = (product_grad * gate * sigma).astype(BF)

        @pl.loop(0, hidden_cols // 256)
        def _(j):
            hidden_block(j * 256, 256)

        if hidden_cols % 256:
            hidden_block(hidden_cols // 256 * 256, 128)
        write(gug[level], gug_out[level])
        if level == last:
            loads["w", GU].wait()

        def mlp_tile(cols):
            return dot(gug[level][...], w[cols, GU : GU + 2 * hidden_cols], NT)

        def take(cols, total):
            upstream[0:own, cols] = total

        rows.reduce(base, own, mlp_tile, take)
        loads["first", level].wait()
        update, add = norm_back(s["first"][...], gain[1:2, :], upstream[0:own, :])
        grad[0:own, :] += update
        gain_part[1:2, :] += add
        if level == 0:
            break
        og[level][p.t] = (present * grad[0:own, :]).astype(BF)
        view = og[level].reshape(2, 2, own, width)
        rows.gather_start(base + 1, view)
        rows.gather_finish(base + 1, view)
        write(og[level], og_out[level])
        if level == last:
            loads["w", WO].wait()
        loads["qkv", level].wait()
        attended_grad = dot(og[level][...].reshape(count, width), w[:, WO : WO + 512], NN)
        cos, sin = level_rows(cosine, own), level_rows(sine, own)
        qkvg[level][...] = attention_back(
            s["qkv"][...].astype(F32), attended_grad, cos, sin, allowed[level], own
        ).astype(BF)
        write(qkvg[level], qkvg_out[level])
        if level == last:
            loads["w", QKV].wait()

        def attention_tile(cols):
            return dot(qkvg[level][...], w[cols, QKV : QKV + 640], NT)

        rows.reduce(base + 1, own, attention_tile, take)
        loads["hidden", level].wait()
        update, add = norm_back(s["hidden"][...], gain[0:1, :], upstream[0:own, :])
        grad[0:own, :] += update
        gain_part[0:1, :] += add

    write(grad, grad_out)
    for copy in writes:
        copy.wait()


def backward(n, w_all, gain, cot_own, cot_all, tables, saved):
    width = w_all.shape[0]
    hidden_cols = (COLS - GU) // 3
    vmem = pl.BlockSpec(memory_space=pltpu.VMEM)
    hbm = pl.BlockSpec(memory_space=pl.ANY)
    operands = [w_all, gain, cot_own, cot_all, tables["cosine"], tables["sine"], tables["act"], tables["act_last"]]
    operands += list(tables["masks"][1:])
    specs = [hbm, vmem, hbm] + [vmem] * 7
    used = []
    for level in range(RECUR):
        for name in ("gu", "first") if level == 0 else ("gu", "first", "qkv", "hidden"):
            operands.append(saved[level][name])
            specs.append(hbm)
            used.append(saved[level][name])
    outs = [((T, own, width), BF) for own in OWN]
    outs += [((T * own, 2 * hidden_cols), BF) for own in OWN]
    outs += [((T, own, width), BF) for own in OWN[1:]]
    outs += [((T * own, 640), BF) for own in OWN[1:]]
    scratch = [pltpu.VMEM(w_all.shape, BF)] + [pltpu.VMEM(u.shape, u.dtype) for u in used]
    scratch += [pltpu.VMEM(*entry) for entry in outs]
    outs += [((OWN[0], width), F32), ((8, width), F32)]
    out_specs = [hbm] * (len(outs) - 1) + [vmem]
    scratch += [pltpu.VMEM((OWN[0], width), F32)] * 2
    scratch += [pltpu.VMEM((2, 2, OWN[0], width), BF), pltpu.VMEM((OWN[0], width), BF)]
    for own in (OWN[2], OWN[2], OWN[1], OWN[1], OWN[0]):
        scratch += [pltpu.VMEM((2, own, width), BF), pltpu.VMEM((own, width), BF)]
    dma = pltpu.SemaphoreType.DMA
    chunks = width // DC
    scratch += [dma((5, chunks))] * 4 + [dma((5, 3))] * 2 + [dma((24,)), dma((16,))]
    res = pl.pallas_call(
        functools.partial(backward_kernel, n),
        out_shape=[jax.ShapeDtypeStruct(*entry) for entry in outs],
        in_specs=specs,
        out_specs=out_specs,
        scratch_shapes=scratch,
        compiler_params=pltpu.CompilerParams(
            collective_id=2, has_side_effects=True, vmem_limit_bytes=62 << 20
        ),
    )(*operands)
    return {
        "dg": res[0:3],
        "gug": res[3:6],
        "og": res[6:8],
        "qkvg": res[8:10],
        "grad": res[10],
        "gain_part": res[11],
    }


PIECE = 384
SEGMENTS = (("down", 1408), ("gu", 2816), ("out", 512), ("qkv", 640))
DEPTH = 3
FIRST = 1
JOINT = 4
PLACES = COLS // PIECE + FIRST


def cut_pieces():
    pieces = [[] for _ in range(COLS // PIECE)]
    at = 0
    for which, size in SEGMENTS:
        done = 0
        while done < size:
            k, inside = divmod(at, PIECE)
            cols = min(size - done, PIECE - inside)
            pieces[k].append((which, done, cols, inside))
            done += cols
            at += cols
    return pieces


def gradient_kernel(n, *refs):
    it = iter(refs)
    (w_all, gain, cosine, sine, act_own, allowed, back) = [next(it) for _ in range(7)]
    grad_in, gain_in, fin_in, hidden_in, qkv_in = [next(it) for _ in range(5)]
    x_in = {name: [next(it) for _ in range(3)] for name in ("down", "gu", "qkv")}
    x_in["out"] = [None] + [next(it) for _ in range(2)]
    y_in = {name: [next(it) for _ in range(3)] for name in ("down", "gu", "out")}
    y_in["qkv"] = [None] + [next(it) for _ in range(2)]
    (act_out, tok_out, dq, dk, dv, dwo, dgate, dup, dwd, gain_sum) = [next(it) for _ in range(10)]
    og_hbm, fin_all, grad_all = [next(it) for _ in range(3)]
    w = next(it)
    y = {name: next(it) for name in ("down", "gu", "out", "qkv")}
    xm, xl, xraw = next(it), next(it), next(it)
    og, hidden, qkv, grad, upstream, gains = [next(it) for _ in range(6)]
    gpeers = next(it)
    stage, landed, across, across_own = [next(it) for _ in range(4)]
    window_tmp = next(it)
    gmate_stage, gmate, gline, gline_own = [next(it) for _ in range(4)]
    final, turned, last_stage, last_landed, fsend, frecv = [next(it) for _ in range(6)]
    chunk_in, fin_chunk, act_chunk, tok_chunk = [next(it) for _ in range(4)]
    part, relay = next(it), next(it)
    sums = [(next(it), next(it))]
    row_sems = [next(it) for _ in range(6)]
    msend, mrecv, lsend, lrecv, lrecv2 = [next(it) for _ in range(5)]
    tsend, trecv = next(it), next(it)
    insem, xsem, outsem, finsem, loadsem = [next(it) for _ in range(5)]

    p = Place(n)
    width = w.shape[0]
    line = p.line
    chunk_rows = width // n
    window = max(128, chunk_rows)
    rows = Rows(p, part, relay, sums, row_sems)
    own = OWN[0]
    count = T * own
    starts = [0, T * OWN[0], T * (OWN[0] + OWN[1])]
    total_rows = T * sum(OWN)
    hidden_cols = (COLS - GU) // 3
    loads, writes = {}, []

    def load(name, src, dst):
        copy = pltpu.make_async_copy(src, dst, insem.at[len(loads)])
        copy.start()
        loads[name] = copy

    def write(src, dst):
        copy = pltpu.make_async_copy(src, dst, outsem.at[len(writes)])
        copy.start()
        writes.append(copy)

    load("grad", grad_in, grad)
    for name in ("down", "gu"):
        for level in range(RECUR):
            load((name, level), y_in[name][level], y[name].at[pl.ds(starts[level], T * OWN[level])])
    load("w", w_all.at[:, pl.ds(0, GU)], w)
    load("qkv", qkv_in, qkv)
    load("hidden", hidden_in, hidden)
    for level in range(RECUR):
        load(("out", level), y_in["out"][level], y["out"].at[pl.ds(starts[level], T * OWN[level])])
    for level in (1, 2):
        load(("qkv", level), y_in["qkv"][level], y["qkv"].at[pl.ds(starts[level], T * OWN[level])])
    p.barrier(True)

    for which in range(3):
        peers_copy(p, fin_in, fin_all, tsend.at[0], trecv.at[0], which).start()
    pltpu.make_async_copy(fin_in, fin_all.at[p.t], tsend.at[0, 3]).start()

    def x_source(which, level):
        return og_hbm if which == "out" and level == 0 else x_in[which][level]

    def level_slice(level):
        return pl.ds(sum(OWN[:level]) * T, OWN[level] * T)

    def x_copy(which, chunk, slot, level, sem):
        start = pl.multiple_of(chunk * chunk_rows // window * window, window)
        src = x_source(which, level).reshape(T * OWN[level], width)
        return pltpu.make_async_copy(
            src.at[:, pl.ds(start, window)], xraw.at[slot, level_slice(level)], sem.at[slot, level]
        )

    pieces = cut_pieces()
    count_pieces = len(pieces)
    held = {}

    def x_load(which, parity, buffer, sem):
        if held.get(id(buffer)) == which:
            return
        held[id(buffer)] = which

        @pl.loop(0, line)
        def _(i):
            for level in range(RECUR):
                x_copy(which, 2 * i + parity, 0, level, sem).start()
            for level in range(RECUR):
                x_copy(which, 2 * i + parity, 0, level, sem).wait()
            buffer[i] = xraw[0].T

    def product(which, start, cols, parity, buffer, j):
        some = buffer[pl.ds(j * JOINT, JOINT)].reshape(JOINT * window, total_rows)
        value = dot(some, y[which][:, start : start + cols], NN).reshape(JOINT, window, cols)
        if window == chunk_rows:
            return value
        window_tmp[:, :, 0:cols] = value
        return window_tmp[:, pl.ds(pl.multiple_of(parity * chunk_rows, chunk_rows), chunk_rows), 0:cols]

    places = []
    for k in range(count_pieces):
        places += [("own", k), ("other", k)] if k < FIRST else [("normal", k)]

    def columns(q):
        return pl.ds(pl.multiple_of(q * PIECE, 128), PIECE)

    def mate_copy(q, i):
        return remote(
            stage.at[lax.rem(q, DEPTH), i], landed.at[i, :, columns(q)], msend.at[q, i], mrecv.at[q, i], p.mate
        )

    def mates(k):
        q = k + FIRST
        if q >= 2 * FIRST + DEPTH:

            @pl.loop(0, line)
            def _(i):
                mate_copy(q - DEPTH, i).wait_send()

        for number, (which, start, cols, inside) in enumerate(pieces[k]):
            x_load(which, 1 - p.b, xm, xsem.at[0])

            last_part = number == len(pieces[k]) - 1

            @pl.loop(0, line // JOINT)
            def _(j):
                value = product(which, start, cols, 1 - p.b, xm, j)
                some = pl.ds(j * JOINT, JOINT)
                stage[q % DEPTH, some, :, inside : inside + cols] = value.astype(BF)
                if last_part:
                    for i in range(JOINT):
                        mate_copy(q, j * JOINT + i).start()

    def own_terms(q):
        kind, k = places[q]
        for number, (which, start, cols, inside) in enumerate(pieces[k]):
            parity = 1 - p.b if kind == "other" else p.b
            buffer, sem = (xm, xsem.at[0]) if kind == "other" else (xl, xsem.at[1])
            x_load(which, parity, buffer, sem)
            at = pl.ds(q * PIECE + inside, cols)

            @pl.loop(0, line // JOINT)
            def _(j):
                value = product(which, start, cols, parity, buffer, j)
                some = pl.ds(j * JOINT, JOINT)
                if kind == "normal":
                    if number == 0:
                        for i in range(JOINT):
                            mate_copy(q, j * JOINT + i).wait_recv()
                    value = value + landed[some, :, at].astype(F32)
                landed[some, :, at] = value.astype(BF)

    def along(q, i, right):
        return remote(
            landed.at[i, :, columns(q)],
            across.at[i, :, columns(q)],
            lsend.at[q, i],
            lrecv.at[q, i],
            p.right if right else p.left,
        )

    def along_last(q, i):
        return remote(
            landed.at[i, :, columns(q)], across_own.at[:, columns(q)], lsend.at[q, i], lrecv2.at[q], p.left
        )

    def relay_step(q, i, receives):
        @pl.when(receives)
        def _():
            along(q, i, True).wait_recv()
            landed[i, :, columns(q)] = (
                landed[i, :, columns(q)].astype(F32) + across[i, :, columns(q)].astype(F32)
            ).astype(BF)

    def relay_pieces(slot):
        q_right = slot - p.a
        q_left = slot - (line - 1 - p.a)

        @pl.when((q_right >= 0) & (q_right < PLACES))
        def _():
            @pl.loop(0, line)
            def _(step):
                i = line - 1 - step

                @pl.when(i > p.a)
                def _():
                    relay_step(q_right, i, p.has_left)
                    along(q_right, i, True).start()

        @pl.when((q_left >= 0) & (q_left < PLACES))
        def _():
            @pl.loop(0, line)
            def _(i):
                @pl.when(i < p.a)
                def _():
                    relay_step(q_left, i, p.has_right)
                    pl.when(i < p.a - 1)(lambda: along(q_left, i, False).start())
                    pl.when(i == p.a - 1)(lambda: along_last(q_left, i).start())

    def last_copy(j):
        return remote(last_stage.at[j], last_landed.at[j], fsend.at[j], frecv.at[j], p.mate)

    staged, turning = [], []

    def line_sum(q, buffer):
        here = pl.ds(q * PIECE, PIECE)
        buffer[...] = landed[p.a, :, here].astype(F32)

        @pl.when(p.has_left)
        def _():
            along(q, p.a, True).wait_recv()
            buffer[...] += across[p.a, :, here].astype(F32)

        @pl.when(p.has_right)
        def _():
            along_last(q, p.a).wait_recv()
            buffer[...] += across_own[:, here].astype(F32)

    def finish(q):
        kind, k = places[q]
        if kind == "own":
            return
        if kind == "other":
            if len(staged) >= 2:
                for copy in staged[len(staged) - 2]:
                    copy.wait()
                staged[len(staged) - 2] = []
            buffer = final.at[len(staged) % 2]
            line_sum(q, buffer)
            last_stage[k] = buffer[...].astype(BF)
            last_copy(k).start()
        else:
            results(q)
        if q >= 3 and places[q - 3][0] == "own":
            results(q - 3)

    def results(q):
        kind, k = places[q]
        number = len(staged)
        if number >= 2:
            for copy in staged[number - 2]:
                copy.wait()
        buffer = final.at[number % 2]
        line_sum(q, buffer)
        if kind == "own":
            last_copy(k).wait_recv()
            buffer[...] += last_landed[k].astype(F32)
            last_copy(k).wait_send()
        copies = []

        def out(src, dst):
            copy = pltpu.make_async_copy(src, dst, finsem.at[k, len(copies)])
            copy.start()
            copies.append(copy)

        for which, start, cols, inside in pieces[k]:
            if which in ("down", "out"):
                for copy in turning:
                    copy.wait()
                turning.clear()
                turned[inside : inside + cols, :] = buffer[:, inside : inside + cols].T
                target = dwd if which == "down" else dwo
                copy = pltpu.make_async_copy(
                    turned.at[pl.ds(inside, cols)], target.at[pl.ds(start, cols)], finsem.at[k, 7]
                )
                copy.start()
                turning.append(copy)
            elif which == "gu":
                middle = min(max(hidden_cols - start, 0), cols)
                if middle:
                    out(buffer.at[:, pl.ds(inside, middle)], dgate.at[:, pl.ds(start, middle)])
                if middle < cols:
                    out(
                        buffer.at[:, pl.ds(inside + middle, cols - middle)],
                        dup.at[:, pl.ds(start + middle - hidden_cols, cols - middle)],
                    )
            else:
                queries = min(max(512 - start, 0), cols)
                if queries:
                    out(buffer.at[:, pl.ds(inside, queries)], dq.at[:, pl.ds(start, queries)])
                if queries < cols:
                    both = buffer[:, inside + queries : inside + queries + 2 * HS].T
                    dk[...] = both[0:HS]
                    dv[...] = both[HS : 2 * HS]
        staged.append(copies)

    def drain():
        @pl.loop(0, PLACES)
        def _(q):
            @pl.loop(0, line)
            def _(i):
                pl.when(q >= max(PLACES - DEPTH, 2 * FIRST))(lambda: mate_copy(q, i).wait_send())
                pl.when(i != p.a)(lambda: along(q, i, True).wait_send())

    loads["grad"].wait()
    present = act_own[0, 0:own, :]
    og[p.t] = (present * grad[...]).astype(BF)
    view = og.reshape(2, 2, own, width)
    rows.gather_start(0, view)
    for level in range(RECUR):
        loads["down", level].wait()
    sent = [FIRST]

    def mates_upto(k):
        while sent[0] <= min(k, count_pieces - 1):
            mates(sent[0])
            sent[0] += 1

    slots = [0]

    def slot():
        s = slots[0]
        slots[0] += 1
        if s < PLACES:
            own_terms(s)
        relay_pieces(s)
        if 0 <= s - line + 1 < PLACES:
            finish(s - line + 1)
        mates_upto(s - FIRST + DEPTH)

    mates(FIRST)
    sent[0] += 1
    slot()
    rows.gather_finish(0, view)
    write(og, og_hbm)
    for level in range(RECUR):
        loads["gu", level].wait()
    mates_upto(FIRST + 2)
    loads["w"].wait()
    loads["qkv"].wait()
    attended_grad = dot(og[...].reshape(count, width), w[:, WO : WO + 512], NN)
    y["qkv"][0:count, :] = attention_back(
        qkv[...].astype(F32), attended_grad, cosine[...], sine[...], allowed, own, slot
    ).astype(BF)
    slot()

    def attention_tile(cols):
        return dot(y["qkv"][0:count, :], w[cols, QKV : QKV + 640], NT)

    def take(cols, total):
        upstream[:, cols] = total

    rows.reduce(0, own, attention_tile, take)
    loads["hidden"].wait()
    update, add = norm_back(hidden[...], gain[0:1, :], upstream[...])
    grad[...] += update
    gains[...] = gain_in[...]
    gains[0:1, :] += add
    for which in range(3):
        peers_copy(p, grad, grad_all, tsend.at[1], trecv.at[1], which).start()
        peers_copy(p, gains, gpeers, tsend.at[2], trecv.at[2], which).start()
    pltpu.make_async_copy(grad, grad_all.at[p.t], tsend.at[1, 3]).start()
    gpeers[p.t] = gains[...]
    for level in range(RECUR):
        loads["out", level].wait()
    for level in (1, 2):
        loads["qkv", level].wait()
    for copy in writes:
        copy.wait()

    def wait_peers(i, src, dst, local=True):
        for which in range(3):
            copy = peers_copy(p, src, dst, tsend.at[i], trecv.at[i], which)
            copy.wait_recv()
            copy.wait_send()
        if local:
            pltpu.make_async_copy(src, dst.at[p.t], tsend.at[i, 3]).wait()

    def outputs():
        wait_peers(0, fin_in, fin_all)
        wait_peers(1, grad, grad_all)
        mine = back[...]

        @pl.loop(0, width // OC)
        def _(c):
            cols = pl.ds(pl.multiple_of(c * OC, OC), OC)
            first = pltpu.make_async_copy(fin_all.at[:, :, cols], fin_chunk, loadsem.at[0])
            second = pltpu.make_async_copy(grad_all.at[:, :, cols], chunk_in, loadsem.at[1])
            first.start()
            second.start()
            first.wait()
            second.wait()
            act_chunk[...] = dot(mine, fin_chunk[...].reshape(count, OC), NN).astype(BF).reshape(
                MB, own // MB, OC
            )
            value = chunk_in[...].reshape(count, OC)
            high = value.astype(BF)
            rest = value - high.astype(F32)
            middle = rest.astype(BF)
            low = (rest - middle.astype(F32)).astype(BF)
            total = dot(mine, high, NN) + (dot(mine, middle, NN) + dot(mine, low, NN))
            tok_chunk[...] = total.reshape(MB, own // MB, OC)
            third = pltpu.make_async_copy(act_chunk, act_out.at[:, :, cols], loadsem.at[0])
            fourth = pltpu.make_async_copy(tok_chunk, tok_out.at[:, :, cols], loadsem.at[1])
            third.start()
            fourth.start()
            third.wait()
            fourth.wait()

    def gain_tile(chunk):
        start = pl.multiple_of(chunk * chunk_rows // window * window, window)
        return (
            gpeers[0, :, pl.ds(start, window)]
            + gpeers[1, :, pl.ds(start, window)]
            + gpeers[2, :, pl.ds(start, window)]
            + gpeers[3, :, pl.ds(start, window)]
        )

    last = PLACES

    def gain_mate(i):
        return remote(gmate_stage.at[i], gmate.at[i], msend.at[last, i], mrecv.at[last, i], p.mate)

    def gain_along(i, right):
        return remote(
            gmate.at[i], gline.at[i], lsend.at[last, i], lrecv.at[last, i], p.right if right else p.left
        )

    def gain_last(i):
        return remote(gmate.at[i], gline_own, lsend.at[last, i], lrecv2.at[last], p.left)

    def gain_mates():
        wait_peers(2, gains, gpeers, False)

        @pl.loop(0, line)
        def _(i):
            gmate_stage[i] = gain_tile(2 * i + 1 - p.b)
            gain_mate(i).start()

    def gain_lines():
        @pl.loop(0, line)
        def _(step):
            odd = lax.rem(step, 2)
            i = jnp.where(odd == 1, step // 2, line - 1 - step // 2)

            @pl.when(i != p.a)
            def _():
                gain_mate(i).wait_recv()
                gmate[i] += gain_tile(2 * i + p.b)

                @pl.when(((i > p.a) & p.has_left) | ((i < p.a) & p.has_right))
                def _():
                    gain_along(i, True).wait_recv()
                    gmate[i] += gline[i]

                pl.when(i > p.a)(lambda: gain_along(i, True).start())
                pl.when(i < p.a - 1)(lambda: gain_along(i, False).start())
                pl.when(i == p.a - 1)(lambda: gain_last(i).start())

        gain_mate(p.a).wait_recv()
        gain_sum[...] = gain_tile(2 * p.a + p.b) + gmate[p.a]

        @pl.when(p.has_left)
        def _():
            gain_along(p.a, True).wait_recv()
            gain_sum[...] += gline[p.a]

        @pl.when(p.has_right)
        def _():
            gain_last(p.a).wait_recv()
            gain_sum[...] += gline_own[...]

        @pl.loop(0, line)
        def _(i):
            gain_mate(i).wait_send()
            pl.when(i != p.a)(lambda: gain_along(i, True).wait_send())

    for s in range(slots[0], PLACES + line - 1):
        slot()
        if s == 5:
            gain_mates()
        if s == 6:
            gain_lines()
        if s == 8:
            outputs()
    drain()
    for copies in staged[-2:] + [turning]:
        for copy in copies:
            copy.wait()


def gradients(n, w_all, gain, tables, saved, bwd, fin):
    width = w_all.shape[0]
    hidden_cols = (COLS - GU) // 3
    line = n // 2
    chunk_rows = width // n
    window = max(128, chunk_rows)
    vmem = pl.BlockSpec(memory_space=pltpu.VMEM)
    hbm = pl.BlockSpec(memory_space=pl.ANY)
    total_rows = T * sum(OWN)
    own = OWN[0]
    operands = [w_all, gain, tables["cosine"], tables["sine"], tables["act"], tables["masks"][0], tables["back"]]
    specs = [hbm] + [vmem] * 6
    operands += [bwd["grad"], bwd["gain_part"], fin, saved[0]["hidden"], saved[0]["qkv"]]
    specs += [hbm, vmem, hbm, hbm, hbm]
    streams = list(bwd["dg"]) + [s["mixed"] for s in saved] + [s["normed"] for s in saved] + list(bwd["og"])
    streams += [s["prod"] for s in saved] + list(bwd["gug"]) + [s["att"] for s in saved] + list(bwd["qkvg"])
    operands += streams
    specs += [hbm] * len(streams)
    outs = [
        ((MB, own // MB, width), BF),
        ((MB, own // MB, width), F32),
        ((chunk_rows, 512), F32),
        ((HS, chunk_rows), F32),
        ((HS, chunk_rows), F32),
        ((512, chunk_rows), F32),
        ((chunk_rows, hidden_cols), F32),
        ((chunk_rows, hidden_cols), F32),
        ((hidden_cols, chunk_rows), F32),
        ((8, window), F32),
        ((T, own, width), BF),
        ((T, own, width), BF),
        ((T, own, width), F32),
    ]
    out_specs = [hbm, hbm, hbm, vmem, vmem, hbm, hbm, hbm, hbm, vmem, hbm, hbm, hbm]
    scratch = [pltpu.VMEM((width, GU), BF)]
    scratch += [pltpu.VMEM((total_rows, c), BF) for c in (hidden_cols, 2 * hidden_cols, 512, 640)]
    scratch += [pltpu.VMEM((line, window, total_rows), BF)] * 2 + [pltpu.VMEM((1, total_rows, window), BF)]
    scratch += [
        pltpu.VMEM((T, own, width), BF),
        pltpu.VMEM((own, width), F32),
        pltpu.VMEM((T * own, 640), BF),
        pltpu.VMEM((own, width), F32),
        pltpu.VMEM((own, width), F32),
        pltpu.VMEM((8, width), F32),
        pltpu.VMEM((T, 8, width), F32),
    ]
    scratch += [
        pltpu.VMEM((DEPTH, line, chunk_rows, PIECE), BF),
        pltpu.VMEM((line, chunk_rows, PLACES * PIECE), BF),
        pltpu.VMEM((line, chunk_rows, PLACES * PIECE), BF),
        pltpu.VMEM((chunk_rows, PLACES * PIECE), BF),
        pltpu.VMEM((JOINT, window, PIECE) if window > chunk_rows else (1, 8, 128), F32),
    ]
    scratch += [pltpu.VMEM((line, 8, window), F32)] * 3 + [pltpu.VMEM((8, window), F32)]
    scratch += [pltpu.VMEM((2, chunk_rows, PIECE), F32), pltpu.VMEM((PIECE, chunk_rows), F32)]
    scratch += [pltpu.VMEM((FIRST, chunk_rows, PIECE), BF)] * 2
    scratch += [pltpu.SemaphoreType.DMA((FIRST,))] * 2
    scratch += [pltpu.VMEM((T, own, OC), F32), pltpu.VMEM((T, own, OC), BF)]
    scratch += [pltpu.VMEM((MB, own // MB, OC), BF), pltpu.VMEM((MB, own // MB, OC), F32)]
    scratch += [pltpu.VMEM((2, 2, own, width), BF), pltpu.VMEM((own, width), BF)]
    scratch += [pltpu.VMEM((2, own, width), BF), pltpu.VMEM((own, width), BF)]
    dma = pltpu.SemaphoreType.DMA
    chunks = width // DC
    k = PLACES + 1
    scratch += [dma((1, chunks))] * 4 + [dma((1, 3))] * 2
    scratch += [dma((k, line))] * 4 + [dma((k,))]
    scratch += [dma((3, 4)), dma((3, 3))]
    scratch += [dma((24,)), dma((2, 2, RECUR)), dma((4,)), dma((k, 8)), dma((2,))]
    res = pl.pallas_call(
        functools.partial(gradient_kernel, n),
        out_shape=[jax.ShapeDtypeStruct(*entry) for entry in outs],
        in_specs=specs,
        out_specs=out_specs,
        scratch_shapes=scratch,
        compiler_params=pltpu.CompilerParams(
            collective_id=3, has_side_effects=True, vmem_limit_bytes=63 << 20
        ),
    )(*operands)
    return res


def hand_out_kernel(count, *refs):
    for i in range(count):
        refs[count + i][...] = refs[i][...]


def hand_out(values):
    vmem = pl.BlockSpec(memory_space=pltpu.VMEM)
    count = len(values)
    return pl.pallas_call(
        functools.partial(hand_out_kernel, count),
        out_shape=[jax.ShapeDtypeStruct(v.shape, v.dtype) for v in values],
        in_specs=[vmem] * count,
        out_specs=[vmem] * count,
        compiler_params=pltpu.CompilerParams(vmem_limit_bytes=40 << 20),
    )(*values)


def shards(n, *args):
    tokens, depth, lengths, cotangent = args[:4]
    attn_gain, mlp_gain = args[11:]
    index = lax.axis_index("tensor")
    w_all, gain, fin, cot_own, cot_all, tables, saved = forward(
        n, tokens, depth, lengths[:, 0], cotangent, args[4:11], attn_gain, mlp_gain
    )
    bwd = backward(n, w_all, gain, cot_own, cot_all, tables, saved)
    res = gradients(n, w_all, gain, tables, saved, bwd, fin)
    gain_sum = res[9]
    activations, tokens_grad, dq, dk, dv, dwo, dgate, dup, dwd = hand_out(res[:9])
    each = attn_gain.shape[0]
    window = gain_sum.shape[1]
    start = lax.rem((lax.axis_index("dp") * T + index) * each, window)
    both = lax.dynamic_slice_in_dim(gain_sum, start, each, axis=1)
    return (activations, tokens_grad, dq, dk.T, dv.T, dwo, dgate, dup, dwd, both[0], both[1])


def solution(mesh):
    rows = P(None, ("dp", "tensor"), None)
    weight_specs = (P("dp", "tensor"),) * 3 + (P("tensor", "dp"),) + (P("dp", "tensor"),) * 2 + (P("tensor", "dp"),)
    gain_specs = (P(("dp", "tensor")),) * 2
    return jax.shard_map(
        functools.partial(shards, mesh.shape["dp"]),
        mesh=mesh,
        in_specs=(rows, P(None, "dp"), P(None, "dp", None), rows) + weight_specs + gain_specs,
        out_specs=(rows, rows) + weight_specs + gain_specs,
        check_vma=False,
    )
```

```python
import functools

import jax
import jax.numpy as jnp
import numpy as np
from jax import lax
from jax.experimental import pallas as pl
from jax.experimental.pallas import tpu as pltpu
from jax.sharding import PartitionSpec as P

HQ = 32
KVH = 4
HS = 64
MB = 2
RECUR = 3
SCALE = HS ** (-0.5)
F32 = jnp.float32
BF = jnp.bfloat16
MESH = pl.DeviceIdType.MESH
NN = (((1,), (0,)), ((), ()))
NT = (((1,), (1,)), ((), ()))
TN = (((0,), (0,)), ((), ()))

OWN = (96, 80, 48)
PIECES = ((0, 24, 0), (24, 24, 1), (48, 16, 0), (64, 16, 1), (80, 8, 0), (88, 8, 1))
T = 4
DC = 512
OC = 256
HEADS = 2


def split_batches(values, own):
    halves = ([], [])
    for owner in range(T):
        for start, rows, b in PIECES:
            if start < own:
                halves[b].append(values[owner * own + start : owner * own + start + rows])
    return [jnp.concatenate(half, axis=0) for half in halves]


def join_batches(halves, own):
    rows_out, at = [], [0, 0]
    for owner in range(T):
        for start, rows, b in PIECES:
            if start < own:
                rows_out.append(halves[b][at[b] : at[b] + rows])
                at[b] += rows
    return jnp.concatenate(rows_out, axis=0)


def dot(left, right, dims):
    return lax.dot_general(left, right, dims, preferred_element_type=F32)


def swap_halves(tile):
    lane = lax.broadcasted_iota(jnp.int32, tile.shape, 1)
    return jnp.where((lane & 63) < 32, pltpu.roll(tile, 96, 1), pltpu.roll(tile, 32, 1))


def attention_shares(query, key, allowed):
    rows = query.shape[0]
    group = query.shape[1] // HS
    stacked = stack_heads(query)
    scores = dot(stacked, key, NT).reshape(group, rows, rows) * SCALE
    scores = jnp.where(allowed.astype(F32)[None] > 0, scores, -1e30)
    raised = jnp.exp(scores - jnp.max(scores, axis=-1, keepdims=True))
    return stacked, raised * (1.0 / jnp.sum(raised, axis=-1, keepdims=True))


def stack_heads(values):
    group = values.shape[1] // HS
    return jnp.concatenate([values[:, h * HS : (h + 1) * HS] for h in range(group)], axis=0)


def unstack_heads(values, rows):
    group = values.shape[0] // rows
    return jnp.concatenate([values[h * rows : (h + 1) * rows] for h in range(group)], axis=1)


def mean_square(values):
    return jnp.mean(values * values, axis=-1, keepdims=True)


class Place:
    def __init__(self, n):
        self.n = n
        self.line = n // 2
        self.dp = lax.axis_index("dp")
        self.t = lax.axis_index("tensor")
        self.a = self.dp // 2
        self.b = lax.rem(self.dp, 2)
        self.hi = self.t // 2
        self.lo = lax.rem(self.t, 2)
        self.has_right = self.a < self.line - 1
        self.has_left = self.a > 0
        self.mate = (self.a * 2 + 1 - self.b, self.t)
        self.right = (jnp.minimum(self.dp + 2, n - 1), self.t)
        self.left = (jnp.maximum(self.dp - 2, 0), self.t)
        self.near = (self.dp, self.hi * 2 + 1 - self.lo)
        self.far = (self.dp, (1 - self.hi) * 2 + self.lo)
        self.diag = (self.dp, (1 - self.hi) * 2 + 1 - self.lo)

    def barrier(self, along):
        sem = pltpu.get_barrier_semaphore()

        def greet(device):
            pl.semaphore_signal(sem, inc=1, device_id=device, device_id_type=MESH)

        for device in (self.near, self.far, self.diag):
            greet(device)
        expected = 3
        if along:
            greet(self.mate)
            pl.when(self.has_right)(lambda: greet(self.right))
            pl.when(self.has_left)(lambda: greet(self.left))
            expected = 4 + self.has_right.astype(jnp.int32) + self.has_left.astype(jnp.int32)
        pl.semaphore_wait(sem, expected)


def remote(src, dst, send, recv, device):
    return pltpu.make_async_remote_copy(
        src_ref=src, dst_ref=dst, send_sem=send, recv_sem=recv, device_id=device, device_id_type=MESH
    )


class LineGather:
    def __init__(self, place, pieces, sems):
        self.p = place
        self.pieces = pieces
        self.msend, self.mrecv, self.rsend, self.rrecv, self.lsend, self.lrecv = sems

    def toward_left(self, w, k, chunk):
        ref = self.pieces[w][1](chunk)
        return remote(ref, ref, self.lsend.at[w, k], self.lrecv.at[w, k], self.p.left)

    def toward_right(self, w, k, chunk):
        ref = self.pieces[w][1](chunk)
        return remote(ref, ref, self.rsend.at[w, k], self.rrecv.at[w, k], self.p.right)

    def toward_mate(self, w, k, chunk):
        ref = self.pieces[w][1](chunk)
        return remote(ref, ref, self.msend.at[w, k], self.mrecv.at[w, k], self.p.mate)

    def first(self, w):
        p = self.p
        return p.a * 2 + 1 - p.b if self.pieces[w][0] == "other" else p.dp

    def own(self, w):
        p = self.p
        kind = self.pieces[w][0]
        chunk = self.first(w)
        if kind == "other":
            self.toward_mate(w - 1, p.a, chunk).wait_recv()
        pl.when(p.has_left)(lambda: self.toward_left(w, 0, chunk).start())
        pl.when(p.has_right)(lambda: self.toward_right(w, 0, chunk).start())
        if kind != "other":
            self.toward_mate(w, p.a, chunk).start()

    def step(self, w, k):
        p = self.p
        normal = self.pieces[w][0] == "normal"

        @pl.when(p.a + k < p.line)
        def _():
            chunk = self.first(w) + 2 * k
            self.toward_left(w, k - 1, chunk).wait_recv()
            pl.when(p.has_left)(lambda: self.toward_left(w, k, chunk).start())
            if normal:
                self.toward_mate(w, p.a + k, chunk).start()

        @pl.when(p.a - k >= 0)
        def _():
            chunk = self.first(w) - 2 * k
            self.toward_right(w, k - 1, chunk).wait_recv()
            pl.when(p.has_right)(lambda: self.toward_right(w, k, chunk).start())
            if normal:
                self.toward_mate(w, p.a - k, chunk).start()

    def steps(self, w):
        for k in range(1, self.p.line):
            self.step(w, k)

    def arrive(self, w):
        p = self.p
        if self.pieces[w][0] == "normal":
            for i in range(p.line):
                self.toward_mate(w, i, 2 * i + 1 - p.b).wait_recv()

    def drain(self, w):
        p = self.p
        kind = self.pieces[w][0]
        if kind == "own":
            self.toward_mate(w, p.a, p.dp).wait_send()
        for i in range(p.line):
            if kind == "normal":
                self.toward_mate(w, i, p.dp).wait_send()
            pl.when(p.has_left & (p.a + i < p.line))(lambda: self.toward_left(w, i, p.dp).wait_send())
            pl.when(p.has_right & (p.a - i >= 0))(lambda: self.toward_right(w, i, p.dp).wait_send())


class Rows:
    def __init__(self, place, part, relay, sums, sems):
        self.p = place
        self.part, self.relay, self.sums = part, relay, sums
        self.s1, self.q1, self.s2, self.q2, self.gs, self.gr = sems

    def first_copy(self, i, own, c):
        p = self.p
        cols = pl.ds(pl.multiple_of(c * DC, DC), DC)
        return remote(
            self.part.at[:, 1 - p.lo, pl.ds(0, own), cols],
            self.sums[i][0].at[:, pl.ds(0, own), cols],
            self.s1.at[i, c],
            self.q1.at[i, c],
            p.near,
        )

    def second_copy(self, i, own, c):
        p = self.p
        cols = pl.ds(pl.multiple_of(c * DC, DC), DC)
        return remote(
            self.relay.at[pl.ds(0, own), cols],
            self.sums[i][1].at[pl.ds(0, own), cols],
            self.s2.at[i, c],
            self.q2.at[i, c],
            p.far,
        )

    def reduce(self, i, own, tile, finish):
        p = self.p
        part, relay = self.part, self.relay
        r1, r2 = self.sums[i]
        chunks = part.shape[-1] // DC

        def pass_on(c):
            cols = pl.ds(pl.multiple_of(c * DC, DC), DC)
            self.first_copy(i, own, c).wait_recv()
            mine = part[1 - p.hi, p.lo, 0:own, cols].astype(F32)
            relay[0:own, cols] = (mine + r1[1 - p.hi, 0:own, cols].astype(F32)).astype(BF)
            self.second_copy(i, own, c).start()

        @pl.loop(0, chunks)
        def _(c):
            cols = pl.ds(pl.multiple_of(c * DC, DC), DC)
            part[:, :, 0:own, cols] = tile(cols).astype(BF).reshape(2, 2, own, DC)
            self.first_copy(i, own, c).start()
            pl.when(c > 0)(lambda: pass_on(c - 1))

        pass_on(chunks - 1)

        @pl.loop(0, chunks)
        def _(c):
            cols = pl.ds(pl.multiple_of(c * DC, DC), DC)
            self.second_copy(i, own, c).wait_recv()
            mine = part[p.hi, p.lo, 0:own, cols].astype(F32)
            finish(cols, mine + r1[p.hi, 0:own, cols].astype(F32) + r2[0:own, cols].astype(F32))

        @pl.loop(0, chunks)
        def _(c):
            self.first_copy(i, own, c).wait_send()
            self.second_copy(i, own, c).wait_send()

    def gather_copy(self, i, buffer, which):
        p = self.p
        here = buffer.at[p.hi, p.lo]
        if which == 0:
            return remote(here, here, self.gs.at[i, 0], self.gr.at[i, 0], p.far)
        if which == 1:
            return remote(here, here, self.gs.at[i, 1], self.gr.at[i, 1], p.near)
        there = buffer.at[1 - p.hi, p.lo]
        return remote(there, there, self.gs.at[i, 2], self.gr.at[i, 2], p.near)

    def gather_start(self, i, buffer):
        self.gather_copy(i, buffer, 0).start()
        self.gather_copy(i, buffer, 1).start()

    def gather_finish(self, i, buffer):
        self.gather_copy(i, buffer, 0).wait_recv()
        self.gather_copy(i, buffer, 2).start()
        self.gather_copy(i, buffer, 1).wait_recv()
        self.gather_copy(i, buffer, 2).wait_recv()
        for which in range(3):
            self.gather_copy(i, buffer, which).wait_send()


def peers_copy(place, src, dst, send, recv, which):
    device = (place.near, place.far, place.diag)[which]
    return remote(src, dst.at[place.t], send.at[which], recv.at[which], device)


def gain_row(gathered, n, row, width):
    each = width // (n * T)
    tiles = []
    for j in range(width // 128):
        total = None
        for i in range(128 // each):
            number = j * (128 // each) + i
            block = gathered[number % T, number // T][row : row + 1]
            total = block if total is None else total + block
        tiles.append(total)
    return jnp.concatenate(tiles, axis=1)


QKV, WO, GU, WD = 0, 640, 1152, 3968
COLS = 5376
RANGES = (
    ("along", 0, 640),
    ("along", 640, 512),
    ("along", 1152, 1408),
    ("along", 2560, 1408),
    ("along", 3968, 512),
    ("across", 4480, 896),
)


def ones(condition):
    return jnp.where(condition, 1.0, 0.0)


def iota(size, axis):
    shape = (size, 1) if axis == 0 else (1, size)
    return lax.broadcasted_iota(jnp.int32, shape, axis).astype(F32)


def quotient(index, step, most):
    total = ones(index >= step)
    for i in range(2, most):
        total = total + ones(index >= step * i)
    return total


def own_places(own_index):
    batch, place, seen = 0.0 * own_index, 0.0 * own_index, [0, 0]
    for start, rows, b in PIECES:
        inside = (own_index >= start) & (own_index < start + rows)
        batch = jnp.where(inside, float(b), batch)
        place = jnp.where(inside, own_index - start + seen[b], place)
        seen[b] += rows
    return batch, place


def fill_tables(p, depth_row, depth_col, lengths, freqs, perm, back, back_own, cosine, sine, allowed, act_own, act_last):
    local = OWN[0] // MB
    total = T * OWN[0]

    def columns(index):
        tensor = quotient(index, OWN[0], T)
        inside = index - tensor * OWN[0]
        batch = ones(inside >= local)
        return batch, tensor * local + inside - batch * local

    batch_row, pos_row = columns(iota(total, 1))
    batch_col, pos_col = columns(iota(total, 0))
    same = batch_row == batch_col
    rank_row = jnp.sum(
        ones(same & ((depth_col > depth_row) | ((depth_col == depth_row) & (pos_col < pos_row)))), axis=0, keepdims=True
    )
    rank_col = jnp.sum(
        ones(same & ((depth_row > depth_col) | ((depth_row == depth_col) & (pos_row < pos_col)))), axis=1, keepdims=True
    )

    def compact(index):
        owner = quotient(index, OWN[0], T)
        batch, place = own_places(index - owner * OWN[0])
        return batch, place * T + owner

    batch_q, rank_q = compact(iota(total, 0))
    hit = (rank_row == rank_q) & (batch_row == batch_q)
    perm[...] = ones(hit).astype(BF)
    batch_p, rank_p = compact(iota(total, 1))
    back[...] = ones((rank_col == rank_p) & (batch_col == batch_p)).astype(BF)
    back_own[...] = back[pl.ds(pl.multiple_of(p.t * OWN[0], OWN[0]), OWN[0]), :]

    ends = []
    for b in range(MB):
        first = lengths[b : b + 1, 0:1].astype(F32)
        ends.append((first, first + lengths[b : b + 1, 1:2].astype(F32)))
    position = jnp.sum(jnp.where(hit, pos_row, 0.0), axis=1, keepdims=True)
    end = [jnp.where(batch_q == 0.0, ends[0][i], ends[1][i]) for i in range(2)]
    start = jnp.where(position >= end[1], end[1], jnp.where(position >= end[0], end[0], 0.0))
    angles = (position - start) * freqs
    cosine[...] = jnp.cos(angles)
    lane = lax.broadcasted_iota(jnp.int32, angles.shape, 1)
    value = jnp.sin(angles)
    sine[...] = jnp.where((lane & 63) < 32, -value, value)

    own_batch, own_place = own_places(iota(OWN[0], 0))
    own_rank = own_place * T + p.t.astype(F32)
    for level in range(RECUR):
        own = OWN[level]
        half = T * own // MB
        counts = [
            jnp.sum(ones((batch_row == float(b)) & (depth_row >= level + 1.0)), axis=1, keepdims=True) for b in range(MB)
        ]
        act_own[level] = ones(own_rank < jnp.where(own_batch == 0.0, counts[0], counts[1]))
        if level == RECUR - 1:
            index = iota(T * own, 0)
            owner = quotient(index, own, T)
            batch, place = own_places(index - owner * own)
            act_last[...] = ones(place * T + owner < jnp.where(batch == 0.0, counts[0], counts[1]))

        def order(index):
            owner = quotient(index, own // MB, T)
            return (index - owner * (own // MB)) * T + owner

        index_col, index_row = iota(half, 0), iota(half, 1)
        order_col, order_row = order(index_col), order(index_row)
        for b in range(MB):
            at_col = jnp.sum(
                jnp.where((rank_row == order_col) & (batch_row == float(b)), pos_row, 0.0), axis=1, keepdims=True
            )
            at_row = jnp.sum(
                jnp.where((rank_col == order_row) & (batch_col == float(b)), pos_col, 0.0), axis=0, keepdims=True
            )
            document_col = ones(at_col >= ends[b][0]) + ones(at_col >= ends[b][1])
            document_row = ones(at_row >= ends[b][0]) + ones(at_row >= ends[b][1])
            ok = (document_col == document_row) & (at_row <= at_col) & (order_row < counts[b])
            allowed[level][b] = ones(ok | (index_col == index_row)).astype(BF)


def forward_kernel(n, *refs):
    it = iter(refs)
    tokens, cotangent, wq, wk, wv, wo, wg, wu, wd = [next(it) for _ in range(9)]
    attn_gain, mlp_gain, depth_row, depth_col, lengths, freqs = [next(it) for _ in range(6)]
    w_out, gain_out, fin_out, cot_own, cot_all = [next(it) for _ in range(5)]
    cosine, sine, back_own, act_own, act_last = [next(it) for _ in range(5)]
    allowed = [next(it) for _ in range(RECUR)]
    names = ("normed", "qkv", "att", "mixed", "gu", "prod", "hidden", "first")
    saved_out = [dict((k, next(it)) for k in names) for _ in range(RECUR)]
    w = next(it)
    perm, back, kv, wo_in, wd_in = [next(it) for _ in range(5)]
    gbuf, gall = next(it), next(it)
    tok, cot = next(it), next(it)
    saved = [dict((k, next(it)) for k in names) for _ in range(RECUR)]
    after, fin, cown = next(it), next(it), next(it)
    part, relay = next(it), next(it)
    sums = [(next(it), next(it)) for _ in range(2 * RECUR)]
    line_sems = [next(it) for _ in range(6)]
    row_sems = [next(it) for _ in range(6)]
    wsem = next(it)
    tsend, trecv, outsem = next(it), next(it), next(it)

    p = Place(n)
    width = tokens.shape[-1]
    rows_chunk = width // n

    def chunk_at(chunk, start, size):
        return w.at[pl.ds(pl.multiple_of(chunk * rows_chunk, rows_chunk), rows_chunk), pl.ds(start, size)]

    pieces = [("normal", lambda chunk: gbuf.at[chunk])]
    number = []
    for kind, start, size in RANGES:
        def at(chunk, start=start, size=size):
            return chunk_at(chunk, start, size)

        number.append(len(pieces))
        pieces += [("own", at), ("other", at)] if kind == "across" else [("normal", at)]
    line = LineGather(p, pieces, line_sems)
    rows = Rows(p, part, relay, sums, row_sems)
    hidden_cols = (COLS - GU) // 3
    writes = []

    def write(src, dst):
        copy = pltpu.make_async_copy(src, dst, outsem.at[len(writes)])
        copy.start()
        writes.append(copy)

    local = [
        pltpu.make_async_copy(wq, chunk_at(p.dp, QKV, 512), wsem.at[0]),
        pltpu.make_async_copy(wk, kv.at[0], wsem.at[1]),
        pltpu.make_async_copy(wv, kv.at[1], wsem.at[2]),
        pltpu.make_async_copy(wo, wo_in, wsem.at[3]),
        pltpu.make_async_copy(wg, chunk_at(p.dp, GU, hidden_cols), wsem.at[4]),
        pltpu.make_async_copy(wu, chunk_at(p.dp, GU + hidden_cols, hidden_cols), wsem.at[5]),
        pltpu.make_async_copy(wd, wd_in, wsem.at[6]),
    ]
    for copy in local:
        copy.start()
    mine_rows = pl.ds(pl.multiple_of(p.dp * rows_chunk, rows_chunk), rows_chunk)
    each = attn_gain.shape[1]
    lane = lax.broadcasted_iota(jnp.int32, (1, 128), 1)
    spot = lax.rem(p.dp * T + p.t, 128 // each)
    inside = (lane >= spot * each) & (lane < (spot + 1) * each)
    for row, gain in enumerate((attn_gain, mlp_gain)):
        value = jnp.concatenate([gain[...]] * (128 // each), axis=1)
        gbuf[p.dp, row : row + 1, :] = jnp.where(inside, value, 0.0)
    gbuf[p.dp, 2:8, :] = jnp.zeros((6, 128), F32)
    p.barrier(True)
    line.own(0)
    for copy in local[0:3]:
        copy.wait()
    w[mine_rows, QKV + 512 : QKV + 640] = jnp.concatenate([kv[0], kv[1]], axis=0).T
    heads_piece, out_piece, gate_piece, up_piece, down_piece, down_last = number
    line.own(heads_piece)
    for which in range(3):
        peers_copy(p, tokens, tok, tsend.at[0], trecv.at[0], which).start()
    pltpu.make_async_copy(tokens, tok.at[p.t], tsend.at[0, 3]).start()
    local[3].wait()
    w[mine_rows, WO : WO + 512] = wo_in[...].T
    line.own(out_piece)
    for which in range(3):
        peers_copy(p, cotangent, cot, tsend.at[1], trecv.at[1], which).start()
    pltpu.make_async_copy(cotangent, cot.at[p.t], tsend.at[1, 3]).start()
    for copy in local[4:6]:
        copy.wait()
    line.own(gate_piece)
    line.steps(0)
    line.arrive(0)
    for which in range(3):
        peers_copy(p, gbuf, gall, tsend.at[2], trecv.at[2], which).start()
    pltpu.make_async_copy(gbuf, gall.at[p.t], tsend.at[2, 3]).start()
    fill_tables(
        p, depth_row[...], depth_col[...], lengths, freqs[...], perm, back, back_own, cosine, sine, allowed, act_own, act_last
    )
    line.steps(heads_piece)
    local[6].wait()
    w[mine_rows, WD : WD + hidden_cols] = wd_in[...].T
    line.own(up_piece)
    line.steps(out_piece)

    def wait_peers(i, src, dst):
        for which in range(3):
            copy = peers_copy(p, src, dst, tsend.at[i], trecv.at[i], which)
            copy.wait_recv()
            copy.wait_send()
        pltpu.make_async_copy(src, dst.at[p.t], tsend.at[i, 3]).wait()

    wait_peers(2, gbuf, gall)
    gain_out[0:1, :] = gain_row(gall, n, 0, width)
    gain_out[1:2, :] = gain_row(gall, n, 1, width)
    gain_out[2:8, :] = jnp.zeros((6, width), F32)

    wait_peers(0, tokens, tok)

    own = OWN[0]
    mine = perm[pl.ds(pl.multiple_of(p.t * own, own), own), :]
    saved[0]["hidden"][...] = dot(mine, tok[...].reshape(T * own, width), NN)

    @pl.loop(0, T)
    def _(owner):
        picked = perm[pl.ds(pl.multiple_of(owner * own, own), own), :]
        hidden = dot(picked, tok[...].reshape(T * own, width), NN)
        inverse = lax.rsqrt(mean_square(hidden) + 1e-05)
        saved[0]["normed"][owner] = (hidden * inverse * gain_out[0:1, :]).astype(BF)

    wait_peers(1, cotangent, cot)
    cown[...] = dot(mine, cot[...].reshape(T * own, width), NN)
    write(cown, cot_own)

    line.own(down_piece)
    line.own(down_last)

    @pl.loop(0, T)
    def _(owner):
        picked = perm[pl.ds(pl.multiple_of(owner * OWN[0], 32), OWN[RECUR - 1]), :]
        cot_all[owner] = dot(picked, cot[...].reshape(T * OWN[0], width), NN).astype(BF)

    line.arrive(heads_piece)

    for level in range(RECUR):
        own = OWN[level]
        count = T * own
        half = count // 2
        s = saved[level]
        if level:
            rows.gather_finish(2 * level - 1, s["normed"].reshape(2, 2, own, width))
        x = s["normed"][...].reshape(count, width)
        qkv = dot(x, w[:, QKV : QKV + 640], NN)
        cos = jnp.concatenate([cosine[owner * OWN[0] : owner * OWN[0] + own, :] for owner in range(T)], axis=0)
        sin = jnp.concatenate([sine[owner * OWN[0] : owner * OWN[0] + own, :] for owner in range(T)], axis=0)
        tiles = []
        for j in range(5):
            tile = qkv[:, j * 128 : (j + 1) * 128]
            turned = tile * cos + swap_halves(tile) * sin
            if j == 4:
                lane = lax.broadcasted_iota(jnp.int32, tile.shape, 1)
                turned = jnp.where(lane < HS, turned, tile)
            tiles.append(turned)
        rotated = jnp.concatenate(tiles, axis=1)
        s["qkv"][...] = rotated.astype(BF)
        write(s["qkv"], saved_out[level]["qkv"])
        heads = []
        for b, block in enumerate(split_batches(rotated, own)):
            query, key, value = (
                block[:, 0:512].astype(BF),
                block[:, 512:576].astype(BF),
                block[:, 576:640].astype(BF),
            )
            _, shares = attention_shares(query, key, allowed[level][b])
            out = dot(shares.astype(BF).reshape(8 * half, half), value, NN)
            heads.append(unstack_heads(out, half))
            if level == 0:
                line.step(gate_piece, 1) if b == 0 else [line.step(gate_piece, k) for k in range(2, p.line)]
        s["att"][...] = join_batches(heads, own).astype(BF)
        write(s["att"], saved_out[level]["att"])
        if level == 0:
            line.arrive(out_piece)
        present = act_own[level, 0:own, :]

        def attention_tile(cols):
            return dot(s["att"][...], w[cols, WO : WO + 512], NT)

        def attention_finish(cols, total):
            s["first"][:, cols] = s["hidden"][:, cols] + present * total

        rows.reduce(2 * level, own, attention_tile, attention_finish)
        first = s["first"][...]
        inverse = lax.rsqrt(mean_square(first) + 1e-05)
        s["mixed"][p.t] = (first * inverse * gain_out[1:2, :]).astype(BF)
        mixed = s["mixed"].reshape(2, 2, own, width)
        rows.gather_start(2 * level, mixed)
        write(s["first"], saved_out[level]["first"])
        if level == 0:
            line.steps(up_piece)
            line.own(down_last + 1)
        rows.gather_finish(2 * level, mixed)
        write(s["mixed"], saved_out[level]["mixed"])

        def hidden_block(start, size):
            x = s["mixed"][...].reshape(count, width)
            gate = dot(x, w[:, pl.ds(pl.multiple_of(GU + start, 128), size)], NN)
            upward = dot(x, w[:, pl.ds(pl.multiple_of(GU + hidden_cols + start, 128), size)], NN)
            cols = pl.ds(pl.multiple_of(start, 128), size)
            s["gu"][:, cols] = gate.astype(BF)
            s["gu"][:, pl.ds(pl.multiple_of(hidden_cols + start, 128), size)] = upward.astype(BF)
            s["prod"][:, cols] = (gate * jax.nn.sigmoid(gate) * upward).astype(BF)

        if level == 0:
            line.steps(down_piece)
            line.step(down_last, 1)
            line.step(down_last + 1, 1)
            line.arrive(gate_piece)
            line.arrive(up_piece)

        @pl.loop(0, hidden_cols // 256)
        def _(j):
            hidden_block(j * 256, 256)

        if hidden_cols % 256:
            hidden_block(hidden_cols // 256 * 256, 128)
        write(s["gu"], saved_out[level]["gu"])
        write(s["prod"], saved_out[level]["prod"])
        if level == 0:
            for k in range(2, p.line):
                line.step(down_last, k)
                line.step(down_last + 1, k)
            line.arrive(down_piece)
            write(w, w_out)

        if level < RECUR - 1:

            def mlp_tile(cols):
                return dot(s["prod"][...], w[cols, WD : WD + 1408], NT)

            def mlp_finish(cols, total):
                after[0:own, cols] = s["first"][:, cols] + present * total

            rows.reduce(2 * level + 1, own, mlp_tile, mlp_finish)
            deeper = OWN[level + 1]
            hidden = after[0:deeper, :]
            saved[level + 1]["hidden"][...] = hidden
            inverse = lax.rsqrt(mean_square(hidden) + 1e-05)
            saved[level + 1]["normed"][p.t] = (hidden * inverse * gain_out[0:1, :]).astype(BF)
            rows.gather_start(2 * level + 1, saved[level + 1]["normed"].reshape(2, 2, deeper, width))
            fin[deeper:own, :] = after[deeper:own, :].astype(BF)

        write(s["hidden"], saved_out[level]["hidden"])
        write(s["normed"], saved_out[level]["normed"])
    fin[0 : OWN[2], :] = jnp.zeros((OWN[2], width), BF)
    write(fin, fin_out)
    for i in range(len(pieces)):
        line.drain(i)
    for copy in writes:
        copy.wait()


def forward(n, tokens, depth, lengths, cotangent, weights, attn_gain, mlp_gain):
    width = tokens.shape[-1]
    hidden_cols = weights[4].shape[1]
    local = OWN[0] // MB
    total = T * OWN[0]
    ordered = depth.reshape(MB, T, local).transpose(1, 0, 2).astype(F32)
    freqs = jnp.asarray(np.tile(10000.0 ** (-np.arange(0, HS, 2) / HS), 4)[None].astype(np.float32))
    vmem = pl.BlockSpec(memory_space=pltpu.VMEM)
    hbm = pl.BlockSpec(memory_space=pl.ANY)

    def saved_shapes(own):
        count = T * own
        return {
            "normed": ((T, own, width), BF),
            "qkv": ((count, 640), BF),
            "att": ((count, 512), BF),
            "mixed": ((T, own, width), BF),
            "gu": ((count, 2 * hidden_cols), BF),
            "prod": ((count, hidden_cols), BF),
            "hidden": ((own, width), F32),
            "first": ((own, width), F32),
        }

    shapes = [((width, COLS), BF), ((8, width), F32), ((OWN[0], width), BF), ((OWN[0], width), F32), ((T, OWN[2], width), BF)]
    specs = [hbm, vmem, hbm, hbm, vmem]
    shapes += [((total, 128), F32)] * 2 + [((OWN[0], total), BF), ((RECUR, OWN[0], 1), F32), ((T * OWN[2], 1), F32)]
    shapes += [((MB, T * own // MB, T * own // MB), BF) for own in OWN]
    specs += [vmem] * (5 + RECUR)
    for own in OWN:
        for entry in saved_shapes(own).values():
            shapes.append(entry)
            specs.append(hbm)
    scratch = [pltpu.VMEM((width, COLS), BF)] + [pltpu.VMEM((total, total), BF)] * 2
    scratch += [pltpu.VMEM((2,) + weights[1].shape[::-1], BF), pltpu.VMEM(weights[3].shape, BF), pltpu.VMEM(weights[6].shape, BF)]
    scratch += [pltpu.VMEM((n, 8, 128), F32), pltpu.VMEM((T, n, 8, 128), F32)]
    scratch += [pltpu.VMEM((T,) + tokens.shape, BF)] * 2
    for own in OWN:
        scratch += [pltpu.VMEM(*entry) for entry in saved_shapes(own).values()]
    scratch += [pltpu.VMEM((OWN[0], width), F32), pltpu.VMEM((OWN[0], width), BF), pltpu.VMEM((OWN[0], width), F32)]
    scratch += [pltpu.VMEM((2, 2, OWN[0], width), BF), pltpu.VMEM((OWN[0], width), BF)]
    for own in OWN:
        for _ in range(2):
            scratch += [pltpu.VMEM((2, own, width), BF), pltpu.VMEM((own, width), BF)]
    dma = pltpu.SemaphoreType.DMA
    count = 1 + sum(2 if kind == "across" else 1 for kind, _, _ in RANGES)
    scratch += [dma((count, n // 2))] * 6
    chunks = width // DC
    scratch += [dma((2 * RECUR, chunks))] * 4 + [dma((2 * RECUR, 3))] * 2
    scratch += [dma((7,)), dma((3, 4)), dma((3, 3)), dma((40,))]
    outs = pl.pallas_call(
        functools.partial(forward_kernel, n),
        out_shape=[jax.ShapeDtypeStruct(*entry) for entry in shapes],
        in_specs=[hbm] * 9 + [vmem] * 6,
        out_specs=specs,
        scratch_shapes=scratch,
        compiler_params=pltpu.CompilerParams(
            collective_id=1, has_side_effects=True, vmem_limit_bytes=62 << 20
        ),
    )(
        tokens,
        cotangent,
        weights[0],
        weights[1].T,
        weights[2].T,
        *weights[3:],
        attn_gain[None],
        mlp_gain[None],
        ordered.reshape(1, total),
        ordered.reshape(total, 1),
        lengths,
        freqs,
    )
    w_all, gain, fin, cot_own, cot_all = outs[:5]
    tables = dict(zip(("cosine", "sine", "back", "act", "act_last"), outs[5:10]))
    tables["masks"] = outs[10:13]
    names = list(saved_shapes(1))
    saved = [dict(zip(names, outs[13 + 8 * level : 21 + 8 * level])) for level in range(RECUR)]
    return w_all, gain, fin, cot_own, cot_all, tables, saved


def share_groups(block, allowed):
    query, key = block[:, 0:512].astype(BF), block[:, 512:576].astype(BF)
    for start in range(0, 512, HEADS * HS):
        yield (start,) + attention_shares(query[:, start : start + HEADS * HS], key, allowed)


def attention_back(rotated, groups, attended_grad, cos, sin, own, between=None):
    half = T * own // 2
    grads = []
    upstream = split_batches(attended_grad, own)
    for b in range(MB):
        key, value = rotated[b][:, 512:576].astype(BF), rotated[b][:, 576:640].astype(BF)
        up_all = upstream[b].astype(BF)
        query_grads, key_grad, value_grad = [], 0.0, 0.0
        for start, stacked, shares in groups[b]:
            up = stack_heads(up_all[:, start : start + HEADS * HS])
            low = shares.astype(BF).reshape(HEADS * half, half)
            shares_grad = dot(up, value, NT).reshape(HEADS, half, half)
            value_grad += dot(low, up, TN)
            spread = jnp.sum(shares * shares_grad, axis=-1, keepdims=True)
            score_grad = (shares * (shares_grad - spread)).astype(BF).reshape(HEADS * half, half)
            query_grads.append(unstack_heads(dot(score_grad, key, NN), half) * SCALE)
            key_grad += dot(score_grad, stacked, TN) * SCALE
        query_grad = jnp.concatenate(query_grads, axis=1)
        grads.append(jnp.concatenate([query_grad, key_grad, value_grad], axis=1))
        if between is not None:
            between()
    joined = join_batches(grads, own)
    tiles = []
    for j in range(5):
        tile = joined[:, j * 128 : (j + 1) * 128]
        turned = tile * cos - swap_halves(tile) * sin
        if j == 4:
            lane = lax.broadcasted_iota(jnp.int32, tile.shape, 1)
            turned = jnp.where(lane < HS, turned, tile)
        tiles.append(turned)
    return jnp.concatenate(tiles, axis=1)


def level_rows(table, own):
    return jnp.concatenate([table[owner * OWN[0] : owner * OWN[0] + own, :] for owner in range(T)], axis=0)


def norm_back(source, gain, upstream):
    inverse = lax.rsqrt(mean_square(source) + 1e-05)
    unit = source * inverse
    gain_part = jnp.sum(upstream * unit, axis=0, keepdims=True)
    scaled = upstream * gain
    return inverse * (scaled - unit * jnp.mean(scaled * unit, axis=-1, keepdims=True)), gain_part


def backward_kernel(n, *refs):
    it = iter(refs)
    (w_all, gain, cot_own, cot_all, cosine, sine, act_own, act_last) = [next(it) for _ in range(8)]
    allowed = [None] + [next(it) for _ in range(2)]
    saved_in = []
    for level in range(RECUR):
        names = ("gu", "first") if level == 0 else ("gu", "first", "qkv", "hidden")
        saved_in.append({k: next(it) for k in names})
    dg_out = [next(it) for _ in range(3)]
    gug_out = [next(it) for _ in range(3)]
    og_out = [None] + [next(it) for _ in range(2)]
    qkvg_out = [None] + [next(it) for _ in range(2)]
    grad_out, gain_part = next(it), next(it)
    w = next(it)
    saved = []
    for level in range(RECUR):
        saved.append({k: next(it) for k in saved_in[level]})
    dg = [next(it) for _ in range(3)]
    gug = [next(it) for _ in range(3)]
    og = [None] + [next(it) for _ in range(2)]
    qkvg = [None] + [next(it) for _ in range(2)]
    grad, upstream, factors = next(it), next(it), next(it)
    part, relay = next(it), next(it)
    sums = [(next(it), next(it)) for _ in range(5)]
    row_sems = [next(it) for _ in range(6)]
    insem, outsem = next(it), next(it)

    p = Place(n)
    width = w.shape[0]
    rows = Rows(p, part, relay, sums, row_sems)
    hidden_cols = (COLS - GU) // 3
    loads, writes = {}, []

    def load(name, src, dst):
        copy = pltpu.make_async_copy(src, dst, insem.at[len(loads)])
        copy.start()
        loads[name] = copy

    def write(src, dst):
        copy = pltpu.make_async_copy(src, dst, outsem.at[len(writes)])
        copy.start()
        writes.append(copy)

    def columns(start, size):
        load(("w", start), w_all.at[:, pl.ds(start, size)], w.at[:, pl.ds(start, size)])

    columns(WD, hidden_cols)
    load("grad", cot_own, grad)
    last = RECUR - 1
    load(("gu", last), saved_in[last]["gu"], saved[last]["gu"])
    columns(GU, 2 * hidden_cols)
    load(("first", last), saved_in[last]["first"], saved[last]["first"])
    columns(WO, 512)
    for name in ("qkv", "hidden"):
        load((name, last), saved_in[last][name], saved[last][name])
    columns(QKV, 640)
    for level in (1, 0):
        for name in saved_in[level]:
            load((name, level), saved_in[level][name], saved[level][name])
    p.barrier(False)
    gain_part[...] = jnp.zeros_like(gain_part)

    for level in range(last, -1, -1):
        own = OWN[level]
        count = T * own
        s = saved[level]
        base = 2 * (last - level)
        present = act_own[level, 0:own, :]
        if level == last:
            dg[level][...] = (cot_all[...].astype(F32).reshape(count, width) * act_last[...]).astype(BF).reshape(
                T, own, width
            )
            loads["grad"].wait()
        else:
            dg[level][p.t] = (present * grad[0:own, :]).astype(BF)
            view = dg[level].reshape(2, 2, own, width)
            rows.gather_start(base, view)
        loads["gu", level].wait()

        @pl.loop(0, hidden_cols // 128)
        def _(j):
            low = pl.ds(pl.multiple_of(j * 128, 128), 128)
            high = pl.ds(pl.multiple_of(hidden_cols + j * 128, 128), 128)
            gate = s["gu"][:, low].astype(F32)
            upward = s["gu"][:, high].astype(F32)
            sigma = jax.nn.sigmoid(gate)
            factors[0:count, low] = upward * sigma * (1.0 + gate * (1.0 - sigma))
            factors[0:count, high] = gate * sigma

        if level == last:
            loads["w", WD].wait()
        else:
            rows.gather_finish(base, view)
        write(dg[level], dg_out[level])

        def hidden_block(start, size):
            wcols = pl.ds(pl.multiple_of(WD + start, 128), size)
            product_grad = dot(dg[level][...].reshape(count, width), w[:, wcols], NN)
            low = pl.ds(pl.multiple_of(start, 128), size)
            high = pl.ds(pl.multiple_of(hidden_cols + start, 128), size)
            gug[level][:, low] = (product_grad * factors[0:count, low]).astype(BF)
            gug[level][:, high] = (product_grad * factors[0:count, high]).astype(BF)

        @pl.loop(0, hidden_cols // 256)
        def _(j):
            hidden_block(j * 256, 256)

        if hidden_cols % 256:
            hidden_block(hidden_cols // 256 * 256, 128)
        write(gug[level], gug_out[level])
        if level == last:
            loads["w", GU].wait()

        def mlp_tile(cols):
            return dot(gug[level][...], w[cols, GU : GU + 2 * hidden_cols], NT)

        def take(cols, total):
            upstream[0:own, cols] = total

        rows.reduce(base, own, mlp_tile, take)
        loads["first", level].wait()
        update, add = norm_back(s["first"][...], gain[1:2, :], upstream[0:own, :])
        grad[0:own, :] += update
        gain_part[1:2, :] += add
        if level == 0:
            break
        og[level][p.t] = (present * grad[0:own, :]).astype(BF)
        view = og[level].reshape(2, 2, own, width)
        rows.gather_start(base + 1, view)
        loads["qkv", level].wait()
        rotated = split_batches(s["qkv"][...].astype(F32), own)
        groups = [list(share_groups(rotated[b], allowed[level][b])) for b in range(MB)]
        rows.gather_finish(base + 1, view)
        write(og[level], og_out[level])
        if level == last:
            loads["w", WO].wait()
        attended_grad = dot(og[level][...].reshape(count, width), w[:, WO : WO + 512], NN)
        cos, sin = level_rows(cosine, own), level_rows(sine, own)
        qkvg[level][...] = attention_back(rotated, groups, attended_grad, cos, sin, own).astype(BF)
        write(qkvg[level], qkvg_out[level])
        if level == last:
            loads["w", QKV].wait()

        def attention_tile(cols):
            return dot(qkvg[level][...], w[cols, QKV : QKV + 640], NT)

        rows.reduce(base + 1, own, attention_tile, take)
        loads["hidden", level].wait()
        update, add = norm_back(s["hidden"][...], gain[0:1, :], upstream[0:own, :])
        grad[0:own, :] += update
        gain_part[0:1, :] += add

    write(grad, grad_out)
    for copy in writes:
        copy.wait()


def backward(n, w_all, gain, cot_own, cot_all, tables, saved):
    width = w_all.shape[0]
    hidden_cols = (COLS - GU) // 3
    vmem = pl.BlockSpec(memory_space=pltpu.VMEM)
    hbm = pl.BlockSpec(memory_space=pl.ANY)
    operands = [w_all, gain, cot_own, cot_all, tables["cosine"], tables["sine"], tables["act"], tables["act_last"]]
    operands += list(tables["masks"][1:])
    specs = [hbm, vmem, hbm] + [vmem] * 7
    used = []
    for level in range(RECUR):
        for name in ("gu", "first") if level == 0 else ("gu", "first", "qkv", "hidden"):
            operands.append(saved[level][name])
            specs.append(hbm)
            used.append(saved[level][name])
    outs = [((T, own, width), BF) for own in OWN]
    outs += [((T * own, 2 * hidden_cols), BF) for own in OWN]
    outs += [((T, own, width), BF) for own in OWN[1:]]
    outs += [((T * own, 640), BF) for own in OWN[1:]]
    scratch = [pltpu.VMEM(w_all.shape, BF)] + [pltpu.VMEM(u.shape, u.dtype) for u in used]
    scratch += [pltpu.VMEM(*entry) for entry in outs]
    outs += [((OWN[0], width), F32), ((8, width), F32)]
    out_specs = [hbm] * (len(outs) - 1) + [vmem]
    scratch += [pltpu.VMEM((OWN[0], width), F32)] * 2 + [pltpu.VMEM((T * OWN[0], 2 * hidden_cols), F32)]
    scratch += [pltpu.VMEM((2, 2, OWN[0], width), BF), pltpu.VMEM((OWN[0], width), BF)]
    for own in (OWN[2], OWN[2], OWN[1], OWN[1], OWN[0]):
        scratch += [pltpu.VMEM((2, own, width), BF), pltpu.VMEM((own, width), BF)]
    dma = pltpu.SemaphoreType.DMA
    chunks = width // DC
    scratch += [dma((5, chunks))] * 4 + [dma((5, 3))] * 2 + [dma((24,)), dma((16,))]
    res = pl.pallas_call(
        functools.partial(backward_kernel, n),
        out_shape=[jax.ShapeDtypeStruct(*entry) for entry in outs],
        in_specs=specs,
        out_specs=out_specs,
        scratch_shapes=scratch,
        compiler_params=pltpu.CompilerParams(
            collective_id=2, has_side_effects=True, vmem_limit_bytes=62 << 20
        ),
    )(*operands)
    return {
        "dg": res[0:3],
        "gug": res[3:6],
        "og": res[6:8],
        "qkvg": res[8:10],
        "grad": res[10],
        "gain_part": res[11],
    }


PIECE = 384
SEGMENTS = (("down", 1408), ("gu", 2816), ("out", 512), ("qkv", 640))
DEPTH = 3
FIRST = 1
JOINT = 2
PLACES = COLS // PIECE + FIRST


def cut_pieces():
    pieces = [[] for _ in range(COLS // PIECE)]
    at = 0
    for which, size in SEGMENTS:
        done = 0
        while done < size:
            k, inside = divmod(at, PIECE)
            cols = min(size - done, PIECE - inside)
            pieces[k].append((which, done, cols, inside))
            done += cols
            at += cols
    return pieces


def gradient_kernel(n, *refs):
    it = iter(refs)
    (w_all, gain, cosine, sine, act_own, allowed, back) = [next(it) for _ in range(7)]
    grad_in, gain_in, fin_in, hidden_in, qkv_in, first_in = [next(it) for _ in range(6)]
    x_in = {name: [next(it) for _ in range(3)] for name in ("down", "gu", "qkv")}
    x_in["out"] = [None] + [next(it) for _ in range(2)]
    y_in = {name: [next(it) for _ in range(3)] for name in ("down", "gu", "out")}
    y_in["qkv"] = [None] + [next(it) for _ in range(2)]
    (act_out, tok_out, dq, dk, dv, dwo, dgate, dup, dwd, gain_sum) = [next(it) for _ in range(10)]
    og_hbm, fin_all, grad_all = [next(it) for _ in range(3)]
    w = next(it)
    y = {name: next(it) for name in ("down", "gu", "out", "qkv")}
    xm, xl, xraw = next(it), next(it), next(it)
    og, hidden, qkv, grad, upstream, gains = [next(it) for _ in range(6)]
    fin, first = next(it), next(it)
    gpeers = next(it)
    stage, landed, across, across_own = [next(it) for _ in range(4)]
    window_tmp = next(it)
    gmate_stage, gmate, gline, gline_own = [next(it) for _ in range(4)]
    final, turned, last_stage, last_landed, fsend, frecv = [next(it) for _ in range(6)]
    chunk_in, fin_chunk, act_chunk, tok_chunk = [next(it) for _ in range(4)]
    part, relay = next(it), next(it)
    sums = [(next(it), next(it))] * 2
    row_sems = [next(it) for _ in range(6)]
    msend, mrecv, lsend, lrecv, lrecv2 = [next(it) for _ in range(5)]
    tsend, trecv = next(it), next(it)
    insem, xsem, outsem, finsem, loadsem = [next(it) for _ in range(5)]

    p = Place(n)
    width = w.shape[0]
    line = p.line
    chunk_rows = width // n
    window = max(128, chunk_rows)
    rows = Rows(p, part, relay, sums, row_sems)
    own = OWN[0]
    count = T * own
    starts = [0, T * OWN[0], T * (OWN[0] + OWN[1])]
    total_rows = T * sum(OWN)
    hidden_cols = (COLS - GU) // 3
    loads, writes = {}, []

    def load(name, src, dst):
        copy = pltpu.make_async_copy(src, dst, insem.at[len(loads)])
        copy.start()
        loads[name] = copy

    def write(src, dst):
        copy = pltpu.make_async_copy(src, dst, outsem.at[len(writes)])
        copy.start()
        writes.append(copy)

    load("grad", grad_in, grad)
    for name in ("down", "gu"):
        for level in range(RECUR):
            load((name, level), y_in[name][level], y[name].at[pl.ds(starts[level], T * OWN[level])])
    load("w", w_all.at[:, pl.ds(0, GU)], w)
    load("fin", fin_in, fin)
    load("first", first_in, first)
    load("qkv", qkv_in, qkv)
    load("hidden", hidden_in, hidden)
    for level in range(RECUR):
        load(("out", level), y_in["out"][level], y["out"].at[pl.ds(starts[level], T * OWN[level])])
    for level in (1, 2):
        load(("qkv", level), y_in["qkv"][level], y["qkv"].at[pl.ds(starts[level], T * OWN[level])])
    p.barrier(True)

    def x_source(which, level):
        return og_hbm if which == "out" and level == 0 else x_in[which][level]

    def level_slice(level):
        return pl.ds(sum(OWN[:level]) * T, OWN[level] * T)

    def x_copy(which, chunk, slot, level, sem):
        start = pl.multiple_of(chunk * chunk_rows // window * window, window)
        src = x_source(which, level).reshape(T * OWN[level], width)
        return pltpu.make_async_copy(
            src.at[:, pl.ds(start, window)], xraw.at[slot, level_slice(level)], sem.at[slot, level]
        )

    pieces = cut_pieces()
    count_pieces = len(pieces)
    held = {}

    def x_load(which, parity, buffer, sem):
        if held.get(id(buffer)) == which:
            return
        held[id(buffer)] = which

        for level in range(RECUR):
            x_copy(which, parity, 0, level, sem).start()

        @pl.loop(0, line)
        def _(i):
            @pl.when(i + 1 < line)
            def _():
                for level in range(RECUR):
                    x_copy(which, 2 * (i + 1) + parity, lax.rem(i + 1, 2), level, sem).start()

            for level in range(RECUR):
                x_copy(which, 2 * i + parity, lax.rem(i, 2), level, sem).wait()
            buffer[i] = xraw[lax.rem(i, 2)].T

    def product(which, start, cols, parity, buffer, j):
        some = buffer[pl.ds(j * JOINT, JOINT)].reshape(JOINT * window, total_rows)
        value = dot(some, y[which][:, start : start + cols], NN).reshape(JOINT, window, cols)
        if window == chunk_rows:
            return value
        window_tmp[:, :, 0:cols] = value
        return window_tmp[:, pl.ds(pl.multiple_of(parity * chunk_rows, chunk_rows), chunk_rows), 0:cols]

    places = []
    for k in range(count_pieces):
        places += [("own", k), ("other", k)] if k < FIRST else [("normal", k)]

    def columns(q):
        return pl.ds(pl.multiple_of(q * PIECE, 128), PIECE)

    def mate_copy(q, i):
        return remote(
            stage.at[lax.rem(q, DEPTH), i], landed.at[i, :, columns(q)], msend.at[q, i], mrecv.at[q, i], p.mate
        )

    def mates(k):
        q = k + FIRST
        if q >= 2 * FIRST + DEPTH:

            @pl.loop(0, line)
            def _(i):
                mate_copy(q - DEPTH, i).wait_send()

        for number, (which, start, cols, inside) in enumerate(pieces[k]):
            x_load(which, 1 - p.b, xm, xsem.at[0])

            last_part = number == len(pieces[k]) - 1

            @pl.loop(0, line // JOINT)
            def _(j):
                value = product(which, start, cols, 1 - p.b, xm, j)
                some = pl.ds(j * JOINT, JOINT)
                stage[q % DEPTH, some, :, inside : inside + cols] = value.astype(BF)
                if last_part:
                    for i in range(JOINT):
                        mate_copy(q, j * JOINT + i).start()

    def own_terms(q):
        kind, k = places[q]
        for number, (which, start, cols, inside) in enumerate(pieces[k]):
            parity = 1 - p.b if kind == "other" else p.b
            buffer, sem = (xm, xsem.at[0]) if kind == "other" else (xl, xsem.at[1])
            x_load(which, parity, buffer, sem)
            at = pl.ds(q * PIECE + inside, cols)

            @pl.loop(0, line // JOINT)
            def _(j):
                value = product(which, start, cols, parity, buffer, j)
                some = pl.ds(j * JOINT, JOINT)
                if kind == "normal":
                    if number == 0:
                        for i in range(JOINT):
                            mate_copy(q, j * JOINT + i).wait_recv()
                    value = value + landed[some, :, at].astype(F32)
                landed[some, :, at] = value.astype(BF)

    def along(q, i, right):
        return remote(
            landed.at[i, :, columns(q)],
            across.at[i, :, columns(q)],
            lsend.at[q, i],
            lrecv.at[q, i],
            p.right if right else p.left,
        )

    def along_last(q, i):
        return remote(
            landed.at[i, :, columns(q)], across_own.at[:, columns(q)], lsend.at[q, i], lrecv2.at[q], p.left
        )

    def relay_step(q, i, receives):
        @pl.when(receives)
        def _():
            along(q, i, True).wait_recv()
            landed[i, :, columns(q)] = (
                landed[i, :, columns(q)].astype(F32) + across[i, :, columns(q)].astype(F32)
            ).astype(BF)

    def relay_pieces(slot):
        q_right = slot - p.a
        q_left = slot - (line - 1 - p.a)

        @pl.when((q_right >= 0) & (q_right < PLACES))
        def _():
            @pl.loop(0, line)
            def _(step):
                i = line - 1 - step

                @pl.when(i > p.a)
                def _():
                    relay_step(q_right, i, p.has_left)
                    along(q_right, i, True).start()

        @pl.when((q_left >= 0) & (q_left < PLACES))
        def _():
            @pl.loop(0, line)
            def _(i):
                @pl.when(i < p.a)
                def _():
                    relay_step(q_left, i, p.has_right)
                    pl.when(i < p.a - 1)(lambda: along(q_left, i, False).start())
                    pl.when(i == p.a - 1)(lambda: along_last(q_left, i).start())

    def last_copy(j):
        return remote(last_stage.at[j], last_landed.at[j], fsend.at[j], frecv.at[j], p.mate)

    staged, turning = [], []

    def line_sum(q, buffer):
        here = pl.ds(q * PIECE, PIECE)
        buffer[...] = landed[p.a, :, here].astype(F32)

        @pl.when(p.has_left)
        def _():
            along(q, p.a, True).wait_recv()
            buffer[...] += across[p.a, :, here].astype(F32)

        @pl.when(p.has_right)
        def _():
            along_last(q, p.a).wait_recv()
            buffer[...] += across_own[:, here].astype(F32)

    def finish(q):
        kind, k = places[q]
        if kind == "own":
            return
        if kind == "other":
            if len(staged) >= 2:
                for copy in staged[len(staged) - 2]:
                    copy.wait()
                staged[len(staged) - 2] = []
            buffer = final.at[len(staged) % 2]
            line_sum(q, buffer)
            last_stage[k] = buffer[...].astype(BF)
            last_copy(k).start()
        else:
            results(q)
        if q >= 3 and places[q - 3][0] == "own":
            results(q - 3)

    def results(q):
        kind, k = places[q]
        number = len(staged)
        if number >= 2:
            for copy in staged[number - 2]:
                copy.wait()
        buffer = final.at[number % 2]
        line_sum(q, buffer)
        if kind == "own":
            last_copy(k).wait_recv()
            buffer[...] += last_landed[k].astype(F32)
            last_copy(k).wait_send()
        copies = []

        def out(src, dst):
            copy = pltpu.make_async_copy(src, dst, finsem.at[k, len(copies)])
            copy.start()
            copies.append(copy)

        for which, start, cols, inside in pieces[k]:
            if which in ("down", "out"):
                for copy in turning:
                    copy.wait()
                turning.clear()
                turned[inside : inside + cols, :] = buffer[:, inside : inside + cols].T
                target = dwd if which == "down" else dwo
                copy = pltpu.make_async_copy(
                    turned.at[pl.ds(inside, cols)], target.at[pl.ds(start, cols)], finsem.at[k, 7]
                )
                copy.start()
                turning.append(copy)
            elif which == "gu":
                middle = min(max(hidden_cols - start, 0), cols)
                if middle:
                    out(buffer.at[:, pl.ds(inside, middle)], dgate.at[:, pl.ds(start, middle)])
                if middle < cols:
                    out(
                        buffer.at[:, pl.ds(inside + middle, cols - middle)],
                        dup.at[:, pl.ds(start + middle - hidden_cols, cols - middle)],
                    )
            else:
                queries = min(max(512 - start, 0), cols)
                if queries:
                    out(buffer.at[:, pl.ds(inside, queries)], dq.at[:, pl.ds(start, queries)])
                if queries < cols:
                    both = buffer[:, inside + queries : inside + queries + 2 * HS].T
                    dk[...] = both[0:HS]
                    dv[...] = both[HS : 2 * HS]
        staged.append(copies)

    def drain():
        @pl.loop(0, PLACES)
        def _(q):
            @pl.loop(0, line)
            def _(i):
                pl.when(q >= max(PLACES - DEPTH, 2 * FIRST))(lambda: mate_copy(q, i).wait_send())
                pl.when(i != p.a)(lambda: along(q, i, True).wait_send())

    loads["grad"].wait()
    present = act_own[0, 0:own, :]
    og[p.t] = (present * grad[...]).astype(BF)
    view = og.reshape(2, 2, own, width)
    rows.gather_start(0, view)
    for level in range(RECUR):
        loads["down", level].wait()
    sent = [FIRST]

    def mates_upto(k):
        while sent[0] <= min(k, count_pieces - 1):
            mates(sent[0])
            sent[0] += 1

    slots = [0]

    def slot():
        s = slots[0]
        slots[0] += 1
        if s < PLACES:
            own_terms(s)
        relay_pieces(s)
        if 0 <= s - line + 1 < PLACES:
            finish(s - line + 1)
        mates_upto(s - FIRST + DEPTH)

    mates(FIRST)
    sent[0] += 1
    slot()
    rows.gather_finish(0, view)
    write(og, og_hbm)
    for level in range(RECUR):
        loads["gu", level].wait()
    mates_upto(FIRST + 2)
    loads["w"].wait()
    loads["qkv"].wait()
    attended_grad = dot(og[...].reshape(count, width), w[:, WO : WO + 512], NN)
    rotated = split_batches(qkv[...].astype(F32), own)
    groups = [share_groups(rotated[b], allowed[b]) for b in range(MB)]
    y["qkv"][0:count, :] = attention_back(
        rotated, groups, attended_grad, cosine[...], sine[...], own, slot
    ).astype(BF)
    slot()

    def attention_tile(cols):
        return dot(y["qkv"][0:count, :], w[cols, QKV : QKV + 640], NT)

    def take(cols, total):
        upstream[:, cols] = total

    rows.reduce(0, own, attention_tile, take)
    loads["hidden"].wait()
    update, add = norm_back(hidden[...], gain[0:1, :], upstream[...])
    grad[...] += update
    gains[...] = gain_in[...]
    gains[0:1, :] += add
    for which in range(3):
        peers_copy(p, grad, grad_all, tsend.at[1], trecv.at[1], which).start()
        peers_copy(p, gains, gpeers, tsend.at[2], trecv.at[2], which).start()
    pltpu.make_async_copy(grad, grad_all.at[p.t], tsend.at[1, 3]).start()
    gpeers[p.t] = gains[...]
    for level in range(RECUR):
        loads["out", level].wait()
    for level in (1, 2):
        loads["qkv", level].wait()
    for copy in writes:
        copy.wait()

    def wait_peers(i, src, dst, local=True):
        for which in range(3):
            copy = peers_copy(p, src, dst, tsend.at[i], trecv.at[i], which)
            copy.wait_recv()
            copy.wait_send()
        if local:
            pltpu.make_async_copy(src, dst.at[p.t], tsend.at[i, 3]).wait()

    def last_branch():
        wait_peers(1, grad, grad_all)
        loads["fin"].wait()
        loads["first"].wait()
        deepest = OWN[2]
        active = act_own[RECUR - 1, 0:deepest, :]

        def fetch(src, dst, i):
            return pltpu.make_async_copy(src, dst, loadsem.at[i])

        def last_tile(cols):
            some = pl.ds(cols.start, DC)
            copies = (
                fetch(w_all.at[some, pl.ds(WD, GU)], w.at[pl.ds(0, DC)], 0),
                fetch(
                    w_all.at[some, pl.ds(WD + GU, hidden_cols - GU)],
                    w.at[pl.ds(DC, DC), pl.ds(0, hidden_cols - GU)],
                    1,
                ),
            )
            for copy in copies:
                copy.start()
            for copy in copies:
                copy.wait()
            left = y["down"][starts[2] : starts[2] + T * deepest, :]
            return dot(left[:, 0:GU], w[0:DC, :], NT) + dot(left[:, GU:], w[DC : 2 * DC, 0 : hidden_cols - GU], NT)

        def last_finish(cols, total):
            fin[0:deepest, cols] = (first[:, cols] + active * total).astype(BF)

        rows.reduce(1, deepest, last_tile, last_finish)
        for which in range(3):
            peers_copy(p, fin, fin_all, tsend.at[0], trecv.at[0], which).start()
        pltpu.make_async_copy(fin, fin_all.at[p.t], tsend.at[0, 3]).start()

    def outputs():
        wait_peers(0, fin, fin_all)
        mine = back[...]

        @pl.loop(0, width // OC)
        def _(c):
            cols = pl.ds(pl.multiple_of(c * OC, OC), OC)
            first = pltpu.make_async_copy(fin_all.at[:, :, cols], fin_chunk, loadsem.at[0])
            second = pltpu.make_async_copy(grad_all.at[:, :, cols], chunk_in, loadsem.at[1])
            first.start()
            second.start()
            first.wait()
            second.wait()
            act_chunk[...] = dot(mine, fin_chunk[...].reshape(count, OC), NN).astype(BF).reshape(
                MB, own // MB, OC
            )
            value = chunk_in[...].reshape(count, OC)
            high = value.astype(BF)
            rest = value - high.astype(F32)
            middle = rest.astype(BF)
            low = (rest - middle.astype(F32)).astype(BF)
            total = dot(mine, high, NN) + (dot(mine, middle, NN) + dot(mine, low, NN))
            tok_chunk[...] = total.reshape(MB, own // MB, OC)
            third = pltpu.make_async_copy(act_chunk, act_out.at[:, :, cols], loadsem.at[0])
            fourth = pltpu.make_async_copy(tok_chunk, tok_out.at[:, :, cols], loadsem.at[1])
            third.start()
            fourth.start()
            third.wait()
            fourth.wait()

    def gain_tile(chunk):
        start = pl.multiple_of(chunk * chunk_rows // window * window, window)
        return (
            gpeers[0, :, pl.ds(start, window)]
            + gpeers[1, :, pl.ds(start, window)]
            + gpeers[2, :, pl.ds(start, window)]
            + gpeers[3, :, pl.ds(start, window)]
        )

    last = PLACES

    def gain_mate(i):
        return remote(gmate_stage.at[i], gmate.at[i], msend.at[last, i], mrecv.at[last, i], p.mate)

    def gain_along(i, right):
        return remote(
            gmate.at[i], gline.at[i], lsend.at[last, i], lrecv.at[last, i], p.right if right else p.left
        )

    def gain_last(i):
        return remote(gmate.at[i], gline_own, lsend.at[last, i], lrecv2.at[last], p.left)

    def gain_mates():
        wait_peers(2, gains, gpeers, False)

        @pl.loop(0, line)
        def _(i):
            gmate_stage[i] = gain_tile(2 * i + 1 - p.b)
            gain_mate(i).start()

    def gain_lines():
        @pl.loop(0, line)
        def _(step):
            odd = lax.rem(step, 2)
            i = jnp.where(odd == 1, step // 2, line - 1 - step // 2)

            @pl.when(i != p.a)
            def _():
                gain_mate(i).wait_recv()
                gmate[i] += gain_tile(2 * i + p.b)

                @pl.when(((i > p.a) & p.has_left) | ((i < p.a) & p.has_right))
                def _():
                    gain_along(i, True).wait_recv()
                    gmate[i] += gline[i]

                pl.when(i > p.a)(lambda: gain_along(i, True).start())
                pl.when(i < p.a - 1)(lambda: gain_along(i, False).start())
                pl.when(i == p.a - 1)(lambda: gain_last(i).start())

        gain_mate(p.a).wait_recv()
        gain_sum[...] = gain_tile(2 * p.a + p.b) + gmate[p.a]

        @pl.when(p.has_left)
        def _():
            gain_along(p.a, True).wait_recv()
            gain_sum[...] += gline[p.a]

        @pl.when(p.has_right)
        def _():
            gain_last(p.a).wait_recv()
            gain_sum[...] += gline_own[...]

        @pl.loop(0, line)
        def _(i):
            gain_mate(i).wait_send()
            pl.when(i != p.a)(lambda: gain_along(i, True).wait_send())

    for s in range(slots[0], PLACES + line - 1):
        slot()
        if s == 5:
            gain_mates()
        if s == 7:
            gain_lines()
        if s == 9:
            last_branch()
        if s == 11:
            outputs()
    drain()
    for copies in staged[-2:] + [turning]:
        for copy in copies:
            copy.wait()


def gradients(n, w_all, gain, tables, saved, bwd, fin):
    width = w_all.shape[0]
    hidden_cols = (COLS - GU) // 3
    line = n // 2
    chunk_rows = width // n
    window = max(128, chunk_rows)
    vmem = pl.BlockSpec(memory_space=pltpu.VMEM)
    hbm = pl.BlockSpec(memory_space=pl.ANY)
    total_rows = T * sum(OWN)
    own = OWN[0]
    operands = [w_all, gain, tables["cosine"], tables["sine"], tables["act"], tables["masks"][0], tables["back"]]
    specs = [hbm] + [vmem] * 6
    operands += [bwd["grad"], bwd["gain_part"], fin, saved[0]["hidden"], saved[0]["qkv"], saved[RECUR - 1]["first"]]
    specs += [hbm, vmem, hbm, hbm, hbm, hbm]
    streams = list(bwd["dg"]) + [s["mixed"] for s in saved] + [s["normed"] for s in saved] + list(bwd["og"])
    streams += [s["prod"] for s in saved] + list(bwd["gug"]) + [s["att"] for s in saved] + list(bwd["qkvg"])
    operands += streams
    specs += [hbm] * len(streams)
    outs = [
        ((MB, own // MB, width), BF),
        ((MB, own // MB, width), F32),
        ((chunk_rows, 512), F32),
        ((HS, chunk_rows), F32),
        ((HS, chunk_rows), F32),
        ((512, chunk_rows), F32),
        ((chunk_rows, hidden_cols), F32),
        ((chunk_rows, hidden_cols), F32),
        ((hidden_cols, chunk_rows), F32),
        ((8, window), F32),
        ((T, own, width), BF),
        ((T, own, width), BF),
        ((T, own, width), F32),
    ]
    out_specs = [hbm, hbm, hbm, vmem, vmem, hbm, hbm, hbm, hbm, vmem, hbm, hbm, hbm]
    scratch = [pltpu.VMEM((width, GU), BF)]
    scratch += [pltpu.VMEM((total_rows, c), BF) for c in (hidden_cols, 2 * hidden_cols, 512, 640)]
    scratch += [pltpu.VMEM((line, window, total_rows), BF)] * 2 + [pltpu.VMEM((2, total_rows, window), BF)]
    scratch += [
        pltpu.VMEM((T, own, width), BF),
        pltpu.VMEM((own, width), F32),
        pltpu.VMEM((T * own, 640), BF),
        pltpu.VMEM((own, width), F32),
        pltpu.VMEM((own, width), F32),
        pltpu.VMEM((8, width), F32),
        pltpu.VMEM((own, width), BF),
        pltpu.VMEM((OWN[2], width), F32),
        pltpu.VMEM((T, 8, width), F32),
    ]
    scratch += [
        pltpu.VMEM((DEPTH, line, chunk_rows, PIECE), BF),
        pltpu.VMEM((line, chunk_rows, PLACES * PIECE), BF),
        pltpu.VMEM((line, chunk_rows, PLACES * PIECE), BF),
        pltpu.VMEM((chunk_rows, PLACES * PIECE), BF),
        pltpu.VMEM((JOINT, window, PIECE) if window > chunk_rows else (1, 8, 128), F32),
    ]
    scratch += [pltpu.VMEM((line, 8, window), F32)] * 3 + [pltpu.VMEM((8, window), F32)]
    scratch += [pltpu.VMEM((2, chunk_rows, PIECE), F32), pltpu.VMEM((PIECE, chunk_rows), F32)]
    scratch += [pltpu.VMEM((FIRST, chunk_rows, PIECE), BF)] * 2
    scratch += [pltpu.SemaphoreType.DMA((FIRST,))] * 2
    scratch += [pltpu.VMEM((T, own, OC), F32), pltpu.VMEM((T, own, OC), BF)]
    scratch += [pltpu.VMEM((MB, own // MB, OC), BF), pltpu.VMEM((MB, own // MB, OC), F32)]
    scratch += [pltpu.VMEM((2, 2, own, width), BF), pltpu.VMEM((own, width), BF)]
    scratch += [pltpu.VMEM((2, own, width), BF), pltpu.VMEM((own, width), BF)]
    dma = pltpu.SemaphoreType.DMA
    chunks = width // DC
    k = PLACES + 1
    scratch += [dma((2, chunks))] * 4 + [dma((2, 3))] * 2
    scratch += [dma((k, line))] * 4 + [dma((k,))]
    scratch += [dma((3, 4)), dma((3, 3))]
    scratch += [dma((24,)), dma((2, 2, RECUR)), dma((4,)), dma((k, 8)), dma((2,))]
    res = pl.pallas_call(
        functools.partial(gradient_kernel, n),
        out_shape=[jax.ShapeDtypeStruct(*entry) for entry in outs],
        in_specs=specs,
        out_specs=out_specs,
        scratch_shapes=scratch,
        compiler_params=pltpu.CompilerParams(
            collective_id=3, has_side_effects=True, vmem_limit_bytes=63 << 20
        ),
    )(*operands)
    return res


def hand_out_kernel(count, *refs):
    for i in range(count):
        refs[count + i][...] = refs[i][...]


def hand_out(values):
    vmem = pl.BlockSpec(memory_space=pltpu.VMEM)
    count = len(values)
    return pl.pallas_call(
        functools.partial(hand_out_kernel, count),
        out_shape=[jax.ShapeDtypeStruct(v.shape, v.dtype) for v in values],
        in_specs=[vmem] * count,
        out_specs=[vmem] * count,
        compiler_params=pltpu.CompilerParams(vmem_limit_bytes=40 << 20),
    )(*values)


def shards(n, *args):
    tokens, depth, lengths, cotangent = args[:4]
    attn_gain, mlp_gain = args[11:]
    index = lax.axis_index("tensor")
    w_all, gain, fin, cot_own, cot_all, tables, saved = forward(
        n, tokens, depth, lengths[:, 0], cotangent, args[4:11], attn_gain, mlp_gain
    )
    bwd = backward(n, w_all, gain, cot_own, cot_all, tables, saved)
    res = gradients(n, w_all, gain, tables, saved, bwd, fin)
    gain_sum = res[9]
    activations, tokens_grad, dq, dk, dv, dwo, dgate, dup, dwd = hand_out(res[:9])
    each = attn_gain.shape[0]
    window = gain_sum.shape[1]
    start = lax.rem((lax.axis_index("dp") * T + index) * each, window)
    both = lax.dynamic_slice_in_dim(gain_sum, start, each, axis=1)
    return (activations, tokens_grad, dq, dk.T, dv.T, dwo, dgate, dup, dwd, both[0], both[1])


def solution(mesh):
    rows = P(None, ("dp", "tensor"), None)
    weight_specs = (P("dp", "tensor"),) * 3 + (P("tensor", "dp"),) + (P("dp", "tensor"),) * 2 + (P("tensor", "dp"),)
    gain_specs = (P(("dp", "tensor")),) * 2
    return jax.shard_map(
        functools.partial(shards, mesh.shape["dp"]),
        mesh=mesh,
        in_specs=(rows, P(None, "dp"), P(None, "dp", None), rows) + weight_specs + gain_specs,
        out_specs=(rows, rows) + weight_specs + gain_specs,
        check_vma=False,
    )
```

```python
import functools

import jax
import jax.numpy as jnp
import numpy as np
from jax import lax
from jax.experimental import pallas as pl
from jax.experimental.pallas import tpu as pltpu
from jax.sharding import PartitionSpec as P

HQ = 32
KVH = 4
HS = 64
MB = 2
RECUR = 3
SCALE = HS ** (-0.5)
F32 = jnp.float32
BF = jnp.bfloat16
MESH = pl.DeviceIdType.MESH
NN = (((1,), (0,)), ((), ()))
NT = (((1,), (1,)), ((), ()))
TN = (((0,), (0,)), ((), ()))

OWN = (96, 80, 48)
PIECES = ((0, 24, 0), (24, 24, 1), (48, 16, 0), (64, 16, 1), (80, 8, 0), (88, 8, 1))
T = 4
DC = 512
OC = 256
HEADS = 2


def split_batches(values, own):
    halves = ([], [])
    for owner in range(T):
        for start, rows, b in PIECES:
            if start < own:
                halves[b].append(values[owner * own + start : owner * own + start + rows])
    return [jnp.concatenate(half, axis=0) for half in halves]


def join_batches(halves, own):
    rows_out, at = [], [0, 0]
    for owner in range(T):
        for start, rows, b in PIECES:
            if start < own:
                rows_out.append(halves[b][at[b] : at[b] + rows])
                at[b] += rows
    return jnp.concatenate(rows_out, axis=0)


def dot(left, right, dims):
    return lax.dot_general(left, right, dims, preferred_element_type=F32)


def swap_halves(tile):
    lane = lax.broadcasted_iota(jnp.int32, tile.shape, 1)
    return jnp.where((lane & 63) < 32, pltpu.roll(tile, 96, 1), pltpu.roll(tile, 32, 1))


def attention_shares(query, key, allowed):
    rows = query.shape[0]
    group = query.shape[1] // HS
    stacked = stack_heads(query)
    scores = dot(stacked, key, NT).reshape(group, rows, rows) * SCALE
    scores = jnp.where(allowed.astype(F32)[None] > 0, scores, -1e30)
    raised = jnp.exp(scores - jnp.max(scores, axis=-1, keepdims=True))
    return stacked, raised * (1.0 / jnp.sum(raised, axis=-1, keepdims=True))


def stack_heads(values):
    group = values.shape[1] // HS
    return jnp.concatenate([values[:, h * HS : (h + 1) * HS] for h in range(group)], axis=0)


def unstack_heads(values, rows):
    group = values.shape[0] // rows
    return jnp.concatenate([values[h * rows : (h + 1) * rows] for h in range(group)], axis=1)


def mean_square(values):
    return jnp.mean(values * values, axis=-1, keepdims=True)


class Place:
    def __init__(self, n):
        self.n = n
        self.line = n // 2
        self.dp = lax.axis_index("dp")
        self.t = lax.axis_index("tensor")
        self.a = self.dp // 2
        self.b = lax.rem(self.dp, 2)
        self.hi = self.t // 2
        self.lo = lax.rem(self.t, 2)
        self.has_right = self.a < self.line - 1
        self.has_left = self.a > 0
        self.mate = (self.a * 2 + 1 - self.b, self.t)
        self.right = (jnp.minimum(self.dp + 2, n - 1), self.t)
        self.left = (jnp.maximum(self.dp - 2, 0), self.t)
        self.near = (self.dp, self.hi * 2 + 1 - self.lo)
        self.far = (self.dp, (1 - self.hi) * 2 + self.lo)
        self.diag = (self.dp, (1 - self.hi) * 2 + 1 - self.lo)

    def barrier(self, along):
        sem = pltpu.get_barrier_semaphore()

        def greet(device):
            pl.semaphore_signal(sem, inc=1, device_id=device, device_id_type=MESH)

        for device in (self.near, self.far, self.diag):
            greet(device)
        expected = 3
        if along:
            greet(self.mate)
            pl.when(self.has_right)(lambda: greet(self.right))
            pl.when(self.has_left)(lambda: greet(self.left))
            expected = 4 + self.has_right.astype(jnp.int32) + self.has_left.astype(jnp.int32)
        pl.semaphore_wait(sem, expected)


def remote(src, dst, send, recv, device):
    return pltpu.make_async_remote_copy(
        src_ref=src, dst_ref=dst, send_sem=send, recv_sem=recv, device_id=device, device_id_type=MESH
    )


class LineGather:
    def __init__(self, place, pieces, sems):
        self.p = place
        self.pieces = pieces
        self.msend, self.mrecv, self.rsend, self.rrecv, self.lsend, self.lrecv = sems

    def toward_left(self, w, k, chunk):
        ref = self.pieces[w][1](chunk)
        return remote(ref, ref, self.lsend.at[w, k], self.lrecv.at[w, k], self.p.left)

    def toward_right(self, w, k, chunk):
        ref = self.pieces[w][1](chunk)
        return remote(ref, ref, self.rsend.at[w, k], self.rrecv.at[w, k], self.p.right)

    def toward_mate(self, w, k, chunk):
        ref = self.pieces[w][1](chunk)
        return remote(ref, ref, self.msend.at[w, k], self.mrecv.at[w, k], self.p.mate)

    def first(self, w):
        p = self.p
        return p.a * 2 + 1 - p.b if self.pieces[w][0] == "other" else p.dp

    def own(self, w):
        p = self.p
        kind = self.pieces[w][0]
        chunk = self.first(w)
        if kind == "other":
            self.toward_mate(w - 1, p.a, chunk).wait_recv()
        pl.when(p.has_left)(lambda: self.toward_left(w, 0, chunk).start())
        pl.when(p.has_right)(lambda: self.toward_right(w, 0, chunk).start())
        if kind != "other":
            self.toward_mate(w, p.a, chunk).start()

    def step(self, w, k):
        p = self.p
        normal = self.pieces[w][0] == "normal"

        @pl.when(p.a + k < p.line)
        def _():
            chunk = self.first(w) + 2 * k
            self.toward_left(w, k - 1, chunk).wait_recv()
            pl.when(p.has_left)(lambda: self.toward_left(w, k, chunk).start())
            if normal:
                self.toward_mate(w, p.a + k, chunk).start()

        @pl.when(p.a - k >= 0)
        def _():
            chunk = self.first(w) - 2 * k
            self.toward_right(w, k - 1, chunk).wait_recv()
            pl.when(p.has_right)(lambda: self.toward_right(w, k, chunk).start())
            if normal:
                self.toward_mate(w, p.a - k, chunk).start()

    def steps(self, w):
        for k in range(1, self.p.line):
            self.step(w, k)

    def arrive(self, w):
        p = self.p
        if self.pieces[w][0] == "normal":
            for i in range(p.line):
                self.toward_mate(w, i, 2 * i + 1 - p.b).wait_recv()

    def drain(self, w):
        p = self.p
        kind = self.pieces[w][0]
        if kind == "own":
            self.toward_mate(w, p.a, p.dp).wait_send()
        for i in range(p.line):
            if kind == "normal":
                self.toward_mate(w, i, p.dp).wait_send()
            pl.when(p.has_left & (p.a + i < p.line))(lambda: self.toward_left(w, i, p.dp).wait_send())
            pl.when(p.has_right & (p.a - i >= 0))(lambda: self.toward_right(w, i, p.dp).wait_send())


class Rows:
    def __init__(self, place, part, relay, sums, sems):
        self.p = place
        self.part, self.relay, self.sums = part, relay, sums
        self.s1, self.q1, self.s2, self.q2, self.gs, self.gr = sems

    def first_copy(self, i, own, c):
        p = self.p
        cols = pl.ds(pl.multiple_of(c * DC, DC), DC)
        return remote(
            self.part.at[:, 1 - p.lo, pl.ds(0, own), cols],
            self.sums[i][0].at[:, pl.ds(0, own), cols],
            self.s1.at[i, c],
            self.q1.at[i, c],
            p.near,
        )

    def second_copy(self, i, own, c):
        p = self.p
        cols = pl.ds(pl.multiple_of(c * DC, DC), DC)
        return remote(
            self.relay.at[pl.ds(0, own), cols],
            self.sums[i][1].at[pl.ds(0, own), cols],
            self.s2.at[i, c],
            self.q2.at[i, c],
            p.far,
        )

    def reduce(self, i, own, tile, finish):
        p = self.p
        part, relay = self.part, self.relay
        r1, r2 = self.sums[i]
        chunks = part.shape[-1] // DC

        def pass_on(c):
            cols = pl.ds(pl.multiple_of(c * DC, DC), DC)
            self.first_copy(i, own, c).wait_recv()
            mine = part[1 - p.hi, p.lo, 0:own, cols].astype(F32)
            relay[0:own, cols] = (mine + r1[1 - p.hi, 0:own, cols].astype(F32)).astype(BF)
            self.second_copy(i, own, c).start()

        @pl.loop(0, chunks)
        def _(c):
            cols = pl.ds(pl.multiple_of(c * DC, DC), DC)
            part[:, :, 0:own, cols] = tile(cols).astype(BF).reshape(2, 2, own, DC)
            self.first_copy(i, own, c).start()
            pl.when(c > 0)(lambda: pass_on(c - 1))

        pass_on(chunks - 1)

        @pl.loop(0, chunks)
        def _(c):
            cols = pl.ds(pl.multiple_of(c * DC, DC), DC)
            self.second_copy(i, own, c).wait_recv()
            mine = part[p.hi, p.lo, 0:own, cols].astype(F32)
            finish(cols, mine + r1[p.hi, 0:own, cols].astype(F32) + r2[0:own, cols].astype(F32))

        @pl.loop(0, chunks)
        def _(c):
            self.first_copy(i, own, c).wait_send()
            self.second_copy(i, own, c).wait_send()

    def gather_copy(self, i, buffer, which):
        p = self.p
        here = buffer.at[p.hi, p.lo]
        if which == 0:
            return remote(here, here, self.gs.at[i, 0], self.gr.at[i, 0], p.far)
        if which == 1:
            return remote(here, here, self.gs.at[i, 1], self.gr.at[i, 1], p.near)
        there = buffer.at[1 - p.hi, p.lo]
        return remote(there, there, self.gs.at[i, 2], self.gr.at[i, 2], p.near)

    def gather_start(self, i, buffer):
        self.gather_copy(i, buffer, 0).start()
        self.gather_copy(i, buffer, 1).start()

    def gather_finish(self, i, buffer):
        self.gather_copy(i, buffer, 0).wait_recv()
        self.gather_copy(i, buffer, 2).start()
        self.gather_copy(i, buffer, 1).wait_recv()
        self.gather_copy(i, buffer, 2).wait_recv()
        for which in range(3):
            self.gather_copy(i, buffer, which).wait_send()


def peers_copy(place, src, dst, send, recv, which):
    device = (place.near, place.far, place.diag)[which]
    return remote(src, dst.at[place.t], send.at[which], recv.at[which], device)


def gain_row(gathered, n, row, width):
    each = width // (n * T)
    tiles = []
    for j in range(width // 128):
        total = None
        for i in range(128 // each):
            number = j * (128 // each) + i
            block = gathered[number % T, number // T][row : row + 1]
            total = block if total is None else total + block
        tiles.append(total)
    return jnp.concatenate(tiles, axis=1)


QKV, WO, GU, WD = 0, 640, 1152, 3968
COLS = 5376
RANGES = (
    ("along", 0, 640),
    ("along", 640, 512),
    ("along", 1152, 1408),
    ("along", 2560, 1408),
    ("along", 3968, 512),
    ("across", 4480, 896),
)


def ones(condition):
    return jnp.where(condition, 1.0, 0.0)


def iota(size, axis):
    shape = (size, 1) if axis == 0 else (1, size)
    return lax.broadcasted_iota(jnp.int32, shape, axis).astype(F32)


def quotient(index, step, most):
    total = ones(index >= step)
    for i in range(2, most):
        total = total + ones(index >= step * i)
    return total


def own_places(own_index):
    batch, place, seen = 0.0 * own_index, 0.0 * own_index, [0, 0]
    for start, rows, b in PIECES:
        inside = (own_index >= start) & (own_index < start + rows)
        batch = jnp.where(inside, float(b), batch)
        place = jnp.where(inside, own_index - start + seen[b], place)
        seen[b] += rows
    return batch, place


def fill_tables(p, depth_row, depth_col, lengths, freqs, perm, back, back_own, cosine, sine, allowed, act_own, act_last):
    local = OWN[0] // MB
    total = T * OWN[0]

    def columns(index):
        tensor = quotient(index, OWN[0], T)
        inside = index - tensor * OWN[0]
        batch = ones(inside >= local)
        return batch, tensor * local + inside - batch * local

    batch_row, pos_row = columns(iota(total, 1))
    batch_col, pos_col = columns(iota(total, 0))
    same = batch_row == batch_col
    rank_row = jnp.sum(
        ones(same & ((depth_col > depth_row) | ((depth_col == depth_row) & (pos_col < pos_row)))), axis=0, keepdims=True
    )
    rank_col = jnp.sum(
        ones(same & ((depth_row > depth_col) | ((depth_row == depth_col) & (pos_row < pos_col)))), axis=1, keepdims=True
    )

    def compact(index):
        owner = quotient(index, OWN[0], T)
        batch, place = own_places(index - owner * OWN[0])
        return batch, place * T + owner

    batch_q, rank_q = compact(iota(total, 0))
    hit = (rank_row == rank_q) & (batch_row == batch_q)
    perm[...] = ones(hit).astype(BF)
    batch_p, rank_p = compact(iota(total, 1))
    back[...] = ones((rank_col == rank_p) & (batch_col == batch_p)).astype(BF)
    back_own[...] = back[pl.ds(pl.multiple_of(p.t * OWN[0], OWN[0]), OWN[0]), :]

    ends = []
    for b in range(MB):
        first = lengths[b : b + 1, 0:1].astype(F32)
        ends.append((first, first + lengths[b : b + 1, 1:2].astype(F32)))
    position = jnp.sum(jnp.where(hit, pos_row, 0.0), axis=1, keepdims=True)
    end = [jnp.where(batch_q == 0.0, ends[0][i], ends[1][i]) for i in range(2)]
    start = jnp.where(position >= end[1], end[1], jnp.where(position >= end[0], end[0], 0.0))
    angles = (position - start) * freqs
    cosine[...] = jnp.cos(angles)
    lane = lax.broadcasted_iota(jnp.int32, angles.shape, 1)
    value = jnp.sin(angles)
    sine[...] = jnp.where((lane & 63) < 32, -value, value)

    own_batch, own_place = own_places(iota(OWN[0], 0))
    own_rank = own_place * T + p.t.astype(F32)
    for level in range(RECUR):
        own = OWN[level]
        half = T * own // MB
        counts = [
            jnp.sum(ones((batch_row == float(b)) & (depth_row >= level + 1.0)), axis=1, keepdims=True) for b in range(MB)
        ]
        act_own[level] = ones(own_rank < jnp.where(own_batch == 0.0, counts[0], counts[1]))
        if level == RECUR - 1:
            index = iota(T * own, 0)
            owner = quotient(index, own, T)
            batch, place = own_places(index - owner * own)
            act_last[...] = ones(place * T + owner < jnp.where(batch == 0.0, counts[0], counts[1]))

        def order(index):
            owner = quotient(index, own // MB, T)
            return (index - owner * (own // MB)) * T + owner

        index_col, index_row = iota(half, 0), iota(half, 1)
        order_col, order_row = order(index_col), order(index_row)
        for b in range(MB):
            at_col = jnp.sum(
                jnp.where((rank_row == order_col) & (batch_row == float(b)), pos_row, 0.0), axis=1, keepdims=True
            )
            at_row = jnp.sum(
                jnp.where((rank_col == order_row) & (batch_col == float(b)), pos_col, 0.0), axis=0, keepdims=True
            )
            document_col = ones(at_col >= ends[b][0]) + ones(at_col >= ends[b][1])
            document_row = ones(at_row >= ends[b][0]) + ones(at_row >= ends[b][1])
            ok = (document_col == document_row) & (at_row <= at_col) & (order_row < counts[b])
            allowed[level][b] = ones(ok | (index_col == index_row)).astype(BF)


def forward_kernel(n, *refs):
    it = iter(refs)
    tokens, cotangent, wq, wk, wv, wo, wg, wu, wd = [next(it) for _ in range(9)]
    attn_gain, mlp_gain, depth_row, depth_col, lengths, freqs = [next(it) for _ in range(6)]
    w_out, gain_out, fin_out, cot_own, cot_all = [next(it) for _ in range(5)]
    cosine, sine, back_own, act_own, act_last = [next(it) for _ in range(5)]
    allowed = [next(it) for _ in range(RECUR)]
    names = ("normed", "qkv", "att", "mixed", "gu", "prod", "hidden", "first")
    saved_out = [dict((k, next(it)) for k in names) for _ in range(RECUR)]
    dg_out = next(it)
    w = next(it)
    dg, product_grad = next(it), next(it)
    perm, back, kv, wo_in, wd_in = [next(it) for _ in range(5)]
    gbuf, gall = next(it), next(it)
    tok, cot = next(it), next(it)
    saved = [dict((k, next(it)) for k in names) for _ in range(RECUR)]
    after, fin, cown = next(it), next(it), next(it)
    part, relay = next(it), next(it)
    sums = [(next(it), next(it)) for _ in range(2 * RECUR - 1)]
    line_sems = [next(it) for _ in range(6)]
    row_sems = [next(it) for _ in range(6)]
    wsem = next(it)
    tsend, trecv, outsem = next(it), next(it), next(it)

    p = Place(n)
    width = tokens.shape[-1]
    rows_chunk = width // n

    def chunk_at(chunk, start, size):
        return w.at[pl.ds(pl.multiple_of(chunk * rows_chunk, rows_chunk), rows_chunk), pl.ds(start, size)]

    pieces = [("normal", lambda chunk: gbuf.at[chunk])]
    number = []
    for kind, start, size in RANGES:
        def at(chunk, start=start, size=size):
            return chunk_at(chunk, start, size)

        number.append(len(pieces))
        pieces += [("own", at), ("other", at)] if kind == "across" else [("normal", at)]
    line = LineGather(p, pieces, line_sems)
    rows = Rows(p, part, relay, sums, row_sems)
    hidden_cols = (COLS - GU) // 3
    writes = []

    def write(src, dst):
        copy = pltpu.make_async_copy(src, dst, outsem.at[len(writes)])
        copy.start()
        writes.append(copy)

    local = [
        pltpu.make_async_copy(wq, chunk_at(p.dp, QKV, 512), wsem.at[0]),
        pltpu.make_async_copy(wk, kv.at[0], wsem.at[1]),
        pltpu.make_async_copy(wv, kv.at[1], wsem.at[2]),
        pltpu.make_async_copy(wo, wo_in, wsem.at[3]),
        pltpu.make_async_copy(wg, chunk_at(p.dp, GU, hidden_cols), wsem.at[4]),
        pltpu.make_async_copy(wu, chunk_at(p.dp, GU + hidden_cols, hidden_cols), wsem.at[5]),
        pltpu.make_async_copy(wd, wd_in, wsem.at[6]),
    ]
    for copy in local:
        copy.start()
    mine_rows = pl.ds(pl.multiple_of(p.dp * rows_chunk, rows_chunk), rows_chunk)
    each = attn_gain.shape[1]
    lane = lax.broadcasted_iota(jnp.int32, (1, 128), 1)
    spot = lax.rem(p.dp * T + p.t, 128 // each)
    inside = (lane >= spot * each) & (lane < (spot + 1) * each)
    for row, gain in enumerate((attn_gain, mlp_gain)):
        value = jnp.concatenate([gain[...]] * (128 // each), axis=1)
        gbuf[p.dp, row : row + 1, :] = jnp.where(inside, value, 0.0)
    gbuf[p.dp, 2:8, :] = jnp.zeros((6, 128), F32)
    p.barrier(True)
    line.own(0)
    for copy in local[0:3]:
        copy.wait()
    w[mine_rows, QKV + 512 : QKV + 640] = jnp.concatenate([kv[0], kv[1]], axis=0).T
    heads_piece, out_piece, gate_piece, up_piece, down_piece, down_last = number
    line.own(heads_piece)
    for which in range(3):
        peers_copy(p, tokens, tok, tsend.at[0], trecv.at[0], which).start()
    pltpu.make_async_copy(tokens, tok.at[p.t], tsend.at[0, 3]).start()
    local[3].wait()
    w[mine_rows, WO : WO + 512] = wo_in[...].T
    line.own(out_piece)
    for which in range(3):
        peers_copy(p, cotangent, cot, tsend.at[1], trecv.at[1], which).start()
    pltpu.make_async_copy(cotangent, cot.at[p.t], tsend.at[1, 3]).start()
    for copy in local[4:6]:
        copy.wait()
    line.own(gate_piece)
    line.steps(0)
    line.arrive(0)
    for which in range(3):
        peers_copy(p, gbuf, gall, tsend.at[2], trecv.at[2], which).start()
    pltpu.make_async_copy(gbuf, gall.at[p.t], tsend.at[2, 3]).start()
    fill_tables(
        p, depth_row[...], depth_col[...], lengths, freqs[...], perm, back, back_own, cosine, sine, allowed, act_own, act_last
    )
    line.steps(heads_piece)
    local[6].wait()
    w[mine_rows, WD : WD + hidden_cols] = wd_in[...].T
    line.own(up_piece)
    line.steps(out_piece)

    def wait_peers(i, src, dst):
        for which in range(3):
            copy = peers_copy(p, src, dst, tsend.at[i], trecv.at[i], which)
            copy.wait_recv()
            copy.wait_send()
        pltpu.make_async_copy(src, dst.at[p.t], tsend.at[i, 3]).wait()

    wait_peers(2, gbuf, gall)
    gain_out[0:1, :] = gain_row(gall, n, 0, width)
    gain_out[1:2, :] = gain_row(gall, n, 1, width)
    gain_out[2:8, :] = jnp.zeros((6, width), F32)

    wait_peers(0, tokens, tok)

    own = OWN[0]
    mine = perm[pl.ds(pl.multiple_of(p.t * own, own), own), :]
    saved[0]["hidden"][...] = dot(mine, tok[...].reshape(T * own, width), NN)

    @pl.loop(0, T)
    def _(owner):
        picked = perm[pl.ds(pl.multiple_of(owner * own, own), own), :]
        hidden = dot(picked, tok[...].reshape(T * own, width), NN)
        inverse = lax.rsqrt(mean_square(hidden) + 1e-05)
        saved[0]["normed"][owner] = (hidden * inverse * gain_out[0:1, :]).astype(BF)

    wait_peers(1, cotangent, cot)
    cown[...] = dot(mine, cot[...].reshape(T * own, width), NN)
    write(cown, cot_own)

    line.own(down_piece)
    line.own(down_last)

    @pl.loop(0, T)
    def _(owner):
        picked = perm[pl.ds(pl.multiple_of(owner * OWN[0], 32), OWN[RECUR - 1]), :]
        cot_all[owner] = dot(picked, cot[...].reshape(T * OWN[0], width), NN).astype(BF)

    line.arrive(heads_piece)

    for level in range(RECUR):
        own = OWN[level]
        count = T * own
        half = count // 2
        s = saved[level]
        if level:
            rows.gather_finish(2 * level - 1, s["normed"].reshape(2, 2, own, width))
        x = s["normed"][...].reshape(count, width)
        qkv = dot(x, w[:, QKV : QKV + 640], NN)
        cos = jnp.concatenate([cosine[owner * OWN[0] : owner * OWN[0] + own, :] for owner in range(T)], axis=0)
        sin = jnp.concatenate([sine[owner * OWN[0] : owner * OWN[0] + own, :] for owner in range(T)], axis=0)
        tiles = []
        for j in range(5):
            tile = qkv[:, j * 128 : (j + 1) * 128]
            turned = tile * cos + swap_halves(tile) * sin
            if j == 4:
                lane = lax.broadcasted_iota(jnp.int32, tile.shape, 1)
                turned = jnp.where(lane < HS, turned, tile)
            tiles.append(turned)
        rotated = jnp.concatenate(tiles, axis=1)
        s["qkv"][...] = rotated.astype(BF)
        write(s["qkv"], saved_out[level]["qkv"])
        heads = []
        for b, block in enumerate(split_batches(rotated, own)):
            query, key, value = (
                block[:, 0:512].astype(BF),
                block[:, 512:576].astype(BF),
                block[:, 576:640].astype(BF),
            )
            _, shares = attention_shares(query, key, allowed[level][b])
            out = dot(shares.astype(BF).reshape(8 * half, half), value, NN)
            heads.append(unstack_heads(out, half))
            if level == 0:
                line.step(gate_piece, 1) if b == 0 else [line.step(gate_piece, k) for k in range(2, p.line)]
        s["att"][...] = join_batches(heads, own).astype(BF)
        write(s["att"], saved_out[level]["att"])
        if level == 0:
            line.arrive(out_piece)
        present = act_own[level, 0:own, :]

        def attention_tile(cols):
            return dot(s["att"][...], w[cols, WO : WO + 512], NT)

        def attention_finish(cols, total):
            s["first"][:, cols] = s["hidden"][:, cols] + present * total

        rows.reduce(2 * level, own, attention_tile, attention_finish)
        first = s["first"][...]
        inverse = lax.rsqrt(mean_square(first) + 1e-05)
        s["mixed"][p.t] = (first * inverse * gain_out[1:2, :]).astype(BF)
        mixed = s["mixed"].reshape(2, 2, own, width)
        rows.gather_start(2 * level, mixed)
        write(s["first"], saved_out[level]["first"])
        if level == 0:
            line.steps(up_piece)
            line.own(down_last + 1)
        if level == RECUR - 1:
            dg[...] = (cot_all[...].astype(F32).reshape(count, width) * act_last[...]).astype(BF).reshape(T, own, width)
            write(dg, dg_out)

            def grad_block(start, size):
                product_grad[:, pl.ds(pl.multiple_of(start, 128), size)] = dot(
                    dg[...].reshape(count, width), w[:, pl.ds(pl.multiple_of(WD + start, 128), size)], NN
                )

            @pl.loop(0, hidden_cols // 256)
            def _(j):
                grad_block(j * 256, 256)

            if hidden_cols % 256:
                grad_block(hidden_cols // 256 * 256, 128)
        rows.gather_finish(2 * level, mixed)
        write(s["mixed"], saved_out[level]["mixed"])

        def hidden_block(start, size):
            x = s["mixed"][...].reshape(count, width)
            gate = dot(x, w[:, pl.ds(pl.multiple_of(GU + start, 128), size)], NN)
            upward = dot(x, w[:, pl.ds(pl.multiple_of(GU + hidden_cols + start, 128), size)], NN)
            cols = pl.ds(pl.multiple_of(start, 128), size)
            high = pl.ds(pl.multiple_of(hidden_cols + start, 128), size)
            sigma = jax.nn.sigmoid(gate)
            s["prod"][:, cols] = (gate * sigma * upward).astype(BF)
            if level == RECUR - 1:
                up = product_grad[:, cols]
                s["gu"][:, cols] = (up * upward * sigma * (1.0 + gate * (1.0 - sigma))).astype(BF)
                s["gu"][:, high] = (up * gate * sigma).astype(BF)
            else:
                s["gu"][:, cols] = gate.astype(BF)
                s["gu"][:, high] = upward.astype(BF)

        if level == 0:
            line.steps(down_piece)
            line.step(down_last, 1)
            line.step(down_last + 1, 1)
            line.arrive(gate_piece)
            line.arrive(up_piece)

        @pl.loop(0, hidden_cols // 256)
        def _(j):
            hidden_block(j * 256, 256)

        if hidden_cols % 256:
            hidden_block(hidden_cols // 256 * 256, 128)
        write(s["gu"], saved_out[level]["gu"])
        write(s["prod"], saved_out[level]["prod"])
        if level == 0:
            for k in range(2, p.line):
                line.step(down_last, k)
                line.step(down_last + 1, k)
            line.arrive(down_piece)
            write(w, w_out)

        if level < RECUR - 1:

            def mlp_tile(cols):
                return dot(s["prod"][...], w[cols, WD : WD + 1408], NT)

            def mlp_finish(cols, total):
                after[0:own, cols] = s["first"][:, cols] + present * total

            rows.reduce(2 * level + 1, own, mlp_tile, mlp_finish)
            deeper = OWN[level + 1]
            hidden = after[0:deeper, :]
            saved[level + 1]["hidden"][...] = hidden
            inverse = lax.rsqrt(mean_square(hidden) + 1e-05)
            saved[level + 1]["normed"][p.t] = (hidden * inverse * gain_out[0:1, :]).astype(BF)
            rows.gather_start(2 * level + 1, saved[level + 1]["normed"].reshape(2, 2, deeper, width))
            fin[deeper:own, :] = after[deeper:own, :].astype(BF)

        write(s["hidden"], saved_out[level]["hidden"])
        write(s["normed"], saved_out[level]["normed"])
    fin[0 : OWN[2], :] = jnp.zeros((OWN[2], width), BF)
    write(fin, fin_out)
    for i in range(len(pieces)):
        line.drain(i)
    for copy in writes:
        copy.wait()


def forward(n, tokens, depth, lengths, cotangent, weights, attn_gain, mlp_gain):
    width = tokens.shape[-1]
    hidden_cols = weights[4].shape[1]
    local = OWN[0] // MB
    total = T * OWN[0]
    ordered = depth.reshape(MB, T, local).transpose(1, 0, 2).astype(F32)
    freqs = jnp.asarray(np.tile(10000.0 ** (-np.arange(0, HS, 2) / HS), 4)[None].astype(np.float32))
    vmem = pl.BlockSpec(memory_space=pltpu.VMEM)
    hbm = pl.BlockSpec(memory_space=pl.ANY)

    def saved_shapes(own):
        count = T * own
        return {
            "normed": ((T, own, width), BF),
            "qkv": ((count, 640), BF),
            "att": ((count, 512), BF),
            "mixed": ((T, own, width), BF),
            "gu": ((count, 2 * hidden_cols), BF),
            "prod": ((count, hidden_cols), BF),
            "hidden": ((own, width), F32),
            "first": ((own, width), F32),
        }

    shapes = [((width, COLS), BF), ((8, width), F32), ((OWN[0], width), BF), ((OWN[0], width), F32), ((T, OWN[2], width), BF)]
    specs = [hbm, vmem, hbm, hbm, vmem]
    shapes += [((total, 128), F32)] * 2 + [((OWN[0], total), BF), ((RECUR, OWN[0], 1), F32), ((T * OWN[2], 1), F32)]
    shapes += [((MB, T * own // MB, T * own // MB), BF) for own in OWN]
    specs += [vmem] * (5 + RECUR)
    for own in OWN:
        for entry in saved_shapes(own).values():
            shapes.append(entry)
            specs.append(hbm)
    shapes.append(((T, OWN[2], width), BF))
    specs.append(hbm)
    scratch = [pltpu.VMEM((width, COLS), BF), pltpu.VMEM((T, OWN[2], width), BF), pltpu.VMEM((T * OWN[2], hidden_cols), F32)]
    scratch += [pltpu.VMEM((total, total), BF)] * 2
    scratch += [pltpu.VMEM((2,) + weights[1].shape[::-1], BF), pltpu.VMEM(weights[3].shape, BF), pltpu.VMEM(weights[6].shape, BF)]
    scratch += [pltpu.VMEM((n, 8, 128), F32), pltpu.VMEM((T, n, 8, 128), F32)]
    scratch += [pltpu.VMEM((T,) + tokens.shape, BF)] * 2
    for own in OWN:
        scratch += [pltpu.VMEM(*entry) for entry in saved_shapes(own).values()]
    scratch += [pltpu.VMEM((OWN[0], width), F32), pltpu.VMEM((OWN[0], width), BF), pltpu.VMEM((OWN[0], width), F32)]
    scratch += [pltpu.VMEM((2, 2, OWN[0], width), BF), pltpu.VMEM((OWN[0], width), BF)]
    for own in [own for own in OWN for _ in range(2)][:-1]:
        scratch += [pltpu.VMEM((2, own, width), BF), pltpu.VMEM((own, width), BF)]
    dma = pltpu.SemaphoreType.DMA
    count = 1 + sum(2 if kind == "across" else 1 for kind, _, _ in RANGES)
    scratch += [dma((count, n // 2))] * 6
    chunks = width // DC
    scratch += [dma((2 * RECUR, chunks))] * 4 + [dma((2 * RECUR, 3))] * 2
    scratch += [dma((7,)), dma((3, 4)), dma((3, 3)), dma((40,))]
    outs = pl.pallas_call(
        functools.partial(forward_kernel, n),
        out_shape=[jax.ShapeDtypeStruct(*entry) for entry in shapes],
        in_specs=[hbm] * 9 + [vmem] * 6,
        out_specs=specs,
        scratch_shapes=scratch,
        compiler_params=pltpu.CompilerParams(
            collective_id=1, has_side_effects=True, vmem_limit_bytes=62 << 20
        ),
    )(
        tokens,
        cotangent,
        weights[0],
        weights[1].T,
        weights[2].T,
        *weights[3:],
        attn_gain[None],
        mlp_gain[None],
        ordered.reshape(1, total),
        ordered.reshape(total, 1),
        lengths,
        freqs,
    )
    w_all, gain, fin, cot_own = outs[:4]
    tables = dict(zip(("cosine", "sine", "back", "act", "act_last"), outs[5:10]))
    tables["masks"] = outs[10:13]
    names = list(saved_shapes(1))
    saved = [dict(zip(names, outs[13 + 8 * level : 21 + 8 * level])) for level in range(RECUR)]
    return w_all, gain, fin, cot_own, outs[37], tables, saved


def share_groups(block, allowed):
    query, key = block[:, 0:512].astype(BF), block[:, 512:576].astype(BF)
    for start in range(0, 512, HEADS * HS):
        yield (start,) + attention_shares(query[:, start : start + HEADS * HS], key, allowed)


def attention_back(rotated, groups, attended_grad, cos, sin, own, between=None):
    half = T * own // 2
    grads = []
    upstream = split_batches(attended_grad, own)
    for b in range(MB):
        key, value = rotated[b][:, 512:576].astype(BF), rotated[b][:, 576:640].astype(BF)
        up_all = upstream[b].astype(BF)
        query_grads, key_grad, value_grad = [], 0.0, 0.0
        for start, stacked, shares in groups[b]:
            up = stack_heads(up_all[:, start : start + HEADS * HS])
            low = shares.astype(BF).reshape(HEADS * half, half)
            shares_grad = dot(up, value, NT).reshape(HEADS, half, half)
            value_grad += dot(low, up, TN)
            spread = jnp.sum(shares * shares_grad, axis=-1, keepdims=True)
            score_grad = (shares * (shares_grad - spread)).astype(BF).reshape(HEADS * half, half)
            query_grads.append(unstack_heads(dot(score_grad, key, NN), half) * SCALE)
            key_grad += dot(score_grad, stacked, TN) * SCALE
        query_grad = jnp.concatenate(query_grads, axis=1)
        grads.append(jnp.concatenate([query_grad, key_grad, value_grad], axis=1))
        if between is not None:
            between()
    joined = join_batches(grads, own)
    tiles = []
    for j in range(5):
        tile = joined[:, j * 128 : (j + 1) * 128]
        turned = tile * cos - swap_halves(tile) * sin
        if j == 4:
            lane = lax.broadcasted_iota(jnp.int32, tile.shape, 1)
            turned = jnp.where(lane < HS, turned, tile)
        tiles.append(turned)
    return jnp.concatenate(tiles, axis=1)


def level_rows(table, own):
    return jnp.concatenate([table[owner * OWN[0] : owner * OWN[0] + own, :] for owner in range(T)], axis=0)


def norm_back(source, gain, upstream):
    inverse = lax.rsqrt(mean_square(source) + 1e-05)
    unit = source * inverse
    gain_part = jnp.sum(upstream * unit, axis=0, keepdims=True)
    scaled = upstream * gain
    return inverse * (scaled - unit * jnp.mean(scaled * unit, axis=-1, keepdims=True)), gain_part


def backward_kernel(n, *refs):
    it = iter(refs)
    w_all, gain, cot_own, cosine, sine, act_own, last_gug = [next(it) for _ in range(7)]
    allowed = [None] + [next(it) for _ in range(2)]
    saved_in = []
    for level in range(RECUR):
        saved_in.append({k: next(it) for k in saved_names(level)})
    dg_out = [next(it) for _ in range(2)]
    gug_out = [next(it) for _ in range(2)]
    og_out = [None] + [next(it) for _ in range(2)]
    qkvg_out = [None] + [next(it) for _ in range(2)]
    grad_out, gain_part = next(it), next(it)
    w = next(it)
    saved = []
    for level in range(RECUR):
        saved.append({k: next(it) for k in saved_in[level]})
    dg = [next(it) for _ in range(2)]
    gug = [next(it) for _ in range(2)]
    og = [None] + [next(it) for _ in range(2)]
    qkvg = [None] + [next(it) for _ in range(2)]
    gug.append(next(it))
    grad, upstream, factors = next(it), next(it), next(it)
    part, relay = next(it), next(it)
    sums = [(next(it), next(it)) for _ in range(5)]
    row_sems = [next(it) for _ in range(6)]
    insem, outsem = next(it), next(it)

    p = Place(n)
    width = w.shape[0]
    rows = Rows(p, part, relay, sums, row_sems)
    hidden_cols = (COLS - GU) // 3
    loads, writes = {}, []

    def load(name, src, dst):
        copy = pltpu.make_async_copy(src, dst, insem.at[len(loads)])
        copy.start()
        loads[name] = copy

    def write(src, dst):
        copy = pltpu.make_async_copy(src, dst, outsem.at[len(writes)])
        copy.start()
        writes.append(copy)

    def columns(start, size):
        load(("w", start), w_all.at[:, pl.ds(start, size)], w.at[:, pl.ds(start, size)])

    last = RECUR - 1
    load("gug", last_gug, gug[last])
    columns(GU, 2 * hidden_cols)
    load("grad", cot_own, grad)
    load(("first", last), saved_in[last]["first"], saved[last]["first"])
    columns(WO, 512)
    for name in ("qkv", "hidden"):
        load((name, last), saved_in[last][name], saved[last][name])
    columns(QKV, 640)
    columns(WD, hidden_cols)
    for level in (1, 0):
        for name in saved_in[level]:
            load((name, level), saved_in[level][name], saved[level][name])
    p.barrier(False)
    gain_part[...] = jnp.zeros_like(gain_part)

    for level in range(last, -1, -1):
        own = OWN[level]
        count = T * own
        s = saved[level]
        base = 2 * (last - level)
        present = act_own[level, 0:own, :]
        if level == last:
            loads["grad"].wait()
            loads["gug"].wait()
            loads["w", GU].wait()
        else:
            dg[level][p.t] = (present * grad[0:own, :]).astype(BF)
            view = dg[level].reshape(2, 2, own, width)
            rows.gather_start(base, view)
            loads["gu", level].wait()

            @pl.loop(0, hidden_cols // 128)
            def _(j):
                low = pl.ds(pl.multiple_of(j * 128, 128), 128)
                high = pl.ds(pl.multiple_of(hidden_cols + j * 128, 128), 128)
                gate = s["gu"][:, low].astype(F32)
                upward = s["gu"][:, high].astype(F32)
                sigma = jax.nn.sigmoid(gate)
                factors[0:count, low] = upward * sigma * (1.0 + gate * (1.0 - sigma))
                factors[0:count, high] = gate * sigma

            if level == 1:
                loads["w", WD].wait()
            rows.gather_finish(base, view)
            write(dg[level], dg_out[level])

            def hidden_block(start, size):
                wcols = pl.ds(pl.multiple_of(WD + start, 128), size)
                product_grad = dot(dg[level][...].reshape(count, width), w[:, wcols], NN)
                low = pl.ds(pl.multiple_of(start, 128), size)
                high = pl.ds(pl.multiple_of(hidden_cols + start, 128), size)
                gug[level][:, low] = (product_grad * factors[0:count, low]).astype(BF)
                gug[level][:, high] = (product_grad * factors[0:count, high]).astype(BF)

            @pl.loop(0, hidden_cols // 256)
            def _(j):
                hidden_block(j * 256, 256)

            if hidden_cols % 256:
                hidden_block(hidden_cols // 256 * 256, 128)
            write(gug[level], gug_out[level])

        def mlp_tile(cols):
            return dot(gug[level][...], w[cols, GU : GU + 2 * hidden_cols], NT)

        def take(cols, total):
            upstream[0:own, cols] = total

        rows.reduce(base, own, mlp_tile, take)
        loads["first", level].wait()
        update, add = norm_back(s["first"][...], gain[1:2, :], upstream[0:own, :])
        grad[0:own, :] += update
        gain_part[1:2, :] += add
        if level == 0:
            break
        og[level][p.t] = (present * grad[0:own, :]).astype(BF)
        view = og[level].reshape(2, 2, own, width)
        rows.gather_start(base + 1, view)
        loads["qkv", level].wait()
        rotated = split_batches(s["qkv"][...].astype(F32), own)
        groups = [list(share_groups(rotated[b], allowed[level][b])) for b in range(MB)]
        rows.gather_finish(base + 1, view)
        write(og[level], og_out[level])
        if level == last:
            loads["w", WO].wait()
        attended_grad = dot(og[level][...].reshape(count, width), w[:, WO : WO + 512], NN)
        cos, sin = level_rows(cosine, own), level_rows(sine, own)
        qkvg[level][...] = attention_back(rotated, groups, attended_grad, cos, sin, own).astype(BF)
        write(qkvg[level], qkvg_out[level])
        if level == last:
            loads["w", QKV].wait()

        def attention_tile(cols):
            return dot(qkvg[level][...], w[cols, QKV : QKV + 640], NT)

        rows.reduce(base + 1, own, attention_tile, take)
        loads["hidden", level].wait()
        update, add = norm_back(s["hidden"][...], gain[0:1, :], upstream[0:own, :])
        grad[0:own, :] += update
        gain_part[0:1, :] += add

    write(grad, grad_out)
    for copy in writes:
        copy.wait()


def saved_names(level):
    return (("gu", "first"), ("gu", "first", "qkv", "hidden"), ("first", "qkv", "hidden"))[level]


def backward(n, w_all, gain, cot_own, tables, saved):
    width = w_all.shape[0]
    hidden_cols = (COLS - GU) // 3
    vmem = pl.BlockSpec(memory_space=pltpu.VMEM)
    hbm = pl.BlockSpec(memory_space=pl.ANY)
    operands = [w_all, gain, cot_own, tables["cosine"], tables["sine"], tables["act"], saved[RECUR - 1]["gu"]]
    operands += list(tables["masks"][1:])
    specs = [hbm, vmem, hbm] + [vmem] * 3 + [hbm] + [vmem] * 2
    used = []
    for level in range(RECUR):
        for name in saved_names(level):
            operands.append(saved[level][name])
            specs.append(hbm)
            used.append(saved[level][name])
    outs = [((T, own, width), BF) for own in OWN[:2]]
    outs += [((T * own, 2 * hidden_cols), BF) for own in OWN[:2]]
    outs += [((T, own, width), BF) for own in OWN[1:]]
    outs += [((T * own, 640), BF) for own in OWN[1:]]
    scratch = [pltpu.VMEM(w_all.shape, BF)] + [pltpu.VMEM(u.shape, u.dtype) for u in used]
    scratch += [pltpu.VMEM(*entry) for entry in outs] + [pltpu.VMEM((T * OWN[2], 2 * hidden_cols), BF)]
    outs += [((OWN[0], width), F32), ((8, width), F32)]
    out_specs = [hbm] * (len(outs) - 1) + [vmem]
    scratch += [pltpu.VMEM((OWN[0], width), F32)] * 2 + [pltpu.VMEM((T * OWN[0], 2 * hidden_cols), F32)]
    scratch += [pltpu.VMEM((2, 2, OWN[0], width), BF), pltpu.VMEM((OWN[0], width), BF)]
    for own in (OWN[2], OWN[2], OWN[1], OWN[1], OWN[0]):
        scratch += [pltpu.VMEM((2, own, width), BF), pltpu.VMEM((own, width), BF)]
    dma = pltpu.SemaphoreType.DMA
    chunks = width // DC
    scratch += [dma((5, chunks))] * 4 + [dma((5, 3))] * 2 + [dma((24,)), dma((16,))]
    res = pl.pallas_call(
        functools.partial(backward_kernel, n),
        out_shape=[jax.ShapeDtypeStruct(*entry) for entry in outs],
        in_specs=specs,
        out_specs=out_specs,
        scratch_shapes=scratch,
        compiler_params=pltpu.CompilerParams(
            collective_id=2, has_side_effects=True, vmem_limit_bytes=62 << 20
        ),
    )(*operands)
    return {
        "dg": res[0:2],
        "gug": res[2:4],
        "og": res[4:6],
        "qkvg": res[6:8],
        "grad": res[8],
        "gain_part": res[9],
    }


PIECE = 384
SEGMENTS = (("down", 1408), ("gu", 2816), ("out", 512), ("qkv", 640))
DEPTH = 3
FIRST = 1
JOINT = 2
PLACES = COLS // PIECE + FIRST


def cut_pieces():
    pieces = [[] for _ in range(COLS // PIECE)]
    at = 0
    for which, size in SEGMENTS:
        done = 0
        while done < size:
            k, inside = divmod(at, PIECE)
            cols = min(size - done, PIECE - inside)
            pieces[k].append((which, done, cols, inside))
            done += cols
            at += cols
    return pieces


def gradient_kernel(n, *refs):
    it = iter(refs)
    (w_all, gain, cosine, sine, act_own, allowed, back) = [next(it) for _ in range(7)]
    grad_in, gain_in, fin_in, hidden_in, qkv_in, first_in = [next(it) for _ in range(6)]
    x_in = {name: [next(it) for _ in range(3)] for name in ("down", "gu", "qkv")}
    x_in["out"] = [None] + [next(it) for _ in range(2)]
    y_in = {name: [next(it) for _ in range(3)] for name in ("down", "gu", "out")}
    y_in["qkv"] = [None] + [next(it) for _ in range(2)]
    (act_out, tok_out, dq, dk, dv, dwo, dgate, dup, dwd, gain_sum) = [next(it) for _ in range(10)]
    og_hbm, fin_all, grad_all = [next(it) for _ in range(3)]
    w = next(it)
    y = {name: next(it) for name in ("down", "gu", "out", "qkv")}
    xm, xl, xraw = next(it), next(it), next(it)
    og, hidden, qkv, grad, upstream, gains = [next(it) for _ in range(6)]
    fin, first = next(it), next(it)
    gpeers = next(it)
    stage, landed, across, across_own = [next(it) for _ in range(4)]
    window_tmp = next(it)
    gmate_stage, gmate, gline, gline_own = [next(it) for _ in range(4)]
    final, turned, last_stage, last_landed, fsend, frecv = [next(it) for _ in range(6)]
    chunk_in, fin_chunk, act_chunk, tok_chunk = [next(it) for _ in range(4)]
    part, relay = next(it), next(it)
    sums = [(next(it), next(it))] * 2
    row_sems = [next(it) for _ in range(6)]
    msend, mrecv, lsend, lrecv, lrecv2 = [next(it) for _ in range(5)]
    tsend, trecv = next(it), next(it)
    insem, xsem, outsem, finsem, loadsem = [next(it) for _ in range(5)]

    p = Place(n)
    width = w.shape[0]
    line = p.line
    chunk_rows = width // n
    window = max(128, chunk_rows)
    rows = Rows(p, part, relay, sums, row_sems)
    own = OWN[0]
    count = T * own
    starts = [0, T * OWN[0], T * (OWN[0] + OWN[1])]
    total_rows = T * sum(OWN)
    hidden_cols = (COLS - GU) // 3
    loads, writes = {}, []

    def load(name, src, dst):
        copy = pltpu.make_async_copy(src, dst, insem.at[len(loads)])
        copy.start()
        loads[name] = copy

    def write(src, dst):
        copy = pltpu.make_async_copy(src, dst, outsem.at[len(writes)])
        copy.start()
        writes.append(copy)

    load("grad", grad_in, grad)
    for name in ("down", "gu"):
        for level in range(RECUR):
            load((name, level), y_in[name][level], y[name].at[pl.ds(starts[level], T * OWN[level])])
    load("w", w_all.at[:, pl.ds(0, GU)], w)
    load("fin", fin_in, fin)
    load("first", first_in, first)
    load("qkv", qkv_in, qkv)
    load("hidden", hidden_in, hidden)
    for level in range(RECUR):
        load(("out", level), y_in["out"][level], y["out"].at[pl.ds(starts[level], T * OWN[level])])
    for level in (1, 2):
        load(("qkv", level), y_in["qkv"][level], y["qkv"].at[pl.ds(starts[level], T * OWN[level])])
    p.barrier(True)

    def x_source(which, level):
        return og_hbm if which == "out" and level == 0 else x_in[which][level]

    def level_slice(level):
        return pl.ds(sum(OWN[:level]) * T, OWN[level] * T)

    def x_copy(which, chunk, slot, level, sem):
        start = pl.multiple_of(chunk * chunk_rows // window * window, window)
        src = x_source(which, level).reshape(T * OWN[level], width)
        return pltpu.make_async_copy(
            src.at[:, pl.ds(start, window)], xraw.at[slot, level_slice(level)], sem.at[slot, level]
        )

    pieces = cut_pieces()
    count_pieces = len(pieces)
    held = {}

    def x_load(which, parity, buffer, sem):
        if held.get(id(buffer)) == which:
            return
        held[id(buffer)] = which

        for level in range(RECUR):
            x_copy(which, parity, 0, level, sem).start()

        @pl.loop(0, line)
        def _(i):
            @pl.when(i + 1 < line)
            def _():
                for level in range(RECUR):
                    x_copy(which, 2 * (i + 1) + parity, lax.rem(i + 1, 2), level, sem).start()

            for level in range(RECUR):
                x_copy(which, 2 * i + parity, lax.rem(i, 2), level, sem).wait()
            buffer[i] = xraw[lax.rem(i, 2)].T

    def product(which, start, cols, parity, buffer, j):
        some = buffer[pl.ds(j * JOINT, JOINT)].reshape(JOINT * window, total_rows)
        value = dot(some, y[which][:, start : start + cols], NN).reshape(JOINT, window, cols)
        if window == chunk_rows:
            return value
        window_tmp[:, :, 0:cols] = value
        return window_tmp[:, pl.ds(pl.multiple_of(parity * chunk_rows, chunk_rows), chunk_rows), 0:cols]

    places = []
    for k in range(count_pieces):
        places += [("own", k), ("other", k)] if k < FIRST else [("normal", k)]

    def columns(q):
        return pl.ds(pl.multiple_of(q * PIECE, 128), PIECE)

    def mate_copy(q, i):
        return remote(
            stage.at[lax.rem(q, DEPTH), i], landed.at[i, :, columns(q)], msend.at[q, i], mrecv.at[q, i], p.mate
        )

    def mates(k):
        q = k + FIRST
        if q >= 2 * FIRST + DEPTH:

            @pl.loop(0, line)
            def _(i):
                mate_copy(q - DEPTH, i).wait_send()

        for number, (which, start, cols, inside) in enumerate(pieces[k]):
            x_load(which, 1 - p.b, xm, xsem.at[0])

            last_part = number == len(pieces[k]) - 1

            @pl.loop(0, line // JOINT)
            def _(j):
                value = product(which, start, cols, 1 - p.b, xm, j)
                some = pl.ds(j * JOINT, JOINT)
                stage[q % DEPTH, some, :, inside : inside + cols] = value.astype(BF)
                if last_part:
                    for i in range(JOINT):
                        mate_copy(q, j * JOINT + i).start()

    def own_terms(q):
        kind, k = places[q]
        for number, (which, start, cols, inside) in enumerate(pieces[k]):
            parity = 1 - p.b if kind == "other" else p.b
            buffer, sem = (xm, xsem.at[0]) if kind == "other" else (xl, xsem.at[1])
            x_load(which, parity, buffer, sem)
            at = pl.ds(q * PIECE + inside, cols)

            @pl.loop(0, line // JOINT)
            def _(j):
                value = product(which, start, cols, parity, buffer, j)
                some = pl.ds(j * JOINT, JOINT)
                if kind == "normal":
                    if number == 0:
                        for i in range(JOINT):
                            mate_copy(q, j * JOINT + i).wait_recv()
                    value = value + landed[some, :, at].astype(F32)
                landed[some, :, at] = value.astype(BF)

    def along(q, i, right):
        return remote(
            landed.at[i, :, columns(q)],
            across.at[i, :, columns(q)],
            lsend.at[q, i],
            lrecv.at[q, i],
            p.right if right else p.left,
        )

    def along_last(q, i):
        return remote(
            landed.at[i, :, columns(q)], across_own.at[:, columns(q)], lsend.at[q, i], lrecv2.at[q], p.left
        )

    def relay_step(q, i, receives):
        @pl.when(receives)
        def _():
            along(q, i, True).wait_recv()
            landed[i, :, columns(q)] = (
                landed[i, :, columns(q)].astype(F32) + across[i, :, columns(q)].astype(F32)
            ).astype(BF)

    def relay_pieces(slot):
        q_right = slot - p.a
        q_left = slot - (line - 1 - p.a)

        @pl.when((q_right >= 0) & (q_right < PLACES))
        def _():
            @pl.loop(0, line)
            def _(step):
                i = line - 1 - step

                @pl.when(i > p.a)
                def _():
                    relay_step(q_right, i, p.has_left)
                    along(q_right, i, True).start()

        @pl.when((q_left >= 0) & (q_left < PLACES))
        def _():
            @pl.loop(0, line)
            def _(i):
                @pl.when(i < p.a)
                def _():
                    relay_step(q_left, i, p.has_right)
                    pl.when(i < p.a - 1)(lambda: along(q_left, i, False).start())
                    pl.when(i == p.a - 1)(lambda: along_last(q_left, i).start())

    def last_copy(j):
        return remote(last_stage.at[j], last_landed.at[j], fsend.at[j], frecv.at[j], p.mate)

    staged, turning = [], []

    def line_sum(q, buffer):
        here = pl.ds(q * PIECE, PIECE)
        buffer[...] = landed[p.a, :, here].astype(F32)

        @pl.when(p.has_left)
        def _():
            along(q, p.a, True).wait_recv()
            buffer[...] += across[p.a, :, here].astype(F32)

        @pl.when(p.has_right)
        def _():
            along_last(q, p.a).wait_recv()
            buffer[...] += across_own[:, here].astype(F32)

    def finish(q):
        kind, k = places[q]
        if kind == "own":
            return
        if kind == "other":
            if len(staged) >= 2:
                for copy in staged[len(staged) - 2]:
                    copy.wait()
                staged[len(staged) - 2] = []
            buffer = final.at[len(staged) % 2]
            line_sum(q, buffer)
            last_stage[k] = buffer[...].astype(BF)
            last_copy(k).start()
        else:
            results(q)
        if q >= 3 and places[q - 3][0] == "own":
            results(q - 3)

    def results(q):
        kind, k = places[q]
        number = len(staged)
        if number >= 2:
            for copy in staged[number - 2]:
                copy.wait()
        buffer = final.at[number % 2]
        line_sum(q, buffer)
        if kind == "own":
            last_copy(k).wait_recv()
            buffer[...] += last_landed[k].astype(F32)
            last_copy(k).wait_send()
        copies = []

        def out(src, dst):
            copy = pltpu.make_async_copy(src, dst, finsem.at[k, len(copies)])
            copy.start()
            copies.append(copy)

        for which, start, cols, inside in pieces[k]:
            if which in ("down", "out"):
                for copy in turning:
                    copy.wait()
                turning.clear()
                turned[inside : inside + cols, :] = buffer[:, inside : inside + cols].T
                target = dwd if which == "down" else dwo
                copy = pltpu.make_async_copy(
                    turned.at[pl.ds(inside, cols)], target.at[pl.ds(start, cols)], finsem.at[k, 7]
                )
                copy.start()
                turning.append(copy)
            elif which == "gu":
                middle = min(max(hidden_cols - start, 0), cols)
                if middle:
                    out(buffer.at[:, pl.ds(inside, middle)], dgate.at[:, pl.ds(start, middle)])
                if middle < cols:
                    out(
                        buffer.at[:, pl.ds(inside + middle, cols - middle)],
                        dup.at[:, pl.ds(start + middle - hidden_cols, cols - middle)],
                    )
            else:
                queries = min(max(512 - start, 0), cols)
                if queries:
                    out(buffer.at[:, pl.ds(inside, queries)], dq.at[:, pl.ds(start, queries)])
                if queries < cols:
                    both = buffer[:, inside + queries : inside + queries + 2 * HS].T
                    dk[...] = both[0:HS]
                    dv[...] = both[HS : 2 * HS]
        staged.append(copies)

    def drain():
        @pl.loop(0, PLACES)
        def _(q):
            @pl.loop(0, line)
            def _(i):
                pl.when(q >= max(PLACES - DEPTH, 2 * FIRST))(lambda: mate_copy(q, i).wait_send())
                pl.when(i != p.a)(lambda: along(q, i, True).wait_send())

    loads["grad"].wait()
    present = act_own[0, 0:own, :]
    og[p.t] = (present * grad[...]).astype(BF)
    view = og.reshape(2, 2, own, width)
    rows.gather_start(0, view)
    for level in range(RECUR):
        loads["down", level].wait()
    sent = [FIRST]

    def mates_upto(k):
        while sent[0] <= min(k, count_pieces - 1):
            mates(sent[0])
            sent[0] += 1

    slots = [0]

    def slot():
        s = slots[0]
        slots[0] += 1
        if s < PLACES:
            own_terms(s)
        relay_pieces(s)
        if 0 <= s - line + 1 < PLACES:
            finish(s - line + 1)
        mates_upto(s - FIRST + DEPTH)

    mates(FIRST)
    sent[0] += 1
    slot()
    rows.gather_finish(0, view)
    write(og, og_hbm)
    for level in range(RECUR):
        loads["gu", level].wait()
    mates_upto(FIRST + 2)
    loads["w"].wait()
    loads["qkv"].wait()
    attended_grad = dot(og[...].reshape(count, width), w[:, WO : WO + 512], NN)
    rotated = split_batches(qkv[...].astype(F32), own)
    groups = [share_groups(rotated[b], allowed[b]) for b in range(MB)]
    y["qkv"][0:count, :] = attention_back(
        rotated, groups, attended_grad, cosine[...], sine[...], own, slot
    ).astype(BF)
    slot()

    def attention_tile(cols):
        return dot(y["qkv"][0:count, :], w[cols, QKV : QKV + 640], NT)

    def take(cols, total):
        upstream[:, cols] = total

    rows.reduce(0, own, attention_tile, take)
    loads["hidden"].wait()
    update, add = norm_back(hidden[...], gain[0:1, :], upstream[...])
    grad[...] += update
    gains[...] = gain_in[...]
    gains[0:1, :] += add
    for which in range(3):
        peers_copy(p, grad, grad_all, tsend.at[1], trecv.at[1], which).start()
        peers_copy(p, gains, gpeers, tsend.at[2], trecv.at[2], which).start()
    pltpu.make_async_copy(grad, grad_all.at[p.t], tsend.at[1, 3]).start()
    gpeers[p.t] = gains[...]
    for level in range(RECUR):
        loads["out", level].wait()
    for level in (1, 2):
        loads["qkv", level].wait()
    for copy in writes:
        copy.wait()

    def wait_peers(i, src, dst, local=True):
        for which in range(3):
            copy = peers_copy(p, src, dst, tsend.at[i], trecv.at[i], which)
            copy.wait_recv()
            copy.wait_send()
        if local:
            pltpu.make_async_copy(src, dst.at[p.t], tsend.at[i, 3]).wait()

    def last_branch():
        wait_peers(1, grad, grad_all)
        loads["fin"].wait()
        loads["first"].wait()
        deepest = OWN[2]
        active = act_own[RECUR - 1, 0:deepest, :]

        def fetch(src, dst, i):
            return pltpu.make_async_copy(src, dst, loadsem.at[i])

        def last_tile(cols):
            some = pl.ds(cols.start, DC)
            copies = (
                fetch(w_all.at[some, pl.ds(WD, GU)], w.at[pl.ds(0, DC)], 0),
                fetch(
                    w_all.at[some, pl.ds(WD + GU, hidden_cols - GU)],
                    w.at[pl.ds(DC, DC), pl.ds(0, hidden_cols - GU)],
                    1,
                ),
            )
            for copy in copies:
                copy.start()
            for copy in copies:
                copy.wait()
            left = y["down"][starts[2] : starts[2] + T * deepest, :]
            return dot(left[:, 0:GU], w[0:DC, :], NT) + dot(left[:, GU:], w[DC : 2 * DC, 0 : hidden_cols - GU], NT)

        def last_finish(cols, total):
            fin[0:deepest, cols] = (first[:, cols] + active * total).astype(BF)

        rows.reduce(1, deepest, last_tile, last_finish)
        for which in range(3):
            peers_copy(p, fin, fin_all, tsend.at[0], trecv.at[0], which).start()
        pltpu.make_async_copy(fin, fin_all.at[p.t], tsend.at[0, 3]).start()

    def outputs():
        wait_peers(0, fin, fin_all)
        mine = back[...]

        @pl.loop(0, width // OC)
        def _(c):
            cols = pl.ds(pl.multiple_of(c * OC, OC), OC)
            first = pltpu.make_async_copy(fin_all.at[:, :, cols], fin_chunk, loadsem.at[0])
            second = pltpu.make_async_copy(grad_all.at[:, :, cols], chunk_in, loadsem.at[1])
            first.start()
            second.start()
            first.wait()
            second.wait()
            act_chunk[...] = dot(mine, fin_chunk[...].reshape(count, OC), NN).astype(BF).reshape(
                MB, own // MB, OC
            )
            value = chunk_in[...].reshape(count, OC)
            high = value.astype(BF)
            rest = value - high.astype(F32)
            middle = rest.astype(BF)
            low = (rest - middle.astype(F32)).astype(BF)
            total = dot(mine, high, NN) + (dot(mine, middle, NN) + dot(mine, low, NN))
            tok_chunk[...] = total.reshape(MB, own // MB, OC)
            third = pltpu.make_async_copy(act_chunk, act_out.at[:, :, cols], loadsem.at[0])
            fourth = pltpu.make_async_copy(tok_chunk, tok_out.at[:, :, cols], loadsem.at[1])
            third.start()
            fourth.start()
            third.wait()
            fourth.wait()

    def gain_tile(chunk):
        start = pl.multiple_of(chunk * chunk_rows // window * window, window)
        return (
            gpeers[0, :, pl.ds(start, window)]
            + gpeers[1, :, pl.ds(start, window)]
            + gpeers[2, :, pl.ds(start, window)]
            + gpeers[3, :, pl.ds(start, window)]
        )

    last = PLACES

    def gain_mate(i):
        return remote(gmate_stage.at[i], gmate.at[i], msend.at[last, i], mrecv.at[last, i], p.mate)

    def gain_along(i, right):
        return remote(
            gmate.at[i], gline.at[i], lsend.at[last, i], lrecv.at[last, i], p.right if right else p.left
        )

    def gain_last(i):
        return remote(gmate.at[i], gline_own, lsend.at[last, i], lrecv2.at[last], p.left)

    def gain_mates():
        wait_peers(2, gains, gpeers, False)

        @pl.loop(0, line)
        def _(i):
            gmate_stage[i] = gain_tile(2 * i + 1 - p.b)
            gain_mate(i).start()

    def gain_lines():
        @pl.loop(0, line)
        def _(step):
            odd = lax.rem(step, 2)
            i = jnp.where(odd == 1, step // 2, line - 1 - step // 2)

            @pl.when(i != p.a)
            def _():
                gain_mate(i).wait_recv()
                gmate[i] += gain_tile(2 * i + p.b)

                @pl.when(((i > p.a) & p.has_left) | ((i < p.a) & p.has_right))
                def _():
                    gain_along(i, True).wait_recv()
                    gmate[i] += gline[i]

                pl.when(i > p.a)(lambda: gain_along(i, True).start())
                pl.when(i < p.a - 1)(lambda: gain_along(i, False).start())
                pl.when(i == p.a - 1)(lambda: gain_last(i).start())

        gain_mate(p.a).wait_recv()
        gain_sum[...] = gain_tile(2 * p.a + p.b) + gmate[p.a]

        @pl.when(p.has_left)
        def _():
            gain_along(p.a, True).wait_recv()
            gain_sum[...] += gline[p.a]

        @pl.when(p.has_right)
        def _():
            gain_last(p.a).wait_recv()
            gain_sum[...] += gline_own[...]

        @pl.loop(0, line)
        def _(i):
            gain_mate(i).wait_send()
            pl.when(i != p.a)(lambda: gain_along(i, True).wait_send())

    for s in range(slots[0], PLACES + line - 1):
        slot()
        if s == 5:
            gain_mates()
        if s == 7:
            gain_lines()
        if s == 9:
            last_branch()
        if s == 11:
            outputs()
    drain()
    for copies in staged[-2:] + [turning]:
        for copy in copies:
            copy.wait()


def gradients(n, w_all, gain, tables, saved, bwd, fin):
    width = w_all.shape[0]
    hidden_cols = (COLS - GU) // 3
    line = n // 2
    chunk_rows = width // n
    window = max(128, chunk_rows)
    vmem = pl.BlockSpec(memory_space=pltpu.VMEM)
    hbm = pl.BlockSpec(memory_space=pl.ANY)
    total_rows = T * sum(OWN)
    own = OWN[0]
    operands = [w_all, gain, tables["cosine"], tables["sine"], tables["act"], tables["masks"][0], tables["back"]]
    specs = [hbm] + [vmem] * 6
    operands += [bwd["grad"], bwd["gain_part"], fin, saved[0]["hidden"], saved[0]["qkv"], saved[RECUR - 1]["first"]]
    specs += [hbm, vmem, hbm, hbm, hbm, hbm]
    streams = list(bwd["dg"]) + [s["mixed"] for s in saved] + [s["normed"] for s in saved] + list(bwd["og"])
    streams += [s["prod"] for s in saved] + list(bwd["gug"]) + [s["att"] for s in saved] + list(bwd["qkvg"])
    operands += streams
    specs += [hbm] * len(streams)
    outs = [
        ((MB, own // MB, width), BF),
        ((MB, own // MB, width), F32),
        ((chunk_rows, 512), F32),
        ((HS, chunk_rows), F32),
        ((HS, chunk_rows), F32),
        ((512, chunk_rows), F32),
        ((chunk_rows, hidden_cols), F32),
        ((chunk_rows, hidden_cols), F32),
        ((hidden_cols, chunk_rows), F32),
        ((8, window), F32),
        ((T, own, width), BF),
        ((T, own, width), BF),
        ((T, own, width), F32),
    ]
    out_specs = [hbm, hbm, hbm, vmem, vmem, hbm, hbm, hbm, hbm, vmem, hbm, hbm, hbm]
    scratch = [pltpu.VMEM((width, GU), BF)]
    scratch += [pltpu.VMEM((total_rows, c), BF) for c in (hidden_cols, 2 * hidden_cols, 512, 640)]
    scratch += [pltpu.VMEM((line, window, total_rows), BF)] * 2 + [pltpu.VMEM((2, total_rows, window), BF)]
    scratch += [
        pltpu.VMEM((T, own, width), BF),
        pltpu.VMEM((own, width), F32),
        pltpu.VMEM((T * own, 640), BF),
        pltpu.VMEM((own, width), F32),
        pltpu.VMEM((own, width), F32),
        pltpu.VMEM((8, width), F32),
        pltpu.VMEM((own, width), BF),
        pltpu.VMEM((OWN[2], width), F32),
        pltpu.VMEM((T, 8, width), F32),
    ]
    scratch += [
        pltpu.VMEM((DEPTH, line, chunk_rows, PIECE), BF),
        pltpu.VMEM((line, chunk_rows, PLACES * PIECE), BF),
        pltpu.VMEM((line, chunk_rows, PLACES * PIECE), BF),
        pltpu.VMEM((chunk_rows, PLACES * PIECE), BF),
        pltpu.VMEM((JOINT, window, PIECE) if window > chunk_rows else (1, 8, 128), F32),
    ]
    scratch += [pltpu.VMEM((line, 8, window), F32)] * 3 + [pltpu.VMEM((8, window), F32)]
    scratch += [pltpu.VMEM((2, chunk_rows, PIECE), F32), pltpu.VMEM((PIECE, chunk_rows), F32)]
    scratch += [pltpu.VMEM((FIRST, chunk_rows, PIECE), BF)] * 2
    scratch += [pltpu.SemaphoreType.DMA((FIRST,))] * 2
    scratch += [pltpu.VMEM((T, own, OC), F32), pltpu.VMEM((T, own, OC), BF)]
    scratch += [pltpu.VMEM((MB, own // MB, OC), BF), pltpu.VMEM((MB, own // MB, OC), F32)]
    scratch += [pltpu.VMEM((2, 2, own, width), BF), pltpu.VMEM((own, width), BF)]
    scratch += [pltpu.VMEM((2, own, width), BF), pltpu.VMEM((own, width), BF)]
    dma = pltpu.SemaphoreType.DMA
    chunks = width // DC
    k = PLACES + 1
    scratch += [dma((2, chunks))] * 4 + [dma((2, 3))] * 2
    scratch += [dma((k, line))] * 4 + [dma((k,))]
    scratch += [dma((3, 4)), dma((3, 3))]
    scratch += [dma((24,)), dma((2, 2, RECUR)), dma((4,)), dma((k, 8)), dma((2,))]
    res = pl.pallas_call(
        functools.partial(gradient_kernel, n),
        out_shape=[jax.ShapeDtypeStruct(*entry) for entry in outs],
        in_specs=specs,
        out_specs=out_specs,
        scratch_shapes=scratch,
        compiler_params=pltpu.CompilerParams(
            collective_id=3, has_side_effects=True, vmem_limit_bytes=63 << 20
        ),
    )(*operands)
    return res


def hand_out_kernel(count, *refs):
    held, sems = refs[2 * count : 3 * count], refs[3 * count]
    into = [pltpu.make_async_copy(refs[i], held[i], sems.at[0, i]) for i in range(count)]
    out = [pltpu.make_async_copy(held[i], refs[count + i], sems.at[1, i]) for i in range(count)]
    for copy in into:
        copy.start()
    for i in range(count):
        into[i].wait()
        out[i].start()
    for copy in out:
        copy.wait()


def hand_out(values):
    hbm = pl.BlockSpec(memory_space=pl.ANY)
    count = len(values)
    return pl.pallas_call(
        functools.partial(hand_out_kernel, count),
        out_shape=[jax.ShapeDtypeStruct(v.shape, v.dtype) for v in values],
        in_specs=[hbm] * count,
        out_specs=[hbm] * count,
        scratch_shapes=[pltpu.VMEM(v.shape, v.dtype) for v in values] + [pltpu.SemaphoreType.DMA((2, count))],
        compiler_params=pltpu.CompilerParams(vmem_limit_bytes=62 << 20),
    )(*values)


def shards(n, *args):
    tokens, depth, lengths, cotangent = args[:4]
    attn_gain, mlp_gain = args[11:]
    index = lax.axis_index("tensor")
    w_all, gain, fin, cot_own, last_dg, tables, saved = forward(
        n, tokens, depth, lengths[:, 0], cotangent, args[4:11], attn_gain, mlp_gain
    )
    bwd = backward(n, w_all, gain, cot_own, tables, saved)
    bwd["dg"] = list(bwd["dg"]) + [last_dg]
    bwd["gug"] = list(bwd["gug"]) + [saved[RECUR - 1]["gu"]]
    res = gradients(n, w_all, gain, tables, saved, bwd, fin)
    gain_sum = res[9]
    activations, tokens_grad, dq, dk, dv, dwo, dgate, dup, dwd = hand_out(res[:9])
    each = attn_gain.shape[0]
    window = gain_sum.shape[1]
    start = lax.rem((lax.axis_index("dp") * T + index) * each, window)
    both = lax.dynamic_slice_in_dim(gain_sum, start, each, axis=1)
    return (activations, tokens_grad, dq, dk.T, dv.T, dwo, dgate, dup, dwd, both[0], both[1])


def solution(mesh):
    rows = P(None, ("dp", "tensor"), None)
    weight_specs = (P("dp", "tensor"),) * 3 + (P("tensor", "dp"),) + (P("dp", "tensor"),) * 2 + (P("tensor", "dp"),)
    gain_specs = (P(("dp", "tensor")),) * 2
    return jax.shard_map(
        functools.partial(shards, mesh.shape["dp"]),
        mesh=mesh,
        in_specs=(rows, P(None, "dp"), P(None, "dp", None), rows) + weight_specs + gain_specs,
        out_specs=(rows, rows) + weight_specs + gain_specs,
        check_vma=False,
    )
```

```python
import functools

import jax
import jax.numpy as jnp
import numpy as np
from jax import lax
from jax.experimental import pallas as pl
from jax.experimental.pallas import tpu as pltpu
from jax.sharding import PartitionSpec as P

HQ = 32
KVH = 4
HS = 64
MB = 2
RECUR = 3
SCALE = HS ** (-0.5)
F32 = jnp.float32
BF = jnp.bfloat16
MESH = pl.DeviceIdType.MESH
NN = (((1,), (0,)), ((), ()))
NT = (((1,), (1,)), ((), ()))
TN = (((0,), (0,)), ((), ()))

OWN = (96, 80, 48)
PIECES = ((0, 24, 0), (24, 24, 1), (48, 16, 0), (64, 16, 1), (80, 8, 0), (88, 8, 1))
T = 4
DC = 512
OC = 256
HEADS = 2


def split_batches(values, own):
    halves = ([], [])
    for owner in range(T):
        for start, rows, b in PIECES:
            if start < own:
                halves[b].append(values[owner * own + start : owner * own + start + rows])
    return [jnp.concatenate(half, axis=0) for half in halves]


def join_batches(halves, own):
    rows_out, at = [], [0, 0]
    for owner in range(T):
        for start, rows, b in PIECES:
            if start < own:
                rows_out.append(halves[b][at[b] : at[b] + rows])
                at[b] += rows
    return jnp.concatenate(rows_out, axis=0)


def dot(left, right, dims):
    return lax.dot_general(left, right, dims, preferred_element_type=F32)


def swap_halves(tile):
    lane = lax.broadcasted_iota(jnp.int32, tile.shape, 1)
    return jnp.where((lane & 63) < 32, pltpu.roll(tile, 96, 1), pltpu.roll(tile, 32, 1))


def attention_shares(query, key, allowed):
    rows = query.shape[0]
    group = query.shape[1] // HS
    stacked = stack_heads(query)
    scores = dot(stacked, key, NT).reshape(group, rows, rows) * SCALE
    scores = jnp.where(allowed.astype(F32)[None] > 0, scores, -1e30)
    raised = jnp.exp(scores - jnp.max(scores, axis=-1, keepdims=True))
    return stacked, raised * (1.0 / jnp.sum(raised, axis=-1, keepdims=True))


def stack_heads(values):
    group = values.shape[1] // HS
    return jnp.concatenate([values[:, h * HS : (h + 1) * HS] for h in range(group)], axis=0)


def unstack_heads(values, rows):
    group = values.shape[0] // rows
    return jnp.concatenate([values[h * rows : (h + 1) * rows] for h in range(group)], axis=1)


def mean_square(values):
    return jnp.mean(values * values, axis=-1, keepdims=True)


class Place:
    def __init__(self, n):
        self.n = n
        self.line = n // 2
        self.dp = lax.axis_index("dp")
        self.t = lax.axis_index("tensor")
        self.a = self.dp // 2
        self.b = lax.rem(self.dp, 2)
        self.hi = self.t // 2
        self.lo = lax.rem(self.t, 2)
        self.has_right = self.a < self.line - 1
        self.has_left = self.a > 0
        self.mate = (self.a * 2 + 1 - self.b, self.t)
        self.right = (jnp.minimum(self.dp + 2, n - 1), self.t)
        self.left = (jnp.maximum(self.dp - 2, 0), self.t)
        self.near = (self.dp, self.hi * 2 + 1 - self.lo)
        self.far = (self.dp, (1 - self.hi) * 2 + self.lo)
        self.diag = (self.dp, (1 - self.hi) * 2 + 1 - self.lo)

    def barrier(self, along):
        sem = pltpu.get_barrier_semaphore()

        def greet(device):
            pl.semaphore_signal(sem, inc=1, device_id=device, device_id_type=MESH)

        for device in (self.near, self.far, self.diag):
            greet(device)
        expected = 3
        if along:
            greet(self.mate)
            pl.when(self.has_right)(lambda: greet(self.right))
            pl.when(self.has_left)(lambda: greet(self.left))
            expected = 4 + self.has_right.astype(jnp.int32) + self.has_left.astype(jnp.int32)
        pl.semaphore_wait(sem, expected)


def remote(src, dst, send, recv, device):
    return pltpu.make_async_remote_copy(
        src_ref=src, dst_ref=dst, send_sem=send, recv_sem=recv, device_id=device, device_id_type=MESH
    )


class LineGather:
    def __init__(self, place, pieces, sems):
        self.p = place
        self.pieces = pieces
        self.msend, self.mrecv, self.rsend, self.rrecv, self.lsend, self.lrecv = sems

    def toward_left(self, w, k, chunk):
        ref = self.pieces[w][1](chunk)
        return remote(ref, ref, self.lsend.at[w, k], self.lrecv.at[w, k], self.p.left)

    def toward_right(self, w, k, chunk):
        ref = self.pieces[w][1](chunk)
        return remote(ref, ref, self.rsend.at[w, k], self.rrecv.at[w, k], self.p.right)

    def toward_mate(self, w, k, chunk):
        ref = self.pieces[w][1](chunk)
        return remote(ref, ref, self.msend.at[w, k], self.mrecv.at[w, k], self.p.mate)

    def first(self, w):
        p = self.p
        return p.a * 2 + 1 - p.b if self.pieces[w][0] == "other" else p.dp

    def own(self, w):
        p = self.p
        kind = self.pieces[w][0]
        chunk = self.first(w)
        if kind == "other":
            self.toward_mate(w - 1, p.a, chunk).wait_recv()
        pl.when(p.has_left)(lambda: self.toward_left(w, 0, chunk).start())
        pl.when(p.has_right)(lambda: self.toward_right(w, 0, chunk).start())
        if kind != "other":
            self.toward_mate(w, p.a, chunk).start()

    def step(self, w, k):
        p = self.p
        normal = self.pieces[w][0] == "normal"

        @pl.when(p.a + k < p.line)
        def _():
            chunk = self.first(w) + 2 * k
            self.toward_left(w, k - 1, chunk).wait_recv()
            pl.when(p.has_left)(lambda: self.toward_left(w, k, chunk).start())
            if normal:
                self.toward_mate(w, p.a + k, chunk).start()

        @pl.when(p.a - k >= 0)
        def _():
            chunk = self.first(w) - 2 * k
            self.toward_right(w, k - 1, chunk).wait_recv()
            pl.when(p.has_right)(lambda: self.toward_right(w, k, chunk).start())
            if normal:
                self.toward_mate(w, p.a - k, chunk).start()

    def steps(self, w):
        for k in range(1, self.p.line):
            self.step(w, k)

    def arrive(self, w):
        p = self.p
        if self.pieces[w][0] == "normal":
            for i in range(p.line):
                self.toward_mate(w, i, 2 * i + 1 - p.b).wait_recv()

    def drain(self, w):
        p = self.p
        kind = self.pieces[w][0]
        if kind == "own":
            self.toward_mate(w, p.a, p.dp).wait_send()
        for i in range(p.line):
            if kind == "normal":
                self.toward_mate(w, i, p.dp).wait_send()
            pl.when(p.has_left & (p.a + i < p.line))(lambda: self.toward_left(w, i, p.dp).wait_send())
            pl.when(p.has_right & (p.a - i >= 0))(lambda: self.toward_right(w, i, p.dp).wait_send())


class Rows:
    def __init__(self, place, part, relay, sums, sems):
        self.p = place
        self.part, self.relay, self.sums = part, relay, sums
        self.s1, self.q1, self.s2, self.q2, self.gs, self.gr = sems

    def first_copy(self, i, own, c):
        p = self.p
        cols = pl.ds(pl.multiple_of(c * DC, DC), DC)
        return remote(
            self.part.at[:, 1 - p.lo, pl.ds(0, own), cols],
            self.sums[i][0].at[:, pl.ds(0, own), cols],
            self.s1.at[i, c],
            self.q1.at[i, c],
            p.near,
        )

    def second_copy(self, i, own, c):
        p = self.p
        cols = pl.ds(pl.multiple_of(c * DC, DC), DC)
        return remote(
            self.relay.at[pl.ds(0, own), cols],
            self.sums[i][1].at[pl.ds(0, own), cols],
            self.s2.at[i, c],
            self.q2.at[i, c],
            p.far,
        )

    def reduce(self, i, own, tile, finish):
        p = self.p
        part, relay = self.part, self.relay
        r1, r2 = self.sums[i]
        chunks = part.shape[-1] // DC

        def pass_on(c):
            cols = pl.ds(pl.multiple_of(c * DC, DC), DC)
            self.first_copy(i, own, c).wait_recv()
            mine = part[1 - p.hi, p.lo, 0:own, cols].astype(F32)
            relay[0:own, cols] = (mine + r1[1 - p.hi, 0:own, cols].astype(F32)).astype(BF)
            self.second_copy(i, own, c).start()

        @pl.loop(0, chunks)
        def _(c):
            cols = pl.ds(pl.multiple_of(c * DC, DC), DC)
            part[:, :, 0:own, cols] = tile(cols).astype(BF).reshape(2, 2, own, DC)
            self.first_copy(i, own, c).start()
            pl.when(c > 0)(lambda: pass_on(c - 1))

        pass_on(chunks - 1)

        @pl.loop(0, chunks)
        def _(c):
            cols = pl.ds(pl.multiple_of(c * DC, DC), DC)
            self.second_copy(i, own, c).wait_recv()
            mine = part[p.hi, p.lo, 0:own, cols].astype(F32)
            finish(cols, mine + r1[p.hi, 0:own, cols].astype(F32) + r2[0:own, cols].astype(F32))

        @pl.loop(0, chunks)
        def _(c):
            self.first_copy(i, own, c).wait_send()
            self.second_copy(i, own, c).wait_send()

    def gather_copy(self, i, buffer, which):
        p = self.p
        here = buffer.at[p.hi, p.lo]
        if which == 0:
            return remote(here, here, self.gs.at[i, 0], self.gr.at[i, 0], p.far)
        if which == 1:
            return remote(here, here, self.gs.at[i, 1], self.gr.at[i, 1], p.near)
        there = buffer.at[1 - p.hi, p.lo]
        return remote(there, there, self.gs.at[i, 2], self.gr.at[i, 2], p.near)

    def gather_start(self, i, buffer):
        self.gather_copy(i, buffer, 0).start()
        self.gather_copy(i, buffer, 1).start()

    def gather_finish(self, i, buffer):
        self.gather_copy(i, buffer, 0).wait_recv()
        self.gather_copy(i, buffer, 2).start()
        self.gather_copy(i, buffer, 1).wait_recv()
        self.gather_copy(i, buffer, 2).wait_recv()
        for which in range(3):
            self.gather_copy(i, buffer, which).wait_send()


def peers_copy(place, src, dst, send, recv, which):
    device = (place.near, place.far, place.diag)[which]
    return remote(src, dst.at[place.t], send.at[which], recv.at[which], device)


def gain_row(gathered, n, row, width):
    each = width // (n * T)
    tiles = []
    for j in range(width // 128):
        total = None
        for i in range(128 // each):
            number = j * (128 // each) + i
            block = gathered[number % T, number // T][row : row + 1]
            total = block if total is None else total + block
        tiles.append(total)
    return jnp.concatenate(tiles, axis=1)


QKV, WO, GU, WD = 0, 640, 1152, 3968
COLS = 5376
RANGES = (
    ("along", 0, 640),
    ("along", 640, 512),
    ("along", 1152, 1408),
    ("along", 2560, 1408),
    ("along", 3968, 512),
    ("across", 4480, 896),
)


def ones(condition):
    return jnp.where(condition, 1.0, 0.0)


def iota(size, axis):
    shape = (size, 1) if axis == 0 else (1, size)
    return lax.broadcasted_iota(jnp.int32, shape, axis).astype(F32)


def quotient(index, step, most):
    total = ones(index >= step)
    for i in range(2, most):
        total = total + ones(index >= step * i)
    return total


def own_places(own_index):
    batch, place, seen = 0.0 * own_index, 0.0 * own_index, [0, 0]
    for start, rows, b in PIECES:
        inside = (own_index >= start) & (own_index < start + rows)
        batch = jnp.where(inside, float(b), batch)
        place = jnp.where(inside, own_index - start + seen[b], place)
        seen[b] += rows
    return batch, place


def fill_tables(p, depth_row, depth_col, lengths, freqs, perm, back, back_own, cosine, sine, allowed, act_own, act_last):
    local = OWN[0] // MB
    total = T * OWN[0]

    def columns(index):
        tensor = quotient(index, OWN[0], T)
        inside = index - tensor * OWN[0]
        batch = ones(inside >= local)
        return batch, tensor * local + inside - batch * local

    batch_row, pos_row = columns(iota(total, 1))
    batch_col, pos_col = columns(iota(total, 0))
    same = batch_row == batch_col
    rank_row = jnp.sum(
        ones(same & ((depth_col > depth_row) | ((depth_col == depth_row) & (pos_col < pos_row)))), axis=0, keepdims=True
    )
    rank_col = jnp.sum(
        ones(same & ((depth_row > depth_col) | ((depth_row == depth_col) & (pos_row < pos_col)))), axis=1, keepdims=True
    )

    def compact(index):
        owner = quotient(index, OWN[0], T)
        batch, place = own_places(index - owner * OWN[0])
        return batch, place * T + owner

    batch_q, rank_q = compact(iota(total, 0))
    hit = (rank_row == rank_q) & (batch_row == batch_q)
    perm[...] = ones(hit).astype(BF)
    batch_p, rank_p = compact(iota(total, 1))
    back[...] = ones((rank_col == rank_p) & (batch_col == batch_p)).astype(BF)
    back_own[...] = back[pl.ds(pl.multiple_of(p.t * OWN[0], OWN[0]), OWN[0]), :]

    ends = []
    for b in range(MB):
        first = lengths[b : b + 1, 0:1].astype(F32)
        ends.append((first, first + lengths[b : b + 1, 1:2].astype(F32)))
    position = jnp.sum(jnp.where(hit, pos_row, 0.0), axis=1, keepdims=True)
    end = [jnp.where(batch_q == 0.0, ends[0][i], ends[1][i]) for i in range(2)]
    start = jnp.where(position >= end[1], end[1], jnp.where(position >= end[0], end[0], 0.0))
    angles = (position - start) * freqs
    cosine[...] = jnp.cos(angles)
    lane = lax.broadcasted_iota(jnp.int32, angles.shape, 1)
    value = jnp.sin(angles)
    sine[...] = jnp.where((lane & 63) < 32, -value, value)

    own_batch, own_place = own_places(iota(OWN[0], 0))
    own_rank = own_place * T + p.t.astype(F32)
    for level in range(RECUR):
        own = OWN[level]
        half = T * own // MB
        counts = [
            jnp.sum(ones((batch_row == float(b)) & (depth_row >= level + 1.0)), axis=1, keepdims=True) for b in range(MB)
        ]
        act_own[level] = ones(own_rank < jnp.where(own_batch == 0.0, counts[0], counts[1]))
        if level == RECUR - 1:
            index = iota(T * own, 0)
            owner = quotient(index, own, T)
            batch, place = own_places(index - owner * own)
            act_last[...] = ones(place * T + owner < jnp.where(batch == 0.0, counts[0], counts[1]))

        def order(index):
            owner = quotient(index, own // MB, T)
            return (index - owner * (own // MB)) * T + owner

        index_col, index_row = iota(half, 0), iota(half, 1)
        order_col, order_row = order(index_col), order(index_row)
        for b in range(MB):
            at_col = jnp.sum(
                jnp.where((rank_row == order_col) & (batch_row == float(b)), pos_row, 0.0), axis=1, keepdims=True
            )
            at_row = jnp.sum(
                jnp.where((rank_col == order_row) & (batch_col == float(b)), pos_col, 0.0), axis=0, keepdims=True
            )
            document_col = ones(at_col >= ends[b][0]) + ones(at_col >= ends[b][1])
            document_row = ones(at_row >= ends[b][0]) + ones(at_row >= ends[b][1])
            ok = (document_col == document_row) & (at_row <= at_col) & (order_row < counts[b])
            allowed[level][b] = ones(ok | (index_col == index_row)).astype(BF)


def forward_kernel(n, *refs):
    it = iter(refs)
    tokens, cotangent, wq, wk, wv, wo, wg, wu, wd = [next(it) for _ in range(9)]
    attn_gain, mlp_gain, depth_row, depth_col, lengths, freqs = [next(it) for _ in range(6)]
    w_out, gain_out, fin_out, cot_own, cot_all = [next(it) for _ in range(5)]
    cosine, sine, back_own, act_own, act_last = [next(it) for _ in range(5)]
    allowed = [next(it) for _ in range(RECUR)]
    names = ("normed", "qkv", "att", "mixed", "gu", "prod", "hidden", "first")
    saved_out = [dict((k, next(it)) for k in names) for _ in range(RECUR)]
    dg_out = next(it)
    w = next(it)
    dg, product_grad = next(it), next(it)
    perm, back, kv, wo_in, wd_in = [next(it) for _ in range(5)]
    gbuf, gall = next(it), next(it)
    tok, cot = next(it), next(it)
    saved = [dict((k, next(it)) for k in names) for _ in range(RECUR)]
    after, fin, cown = next(it), next(it), next(it)
    part, relay = next(it), next(it)
    sums = [(next(it), next(it)) for _ in range(2 * RECUR - 1)]
    line_sems = [next(it) for _ in range(6)]
    row_sems = [next(it) for _ in range(6)]
    wsem = next(it)
    tsend, trecv, outsem = next(it), next(it), next(it)

    p = Place(n)
    width = tokens.shape[-1]
    rows_chunk = width // n

    def chunk_at(chunk, start, size):
        return w.at[pl.ds(pl.multiple_of(chunk * rows_chunk, rows_chunk), rows_chunk), pl.ds(start, size)]

    pieces = [("normal", lambda chunk: gbuf.at[chunk])]
    number = []
    for kind, start, size in RANGES:
        def at(chunk, start=start, size=size):
            return chunk_at(chunk, start, size)

        number.append(len(pieces))
        pieces += [("own", at), ("other", at)] if kind == "across" else [("normal", at)]
    line = LineGather(p, pieces, line_sems)
    rows = Rows(p, part, relay, sums, row_sems)
    hidden_cols = (COLS - GU) // 3
    writes = []

    def write(src, dst):
        copy = pltpu.make_async_copy(src, dst, outsem.at[len(writes)])
        copy.start()
        writes.append(copy)

    local = [
        pltpu.make_async_copy(wq, chunk_at(p.dp, QKV, 512), wsem.at[0]),
        pltpu.make_async_copy(wk, kv.at[0], wsem.at[1]),
        pltpu.make_async_copy(wv, kv.at[1], wsem.at[2]),
        pltpu.make_async_copy(wo, wo_in, wsem.at[3]),
        pltpu.make_async_copy(wg, chunk_at(p.dp, GU, hidden_cols), wsem.at[4]),
        pltpu.make_async_copy(wu, chunk_at(p.dp, GU + hidden_cols, hidden_cols), wsem.at[5]),
        pltpu.make_async_copy(wd, wd_in, wsem.at[6]),
    ]
    for copy in local:
        copy.start()
    mine_rows = pl.ds(pl.multiple_of(p.dp * rows_chunk, rows_chunk), rows_chunk)
    each = attn_gain.shape[1]
    lane = lax.broadcasted_iota(jnp.int32, (1, 128), 1)
    spot = lax.rem(p.dp * T + p.t, 128 // each)
    inside = (lane >= spot * each) & (lane < (spot + 1) * each)
    for row, gain in enumerate((attn_gain, mlp_gain)):
        value = jnp.concatenate([gain[...]] * (128 // each), axis=1)
        gbuf[p.dp, row : row + 1, :] = jnp.where(inside, value, 0.0)
    gbuf[p.dp, 2:8, :] = jnp.zeros((6, 128), F32)
    p.barrier(True)
    line.own(0)
    for copy in local[0:3]:
        copy.wait()
    w[mine_rows, QKV + 512 : QKV + 640] = jnp.concatenate([kv[0], kv[1]], axis=0).T
    heads_piece, out_piece, gate_piece, up_piece, down_piece, down_last = number
    line.own(heads_piece)
    for which in range(3):
        peers_copy(p, tokens, tok, tsend.at[0], trecv.at[0], which).start()
    pltpu.make_async_copy(tokens, tok.at[p.t], tsend.at[0, 3]).start()
    local[3].wait()
    w[mine_rows, WO : WO + 512] = wo_in[...].T
    line.own(out_piece)
    for which in range(3):
        peers_copy(p, cotangent, cot, tsend.at[1], trecv.at[1], which).start()
    pltpu.make_async_copy(cotangent, cot.at[p.t], tsend.at[1, 3]).start()
    for copy in local[4:6]:
        copy.wait()
    line.own(gate_piece)
    line.steps(0)
    line.arrive(0)
    for which in range(3):
        peers_copy(p, gbuf, gall, tsend.at[2], trecv.at[2], which).start()
    pltpu.make_async_copy(gbuf, gall.at[p.t], tsend.at[2, 3]).start()
    fill_tables(
        p, depth_row[...], depth_col[...], lengths, freqs[...], perm, back, back_own, cosine, sine, allowed, act_own, act_last
    )
    line.steps(heads_piece)
    local[6].wait()
    w[mine_rows, WD : WD + hidden_cols] = wd_in[...].T
    line.own(up_piece)
    line.steps(out_piece)

    def wait_peers(i, src, dst):
        for which in range(3):
            copy = peers_copy(p, src, dst, tsend.at[i], trecv.at[i], which)
            copy.wait_recv()
            copy.wait_send()
        pltpu.make_async_copy(src, dst.at[p.t], tsend.at[i, 3]).wait()

    wait_peers(2, gbuf, gall)
    gain_out[0:1, :] = gain_row(gall, n, 0, width)
    gain_out[1:2, :] = gain_row(gall, n, 1, width)
    gain_out[2:8, :] = jnp.zeros((6, width), F32)

    wait_peers(0, tokens, tok)

    own = OWN[0]
    mine = perm[pl.ds(pl.multiple_of(p.t * own, own), own), :]
    saved[0]["hidden"][...] = dot(mine, tok[...].reshape(T * own, width), NN)

    @pl.loop(0, T)
    def _(owner):
        picked = perm[pl.ds(pl.multiple_of(owner * own, own), own), :]
        hidden = dot(picked, tok[...].reshape(T * own, width), NN)
        inverse = lax.rsqrt(mean_square(hidden) + 1e-05)
        saved[0]["normed"][owner] = (hidden * inverse * gain_out[0:1, :]).astype(BF)

    wait_peers(1, cotangent, cot)
    cown[...] = dot(mine, cot[...].reshape(T * own, width), NN)
    write(cown, cot_own)

    line.own(down_piece)
    line.own(down_last)

    @pl.loop(0, T)
    def _(owner):
        picked = perm[pl.ds(pl.multiple_of(owner * OWN[0], 32), OWN[RECUR - 1]), :]
        cot_all[owner] = dot(picked, cot[...].reshape(T * OWN[0], width), NN).astype(BF)

    line.arrive(heads_piece)

    for level in range(RECUR):
        own = OWN[level]
        count = T * own
        half = count // 2
        s = saved[level]
        if level:
            rows.gather_finish(2 * level - 1, s["normed"].reshape(2, 2, own, width))
        x = s["normed"][...].reshape(count, width)
        qkv = dot(x, w[:, QKV : QKV + 640], NN)
        cos = jnp.concatenate([cosine[owner * OWN[0] : owner * OWN[0] + own, :] for owner in range(T)], axis=0)
        sin = jnp.concatenate([sine[owner * OWN[0] : owner * OWN[0] + own, :] for owner in range(T)], axis=0)
        tiles = []
        for j in range(5):
            tile = qkv[:, j * 128 : (j + 1) * 128]
            turned = tile * cos + swap_halves(tile) * sin
            if j == 4:
                lane = lax.broadcasted_iota(jnp.int32, tile.shape, 1)
                turned = jnp.where(lane < HS, turned, tile)
            tiles.append(turned)
        rotated = jnp.concatenate(tiles, axis=1)
        s["qkv"][...] = rotated.astype(BF)
        write(s["qkv"], saved_out[level]["qkv"])
        heads = []
        for b, block in enumerate(split_batches(rotated, own)):
            query, key, value = (
                block[:, 0:512].astype(BF),
                block[:, 512:576].astype(BF),
                block[:, 576:640].astype(BF),
            )
            _, shares = attention_shares(query, key, allowed[level][b])
            out = dot(shares.astype(BF).reshape(8 * half, half), value, NN)
            heads.append(unstack_heads(out, half))
            if level == 0:
                line.step(gate_piece, 1) if b == 0 else [line.step(gate_piece, k) for k in range(2, p.line)]
        s["att"][...] = join_batches(heads, own).astype(BF)
        write(s["att"], saved_out[level]["att"])
        if level == 0:
            line.arrive(out_piece)
        present = act_own[level, 0:own, :]

        def attention_tile(cols):
            return dot(s["att"][...], w[cols, WO : WO + 512], NT)

        def attention_finish(cols, total):
            s["first"][:, cols] = s["hidden"][:, cols] + present * total

        rows.reduce(2 * level, own, attention_tile, attention_finish)
        first = s["first"][...]
        inverse = lax.rsqrt(mean_square(first) + 1e-05)
        s["mixed"][p.t] = (first * inverse * gain_out[1:2, :]).astype(BF)
        mixed = s["mixed"].reshape(2, 2, own, width)
        rows.gather_start(2 * level, mixed)
        write(s["first"], saved_out[level]["first"])
        if level == 0:
            line.steps(up_piece)
            line.own(down_last + 1)
        if level == RECUR - 1:
            dg[...] = (cot_all[...].astype(F32).reshape(count, width) * act_last[...]).astype(BF).reshape(T, own, width)
            write(dg, dg_out)

            def grad_block(start, size):
                product_grad[:, pl.ds(pl.multiple_of(start, 128), size)] = dot(
                    dg[...].reshape(count, width), w[:, pl.ds(pl.multiple_of(WD + start, 128), size)], NN
                )

            @pl.loop(0, hidden_cols // 256)
            def _(j):
                grad_block(j * 256, 256)

            if hidden_cols % 256:
                grad_block(hidden_cols // 256 * 256, 128)
        rows.gather_finish(2 * level, mixed)
        write(s["mixed"], saved_out[level]["mixed"])

        def hidden_block(start, size):
            x = s["mixed"][...].reshape(count, width)
            gate = dot(x, w[:, pl.ds(pl.multiple_of(GU + start, 128), size)], NN)
            upward = dot(x, w[:, pl.ds(pl.multiple_of(GU + hidden_cols + start, 128), size)], NN)
            cols = pl.ds(pl.multiple_of(start, 128), size)
            high = pl.ds(pl.multiple_of(hidden_cols + start, 128), size)
            sigma = jax.nn.sigmoid(gate)
            s["prod"][:, cols] = (gate * sigma * upward).astype(BF)
            if level == RECUR - 1:
                up = product_grad[:, cols]
                s["gu"][:, cols] = (up * upward * sigma * (1.0 + gate * (1.0 - sigma))).astype(BF)
                s["gu"][:, high] = (up * gate * sigma).astype(BF)
            else:
                s["gu"][:, cols] = gate.astype(BF)
                s["gu"][:, high] = upward.astype(BF)

        if level == 0:
            line.steps(down_piece)
            line.step(down_last, 1)
            line.step(down_last + 1, 1)
            line.arrive(gate_piece)
            line.arrive(up_piece)
            write(w.at[:, pl.ds(0, WD)], w_out.at[:, pl.ds(0, WD)])

        @pl.loop(0, hidden_cols // 256)
        def _(j):
            hidden_block(j * 256, 256)

        if hidden_cols % 256:
            hidden_block(hidden_cols // 256 * 256, 128)
        write(s["gu"], saved_out[level]["gu"])
        write(s["prod"], saved_out[level]["prod"])
        if level == 0:
            for k in range(2, p.line):
                line.step(down_last, k)
                line.step(down_last + 1, k)
            line.arrive(down_piece)
            write(w.at[:, pl.ds(WD, hidden_cols)], w_out.at[:, pl.ds(WD, hidden_cols)])

        if level < RECUR - 1:

            def mlp_tile(cols):
                return dot(s["prod"][...], w[cols, WD : WD + 1408], NT)

            def mlp_finish(cols, total):
                after[0:own, cols] = s["first"][:, cols] + present * total

            rows.reduce(2 * level + 1, own, mlp_tile, mlp_finish)
            deeper = OWN[level + 1]
            hidden = after[0:deeper, :]
            saved[level + 1]["hidden"][...] = hidden
            inverse = lax.rsqrt(mean_square(hidden) + 1e-05)
            saved[level + 1]["normed"][p.t] = (hidden * inverse * gain_out[0:1, :]).astype(BF)
            rows.gather_start(2 * level + 1, saved[level + 1]["normed"].reshape(2, 2, deeper, width))
            fin[deeper:own, :] = after[deeper:own, :].astype(BF)

        write(s["hidden"], saved_out[level]["hidden"])
        write(s["normed"], saved_out[level]["normed"])
    fin[0 : OWN[2], :] = jnp.zeros((OWN[2], width), BF)
    write(fin, fin_out)
    for i in range(len(pieces)):
        line.drain(i)
    for copy in writes:
        copy.wait()


def forward(n, tokens, depth, lengths, cotangent, weights, attn_gain, mlp_gain):
    width = tokens.shape[-1]
    hidden_cols = weights[4].shape[1]
    local = OWN[0] // MB
    total = T * OWN[0]
    ordered = depth.reshape(MB, T, local).transpose(1, 0, 2).astype(F32)
    freqs = jnp.asarray(np.tile(10000.0 ** (-np.arange(0, HS, 2) / HS), 4)[None].astype(np.float32))
    vmem = pl.BlockSpec(memory_space=pltpu.VMEM)
    hbm = pl.BlockSpec(memory_space=pl.ANY)

    def saved_shapes(own):
        count = T * own
        return {
            "normed": ((T, own, width), BF),
            "qkv": ((count, 640), BF),
            "att": ((count, 512), BF),
            "mixed": ((T, own, width), BF),
            "gu": ((count, 2 * hidden_cols), BF),
            "prod": ((count, hidden_cols), BF),
            "hidden": ((own, width), F32),
            "first": ((own, width), F32),
        }

    shapes = [((width, COLS), BF), ((8, width), F32), ((OWN[0], width), BF), ((OWN[0], width), F32), ((T, OWN[2], width), BF)]
    specs = [hbm, vmem, hbm, hbm, vmem]
    shapes += [((total, 128), F32)] * 2 + [((OWN[0], total), BF), ((RECUR, OWN[0], 1), F32), ((T * OWN[2], 1), F32)]
    shapes += [((MB, T * own // MB, T * own // MB), BF) for own in OWN]
    specs += [vmem] * (5 + RECUR)
    for own in OWN:
        for entry in saved_shapes(own).values():
            shapes.append(entry)
            specs.append(hbm)
    shapes.append(((T, OWN[2], width), BF))
    specs.append(hbm)
    scratch = [pltpu.VMEM((width, COLS), BF), pltpu.VMEM((T, OWN[2], width), BF), pltpu.VMEM((T * OWN[2], hidden_cols), F32)]
    scratch += [pltpu.VMEM((total, total), BF)] * 2
    scratch += [pltpu.VMEM((2,) + weights[1].shape[::-1], BF), pltpu.VMEM(weights[3].shape, BF), pltpu.VMEM(weights[6].shape, BF)]
    scratch += [pltpu.VMEM((n, 8, 128), F32), pltpu.VMEM((T, n, 8, 128), F32)]
    scratch += [pltpu.VMEM((T,) + tokens.shape, BF)] * 2
    for own in OWN:
        scratch += [pltpu.VMEM(*entry) for entry in saved_shapes(own).values()]
    scratch += [pltpu.VMEM((OWN[0], width), F32), pltpu.VMEM((OWN[0], width), BF), pltpu.VMEM((OWN[0], width), F32)]
    scratch += [pltpu.VMEM((2, 2, OWN[0], width), BF), pltpu.VMEM((OWN[0], width), BF)]
    for own in [own for own in OWN for _ in range(2)][:-1]:
        scratch += [pltpu.VMEM((2, own, width), BF), pltpu.VMEM((own, width), BF)]
    dma = pltpu.SemaphoreType.DMA
    count = 1 + sum(2 if kind == "across" else 1 for kind, _, _ in RANGES)
    scratch += [dma((count, n // 2))] * 6
    chunks = width // DC
    scratch += [dma((2 * RECUR, chunks))] * 4 + [dma((2 * RECUR, 3))] * 2
    scratch += [dma((7,)), dma((3, 4)), dma((3, 3)), dma((40,))]
    outs = pl.pallas_call(
        functools.partial(forward_kernel, n),
        out_shape=[jax.ShapeDtypeStruct(*entry) for entry in shapes],
        in_specs=[hbm] * 9 + [vmem] * 6,
        out_specs=specs,
        scratch_shapes=scratch,
        compiler_params=pltpu.CompilerParams(
            collective_id=1, has_side_effects=True, vmem_limit_bytes=62 << 20
        ),
    )(
        tokens,
        cotangent,
        weights[0],
        weights[1].T,
        weights[2].T,
        *weights[3:],
        attn_gain[None],
        mlp_gain[None],
        ordered.reshape(1, total),
        ordered.reshape(total, 1),
        lengths,
        freqs,
    )
    w_all, gain, fin, cot_own = outs[:4]
    tables = dict(zip(("cosine", "sine", "back", "act", "act_last"), outs[5:10]))
    tables["masks"] = outs[10:13]
    names = list(saved_shapes(1))
    saved = [dict(zip(names, outs[13 + 8 * level : 21 + 8 * level])) for level in range(RECUR)]
    return w_all, gain, fin, cot_own, outs[37], tables, saved


def share_groups(block, allowed):
    query, key = block[:, 0:512].astype(BF), block[:, 512:576].astype(BF)
    for start in range(0, 512, HEADS * HS):
        yield (start,) + attention_shares(query[:, start : start + HEADS * HS], key, allowed)


def attention_back(rotated, groups, attended_grad, cos, sin, own, between=None):
    half = T * own // 2
    grads = []
    upstream = split_batches(attended_grad, own)
    for b in range(MB):
        key, value = rotated[b][:, 512:576].astype(BF), rotated[b][:, 576:640].astype(BF)
        up_all = upstream[b].astype(BF)
        query_grads, key_grad, value_grad = [], 0.0, 0.0
        for start, stacked, shares in groups[b]:
            up = stack_heads(up_all[:, start : start + HEADS * HS])
            low = shares.astype(BF).reshape(HEADS * half, half)
            shares_grad = dot(up, value, NT).reshape(HEADS, half, half)
            value_grad += dot(low, up, TN)
            spread = jnp.sum(shares * shares_grad, axis=-1, keepdims=True)
            score_grad = (shares * (shares_grad - spread)).astype(BF).reshape(HEADS * half, half)
            query_grads.append(unstack_heads(dot(score_grad, key, NN), half) * SCALE)
            key_grad += dot(score_grad, stacked, TN) * SCALE
        query_grad = jnp.concatenate(query_grads, axis=1)
        grads.append(jnp.concatenate([query_grad, key_grad, value_grad], axis=1))
        if between is not None:
            between()
    joined = join_batches(grads, own)
    tiles = []
    for j in range(5):
        tile = joined[:, j * 128 : (j + 1) * 128]
        turned = tile * cos - swap_halves(tile) * sin
        if j == 4:
            lane = lax.broadcasted_iota(jnp.int32, tile.shape, 1)
            turned = jnp.where(lane < HS, turned, tile)
        tiles.append(turned)
    return jnp.concatenate(tiles, axis=1)


def level_rows(table, own):
    return jnp.concatenate([table[owner * OWN[0] : owner * OWN[0] + own, :] for owner in range(T)], axis=0)


def norm_back(source, gain, upstream):
    inverse = lax.rsqrt(mean_square(source) + 1e-05)
    unit = source * inverse
    gain_part = jnp.sum(upstream * unit, axis=0, keepdims=True)
    scaled = upstream * gain
    return inverse * (scaled - unit * jnp.mean(scaled * unit, axis=-1, keepdims=True)), gain_part


def backward_kernel(n, *refs):
    it = iter(refs)
    w_all, gain, cot_own, cosine, sine, act_own, last_gug = [next(it) for _ in range(7)]
    allowed = [None] + [next(it) for _ in range(2)]
    saved_in = []
    for level in range(RECUR):
        saved_in.append({k: next(it) for k in saved_names(level)})
    dg_out = [next(it) for _ in range(2)]
    gug_out = [next(it) for _ in range(2)]
    og_out = [None] + [next(it) for _ in range(2)]
    qkvg_out = [None] + [next(it) for _ in range(2)]
    grad_out, gain_part = next(it), next(it)
    w = next(it)
    saved = []
    for level in range(RECUR):
        saved.append({k: next(it) for k in saved_in[level]})
    dg = [next(it) for _ in range(2)]
    gug = [next(it) for _ in range(2)]
    og = [None] + [next(it) for _ in range(2)]
    qkvg = [None] + [next(it) for _ in range(2)]
    gug.append(next(it))
    grad, upstream, factors = next(it), next(it), next(it)
    part, relay = next(it), next(it)
    sums = [(next(it), next(it)) for _ in range(5)]
    row_sems = [next(it) for _ in range(6)]
    insem, outsem = next(it), next(it)

    p = Place(n)
    width = w.shape[0]
    rows = Rows(p, part, relay, sums, row_sems)
    hidden_cols = (COLS - GU) // 3
    loads, writes = {}, []

    def load(name, src, dst):
        copy = pltpu.make_async_copy(src, dst, insem.at[len(loads)])
        copy.start()
        loads[name] = copy

    def write(src, dst):
        copy = pltpu.make_async_copy(src, dst, outsem.at[len(writes)])
        copy.start()
        writes.append(copy)

    def columns(start, size):
        load(("w", start), w_all.at[:, pl.ds(start, size)], w.at[:, pl.ds(start, size)])

    last = RECUR - 1
    load("gug", last_gug, gug[last])
    columns(GU, 2 * hidden_cols)
    load("grad", cot_own, grad)
    load(("first", last), saved_in[last]["first"], saved[last]["first"])
    columns(WO, 512)
    for name in ("qkv", "hidden"):
        load((name, last), saved_in[last][name], saved[last][name])
    columns(QKV, 640)
    columns(WD, hidden_cols)
    for level in (1, 0):
        for name in saved_in[level]:
            load((name, level), saved_in[level][name], saved[level][name])
    p.barrier(False)
    gain_part[...] = jnp.zeros_like(gain_part)

    for level in range(last, -1, -1):
        own = OWN[level]
        count = T * own
        s = saved[level]
        base = 2 * (last - level)
        present = act_own[level, 0:own, :]
        if level == last:
            loads["grad"].wait()
            loads["gug"].wait()
            loads["w", GU].wait()
        else:
            dg[level][p.t] = (present * grad[0:own, :]).astype(BF)
            view = dg[level].reshape(2, 2, own, width)
            rows.gather_start(base, view)
            loads["gu", level].wait()

            @pl.loop(0, hidden_cols // 128)
            def _(j):
                low = pl.ds(pl.multiple_of(j * 128, 128), 128)
                high = pl.ds(pl.multiple_of(hidden_cols + j * 128, 128), 128)
                gate = s["gu"][:, low].astype(F32)
                upward = s["gu"][:, high].astype(F32)
                sigma = jax.nn.sigmoid(gate)
                factors[0:count, low] = upward * sigma * (1.0 + gate * (1.0 - sigma))
                factors[0:count, high] = gate * sigma

            if level == 1:
                loads["w", WD].wait()
            rows.gather_finish(base, view)
            write(dg[level], dg_out[level])

            def hidden_block(start, size):
                wcols = pl.ds(pl.multiple_of(WD + start, 128), size)
                product_grad = dot(dg[level][...].reshape(count, width), w[:, wcols], NN)
                low = pl.ds(pl.multiple_of(start, 128), size)
                high = pl.ds(pl.multiple_of(hidden_cols + start, 128), size)
                gug[level][:, low] = (product_grad * factors[0:count, low]).astype(BF)
                gug[level][:, high] = (product_grad * factors[0:count, high]).astype(BF)

            @pl.loop(0, hidden_cols // 256)
            def _(j):
                hidden_block(j * 256, 256)

            if hidden_cols % 256:
                hidden_block(hidden_cols // 256 * 256, 128)
            write(gug[level], gug_out[level])

        def mlp_tile(cols):
            return dot(gug[level][...], w[cols, GU : GU + 2 * hidden_cols], NT)

        def take(cols, total):
            upstream[0:own, cols] = total

        rows.reduce(base, own, mlp_tile, take)
        loads["first", level].wait()
        update, add = norm_back(s["first"][...], gain[1:2, :], upstream[0:own, :])
        grad[0:own, :] += update
        gain_part[1:2, :] += add
        if level == 0:
            break
        og[level][p.t] = (present * grad[0:own, :]).astype(BF)
        view = og[level].reshape(2, 2, own, width)
        rows.gather_start(base + 1, view)
        loads["qkv", level].wait()
        rotated = split_batches(s["qkv"][...].astype(F32), own)
        groups = [list(share_groups(rotated[b], allowed[level][b])) for b in range(MB)]
        rows.gather_finish(base + 1, view)
        write(og[level], og_out[level])
        if level == last:
            loads["w", WO].wait()
        attended_grad = dot(og[level][...].reshape(count, width), w[:, WO : WO + 512], NN)
        cos, sin = level_rows(cosine, own), level_rows(sine, own)
        qkvg[level][...] = attention_back(rotated, groups, attended_grad, cos, sin, own).astype(BF)
        write(qkvg[level], qkvg_out[level])
        if level == last:
            loads["w", QKV].wait()

        def attention_tile(cols):
            return dot(qkvg[level][...], w[cols, QKV : QKV + 640], NT)

        rows.reduce(base + 1, own, attention_tile, take)
        loads["hidden", level].wait()
        update, add = norm_back(s["hidden"][...], gain[0:1, :], upstream[0:own, :])
        grad[0:own, :] += update
        gain_part[0:1, :] += add

    write(grad, grad_out)
    for copy in writes:
        copy.wait()


def saved_names(level):
    return (("gu", "first"), ("gu", "first", "qkv", "hidden"), ("first", "qkv", "hidden"))[level]


def backward(n, w_all, gain, cot_own, tables, saved):
    width = w_all.shape[0]
    hidden_cols = (COLS - GU) // 3
    vmem = pl.BlockSpec(memory_space=pltpu.VMEM)
    hbm = pl.BlockSpec(memory_space=pl.ANY)
    operands = [w_all, gain, cot_own, tables["cosine"], tables["sine"], tables["act"], saved[RECUR - 1]["gu"]]
    operands += list(tables["masks"][1:])
    specs = [hbm, vmem, hbm] + [vmem] * 3 + [hbm] + [vmem] * 2
    used = []
    for level in range(RECUR):
        for name in saved_names(level):
            operands.append(saved[level][name])
            specs.append(hbm)
            used.append(saved[level][name])
    outs = [((T, own, width), BF) for own in OWN[:2]]
    outs += [((T * own, 2 * hidden_cols), BF) for own in OWN[:2]]
    outs += [((T, own, width), BF) for own in OWN[1:]]
    outs += [((T * own, 640), BF) for own in OWN[1:]]
    scratch = [pltpu.VMEM(w_all.shape, BF)] + [pltpu.VMEM(u.shape, u.dtype) for u in used]
    scratch += [pltpu.VMEM(*entry) for entry in outs] + [pltpu.VMEM((T * OWN[2], 2 * hidden_cols), BF)]
    outs += [((OWN[0], width), F32), ((8, width), F32)]
    out_specs = [hbm] * (len(outs) - 1) + [vmem]
    scratch += [pltpu.VMEM((OWN[0], width), F32)] * 2 + [pltpu.VMEM((T * OWN[0], 2 * hidden_cols), F32)]
    scratch += [pltpu.VMEM((2, 2, OWN[0], width), BF), pltpu.VMEM((OWN[0], width), BF)]
    for own in (OWN[2], OWN[2], OWN[1], OWN[1], OWN[0]):
        scratch += [pltpu.VMEM((2, own, width), BF), pltpu.VMEM((own, width), BF)]
    dma = pltpu.SemaphoreType.DMA
    chunks = width // DC
    scratch += [dma((5, chunks))] * 4 + [dma((5, 3))] * 2 + [dma((24,)), dma((16,))]
    res = pl.pallas_call(
        functools.partial(backward_kernel, n),
        out_shape=[jax.ShapeDtypeStruct(*entry) for entry in outs],
        in_specs=specs,
        out_specs=out_specs,
        scratch_shapes=scratch,
        compiler_params=pltpu.CompilerParams(
            collective_id=2, has_side_effects=True, vmem_limit_bytes=62 << 20
        ),
    )(*operands)
    return {
        "dg": res[0:2],
        "gug": res[2:4],
        "og": res[4:6],
        "qkvg": res[6:8],
        "grad": res[8],
        "gain_part": res[9],
    }


PIECE = 384
SEGMENTS = (("down", 1408), ("gu", 2816), ("out", 512), ("qkv", 640))
DEPTH = 3
FIRST = 1
JOINT = 2
PLACES = COLS // PIECE + FIRST


def cut_pieces():
    pieces = [[] for _ in range(COLS // PIECE)]
    at = 0
    for which, size in SEGMENTS:
        done = 0
        while done < size:
            k, inside = divmod(at, PIECE)
            cols = min(size - done, PIECE - inside)
            pieces[k].append((which, done, cols, inside))
            done += cols
            at += cols
    return pieces


def gradient_kernel(n, *refs):
    it = iter(refs)
    (w_all, gain, cosine, sine, act_own, allowed, back) = [next(it) for _ in range(7)]
    grad_in, gain_in, fin_in, hidden_in, qkv_in, first_in = [next(it) for _ in range(6)]
    x_in = {name: [next(it) for _ in range(3)] for name in ("down", "gu", "qkv")}
    x_in["out"] = [None] + [next(it) for _ in range(2)]
    y_in = {name: [next(it) for _ in range(3)] for name in ("down", "gu", "out")}
    y_in["qkv"] = [None] + [next(it) for _ in range(2)]
    (act_out, tok_out, dq, dk, dv, dwo, dgate, dup, dwd, gain_sum) = [next(it) for _ in range(10)]
    og_hbm, fin_all, grad_all = [next(it) for _ in range(3)]
    w = next(it)
    y = {name: next(it) for name in ("down", "gu", "out", "qkv")}
    xm, xl, xraw = next(it), next(it), next(it)
    og, hidden, qkv, grad, upstream, gains = [next(it) for _ in range(6)]
    fin, first = next(it), next(it)
    gpeers = next(it)
    stage, landed, across, across_own = [next(it) for _ in range(4)]
    window_tmp = next(it)
    gmate_stage, gmate, gline, gline_own = [next(it) for _ in range(4)]
    final, turned, last_stage, last_landed, fsend, frecv = [next(it) for _ in range(6)]
    chunk_in, fin_chunk, act_chunk, tok_chunk = [next(it) for _ in range(4)]
    part, relay = next(it), next(it)
    sums = [(next(it), next(it))] * 2
    row_sems = [next(it) for _ in range(6)]
    msend, mrecv, lsend, lrecv, lrecv2 = [next(it) for _ in range(5)]
    tsend, trecv = next(it), next(it)
    insem, xsem, outsem, finsem, loadsem = [next(it) for _ in range(5)]

    p = Place(n)
    width = w.shape[0]
    line = p.line
    chunk_rows = width // n
    window = max(128, chunk_rows)
    rows = Rows(p, part, relay, sums, row_sems)
    own = OWN[0]
    count = T * own
    starts = [0, T * OWN[0], T * (OWN[0] + OWN[1])]
    total_rows = T * sum(OWN)
    hidden_cols = (COLS - GU) // 3
    loads, writes = {}, []

    def load(name, src, dst):
        copy = pltpu.make_async_copy(src, dst, insem.at[len(loads)])
        copy.start()
        loads[name] = copy

    def write(src, dst):
        copy = pltpu.make_async_copy(src, dst, outsem.at[len(writes)])
        copy.start()
        writes.append(copy)

    load("grad", grad_in, grad)
    for name in ("down", "gu"):
        for level in range(RECUR):
            load((name, level), y_in[name][level], y[name].at[pl.ds(starts[level], T * OWN[level])])
    load("w", w_all.at[:, pl.ds(0, GU)], w)
    load("fin", fin_in, fin)
    load("first", first_in, first)
    load("qkv", qkv_in, qkv)
    load("hidden", hidden_in, hidden)
    for level in range(RECUR):
        load(("out", level), y_in["out"][level], y["out"].at[pl.ds(starts[level], T * OWN[level])])
    for level in (1, 2):
        load(("qkv", level), y_in["qkv"][level], y["qkv"].at[pl.ds(starts[level], T * OWN[level])])
    p.barrier(True)

    def x_source(which, level):
        return og_hbm if which == "out" and level == 0 else x_in[which][level]

    def level_slice(level):
        return pl.ds(sum(OWN[:level]) * T, OWN[level] * T)

    def x_copy(which, chunk, slot, level, sem):
        start = pl.multiple_of(chunk * chunk_rows // window * window, window)
        src = x_source(which, level).reshape(T * OWN[level], width)
        return pltpu.make_async_copy(
            src.at[:, pl.ds(start, window)], xraw.at[slot, level_slice(level)], sem.at[slot, level]
        )

    pieces = cut_pieces()
    count_pieces = len(pieces)
    held = {}

    def x_load(which, parity, buffer, sem):
        if held.get(id(buffer)) == which:
            return
        held[id(buffer)] = which

        for level in range(RECUR):
            x_copy(which, parity, 0, level, sem).start()

        @pl.loop(0, line)
        def _(i):
            @pl.when(i + 1 < line)
            def _():
                for level in range(RECUR):
                    x_copy(which, 2 * (i + 1) + parity, lax.rem(i + 1, 2), level, sem).start()

            for level in range(RECUR):
                x_copy(which, 2 * i + parity, lax.rem(i, 2), level, sem).wait()
            buffer[i] = xraw[lax.rem(i, 2)].T

    def product(which, start, cols, parity, buffer, j):
        some = buffer[pl.ds(j * JOINT, JOINT)].reshape(JOINT * window, total_rows)
        value = dot(some, y[which][:, start : start + cols], NN).reshape(JOINT, window, cols)
        if window == chunk_rows:
            return value
        window_tmp[:, :, 0:cols] = value
        return window_tmp[:, pl.ds(pl.multiple_of(parity * chunk_rows, chunk_rows), chunk_rows), 0:cols]

    places = []
    for k in range(count_pieces):
        places += [("own", k), ("other", k)] if k < FIRST else [("normal", k)]

    def columns(q):
        return pl.ds(pl.multiple_of(q * PIECE, 128), PIECE)

    def mate_copy(q, i):
        return remote(
            stage.at[lax.rem(q, DEPTH), i], landed.at[i, :, columns(q)], msend.at[q, i], mrecv.at[q, i], p.mate
        )

    def mates(k):
        q = k + FIRST
        if q >= 2 * FIRST + DEPTH:

            @pl.loop(0, line)
            def _(i):
                mate_copy(q - DEPTH, i).wait_send()

        for number, (which, start, cols, inside) in enumerate(pieces[k]):
            x_load(which, 1 - p.b, xm, xsem.at[0])

            last_part = number == len(pieces[k]) - 1

            @pl.loop(0, line // JOINT)
            def _(j):
                value = product(which, start, cols, 1 - p.b, xm, j)
                some = pl.ds(j * JOINT, JOINT)
                stage[q % DEPTH, some, :, inside : inside + cols] = value.astype(BF)
                if last_part:
                    for i in range(JOINT):
                        mate_copy(q, j * JOINT + i).start()

    def own_terms(q):
        kind, k = places[q]
        for number, (which, start, cols, inside) in enumerate(pieces[k]):
            parity = 1 - p.b if kind == "other" else p.b
            buffer, sem = (xm, xsem.at[0]) if kind == "other" else (xl, xsem.at[1])
            x_load(which, parity, buffer, sem)
            at = pl.ds(q * PIECE + inside, cols)

            @pl.loop(0, line // JOINT)
            def _(j):
                value = product(which, start, cols, parity, buffer, j)
                some = pl.ds(j * JOINT, JOINT)
                if kind == "normal":
                    if number == 0:
                        for i in range(JOINT):
                            mate_copy(q, j * JOINT + i).wait_recv()
                    value = value + landed[some, :, at].astype(F32)
                landed[some, :, at] = value.astype(BF)

    def along(q, i, right):
        return remote(
            landed.at[i, :, columns(q)],
            across.at[i, :, columns(q)],
            lsend.at[q, i],
            lrecv.at[q, i],
            p.right if right else p.left,
        )

    def along_last(q, i):
        return remote(
            landed.at[i, :, columns(q)], across_own.at[:, columns(q)], lsend.at[q, i], lrecv2.at[q], p.left
        )

    def relay_step(q, i, receives):
        @pl.when(receives)
        def _():
            along(q, i, True).wait_recv()
            landed[i, :, columns(q)] = (
                landed[i, :, columns(q)].astype(F32) + across[i, :, columns(q)].astype(F32)
            ).astype(BF)

    def relay_pieces(slot):
        q_right = slot - p.a
        q_left = slot - (line - 1 - p.a)

        @pl.when((q_right >= 0) & (q_right < PLACES))
        def _():
            @pl.loop(0, line)
            def _(step):
                i = line - 1 - step

                @pl.when(i > p.a)
                def _():
                    relay_step(q_right, i, p.has_left)
                    along(q_right, i, True).start()

        @pl.when((q_left >= 0) & (q_left < PLACES))
        def _():
            @pl.loop(0, line)
            def _(i):
                @pl.when(i < p.a)
                def _():
                    relay_step(q_left, i, p.has_right)
                    pl.when(i < p.a - 1)(lambda: along(q_left, i, False).start())
                    pl.when(i == p.a - 1)(lambda: along_last(q_left, i).start())

    def last_copy(j):
        return remote(last_stage.at[j], last_landed.at[j], fsend.at[j], frecv.at[j], p.mate)

    staged, turning = [], []

    def line_sum(q, buffer):
        here = pl.ds(q * PIECE, PIECE)
        buffer[...] = landed[p.a, :, here].astype(F32)

        @pl.when(p.has_left)
        def _():
            along(q, p.a, True).wait_recv()
            buffer[...] += across[p.a, :, here].astype(F32)

        @pl.when(p.has_right)
        def _():
            along_last(q, p.a).wait_recv()
            buffer[...] += across_own[:, here].astype(F32)

    def finish(q):
        kind, k = places[q]
        if kind == "own":
            return
        if kind == "other":
            if len(staged) >= 2:
                for copy in staged[len(staged) - 2]:
                    copy.wait()
                staged[len(staged) - 2] = []
            buffer = final.at[len(staged) % 2]
            line_sum(q, buffer)
            last_stage[k] = buffer[...].astype(BF)
            last_copy(k).start()
        else:
            results(q)
        if q >= 3 and places[q - 3][0] == "own":
            results(q - 3)

    def results(q):
        kind, k = places[q]
        number = len(staged)
        if number >= 2:
            for copy in staged[number - 2]:
                copy.wait()
        buffer = final.at[number % 2]
        line_sum(q, buffer)
        if kind == "own":
            last_copy(k).wait_recv()
            buffer[...] += last_landed[k].astype(F32)
            last_copy(k).wait_send()
        copies = []

        def out(src, dst):
            copy = pltpu.make_async_copy(src, dst, finsem.at[k, len(copies)])
            copy.start()
            copies.append(copy)

        for which, start, cols, inside in pieces[k]:
            if which in ("down", "out"):
                for copy in turning:
                    copy.wait()
                turning.clear()
                turned[inside : inside + cols, :] = buffer[:, inside : inside + cols].T
                target = dwd if which == "down" else dwo
                copy = pltpu.make_async_copy(
                    turned.at[pl.ds(inside, cols)], target.at[pl.ds(start, cols)], finsem.at[k, 7]
                )
                copy.start()
                turning.append(copy)
            elif which == "gu":
                middle = min(max(hidden_cols - start, 0), cols)
                if middle:
                    out(buffer.at[:, pl.ds(inside, middle)], dgate.at[:, pl.ds(start, middle)])
                if middle < cols:
                    out(
                        buffer.at[:, pl.ds(inside + middle, cols - middle)],
                        dup.at[:, pl.ds(start + middle - hidden_cols, cols - middle)],
                    )
            else:
                queries = min(max(512 - start, 0), cols)
                if queries:
                    out(buffer.at[:, pl.ds(inside, queries)], dq.at[:, pl.ds(start, queries)])
                if queries < cols:
                    both = buffer[:, inside + queries : inside + queries + 2 * HS].T
                    dk[...] = both[0:HS]
                    dv[...] = both[HS : 2 * HS]
        staged.append(copies)

    def drain():
        @pl.loop(0, PLACES)
        def _(q):
            @pl.loop(0, line)
            def _(i):
                pl.when(q >= max(PLACES - DEPTH, 2 * FIRST))(lambda: mate_copy(q, i).wait_send())
                pl.when(i != p.a)(lambda: along(q, i, True).wait_send())

    loads["grad"].wait()
    present = act_own[0, 0:own, :]
    og[p.t] = (present * grad[...]).astype(BF)
    view = og.reshape(2, 2, own, width)
    rows.gather_start(0, view)
    for level in range(RECUR):
        loads["down", level].wait()
    sent = [FIRST]

    def mates_upto(k):
        while sent[0] <= min(k, count_pieces - 1):
            mates(sent[0])
            sent[0] += 1

    slots = [0]

    def slot():
        s = slots[0]
        slots[0] += 1
        if s < PLACES:
            own_terms(s)
        relay_pieces(s)
        if 0 <= s - line + 1 < PLACES:
            finish(s - line + 1)
        mates_upto(s - FIRST + DEPTH)

    mates(FIRST)
    sent[0] += 1
    slot()
    rows.gather_finish(0, view)
    write(og, og_hbm)
    for level in range(RECUR):
        loads["gu", level].wait()
    mates_upto(FIRST + 2)
    loads["w"].wait()
    loads["qkv"].wait()
    attended_grad = dot(og[...].reshape(count, width), w[:, WO : WO + 512], NN)
    rotated = split_batches(qkv[...].astype(F32), own)
    groups = [share_groups(rotated[b], allowed[b]) for b in range(MB)]
    y["qkv"][0:count, :] = attention_back(
        rotated, groups, attended_grad, cosine[...], sine[...], own, slot
    ).astype(BF)
    slot()

    def attention_tile(cols):
        return dot(y["qkv"][0:count, :], w[cols, QKV : QKV + 640], NT)

    def take(cols, total):
        upstream[:, cols] = total

    rows.reduce(0, own, attention_tile, take)
    loads["hidden"].wait()
    update, add = norm_back(hidden[...], gain[0:1, :], upstream[...])
    grad[...] += update
    gains[...] = gain_in[...]
    gains[0:1, :] += add
    for which in range(3):
        peers_copy(p, grad, grad_all, tsend.at[1], trecv.at[1], which).start()
        peers_copy(p, gains, gpeers, tsend.at[2], trecv.at[2], which).start()
    pltpu.make_async_copy(grad, grad_all.at[p.t], tsend.at[1, 3]).start()
    gpeers[p.t] = gains[...]
    for level in range(RECUR):
        loads["out", level].wait()
    for level in (1, 2):
        loads["qkv", level].wait()
    for copy in writes:
        copy.wait()

    def wait_peers(i, src, dst, local=True):
        for which in range(3):
            copy = peers_copy(p, src, dst, tsend.at[i], trecv.at[i], which)
            copy.wait_recv()
            copy.wait_send()
        if local:
            pltpu.make_async_copy(src, dst.at[p.t], tsend.at[i, 3]).wait()

    def last_branch():
        wait_peers(1, grad, grad_all)
        loads["fin"].wait()
        loads["first"].wait()
        deepest = OWN[2]
        active = act_own[RECUR - 1, 0:deepest, :]

        def fetch(src, dst, i):
            return pltpu.make_async_copy(src, dst, loadsem.at[i])

        def last_tile(cols):
            some = pl.ds(cols.start, DC)
            copies = (
                fetch(w_all.at[some, pl.ds(WD, GU)], w.at[pl.ds(0, DC)], 0),
                fetch(
                    w_all.at[some, pl.ds(WD + GU, hidden_cols - GU)],
                    w.at[pl.ds(DC, DC), pl.ds(0, hidden_cols - GU)],
                    1,
                ),
            )
            for copy in copies:
                copy.start()
            for copy in copies:
                copy.wait()
            left = y["down"][starts[2] : starts[2] + T * deepest, :]
            return dot(left[:, 0:GU], w[0:DC, :], NT) + dot(left[:, GU:], w[DC : 2 * DC, 0 : hidden_cols - GU], NT)

        def last_finish(cols, total):
            fin[0:deepest, cols] = (first[:, cols] + active * total).astype(BF)

        rows.reduce(1, deepest, last_tile, last_finish)
        for which in range(3):
            peers_copy(p, fin, fin_all, tsend.at[0], trecv.at[0], which).start()
        pltpu.make_async_copy(fin, fin_all.at[p.t], tsend.at[0, 3]).start()

    def outputs():
        wait_peers(0, fin, fin_all)
        mine = back[...]

        @pl.loop(0, width // OC)
        def _(c):
            cols = pl.ds(pl.multiple_of(c * OC, OC), OC)
            first = pltpu.make_async_copy(fin_all.at[:, :, cols], fin_chunk, loadsem.at[0])
            second = pltpu.make_async_copy(grad_all.at[:, :, cols], chunk_in, loadsem.at[1])
            first.start()
            second.start()
            first.wait()
            second.wait()
            act_chunk[...] = dot(mine, fin_chunk[...].reshape(count, OC), NN).astype(BF).reshape(
                MB, own // MB, OC
            )
            value = chunk_in[...].reshape(count, OC)
            high = value.astype(BF)
            rest = value - high.astype(F32)
            middle = rest.astype(BF)
            low = (rest - middle.astype(F32)).astype(BF)
            total = dot(mine, high, NN) + (dot(mine, middle, NN) + dot(mine, low, NN))
            tok_chunk[...] = total.reshape(MB, own // MB, OC)
            third = pltpu.make_async_copy(act_chunk, act_out.at[:, :, cols], loadsem.at[0])
            fourth = pltpu.make_async_copy(tok_chunk, tok_out.at[:, :, cols], loadsem.at[1])
            third.start()
            fourth.start()
            third.wait()
            fourth.wait()

    def gain_tile(chunk):
        start = pl.multiple_of(chunk * chunk_rows // window * window, window)
        return (
            gpeers[0, :, pl.ds(start, window)]
            + gpeers[1, :, pl.ds(start, window)]
            + gpeers[2, :, pl.ds(start, window)]
            + gpeers[3, :, pl.ds(start, window)]
        )

    last = PLACES

    def gain_mate(i):
        return remote(gmate_stage.at[i], gmate.at[i], msend.at[last, i], mrecv.at[last, i], p.mate)

    def gain_along(i, right):
        return remote(
            gmate.at[i], gline.at[i], lsend.at[last, i], lrecv.at[last, i], p.right if right else p.left
        )

    def gain_last(i):
        return remote(gmate.at[i], gline_own, lsend.at[last, i], lrecv2.at[last], p.left)

    def gain_mates():
        wait_peers(2, gains, gpeers, False)

        @pl.loop(0, line)
        def _(i):
            gmate_stage[i] = gain_tile(2 * i + 1 - p.b)
            gain_mate(i).start()

    def gain_lines():
        @pl.loop(0, line)
        def _(step):
            odd = lax.rem(step, 2)
            i = jnp.where(odd == 1, step // 2, line - 1 - step // 2)

            @pl.when(i != p.a)
            def _():
                gain_mate(i).wait_recv()
                gmate[i] += gain_tile(2 * i + p.b)

                @pl.when(((i > p.a) & p.has_left) | ((i < p.a) & p.has_right))
                def _():
                    gain_along(i, True).wait_recv()
                    gmate[i] += gline[i]

                pl.when(i > p.a)(lambda: gain_along(i, True).start())
                pl.when(i < p.a - 1)(lambda: gain_along(i, False).start())
                pl.when(i == p.a - 1)(lambda: gain_last(i).start())

        gain_mate(p.a).wait_recv()
        gain_sum[...] = gain_tile(2 * p.a + p.b) + gmate[p.a]

        @pl.when(p.has_left)
        def _():
            gain_along(p.a, True).wait_recv()
            gain_sum[...] += gline[p.a]

        @pl.when(p.has_right)
        def _():
            gain_last(p.a).wait_recv()
            gain_sum[...] += gline_own[...]

        @pl.loop(0, line)
        def _(i):
            gain_mate(i).wait_send()
            pl.when(i != p.a)(lambda: gain_along(i, True).wait_send())

    for s in range(slots[0], PLACES + line - 1):
        slot()
        if s == 5:
            gain_mates()
        if s == 7:
            gain_lines()
        if s == 9:
            last_branch()
        if s == 11:
            outputs()
    drain()
    for copies in staged[-2:] + [turning]:
        for copy in copies:
            copy.wait()


def gradients(n, w_all, gain, tables, saved, bwd, fin):
    width = w_all.shape[0]
    hidden_cols = (COLS - GU) // 3
    line = n // 2
    chunk_rows = width // n
    window = max(128, chunk_rows)
    vmem = pl.BlockSpec(memory_space=pltpu.VMEM)
    hbm = pl.BlockSpec(memory_space=pl.ANY)
    total_rows = T * sum(OWN)
    own = OWN[0]
    operands = [w_all, gain, tables["cosine"], tables["sine"], tables["act"], tables["masks"][0], tables["back"]]
    specs = [hbm] + [vmem] * 6
    operands += [bwd["grad"], bwd["gain_part"], fin, saved[0]["hidden"], saved[0]["qkv"], saved[RECUR - 1]["first"]]
    specs += [hbm, vmem, hbm, hbm, hbm, hbm]
    streams = list(bwd["dg"]) + [s["mixed"] for s in saved] + [s["normed"] for s in saved] + list(bwd["og"])
    streams += [s["prod"] for s in saved] + list(bwd["gug"]) + [s["att"] for s in saved] + list(bwd["qkvg"])
    operands += streams
    specs += [hbm] * len(streams)
    outs = [
        ((MB, own // MB, width), BF),
        ((MB, own // MB, width), F32),
        ((chunk_rows, 512), F32),
        ((HS, chunk_rows), F32),
        ((HS, chunk_rows), F32),
        ((512, chunk_rows), F32),
        ((chunk_rows, hidden_cols), F32),
        ((chunk_rows, hidden_cols), F32),
        ((hidden_cols, chunk_rows), F32),
        ((8, window), F32),
        ((T, own, width), BF),
        ((T, own, width), BF),
        ((T, own, width), F32),
    ]
    out_specs = [hbm, hbm, hbm, vmem, vmem, hbm, hbm, hbm, hbm, vmem, hbm, hbm, hbm]
    scratch = [pltpu.VMEM((width, GU), BF)]
    scratch += [pltpu.VMEM((total_rows, c), BF) for c in (hidden_cols, 2 * hidden_cols, 512, 640)]
    scratch += [pltpu.VMEM((line, window, total_rows), BF)] * 2 + [pltpu.VMEM((2, total_rows, window), BF)]
    scratch += [
        pltpu.VMEM((T, own, width), BF),
        pltpu.VMEM((own, width), F32),
        pltpu.VMEM((T * own, 640), BF),
        pltpu.VMEM((own, width), F32),
        pltpu.VMEM((own, width), F32),
        pltpu.VMEM((8, width), F32),
        pltpu.VMEM((own, width), BF),
        pltpu.VMEM((OWN[2], width), F32),
        pltpu.VMEM((T, 8, width), F32),
    ]
    scratch += [
        pltpu.VMEM((DEPTH, line, chunk_rows, PIECE), BF),
        pltpu.VMEM((line, chunk_rows, PLACES * PIECE), BF),
        pltpu.VMEM((line, chunk_rows, PLACES * PIECE), BF),
        pltpu.VMEM((chunk_rows, PLACES * PIECE), BF),
        pltpu.VMEM((JOINT, window, PIECE) if window > chunk_rows else (1, 8, 128), F32),
    ]
    scratch += [pltpu.VMEM((line, 8, window), F32)] * 3 + [pltpu.VMEM((8, window), F32)]
    scratch += [pltpu.VMEM((2, chunk_rows, PIECE), F32), pltpu.VMEM((PIECE, chunk_rows), F32)]
    scratch += [pltpu.VMEM((FIRST, chunk_rows, PIECE), BF)] * 2
    scratch += [pltpu.SemaphoreType.DMA((FIRST,))] * 2
    scratch += [pltpu.VMEM((T, own, OC), F32), pltpu.VMEM((T, own, OC), BF)]
    scratch += [pltpu.VMEM((MB, own // MB, OC), BF), pltpu.VMEM((MB, own // MB, OC), F32)]
    scratch += [pltpu.VMEM((2, 2, own, width), BF), pltpu.VMEM((own, width), BF)]
    scratch += [pltpu.VMEM((2, own, width), BF), pltpu.VMEM((own, width), BF)]
    dma = pltpu.SemaphoreType.DMA
    chunks = width // DC
    k = PLACES + 1
    scratch += [dma((2, chunks))] * 4 + [dma((2, 3))] * 2
    scratch += [dma((k, line))] * 4 + [dma((k,))]
    scratch += [dma((3, 4)), dma((3, 3))]
    scratch += [dma((24,)), dma((2, 2, RECUR)), dma((4,)), dma((k, 8)), dma((2,))]
    res = pl.pallas_call(
        functools.partial(gradient_kernel, n),
        out_shape=[jax.ShapeDtypeStruct(*entry) for entry in outs],
        in_specs=specs,
        out_specs=out_specs,
        scratch_shapes=scratch,
        compiler_params=pltpu.CompilerParams(
            collective_id=3, has_side_effects=True, vmem_limit_bytes=63 << 20
        ),
    )(*operands)
    return res


def hand_out_kernel(count, *refs):
    held, sems = refs[2 * count : 3 * count], refs[3 * count]
    into = [pltpu.make_async_copy(refs[i], held[i], sems.at[0, i]) for i in range(count)]
    out = [pltpu.make_async_copy(held[i], refs[count + i], sems.at[1, i]) for i in range(count)]
    for copy in into:
        copy.start()
    for i in range(count):
        into[i].wait()
        out[i].start()
    for copy in out:
        copy.wait()


def hand_out(values):
    hbm = pl.BlockSpec(memory_space=pl.ANY)
    count = len(values)
    return pl.pallas_call(
        functools.partial(hand_out_kernel, count),
        out_shape=[jax.ShapeDtypeStruct(v.shape, v.dtype) for v in values],
        in_specs=[hbm] * count,
        out_specs=[hbm] * count,
        scratch_shapes=[pltpu.VMEM(v.shape, v.dtype) for v in values] + [pltpu.SemaphoreType.DMA((2, count))],
        compiler_params=pltpu.CompilerParams(vmem_limit_bytes=62 << 20),
    )(*values)


def shards(n, *args):
    tokens, depth, lengths, cotangent = args[:4]
    attn_gain, mlp_gain = args[11:]
    index = lax.axis_index("tensor")
    w_all, gain, fin, cot_own, last_dg, tables, saved = forward(
        n, tokens, depth, lengths[:, 0], cotangent, args[4:11], attn_gain, mlp_gain
    )
    bwd = backward(n, w_all, gain, cot_own, tables, saved)
    bwd["dg"] = list(bwd["dg"]) + [last_dg]
    bwd["gug"] = list(bwd["gug"]) + [saved[RECUR - 1]["gu"]]
    res = gradients(n, w_all, gain, tables, saved, bwd, fin)
    gain_sum = res[9]
    activations, tokens_grad, dq, dk, dv, dwo, dgate, dup, dwd = hand_out(res[:9])
    each = attn_gain.shape[0]
    window = gain_sum.shape[1]
    start = lax.rem((lax.axis_index("dp") * T + index) * each, window)
    both = lax.dynamic_slice_in_dim(gain_sum, start, each, axis=1)
    return (activations, tokens_grad, dq, dk.T, dv.T, dwo, dgate, dup, dwd, both[0], both[1])


def solution(mesh):
    rows = P(None, ("dp", "tensor"), None)
    weight_specs = (P("dp", "tensor"),) * 3 + (P("tensor", "dp"),) + (P("dp", "tensor"),) * 2 + (P("tensor", "dp"),)
    gain_specs = (P(("dp", "tensor")),) * 2
    return jax.shard_map(
        functools.partial(shards, mesh.shape["dp"]),
        mesh=mesh,
        in_specs=(rows, P(None, "dp"), P(None, "dp", None), rows) + weight_specs + gain_specs,
        out_specs=(rows, rows) + weight_specs + gain_specs,
        check_vma=False,
    )
```
